32 devices in a mesh: dp: 4 (over y, core), fsdp: 8 (over z, x).
Axes of the slice: x: 2, y: 2, z: 4, core: 2. Of those that a mesh axis runs over, the one named last changes fastest.
Arguments:
- inputs: bfloat16 [256, 324, 256], P(('dp', 'fsdp')), may hold values from -6 to 6
- classes: int32 [256], P(('dp', 'fsdp')), may hold values from 0 to 2
- offset_table: int32 [3, 324, 324], replicated, may hold values from 0 to 323, as said below
- bias_table: float32 [4, 324], replicated, may hold values from -5 to 5
- qkv_weight: bfloat16 [256, 768], P('fsdp'), may hold values from -0.375 to 0.375
- qkv_gain: bfloat16 [768], P('fsdp'), may hold values from 0.5 to 1.5
- qkv_shift: bfloat16 [768], P('fsdp'), may hold values from -3 to 3
- out_weight: bfloat16 [512, 256], P('fsdp'), may hold values from -0.25 to 0.25
- out_gain: bfloat16 [256], P('fsdp'), may hold values from 0.5 to 1.5
- out_shift: bfloat16 [256], P('fsdp'), may hold values from -3 to 3
- up_weight: bfloat16 [256, 512], P('fsdp'), may hold values from -0.375 to 0.375
- up_gain: bfloat16 [512], P('fsdp'), may hold values from 0.5 to 1.5
- up_shift: bfloat16 [512], P('fsdp'), may hold values from -3 to 3
- down_weight: bfloat16 [512, 256], P('fsdp'), may hold values from -0.25 to 0.25
- down_gain: bfloat16 [256], P('fsdp'), may hold values from 0.5 to 1.5
- down_shift: bfloat16 [256], P('fsdp'), may hold values from -3 to 3
- cotangent: bfloat16 [256, 324, 256], P(('dp', 'fsdp')), may hold values from -6 to 6
Outputs:
- output: bfloat16 [256, 324, 256], P(('dp', 'fsdp'))
- input_grad: float32 [256, 324, 256], P(('dp', 'fsdp'))
- table_grad: float32 [4, 324], replicated
- qkv_weight_grad: float32 [256, 768], P('fsdp')
- qkv_gain_grad: float32 [768], P('fsdp')
- qkv_shift_grad: float32 [768], P('fsdp')
- out_weight_grad: float32 [512, 256], P('fsdp')
- out_gain_grad: float32 [256], P('fsdp')
- out_shift_grad: float32 [256], P('fsdp')
- up_weight_grad: float32 [256, 512], P('fsdp')
- up_gain_grad: float32 [512], P('fsdp')
- up_shift_grad: float32 [512], P('fsdp')
- down_weight_grad: float32 [512, 256], P('fsdp')
- down_gain_grad: float32 [256], P('fsdp')
- down_shift_grad: float32 [256], P('fsdp')
The draws below stay inside these ranges and needn't reach their ends.
Inputs may be any that keep to these rules, and one draw needn't show every extreme that they name: For class c of side s in (10, 14, 18) and n = s*s, the first n slots of an image hold the grid's cells in an order drawn per class; offset_table[c, q, p] = |row_q - row_p| * 18 + |col_q - col_p| for q, p < n and 0 elsewhere.
All inputs are finite; a program needn't handle non-finite values.
Results may differ from the reference program's by a relative error of at most 0.03.
Values may be sent and summed in bfloat16 or wider, within the bound.
A program may use at most 320 MiB of HBM per device.

```python
from functools import partial
import jax
import jax.numpy as jnp
from jax import lax

D = 256
HEADS = 4
KEY = 32
VALD = 128
FF = 512
GRID = 18
CLASSES = 3
SLOT = 324
NOFF = 324
QKV = 768
DH = 512
IMAGES = 256


def draw_offset_table(key, part):
    key = jax.random.fold_in(key, 7)
    tables = []
    for number in range(3):
        extent = (GRID - 8, GRID - 4, GRID)[number]
        amount = extent * extent
        placing = jax.random.permutation(jax.random.fold_in(key, number), amount)
        row_place = placing // extent
        col_place = placing % extent
        offsets = jnp.abs(row_place[:, None] - row_place[None, :]) * GRID + jnp.abs(col_place[:, None] - col_place[None, :])
        tables.append(jnp.pad(offsets, ((0, SLOT - amount), (0, SLOT - amount))))
    return jnp.stack(tables).astype(jnp.int32)


def touch_ends(values, rng, low, high):
    place = [jax.random.randint(jax.random.fold_in(rng, axis), (), 0, length) for axis, length in enumerate(values.shape)]
    longest = values.shape.index(max(values.shape))
    next_to = place[:longest] + [(place[longest] + 1) % values.shape[longest]] + place[longest + 1:]
    return values.at[tuple(place)].set(low).at[tuple(next_to)].set(high)


def levels(rng, dims, split, least, high):
    def one(axis_at, blocks):
        steps = jax.random.uniform(jax.random.fold_in(jax.random.fold_in(rng, 6), axis_at), (blocks,), jnp.float32, least / len(split), high / len(split))
        return jnp.repeat(jnp.exp(steps), dims[axis_at] // blocks).reshape((-1,) + (1,) * (len(dims) - axis_at - 1))

    factor_of = one(*split[0])
    for cut in split[1:]:
        factor_of = factor_of * one(*cut)
    return factor_of


def noise(rng, shape, width, most, cuts=(), held_as=jnp.bfloat16):
    values = jax.random.normal(rng, shape, jnp.float32) * width
    if len(cuts) > 0:
        values = levels(rng, shape, cuts, -0.22, 0.18) * values
    return jnp.clip(values, min=-most, max=most).astype(held_as)


def setup_inputs(seed: int = 0) -> dict:
    streams_of = jax.random.split(jax.random.key(seed), 18)
    return {
        "inputs": noise(streams_of[0], (IMAGES, SLOT, D), 1.0, 6.0, ((0, 32),)),
        "classes": touch_ends(jax.random.randint(streams_of[1], (IMAGES,), 0, CLASSES), jax.random.fold_in(streams_of[1], 1), 0, CLASSES - 1).astype(jnp.int32),
        "offset_table": draw_offset_table(jax.random.fold_in(streams_of[17], 71), 0),
        "bias_table": noise(streams_of[3], (HEADS, NOFF), 1.0, 5.0, (), jnp.float32),
        "qkv_weight": noise(streams_of[4], (D, QKV), D ** -0.5, 0.375, ((0, 8),)),
        "qkv_gain": jnp.clip(1.0 + 0.1 * jax.random.normal(streams_of[5], (QKV,), jnp.float32), 0.5, 1.5).astype(jnp.bfloat16),
        "qkv_shift": noise(streams_of[6], (QKV,), 0.5, 3.0, ((0, 8),)),
        "out_weight": noise(streams_of[7], (DH, D), DH ** -0.5, 0.25, ((0, 8),)),
        "out_gain": jnp.clip(1.0 + 0.1 * jax.random.normal(streams_of[8], (D,), jnp.float32), 0.5, 1.5).astype(jnp.bfloat16),
        "out_shift": noise(streams_of[9], (D,), 0.5, 3.0, ((0, 8),)),
        "up_weight": noise(streams_of[10], (D, FF), D ** -0.5, 0.375, ((0, 8),)),
        "up_gain": jnp.clip(1.0 + 0.1 * jax.random.normal(streams_of[11], (FF,), jnp.float32), 0.5, 1.5).astype(jnp.bfloat16),
        "up_shift": noise(streams_of[12], (FF,), 0.5, 3.0, ((0, 8),)),
        "down_weight": noise(streams_of[13], (FF, D), FF ** -0.5, 0.25, ((0, 8),)),
        "down_gain": jnp.clip(1.0 + 0.1 * jax.random.normal(streams_of[14], (D,), jnp.float32), 0.5, 1.5).astype(jnp.bfloat16),
        "down_shift": noise(streams_of[15], (D,), 0.5, 3.0, ((0, 8),)),
        "cotangent": noise(streams_of[16], (IMAGES, SLOT, D), 1.0, 6.0, ((0, 32),)),
    }


EPS = 1e-05
group_size = 8

@jax.custom_vjp
def low(v):
    return lax.optimization_barrier(v.astype(jnp.bfloat16)).astype(jnp.float32)

@jax.custom_vjp
def low_back(v):
    return v

def low_keep(v):
    return (low(v), None)

def low_pass(kept, grad):
    return (grad,)

def back_keep(v):
    return (v, None)

def back_low(kept, grad):
    return (low(grad),)
low.defvjp(low_keep, low_pass)
low_back.defvjp(back_keep, back_low)

def token_mask(classes):
    limits = jnp.where(classes == 0, (GRID - 8) * (GRID - 8), jnp.where(classes == 1, (GRID - 4) * (GRID - 4), SLOT))
    return (jnp.arange(SLOT)[None, :] < limits[:, None]).astype(jnp.float32)

def matmul(left, right):
    return jnp.dot(left, right, precision=lax.Precision.HIGHEST, preferred_element_type=jnp.float32)

def batch_norm(value, weights, total, gain, shift):
    center = lax.optimization_barrier(jnp.sum(value * weights, axis=0)) / total
    square = lax.optimization_barrier(jnp.sum(value * value * weights, axis=0)) / total
    scale = lax.rsqrt(square - center * center + EPS)
    return (value - center) * scale * gain + shift

def attend_group(bias_table, offset_table, pieces):
    query, keys, values, group_classes, keep = pieces
    index = offset_table[group_classes]
    bias = jnp.moveaxis(bias_table[:, index], 0, 1)
    dots = jnp.einsum('gqhk,gphk->ghqp', query, keys, precision=lax.Precision.HIGHEST)
    scores = low_back(dots * KEY ** (-0.5)) + bias
    scores = jnp.where(keep[:, None, None, :] > 0, scores, -1e+30)
    top = lax.optimization_barrier(jnp.max(scores, axis=-1, keepdims=True))
    expo = jnp.exp(scores - top)
    probs = low(expo / lax.optimization_barrier(jnp.sum(expo, axis=-1, keepdims=True)))
    return jnp.einsum('ghqp,gphv->gqhv', probs, values, precision=lax.Precision.HIGHEST)

def forward(mask, classes, offset_table, inputs, bias_table, qkv_weight, qkv_gain, qkv_shift, out_weight, out_gain, out_shift, up_weight, up_gain, up_shift, down_weight, down_gain, down_shift):
    images = inputs.shape[0]
    flat = inputs.reshape(-1, inputs.shape[-1])
    weights = mask.reshape(-1, 1)
    total = jnp.sum(mask)
    mixed = low(batch_norm(low_back(matmul(flat, qkv_weight)), weights, total, qkv_gain, qkv_shift))
    mixed = mixed.reshape(images // group_size, group_size, SLOT, HEADS, 2 * KEY + VALD)
    query = mixed[..., :KEY]
    keys = mixed[..., KEY:2 * KEY]
    values = mixed[..., 2 * KEY:]
    attended = lax.map(jax.checkpoint(partial(attend_group, bias_table, offset_table)), (query, keys, values, classes.reshape(-1, group_size), mask.reshape(-1, group_size, SLOT)))
    attended = low_back(attended.reshape(flat.shape[0], HEADS * VALD))
    activated = low(jax.nn.silu(attended))
    middle = flat + batch_norm(low_back(matmul(activated, out_weight)), weights, total, out_gain, out_shift)
    hidden = low(jax.nn.silu(batch_norm(low_back(matmul(low(middle), up_weight)), weights, total, up_gain, up_shift)))
    result = (middle + batch_norm(low_back(matmul(hidden, down_weight)), weights, total, down_gain, down_shift)) * weights
    return result.reshape(inputs.shape)

def reference(inputs, classes, offset_table, bias_table, qkv_weight, qkv_gain, qkv_shift, out_weight, out_gain, out_shift, up_weight, up_gain, up_shift, down_weight, down_gain, down_shift, cotangent):
    mask = token_mask(classes)
    params = [array.astype(jnp.float32) for array in (inputs, bias_table, qkv_weight, qkv_gain, qkv_shift, out_weight, out_gain, out_shift, up_weight, up_gain, up_shift, down_weight, down_gain, down_shift)]
    output, pullback = jax.vjp(partial(forward, mask, classes, offset_table), *params)
    grads = pullback(cotangent.astype(jnp.float32))
    return (output.astype(jnp.bfloat16), grads[0], grads[1], grads[2], grads[3], grads[4], grads[5], grads[6], grads[7], grads[8], grads[9], grads[10], grads[11], grads[12], grads[13])
```

```python
import jax
import jax.numpy as jnp
from jax import lax
from jax.experimental import pallas as pl
from jax.experimental.pallas import tpu as pltpu
from jax.sharding import PartitionSpec as P

HEADS = 4
KEY = 32
VALD = 128
GRID = 18
CLASSES = 3
SLOT = 324
NOFF = 324


EPS = 1e-05
LOG2E = 1.4426950408889634
LN2 = 0.6931471805599453
ROWS = 336
PARTS = ((10, 100, 112, 128), (14, 196, 208, 256), (18, 324, 336, 384))
VMEM = pl.BlockSpec(memory_space=pltpu.VMEM)


def dot_nn(left, right):
    return jnp.dot(left, right, preferred_element_type=jnp.float32)


def dot_nt(left, right):
    return lax.dot_general(left, right, (((1,), (1,)), ((), ())), preferred_element_type=jnp.float32)


def dot_tn(left, right):
    return lax.dot_general(left, right, (((0,), (0,)), ((), ())), preferred_element_type=jnp.float32)


def pad_rows(value, rows):
    if value.shape[0] == rows:
        return value
    return jnp.concatenate([value, jnp.zeros((rows - value.shape[0], value.shape[1]), value.dtype)], axis=0)


def pad_lanes(value, lanes):
    if value.shape[1] == lanes:
        return value
    return jnp.concatenate([value, jnp.zeros((value.shape[0], lanes - value.shape[1]), value.dtype)], axis=1)


def bias_tables(off_ref, table_ref, index_ref, outs):
    tables = []
    for head in range(HEADS):
        row = pad_lanes(table_ref[head : head + 1, :], 384) * LOG2E
        tables.append([jnp.broadcast_to(row[:, 128 * k : 128 * k + 128], (8, 128)) for k in range(3)])
    index_ref[...] = jnp.zeros_like(index_ref)
    for number, (_, amount, rows, lanes) in enumerate(PARTS):
        index_ref[:SLOT, :SLOT] = off_ref[number]

        def tile(step, _, amount=amount, lanes=lanes, out=outs[number]):
            at = pl.multiple_of(step * 8, 8)
            for block in range(lanes // 128):
                index = index_ref[pl.ds(at, 8), 128 * block : 128 * block + 128]
                low = index & 127
                part = index >> 7
                valid = lax.broadcasted_iota(jnp.int32, (8, 128), 1) + 128 * block < amount
                for head in range(HEADS):
                    found = [
                        jnp.take_along_axis(tables[head][k], low, axis=1, mode="promise_in_bounds")
                        for k in range(3)
                    ]
                    value = jnp.where(part == 0, found[0], jnp.where(part == 1, found[1], found[2]))
                    column = (head % 2) * lanes + 128 * block
                    out[head // 2, pl.ds(at, 8), column : column + 128] = jnp.where(valid, value, -1e30)
            return 0

        lax.fori_loop(0, rows // 8, tile, 0)


def head_keys(keys, pair, lanes):
    owner = lax.broadcasted_iota(jnp.int32, keys.shape, 1) // KEY
    zero = jnp.zeros_like(keys)
    return jnp.concatenate(
        [pad_rows(jnp.where(owner == 2 * pair + side, keys, zero), lanes) for side in range(2)], axis=0
    )


def pair_values(values, lanes):
    zero = jnp.zeros((lanes, VALD), values.dtype)
    top = jnp.concatenate([pad_rows(values[:, :VALD], lanes), zero], axis=1)
    low = jnp.concatenate([zero, pad_rows(values[:, VALD:], lanes)], axis=1)
    return jnp.concatenate([top, low], axis=0)


def attend_kernel(class_ref, mixed_ref, bias0, bias1, bias2, att_ref, p_ref, r_ref):
    kind = class_ref[pl.program_id(0)]
    for number, (_, amount, rows, lanes) in enumerate(PARTS):

        @pl.when(kind == number)
        def _(amount=amount, rows=rows, lanes=lanes, bias=(bias0, bias1, bias2)[number]):
            query = mixed_ref[0, :rows, :128]
            keys = mixed_ref[0, :rows, 128:256]
            kept = lax.broadcasted_iota(jnp.int32, (rows, VALD), 0) < amount
            lane = lax.broadcasted_iota(jnp.int32, (rows, 128), 1)
            shares = jnp.zeros((rows, 128), jnp.float32)
            for pair in range(2):
                scores = dot_nt(query, head_keys(keys, pair, lanes)) + bias[pair]
                parts, inverse = [], []
                for side in range(2):
                    own = scores[:, side * lanes : (side + 1) * lanes]
                    expo = jnp.exp2(own - jnp.max(own, axis=1, keepdims=True))
                    share = 1.0 / jnp.sum(expo, axis=1, keepdims=True)
                    shares = jnp.where(lane == 2 * pair + side, share, shares)
                    parts.append(expo.astype(jnp.bfloat16))
                    inverse.append(share)
                both = jnp.concatenate(parts, axis=1)
                p_ref[0, :rows, 2 * pair * lanes : 2 * (pair + 1) * lanes] = both
                values = mixed_ref[0, :rows, 256 + 256 * pair : 512 + 256 * pair]
                sums = dot_nn(both, pair_values(values, lanes))
                for side in range(2):
                    own = sums[:, side * VALD : (side + 1) * VALD] * inverse[side]
                    at = (2 * pair + side) * VALD
                    att_ref[0, :rows, at : at + VALD] = jnp.where(kept, own, 0.0).astype(jnp.bfloat16)
            r_ref[0, :rows, :] = shares
            if rows < ROWS:
                att_ref[0, rows:, :] = jnp.zeros((ROWS - rows, att_ref.shape[2]), jnp.bfloat16)


def back_kernel(class_ref, mixed_ref, p_ref, r_ref, g_ref, att_ref, gmix_ref, acc0, acc1, acc2):
    accs = (acc0, acc1, acc2)

    @pl.when(pl.program_id(0) == 0)
    def _():
        for acc in accs:
            acc[...] = jnp.zeros_like(acc)

    kind = class_ref[pl.program_id(0)]
    for number, (_, amount, rows, lanes) in enumerate(PARTS):

        @pl.when(kind == number)
        def _(rows=rows, lanes=lanes, acc=accs[number]):
            query = mixed_ref[0, :rows, :128]
            keys = mixed_ref[0, :rows, 128:256]
            owner = lax.broadcasted_iota(jnp.int32, (rows, 128), 1) // KEY
            d_query = jnp.zeros((rows, 128), jnp.float32)
            d_keys = jnp.zeros((rows, 128), jnp.float32)
            for pair in range(2):
                grads, deltas = [], []
                for side in range(2):
                    head = 2 * pair + side
                    at = head * VALD
                    grad = g_ref[0, :rows, at : at + VALD].astype(jnp.float32) * r_ref[0, :rows, head : head + 1]
                    own = att_ref[0, :rows, at : at + VALD].astype(jnp.float32)
                    deltas.append(jnp.sum(grad * own, axis=1, keepdims=True))
                    grads.append(grad.astype(jnp.bfloat16))
                both = jnp.concatenate(grads, axis=1)
                values = mixed_ref[0, :rows, 256 + 256 * pair : 512 + 256 * pair]
                d_probs = dot_nt(both, pair_values(values, lanes))
                probs = p_ref[0, :rows, 2 * pair * lanes : 2 * (pair + 1) * lanes]
                low = []
                for side in range(2):
                    cut = slice(side * lanes, (side + 1) * lanes)
                    d_score = probs[:, cut].astype(jnp.float32) * (d_probs[:, cut] - deltas[side])
                    acc[pair, :, cut] += d_score
                    low.append(d_score.astype(jnp.bfloat16))
                d_low = jnp.concatenate(low, axis=1)
                d_query = d_query + dot_nn(d_low, head_keys(keys, pair, lanes))
                turned = dot_tn(d_low, query)
                d_values = dot_tn(probs, both)
                for side in range(2):
                    head = 2 * pair + side
                    d_keys = jnp.where(owner == head, turned[side * lanes : side * lanes + rows], d_keys)
                    at = 256 + head * VALD
                    gmix_ref[0, :rows, at : at + VALD] = d_values[
                        side * lanes : side * lanes + rows, side * VALD : (side + 1) * VALD
                    ].astype(jnp.bfloat16)
            gmix_ref[0, :rows, :128] = (d_query * KEY ** (-0.5)).astype(jnp.bfloat16)
            gmix_ref[0, :rows, 128:256] = (d_keys * LN2).astype(jnp.bfloat16)
            if rows < ROWS:
                gmix_ref[0, rows:, :] = jnp.zeros((ROWS - rows, gmix_ref.shape[2]), jnp.bfloat16)


def table_sums(off_ref, accs):
    totals = [jnp.zeros((24, 640), jnp.float32) for _ in range(HEADS)]
    for number, (side_of, amount, rows, lanes) in enumerate(PARTS):
        offsets = off_ref[number]
        row = lax.broadcasted_iota(jnp.int32, (SLOT, 1), 0)
        most = jnp.max(offsets, axis=1, keepdims=True)
        corner = jnp.min(jnp.where(most == (side_of - 1) * (GRID + 1), row, SLOT), axis=0, keepdims=True)
        place = jnp.sum(jnp.where(row == corner, offsets, 0), axis=0, keepdims=True)
        place = jnp.where(lax.broadcasted_iota(jnp.int32, (1, SLOT), 1) < amount, place, -1)
        wide = jnp.concatenate([place, jnp.full((1, 384 - SLOT), -1, jnp.int32)], axis=1)
        cell = lax.broadcasted_iota(jnp.int32, (24 * side_of, 1), 0)
        cell_row = (cell * 2731) >> 16
        cell_col = cell - 24 * cell_row
        code = jnp.where(cell_col < side_of, cell_row * GRID + cell_col, -2)
        left = (code == wide[:, :rows]).astype(jnp.float32).astype(jnp.bfloat16)
        spot = lax.broadcasted_iota(jnp.int32, (384, 1), 0)
        right = (spot == wide[:, :lanes]).astype(jnp.float32).astype(jnp.bfloat16)
        for head in range(HEADS):
            at = (head % 2) * lanes
            score = accs[number][head // 2, :, at : at + lanes].astype(jnp.bfloat16)
            sorted_rows = dot_nn(left, score).astype(jnp.bfloat16)
            both = dot_nt(sorted_rows, right)
            for line in range(side_of):
                part = pad_lanes(both[24 * line : 24 * line + 24], 640)
                totals[head] = totals[head] + pltpu.roll(part, (GRID - 1 - line) * GRID, 1)
    lane = lax.broadcasted_iota(jnp.int32, (24, 640), 1)
    lane_row = (lane * 3641) >> 16
    away = jnp.abs(lane - GRID * lane_row - lax.broadcasted_iota(jnp.int32, (24, 640), 0))
    wide_row = lax.broadcasted_iota(jnp.int32, (640, 1), 0)
    wide_row = jnp.abs(((wide_row * 3641) >> 16) - (GRID - 1))
    out_lane = lax.broadcasted_iota(jnp.int32, (1, 384), 1)
    out_row = (out_lane * 3641) >> 16
    fold = (wide_row == out_row).astype(jnp.float32).astype(jnp.bfloat16)
    out_col = out_lane - GRID * out_row
    pick = lax.broadcasted_iota(jnp.int32, (24, 1), 0) == out_col
    rows_out = []
    for head in range(HEADS):
        lines = [
            jnp.sum(jnp.where(away == d, totals[head], 0.0), axis=0, keepdims=True) for d in range(GRID)
        ]
        lines = pad_rows(jnp.concatenate(lines, axis=0), 24)
        high = lines.astype(jnp.bfloat16)
        low = (lines - high.astype(jnp.float32)).astype(jnp.bfloat16)
        spread = dot_nn(high, fold) + dot_nn(low, fold)
        rows_out.append(jnp.sum(jnp.where(pick, spread, 0.0), axis=0, keepdims=True))
    return jnp.concatenate(rows_out, axis=0)


def bias_kernel(off_ref, table_ref, out0, out1, out2, index_ref):
    bias_tables(off_ref, table_ref, index_ref, (out0, out1, out2))


def bias_call(offset_table, bias_table):
    return pl.pallas_call(
        bias_kernel,
        out_shape=[jax.ShapeDtypeStruct((2, r, 2 * l), jnp.float32) for _, _, r, l in PARTS],
        in_specs=[VMEM, VMEM],
        out_specs=[VMEM] * 3,
        scratch_shapes=[pltpu.VMEM((ROWS, 384), jnp.int32)],
        compiler_params=pltpu.CompilerParams(vmem_limit_bytes=48 * 2**20),
    )(offset_table, bias_table)


def image_spec(width):
    return pl.BlockSpec((1, ROWS, width), lambda i, c: (i, 0, 0))


def whole_spec(shape):
    return pl.BlockSpec(shape, lambda i, c: (0,) * len(shape))


def attend_call(classes, mixed, biases):
    images = mixed.shape[0]
    return pl.pallas_call(
        attend_kernel,
        grid_spec=pltpu.PrefetchScalarGridSpec(
            num_scalar_prefetch=1,
            grid=(images,),
            in_specs=[image_spec(768)] + [whole_spec(b.shape) for b in biases],
            out_specs=[image_spec(512), image_spec(1536), image_spec(128)],
        ),
        out_shape=[
            jax.ShapeDtypeStruct((images, ROWS, 512), jnp.bfloat16),
            jax.ShapeDtypeStruct((images, ROWS, 1536), jnp.bfloat16),
            jax.ShapeDtypeStruct((images, ROWS, 128), jnp.float32),
        ],
        compiler_params=pltpu.CompilerParams(vmem_limit_bytes=48 * 2**20),
    )(classes, mixed, *biases)


def back_call(classes, mixed, probs, shares, grad, attended):
    images = mixed.shape[0]
    shapes = [(2, r, 2 * l) for _, _, r, l in PARTS]
    return pl.pallas_call(
        back_kernel,
        grid_spec=pltpu.PrefetchScalarGridSpec(
            num_scalar_prefetch=1,
            grid=(images,),
            in_specs=[image_spec(768), image_spec(1536), image_spec(128), image_spec(512), image_spec(512)],
            out_specs=[image_spec(768)] + [whole_spec(s) for s in shapes],
        ),
        out_shape=[jax.ShapeDtypeStruct((images, ROWS, 768), jnp.bfloat16)]
        + [jax.ShapeDtypeStruct(s, jnp.float32) for s in shapes],
        compiler_params=pltpu.CompilerParams(vmem_limit_bytes=48 * 2**20),
    )(classes, mixed, probs, shares, grad, attended)


def table_kernel(off_ref, acc0, acc1, acc2, out_ref):
    out_ref[...] = table_sums(off_ref, (acc0, acc1, acc2))


def table_call(offset_table, accs):
    return pl.pallas_call(
        table_kernel,
        out_shape=jax.ShapeDtypeStruct((HEADS, 384), jnp.float32),
        in_specs=[VMEM] * 4,
        out_specs=VMEM,
        compiler_params=pltpu.CompilerParams(vmem_limit_bytes=48 * 2**20),
    )(offset_table, *accs)


def arrange(columns):
    lead = columns.shape[:-1]
    heads = columns.reshape(lead + (HEADS, 2 * KEY + VALD))
    parts = (heads[..., :KEY], heads[..., KEY : 2 * KEY], heads[..., 2 * KEY :])
    return jnp.concatenate([part.reshape(lead + (-1,)) for part in parts], axis=-1)


def restore(columns):
    lead = columns.shape[:-1]
    query = columns[..., :128].reshape(lead + (HEADS, KEY))
    keys = columns[..., 128:256].reshape(lead + (HEADS, KEY))
    values = columns[..., 256:].reshape(lead + (HEADS, VALD))
    return jnp.concatenate([query, keys, values], axis=-1).reshape(lead + (-1,))


def silu_slope(value):
    sigma = jax.nn.sigmoid(value)
    return sigma * (1.0 + value * (1.0 - sigma))


def norm_forward(value, weights, gain, shift):
    sums = lax.psum(
        (
            jnp.sum(value * weights, axis=0),
            jnp.sum(value * value * weights, axis=0),
            jnp.sum(weights),
        ),
        ("dp", "fsdp"),
    )
    total = sums[2]
    center = sums[0] / total
    square = sums[1] / total
    scale = lax.rsqrt(square - center * center + EPS)
    normed = (value - center) * scale
    return (normed * gain.astype(jnp.float32) + shift.astype(jnp.float32), normed, scale, total)


def norm_backward(grad, normed, scale, total, gain, weights):
    sums = lax.psum((jnp.sum(grad, axis=0), jnp.sum(grad * normed, axis=0)), ("dp", "fsdp"))
    shift_grad = sums[0]
    gain_grad = sums[1]
    gain_f = gain.astype(jnp.float32)
    inner = gain_f * (shift_grad + normed * gain_grad) / total
    return (scale * (grad * gain_f - weights * inner), gain_grad, shift_grad)


def attention_scores(query, keys, bias, keep):
    dots = jnp.einsum("iqhk,iphk->ihqp", query, keys, preferred_element_type=jnp.float32)
    scores = dots * KEY ** (-0.5) + bias
    return jnp.where(keep[:, None, None, :] > 0, scores, -1e30)


def left_product(left, right):
    return jnp.einsum("na,nb->ab", left, right, preferred_element_type=jnp.float32)


def right_product(left, right):
    return jnp.einsum("nb,ab->na", left, right, preferred_element_type=jnp.float32)


def own_slice(vector):
    width = vector.shape[0] // lax.axis_size("fsdp")
    return lax.dynamic_slice_in_dim(vector, lax.axis_index("fsdp") * width, width)


def shards(
    inputs,
    classes,
    offset_table,
    bias_table,
    qkv_weight,
    qkv_gain,
    qkv_shift,
    out_weight,
    out_gain,
    out_shift,
    up_weight,
    up_gain,
    up_shift,
    down_weight,
    down_gain,
    down_shift,
    cotangent,
):
    gathered = (
        lax.all_gather(qkv_weight, "fsdp", axis=0, tiled=True),
        lax.all_gather(qkv_gain, "fsdp", axis=0, tiled=True),
        lax.all_gather(qkv_shift, "fsdp", axis=0, tiled=True),
        lax.all_gather(out_weight, "fsdp", axis=0, tiled=True),
        lax.all_gather(out_gain, "fsdp", axis=0, tiled=True),
        lax.all_gather(out_shift, "fsdp", axis=0, tiled=True),
        lax.all_gather(up_weight, "fsdp", axis=0, tiled=True),
        lax.all_gather(up_gain, "fsdp", axis=0, tiled=True),
        lax.all_gather(up_shift, "fsdp", axis=0, tiled=True),
        lax.all_gather(down_weight, "fsdp", axis=0, tiled=True),
        lax.all_gather(down_gain, "fsdp", axis=0, tiled=True),
        lax.all_gather(down_shift, "fsdp", axis=0, tiled=True),
    )
    qkv_full, qkv_gains, qkv_shifts, out_full, out_gains, out_shifts = gathered[:6]
    images = inputs.shape[0]
    length = images * SLOT
    limits = jnp.where(
        classes == 0,
        (GRID - 8) * (GRID - 8),
        jnp.where(classes == 1, (GRID - 4) * (GRID - 4), SLOT),
    )
    keep = (jnp.arange(SLOT)[None, :] < limits[:, None]).astype(jnp.float32)
    weights = keep.reshape(-1, 1)
    flat = inputs.reshape(length, -1)
    z_qkv = jnp.dot(flat, qkv_full, preferred_element_type=jnp.float32)
    mixed_f, hat_qkv, scale_qkv, total = norm_forward(z_qkv, weights, qkv_gains, qkv_shifts)
    mixed = mixed_f.astype(jnp.bfloat16).reshape(images, SLOT, HEADS, -1)
    scaled = jnp.where(jnp.arange(KEY * 6) < KEY, KEY ** (-0.5) * LOG2E, 1.0)
    mixed = arrange((mixed_f.reshape(images, SLOT, HEADS, -1) * scaled).astype(jnp.bfloat16).reshape(images, SLOT, -1))
    mixed = jnp.pad(mixed, ((0, 0), (0, ROWS - SLOT), (0, 0)))
    biases = bias_call(offset_table, bias_table)
    attended_low, probs, shares = attend_call(classes, mixed, biases)
    attended = attended_low[:, :SLOT].astype(jnp.float32).reshape(length, -1)
    activated = jax.nn.silu(attended).astype(jnp.bfloat16)
    z_out = jnp.dot(activated, out_full, preferred_element_type=jnp.float32)
    branch, hat_out, scale_out, unused_out = norm_forward(z_out, weights, out_gains, out_shifts)
    middle = flat.astype(jnp.float32) + branch
    middle_low = middle.astype(jnp.bfloat16)
    second = gathered[6:]
    up_full, up_gains, up_shifts, down_full, down_gains, down_shifts = second
    z_up = jnp.dot(middle_low, up_full, preferred_element_type=jnp.float32)
    up_normed, hat_up, scale_up, unused_up = norm_forward(z_up, weights, up_gains, up_shifts)
    hidden = jax.nn.silu(up_normed).astype(jnp.bfloat16)
    z_down = jnp.dot(hidden, down_full, preferred_element_type=jnp.float32)
    down_normed, hat_down, scale_down, unused_down = norm_forward(
        z_down, weights, down_gains, down_shifts
    )
    output = ((middle + down_normed) * weights).astype(jnp.bfloat16).reshape(inputs.shape)
    grad_out = cotangent.astype(jnp.float32).reshape(length, -1) * weights
    dz_down, down_gain_grad, down_shift_grad = norm_backward(
        grad_out, hat_down, scale_down, total, down_gains, weights
    )
    dz_down_low = dz_down.astype(jnp.bfloat16)
    down_grad = left_product(hidden, dz_down_low)
    grad_up = right_product(dz_down_low, down_full) * silu_slope(up_normed)
    dz_up, up_gain_grad, up_shift_grad = norm_backward(
        grad_up, hat_up, scale_up, total, up_gains, weights
    )
    dz_up_low = dz_up.astype(jnp.bfloat16)
    up_grad = left_product(middle_low, dz_up_low)
    grad_middle = grad_out + right_product(dz_up_low, up_full)
    dz_out, out_gain_grad, out_shift_grad = norm_backward(
        grad_middle, hat_out, scale_out, total, out_gains, weights
    )
    dz_out_low = dz_out.astype(jnp.bfloat16)
    out_grad = left_product(activated, dz_out_low)
    grad_att = (right_product(dz_out_low, out_full) * silu_slope(attended)).astype(jnp.bfloat16)
    grad_att = jnp.pad(grad_att.reshape(images, SLOT, -1), ((0, 0), (0, ROWS - SLOT), (0, 0)))
    grad_mixed, *accs = back_call(classes, mixed, probs, shares, grad_att, attended_low)
    local_table = table_call(offset_table, accs)[:, :NOFF]
    grad_mixed = restore(grad_mixed[:, :SLOT]).astype(jnp.float32).reshape(length, -1)
    dz_qkv, qkv_gain_grad, qkv_shift_grad = norm_backward(
        grad_mixed, hat_qkv, scale_qkv, total, qkv_gains, weights
    )
    dz_qkv_low = dz_qkv.astype(jnp.bfloat16)
    qkv_grad = left_product(flat, dz_qkv_low)
    input_grad = (grad_middle + right_product(dz_qkv_low, qkv_full)).reshape(inputs.shape)
    table_grad = lax.psum(local_table, ("dp", "fsdp"))
    whole = (
        lax.psum(qkv_grad.astype(jnp.bfloat16), "dp").astype(jnp.float32),
        lax.psum(out_grad.astype(jnp.bfloat16), "dp").astype(jnp.float32),
        lax.psum(up_grad.astype(jnp.bfloat16), "dp").astype(jnp.float32),
        lax.psum(down_grad.astype(jnp.bfloat16), "dp").astype(jnp.float32),
    )
    summed = (
        lax.psum_scatter(
            whole[0].astype(jnp.bfloat16), "fsdp", scatter_dimension=0, tiled=True
        ).astype(jnp.float32),
        lax.psum_scatter(
            whole[1].astype(jnp.bfloat16), "fsdp", scatter_dimension=0, tiled=True
        ).astype(jnp.float32),
        lax.psum_scatter(
            whole[2].astype(jnp.bfloat16), "fsdp", scatter_dimension=0, tiled=True
        ).astype(jnp.float32),
        lax.psum_scatter(
            whole[3].astype(jnp.bfloat16), "fsdp", scatter_dimension=0, tiled=True
        ).astype(jnp.float32),
    )
    return (
        output,
        input_grad,
        table_grad,
        summed[0],
        own_slice(qkv_gain_grad),
        own_slice(qkv_shift_grad),
        summed[1],
        own_slice(out_gain_grad),
        own_slice(out_shift_grad),
        summed[2],
        own_slice(up_gain_grad),
        own_slice(up_shift_grad),
        summed[3],
        own_slice(down_gain_grad),
        own_slice(down_shift_grad),
    )


def solution(mesh):
    placed = (
        P(("dp", "fsdp"), None, None),
        P(("dp", "fsdp")),
        P(),
        P(),
        P("fsdp", None),
        P("fsdp"),
        P("fsdp"),
        P("fsdp", None),
        P("fsdp"),
        P("fsdp"),
        P("fsdp", None),
        P("fsdp"),
        P("fsdp"),
        P("fsdp", None),
        P("fsdp"),
        P("fsdp"),
        P(("dp", "fsdp"), None, None),
    )
    return jax.shard_map(
        shards,
        mesh=mesh,
        in_specs=placed,
        out_specs=(
            P(("dp", "fsdp"), None, None),
            P(("dp", "fsdp"), None, None),
            P(),
            P("fsdp", None),
            P("fsdp"),
            P("fsdp"),
            P("fsdp", None),
            P("fsdp"),
            P("fsdp"),
            P("fsdp", None),
            P("fsdp"),
            P("fsdp"),
            P("fsdp", None),
            P("fsdp"),
            P("fsdp"),
        ),
        check_vma=False,
    )
```

```python
import functools

import jax
import jax.numpy as jnp
from jax import lax
from jax.experimental import pallas as pl
from jax.experimental.pallas import tpu as pltpu
from jax.sharding import PartitionSpec as P

HEADS = 4
KEY = 32
VALD = 128
GRID = 18
CLASSES = 3
SLOT = 324
NOFF = 324


EPS = 1e-05
LOG2E = 1.4426950408889634
LN2 = 0.6931471805599453
ROWS = 336
PARTS = ((10, 100, 112, 128), (14, 196, 208, 256), (18, 324, 336, 384))
VMEM = pl.BlockSpec(memory_space=pltpu.VMEM)


def dot_nn(left, right):
    return jnp.dot(left, right, preferred_element_type=jnp.float32)


def dot_nt(left, right):
    return lax.dot_general(left, right, (((1,), (1,)), ((), ())), preferred_element_type=jnp.float32)


def dot_tn(left, right):
    return lax.dot_general(left, right, (((0,), (0,)), ((), ())), preferred_element_type=jnp.float32)


def pad_rows(value, rows):
    if value.shape[0] == rows:
        return value
    return jnp.concatenate([value, jnp.zeros((rows - value.shape[0], value.shape[1]), value.dtype)], axis=0)


def pad_lanes(value, lanes):
    if value.shape[1] == lanes:
        return value
    return jnp.concatenate([value, jnp.zeros((value.shape[0], lanes - value.shape[1]), value.dtype)], axis=1)


def bias_tables(off_ref, table_ref, index_ref, outs):
    tables = []
    for head in range(HEADS):
        row = pad_lanes(table_ref[head : head + 1, :], 384) * LOG2E
        tables.append([jnp.broadcast_to(row[:, 128 * k : 128 * k + 128], (8, 128)) for k in range(3)])
    index_ref[...] = jnp.zeros_like(index_ref)
    for number, (_, amount, rows, lanes) in enumerate(PARTS):
        index_ref[:SLOT, :SLOT] = off_ref[number]

        def tile(step, _, amount=amount, lanes=lanes, out=outs[number]):
            at = pl.multiple_of(step * 8, 8)
            for block in range(lanes // 128):
                index = index_ref[pl.ds(at, 8), 128 * block : 128 * block + 128]
                low = index & 127
                part = index >> 7
                valid = lax.broadcasted_iota(jnp.int32, (8, 128), 1) + 128 * block < amount
                for head in range(HEADS):
                    found = [
                        jnp.take_along_axis(tables[head][k], low, axis=1, mode="promise_in_bounds")
                        for k in range(3)
                    ]
                    value = jnp.where(part == 0, found[0], jnp.where(part == 1, found[1], found[2]))
                    column = (head % 2) * lanes + 128 * block
                    out[head // 2, pl.ds(at, 8), column : column + 128] = jnp.where(valid, value, -1e30)
            return 0

        lax.fori_loop(0, rows // 8, tile, 0)


def head_keys(keys, pair, lanes):
    owner = lax.broadcasted_iota(jnp.int32, keys.shape, 1) // KEY
    zero = jnp.zeros_like(keys)
    return jnp.concatenate(
        [pad_rows(jnp.where(owner == 2 * pair + side, keys, zero), lanes) for side in range(2)], axis=0
    )


def pair_values(values, lanes):
    zero = jnp.zeros((lanes, VALD), values.dtype)
    top = jnp.concatenate([pad_rows(values[:, :VALD], lanes), zero], axis=1)
    low = jnp.concatenate([zero, pad_rows(values[:, VALD:], lanes)], axis=1)
    return jnp.concatenate([top, low], axis=0)


def attend_kernel(class_ref, mixed_ref, bias0, bias1, bias2, att_ref, p_ref, r_ref):
    kind = class_ref[pl.program_id(0)]
    for number, (_, amount, rows, lanes) in enumerate(PARTS):

        @pl.when(kind == number)
        def _(amount=amount, rows=rows, lanes=lanes, bias=(bias0, bias1, bias2)[number]):
            query = mixed_ref[0, :rows, :128]
            keys = mixed_ref[0, :rows, 128:256]
            kept = lax.broadcasted_iota(jnp.int32, (rows, VALD), 0) < amount
            lane = lax.broadcasted_iota(jnp.int32, (rows, 128), 1)
            shares = jnp.zeros((rows, 128), jnp.float32)
            for pair in range(2):
                scores = dot_nt(query, head_keys(keys, pair, lanes)) + bias[pair]
                parts, inverse = [], []
                for side in range(2):
                    own = scores[:, side * lanes : (side + 1) * lanes]
                    expo = jnp.exp2(own - jnp.max(own, axis=1, keepdims=True))
                    share = 1.0 / jnp.sum(expo, axis=1, keepdims=True)
                    shares = jnp.where(lane == 2 * pair + side, share, shares)
                    parts.append(expo.astype(jnp.bfloat16))
                    inverse.append(share)
                both = jnp.concatenate(parts, axis=1)
                p_ref[0, :rows, 2 * pair * lanes : 2 * (pair + 1) * lanes] = both
                values = mixed_ref[0, :rows, 256 + 256 * pair : 512 + 256 * pair]
                sums = dot_nn(both, pair_values(values, lanes))
                for side in range(2):
                    own = sums[:, side * VALD : (side + 1) * VALD] * inverse[side]
                    at = (2 * pair + side) * VALD
                    att_ref[0, :rows, at : at + VALD] = jnp.where(kept, own, 0.0).astype(jnp.bfloat16)
            r_ref[0, :rows, :] = shares
            if rows < ROWS:
                att_ref[0, rows:, :] = jnp.zeros((ROWS - rows, att_ref.shape[2]), jnp.bfloat16)


def back_kernel(class_ref, mixed_ref, p_ref, r_ref, g_ref, att_ref, gmix_ref, acc0, acc1, acc2):
    accs = (acc0, acc1, acc2)

    @pl.when(pl.program_id(0) == 0)
    def _():
        for acc in accs:
            acc[...] = jnp.zeros_like(acc)

    kind = class_ref[pl.program_id(0)]
    for number, (_, amount, rows, lanes) in enumerate(PARTS):

        @pl.when(kind == number)
        def _(rows=rows, lanes=lanes, acc=accs[number]):
            query = mixed_ref[0, :rows, :128]
            keys = mixed_ref[0, :rows, 128:256]
            owner = lax.broadcasted_iota(jnp.int32, (rows, 128), 1) // KEY
            d_query = jnp.zeros((rows, 128), jnp.float32)
            d_keys = jnp.zeros((rows, 128), jnp.float32)
            for pair in range(2):
                grads, deltas = [], []
                for side in range(2):
                    head = 2 * pair + side
                    at = head * VALD
                    grad = g_ref[0, :rows, at : at + VALD].astype(jnp.float32) * r_ref[0, :rows, head : head + 1]
                    own = att_ref[0, :rows, at : at + VALD].astype(jnp.float32)
                    deltas.append(jnp.sum(grad * own, axis=1, keepdims=True))
                    grads.append(grad.astype(jnp.bfloat16))
                both = jnp.concatenate(grads, axis=1)
                values = mixed_ref[0, :rows, 256 + 256 * pair : 512 + 256 * pair]
                d_probs = dot_nt(both, pair_values(values, lanes))
                probs = p_ref[0, :rows, 2 * pair * lanes : 2 * (pair + 1) * lanes]
                low = []
                for side in range(2):
                    cut = slice(side * lanes, (side + 1) * lanes)
                    d_score = probs[:, cut].astype(jnp.float32) * (d_probs[:, cut] - deltas[side])
                    acc[pair, :, cut] += d_score
                    low.append(d_score.astype(jnp.bfloat16))
                d_low = jnp.concatenate(low, axis=1)
                d_query = d_query + dot_nn(d_low, head_keys(keys, pair, lanes))
                turned = dot_tn(d_low, query)
                d_values = dot_tn(probs, both)
                for side in range(2):
                    head = 2 * pair + side
                    d_keys = jnp.where(owner == head, turned[side * lanes : side * lanes + rows], d_keys)
                    at = 256 + head * VALD
                    gmix_ref[0, :rows, at : at + VALD] = d_values[
                        side * lanes : side * lanes + rows, side * VALD : (side + 1) * VALD
                    ].astype(jnp.bfloat16)
            gmix_ref[0, :rows, :128] = (d_query * KEY ** (-0.5)).astype(jnp.bfloat16)
            gmix_ref[0, :rows, 128:256] = (d_keys * LN2).astype(jnp.bfloat16)
            if rows < ROWS:
                gmix_ref[0, rows:, :] = jnp.zeros((ROWS - rows, gmix_ref.shape[2]), jnp.bfloat16)


def table_sums(off_ref, accs):
    totals = [jnp.zeros((24, 640), jnp.float32) for _ in range(HEADS)]
    for number, (side_of, amount, rows, lanes) in enumerate(PARTS):
        offsets = off_ref[number]
        row = lax.broadcasted_iota(jnp.int32, (SLOT, 1), 0)
        most = jnp.max(offsets, axis=1, keepdims=True)
        corner = jnp.min(jnp.where(most == (side_of - 1) * (GRID + 1), row, SLOT), axis=0, keepdims=True)
        place = jnp.sum(jnp.where(row == corner, offsets, 0), axis=0, keepdims=True)
        place = jnp.where(lax.broadcasted_iota(jnp.int32, (1, SLOT), 1) < amount, place, -1)
        wide = jnp.concatenate([place, jnp.full((1, 384 - SLOT), -1, jnp.int32)], axis=1)
        cell = lax.broadcasted_iota(jnp.int32, (24 * side_of, 1), 0)
        cell_row = (cell * 2731) >> 16
        cell_col = cell - 24 * cell_row
        code = jnp.where(cell_col < side_of, cell_row * GRID + cell_col, -2)
        left = (code == wide[:, :rows]).astype(jnp.float32).astype(jnp.bfloat16)
        spot = lax.broadcasted_iota(jnp.int32, (384, 1), 0)
        right = (spot == wide[:, :lanes]).astype(jnp.float32).astype(jnp.bfloat16)
        for head in range(HEADS):
            at = (head % 2) * lanes
            score = accs[number][head // 2, :, at : at + lanes].astype(jnp.bfloat16)
            sorted_rows = dot_nn(left, score).astype(jnp.bfloat16)
            both = dot_nt(sorted_rows, right)
            for line in range(side_of):
                part = pad_lanes(both[24 * line : 24 * line + 24], 640)
                totals[head] = totals[head] + pltpu.roll(part, (GRID - 1 - line) * GRID, 1)
    lane = lax.broadcasted_iota(jnp.int32, (24, 640), 1)
    lane_row = (lane * 3641) >> 16
    away = jnp.abs(lane - GRID * lane_row - lax.broadcasted_iota(jnp.int32, (24, 640), 0))
    wide_row = lax.broadcasted_iota(jnp.int32, (640, 1), 0)
    wide_row = jnp.abs(((wide_row * 3641) >> 16) - (GRID - 1))
    out_lane = lax.broadcasted_iota(jnp.int32, (1, 384), 1)
    out_row = (out_lane * 3641) >> 16
    fold = (wide_row == out_row).astype(jnp.float32).astype(jnp.bfloat16)
    out_col = out_lane - GRID * out_row
    pick = lax.broadcasted_iota(jnp.int32, (24, 1), 0) == out_col
    rows_out = []
    for head in range(HEADS):
        lines = [
            jnp.sum(jnp.where(away == d, totals[head], 0.0), axis=0, keepdims=True) for d in range(GRID)
        ]
        lines = pad_rows(jnp.concatenate(lines, axis=0), 24)
        high = lines.astype(jnp.bfloat16)
        low = (lines - high.astype(jnp.float32)).astype(jnp.bfloat16)
        spread = dot_nn(high, fold) + dot_nn(low, fold)
        rows_out.append(jnp.sum(jnp.where(pick, spread, 0.0), axis=0, keepdims=True))
    return jnp.concatenate(rows_out, axis=0)


def image_spec(width):
    return pl.BlockSpec((1, ROWS, width), lambda i, c: (i, 0, 0))


def whole_spec(shape):
    return pl.BlockSpec(shape, lambda i, c: (0,) * len(shape))


def attend_call(classes, mixed, biases):
    images = mixed.shape[0]
    return pl.pallas_call(
        attend_kernel,
        grid_spec=pltpu.PrefetchScalarGridSpec(
            num_scalar_prefetch=1,
            grid=(images,),
            in_specs=[image_spec(768)] + [whole_spec(b.shape) for b in biases],
            out_specs=[image_spec(512), image_spec(1536), image_spec(128)],
        ),
        out_shape=[
            jax.ShapeDtypeStruct((images, ROWS, 512), jnp.bfloat16),
            jax.ShapeDtypeStruct((images, ROWS, 1536), jnp.bfloat16),
            jax.ShapeDtypeStruct((images, ROWS, 128), jnp.float32),
        ],
        compiler_params=pltpu.CompilerParams(vmem_limit_bytes=48 * 2**20),
    )(classes, mixed, *biases)


def back_call(classes, mixed, probs, shares, grad, attended):
    images = mixed.shape[0]
    shapes = [(2, r, 2 * l) for _, _, r, l in PARTS]
    return pl.pallas_call(
        back_kernel,
        grid_spec=pltpu.PrefetchScalarGridSpec(
            num_scalar_prefetch=1,
            grid=(images,),
            in_specs=[image_spec(768), image_spec(1536), image_spec(128), image_spec(512), image_spec(512)],
            out_specs=[image_spec(768)] + [whole_spec(s) for s in shapes],
        ),
        out_shape=[jax.ShapeDtypeStruct((images, ROWS, 768), jnp.bfloat16)]
        + [jax.ShapeDtypeStruct(s, jnp.float32) for s in shapes],
        compiler_params=pltpu.CompilerParams(vmem_limit_bytes=48 * 2**20),
    )(classes, mixed, probs, shares, grad, attended)


def table_kernel(off_ref, acc0, acc1, acc2, out_ref):
    out_ref[...] = table_sums(off_ref, (acc0, acc1, acc2))


def table_call(offset_table, accs):
    return pl.pallas_call(
        table_kernel,
        out_shape=jax.ShapeDtypeStruct((HEADS, 384), jnp.float32),
        in_specs=[VMEM] * 4,
        out_specs=VMEM,
        compiler_params=pltpu.CompilerParams(vmem_limit_bytes=48 * 2**20),
    )(offset_table, *accs)


MESH = pl.DeviceIdType.MESH
ANY = pl.BlockSpec(memory_space=pl.ANY)
SMEM = pl.BlockSpec(memory_space=pltpu.SMEM)


class Place:
    def __init__(self, dp_size, fs_size):
        self.dp_size, self.fs_size = dp_size, fs_size
        self.size = dp_size * fs_size
        self.dp, self.fs = lax.axis_index("dp"), lax.axis_index("fsdp")
        self.me = self.dp * fs_size + self.fs
        self.core = lax.rem(self.dp, 2)
        self.partner = (self.dp + 1 - 2 * self.core, self.fs)

    def other(self, step):
        spot = lax.rem(self.me + step, self.size)
        return (spot // self.fs_size, lax.rem(spot, self.fs_size))

    def greet(self):
        barrier = pltpu.get_barrier_semaphore()

        def signal(step, _):
            pl.semaphore_signal(barrier, inc=1, device_id=self.other(step), device_id_type=MESH)
            return 0

        lax.fori_loop(1, self.size, signal, 0)

    def meet(self):
        pl.semaphore_wait(pltpu.get_barrier_semaphore(), self.size - 1)

    def spread(self, buf, value, send, recv):
        buf[self.me] = value

        def start(step, _):
            push(buf.at[self.me], buf.at[self.me], send, recv, self.other(step))
            return 0

        lax.fori_loop(1, self.size, start, 0)

    def collect(self, buf, recv):
        await_bytes(buf.at[pl.ds(0, self.size - 1)], recv)
        return jnp.sum(buf[...], axis=0)

    def settle(self, buf, send):
        await_bytes(buf.at[pl.ds(0, self.size - 1)], send)


def push(source, target, send, recv, device):
    pltpu.make_async_remote_copy(
        src_ref=source, dst_ref=target, send_sem=send, recv_sem=recv, device_id=device, device_id_type=MESH
    ).start()


def await_bytes(ref, sem):
    pltpu.make_async_copy(ref, ref, sem).wait()


def halves(width):
    return (width // 2,) * 2


def gather_start(place, buf, send, recv):
    half = buf.shape[2] // 2

    def start(step, _):
        target = lax.rem(place.fs + step, place.fs_size)
        for core in range(2):

            @pl.when(place.core == core)
            def _():
                part = buf.at[place.fs, :, pl.ds(core * half, half)]
                push(part, part, send, recv, (place.dp, target))

        return 0

    lax.fori_loop(1, place.fs_size, start, 0)


def gather_pass(place, buf, recv, send2, recv2):
    half = buf.shape[2] // 2
    for core in range(2):

        @pl.when(place.core == core)
        def _():
            await_bytes(buf.at[pl.ds(0, place.fs_size - 1), :, pl.ds(core * half, half)], recv)
            part = buf.at[:, :, pl.ds(core * half, half)]
            push(part, part, send2, recv2, place.partner)


def gather_end(place, buf, recv2):
    half = buf.shape[2] // 2
    await_bytes(buf.at[:, :, pl.ds(0, half)], recv2)


def gather_settle(place, buf, send, send2):
    half = buf.shape[2] // 2
    await_bytes(buf.at[pl.ds(0, place.fs_size - 1), :, pl.ds(0, half)], send)
    await_bytes(buf.at[:, :, pl.ds(0, half)], send2)


def flat_weight(buf):
    shards, rows, width = buf.shape
    if rows % 16 == 0:
        return buf[...].reshape(shards * rows, width)
    wide = jnp.concatenate([buf[k].astype(jnp.float32) for k in range(shards)], axis=0)
    return wide.astype(jnp.bfloat16)


def split_low(value):
    high = value.astype(jnp.bfloat16)
    return high, (value - high.astype(jnp.float32)).astype(jnp.bfloat16)


def precise(left, right):
    high, low = split_low(left)
    return dot_nn(high, right) + dot_nn(low, right)


def arrange(columns):
    blocks = [columns[:, (2 * KEY + VALD) * h : (2 * KEY + VALD) * (h + 1)] for h in range(HEADS)]
    parts = [b[:, :KEY] for b in blocks] + [b[:, KEY : 2 * KEY] for b in blocks] + [b[:, 2 * KEY :] for b in blocks]
    return jnp.concatenate(parts, axis=1)


def restore(columns):
    parts = []
    for h in range(HEADS):
        parts += [
            columns[:, KEY * h : KEY * (h + 1)],
            columns[:, 128 + KEY * h : 128 + KEY * (h + 1)],
            columns[:, 256 + VALD * h : 256 + VALD * (h + 1)],
        ]
    return jnp.concatenate(parts, axis=1)


def limits_of(kind):
    return jnp.where(kind == 0, (GRID - 8) ** 2, jnp.where(kind == 1, (GRID - 4) ** 2, SLOT))


def assemble(buf, widths, lanes):
    turned = {}
    for width in sorted(set(widths)):
        turned[width] = sum(
            pltpu.roll(pad_lanes(buf[k], lanes), k * width, 1) if k else pad_lanes(buf[k], lanes)
            for k in range(buf.shape[0])
        )
    return [turned[width][k : k + 1] for k, width in enumerate(widths)]


def first_kernel(dp_size, fs_size, *refs):
    class_ref, x_ref, off_ref, table_ref = refs[:4]
    shards, vectors = refs[4:8], refs[8:16]
    mixed_out, xs_out, bias_out, weight_out, vec_out = refs[16], refs[17], refs[18:21], refs[21:25], refs[25]
    xs, z, mixed, index = refs[26:30]
    bias, weights = refs[30:33], refs[33:37]
    vbuf, stat = refs[37:39]
    send, recv, send2, recv2, local = refs[39:44]
    place = Place(dp_size, fs_size)
    images = x_ref.shape[0]

    for k in range(4):
        own = shards[k][...]
        if k == 0:
            own = arrange(own.astype(jnp.float32)).astype(jnp.bfloat16)
        weights[k][place.fs] = own
    vbuf[place.fs] = jnp.concatenate(
        [pad_lanes(v[...].astype(jnp.float32), 128) for v in vectors], axis=0
    )
    place.greet()

    def load(image, count):
        limit = limits_of(class_ref[image])
        row = lax.broadcasted_iota(jnp.int32, (SLOT, 1), 0)
        value = jnp.where(row < limit, x_ref[image].astype(jnp.float32), 0.0)
        xs[image] = pad_rows(value, ROWS).astype(jnp.bfloat16)
        return count + limit

    count = lax.fori_loop(0, images, load, 0)
    flat = xs[...].reshape(images * ROWS, xs.shape[2])
    gram = dot_tn(flat, flat)
    total_x = dot_nn(jnp.ones((8, images * ROWS), jnp.bfloat16), flat)

    place.meet()
    gather_start(place, weights[0], send.at[0], recv.at[0])

    def start(step, _):
        target = lax.rem(place.fs + step, place.fs_size)
        push(vbuf.at[place.fs], vbuf.at[place.fs], send.at[4], recv.at[4], (place.dp, target))
        return 0

    lax.fori_loop(1, place.fs_size, start, 0)
    for k in range(1, 4):
        gather_start(place, weights[k], send.at[k], recv.at[k])
    xs_copy = pltpu.make_async_copy(xs, xs_out, local.at[0])
    xs_copy.start()
    bias_tables(off_ref, table_ref, index, bias)
    copies = [xs_copy]
    for k in range(3):
        copies.append(pltpu.make_async_copy(bias[k], bias_out[k], local.at[1 + k]))
        copies[-1].start()

    gather_pass(place, weights[0], recv.at[0], send2.at[0], recv2.at[0])
    gather_end(place, weights[0], recv2.at[0])
    weight = flat_weight(weights[0])
    high, low = split_low(gram)
    spread = dot_nn(high, weight) + dot_nn(low, weight)
    squares = jnp.sum(weight.astype(jnp.float32) * spread, axis=0, keepdims=True)
    sums = precise(total_x, weight)[:1]
    tail = jnp.full((1, 128), count.astype(jnp.float32))
    place.spread(
        stat,
        jnp.concatenate(
            [jnp.concatenate([sums, tail], axis=1), jnp.concatenate([squares, tail], axis=1)], axis=0
        ),
        send.at[5],
        recv.at[5],
    )

    def product(image, _):
        z[image] = dot_nn(xs[image], weight)
        return 0

    lax.fori_loop(0, images, product, 0)
    for k in range(1, 4):
        gather_pass(place, weights[k], recv.at[k], send2.at[k], recv2.at[k])
    await_bytes(vbuf.at[pl.ds(0, place.fs_size - 1)], recv.at[4])
    widths = [v.shape[1] for v in vectors]
    full = assemble(vbuf, widths, 768)
    full[0], full[1] = arrange(full[0]), arrange(full[1])

    got = place.collect(stat, recv.at[5])
    whole = got[0:1, 768:769]
    center = got[0:1, :768] / whole
    square = got[1:2, :768] / whole
    scale = lax.rsqrt(square - center * center + EPS)
    vec_out[...] = jnp.concatenate(
        full + [scale, center, jnp.broadcast_to(whole, (1, 768)), jnp.zeros((5, 768), jnp.float32)], axis=0
    )
    gain = scale * full[0]
    shift = full[1] - center * gain
    fold = jnp.where(lax.broadcasted_iota(jnp.int32, (1, 768), 1) < 128, KEY ** (-0.5) * LOG2E, 1.0)
    gain, shift = gain * fold, shift * fold

    def normal(image, _):
        mixed[image] = (z[image] * gain + shift).astype(jnp.bfloat16)
        pltpu.make_async_copy(mixed.at[image], mixed_out.at[image], local.at[8 + image]).start()
        return 0

    lax.fori_loop(0, images, normal, 0)
    for k in range(4):
        if k > 0:
            gather_end(place, weights[k], recv2.at[k])
        copies.append(pltpu.make_async_copy(weights[k], weight_out[k], local.at[4 + k]))
        copies[-1].start()
    for k in range(4):
        gather_settle(place, weights[k], send.at[k], send2.at[k])
    await_bytes(vbuf.at[pl.ds(0, place.fs_size - 1)], send.at[4])
    place.settle(stat, send.at[5])
    for copy in copies:
        copy.wait()

    def finish(image, _):
        pltpu.make_async_copy(mixed.at[image], mixed_out.at[image], local.at[8 + image]).wait()
        return 0

    lax.fori_loop(0, images, finish, 0)


def first_call(dp_size, fs_size, classes, inputs, offset_table, bias_table, weights, vectors):
    images, model = inputs.shape[0], inputs.shape[2]
    vectors = [v.reshape(1, -1) for v in vectors]
    shapes = [(fs_size,) + w.shape for w in weights]
    biases = [(2, r, 2 * l) for _, _, r, l in PARTS]
    bf, f32 = jnp.bfloat16, jnp.float32
    return pl.pallas_call(
        functools.partial(first_kernel, dp_size, fs_size),
        out_shape=[
            jax.ShapeDtypeStruct((images, ROWS, 768), bf),
            jax.ShapeDtypeStruct((images, ROWS, model), bf),
        ]
        + [jax.ShapeDtypeStruct(s, f32) for s in biases]
        + [jax.ShapeDtypeStruct(s, bf) for s in shapes]
        + [jax.ShapeDtypeStruct((16, 768), f32)],
        in_specs=[SMEM] + [VMEM] * 15,
        out_specs=[ANY] * 9 + [VMEM],
        scratch_shapes=[
            pltpu.VMEM((images, ROWS, model), bf),
            pltpu.VMEM((images, ROWS, 768), f32),
            pltpu.VMEM((images, ROWS, 768), bf),
            pltpu.VMEM((ROWS, 384), jnp.int32),
        ]
        + [pltpu.VMEM(s, f32) for s in biases]
        + [pltpu.VMEM(s, bf) for s in shapes]
        + [
            pltpu.VMEM((fs_size, 8, 128), f32),
            pltpu.VMEM((dp_size * fs_size, 2, 896), f32),
            pltpu.SemaphoreType.DMA((6,)),
            pltpu.SemaphoreType.DMA((6,)),
            pltpu.SemaphoreType.DMA((4,)),
            pltpu.SemaphoreType.DMA((4,)),
            pltpu.SemaphoreType.DMA((8 + images,)),
        ],
        compiler_params=pltpu.CompilerParams(
            collective_id=0, has_side_effects=True, vmem_limit_bytes=56 * 2**20
        ),
    )(classes, inputs, offset_table, bias_table, *weights, *vectors)


def silu_slope(value):
    sigma = jax.nn.sigmoid(value)
    return sigma * (1.0 + value * (1.0 - sigma))


def norm_forward(value, weights, gain, shift):
    sums = lax.psum(
        (
            jnp.sum(value * weights, axis=0),
            jnp.sum(value * value * weights, axis=0),
            jnp.sum(weights),
        ),
        ("dp", "fsdp"),
    )
    total = sums[2]
    center = sums[0] / total
    square = sums[1] / total
    scale = lax.rsqrt(square - center * center + EPS)
    normed = (value - center) * scale
    return (normed * gain.astype(jnp.float32) + shift.astype(jnp.float32), normed, scale, total)


def norm_backward(grad, normed, scale, total, gain, weights):
    sums = lax.psum((jnp.sum(grad, axis=0), jnp.sum(grad * normed, axis=0)), ("dp", "fsdp"))
    shift_grad = sums[0]
    gain_grad = sums[1]
    gain_f = gain.astype(jnp.float32)
    inner = gain_f * (shift_grad + normed * gain_grad) / total
    return (scale * (grad * gain_f - weights * inner), gain_grad, shift_grad)


def attention_scores(query, keys, bias, keep):
    dots = jnp.einsum("iqhk,iphk->ihqp", query, keys, preferred_element_type=jnp.float32)
    scores = dots * KEY ** (-0.5) + bias
    return jnp.where(keep[:, None, None, :] > 0, scores, -1e30)


def left_product(left, right):
    return jnp.einsum("na,nb->ab", left, right, preferred_element_type=jnp.float32)


def right_product(left, right):
    return jnp.einsum("nb,ab->na", left, right, preferred_element_type=jnp.float32)


def own_slice(vector):
    width = vector.shape[0] // lax.axis_size("fsdp")
    return lax.dynamic_slice_in_dim(vector, lax.axis_index("fsdp") * width, width)


def shards(
    inputs,
    classes,
    offset_table,
    bias_table,
    qkv_weight,
    qkv_gain,
    qkv_shift,
    out_weight,
    out_gain,
    out_shift,
    up_weight,
    up_gain,
    up_shift,
    down_weight,
    down_gain,
    down_shift,
    cotangent,
):
    dp_size, fs_size = lax.axis_size("dp"), lax.axis_size("fsdp")
    first = first_call(dp_size, fs_size, classes, inputs, offset_table, bias_table,
        (qkv_weight, out_weight, up_weight, down_weight),
        (qkv_gain, qkv_shift, out_gain, out_shift, up_gain, up_shift, down_gain, down_shift))
    mixed, xs, biases, weights_full, vec = first[0], first[1], first[2:5], first[5:9], first[9]
    qkv_full, out_full, up_full, down_full = [w.reshape(-1, w.shape[2]) for w in weights_full]
    qkv_gains, qkv_shifts = vec[0], vec[1]
    out_gains, out_shifts = vec[2, :256], vec[3, :256]
    up_gains, up_shifts = vec[4, :512], vec[5, :512]
    down_gains, down_shifts = vec[6, :256], vec[7, :256]
    total = vec[10, 0]
    images = inputs.shape[0]
    length = images * SLOT
    limits = jnp.where(
        classes == 0,
        (GRID - 8) * (GRID - 8),
        jnp.where(classes == 1, (GRID - 4) * (GRID - 4), SLOT),
    )
    keep = (jnp.arange(SLOT)[None, :] < limits[:, None]).astype(jnp.float32)
    weights = keep.reshape(-1, 1)
    flat = inputs.reshape(length, -1)
    z_qkv = jnp.dot(flat, qkv_full, preferred_element_type=jnp.float32)
    hat_qkv, scale_qkv = (z_qkv - vec[9]) * vec[8], vec[8]
    attended_low, probs, shares = attend_call(classes, mixed, biases)
    attended = attended_low[:, :SLOT].astype(jnp.float32).reshape(length, -1)
    activated = jax.nn.silu(attended).astype(jnp.bfloat16)
    z_out = jnp.dot(activated, out_full, preferred_element_type=jnp.float32)
    branch, hat_out, scale_out, unused_out = norm_forward(z_out, weights, out_gains, out_shifts)
    middle = flat.astype(jnp.float32) + branch
    middle_low = middle.astype(jnp.bfloat16)
    z_up = jnp.dot(middle_low, up_full, preferred_element_type=jnp.float32)
    up_normed, hat_up, scale_up, unused_up = norm_forward(z_up, weights, up_gains, up_shifts)
    hidden = jax.nn.silu(up_normed).astype(jnp.bfloat16)
    z_down = jnp.dot(hidden, down_full, preferred_element_type=jnp.float32)
    down_normed, hat_down, scale_down, unused_down = norm_forward(
        z_down, weights, down_gains, down_shifts
    )
    output = ((middle + down_normed) * weights).astype(jnp.bfloat16).reshape(inputs.shape)
    grad_out = cotangent.astype(jnp.float32).reshape(length, -1) * weights
    dz_down, down_gain_grad, down_shift_grad = norm_backward(
        grad_out, hat_down, scale_down, total, down_gains, weights
    )
    dz_down_low = dz_down.astype(jnp.bfloat16)
    down_grad = left_product(hidden, dz_down_low)
    grad_up = right_product(dz_down_low, down_full) * silu_slope(up_normed)
    dz_up, up_gain_grad, up_shift_grad = norm_backward(
        grad_up, hat_up, scale_up, total, up_gains, weights
    )
    dz_up_low = dz_up.astype(jnp.bfloat16)
    up_grad = left_product(middle_low, dz_up_low)
    grad_middle = grad_out + right_product(dz_up_low, up_full)
    dz_out, out_gain_grad, out_shift_grad = norm_backward(
        grad_middle, hat_out, scale_out, total, out_gains, weights
    )
    dz_out_low = dz_out.astype(jnp.bfloat16)
    out_grad = left_product(activated, dz_out_low)
    grad_att = (right_product(dz_out_low, out_full) * silu_slope(attended)).astype(jnp.bfloat16)
    grad_att = jnp.pad(grad_att.reshape(images, SLOT, -1), ((0, 0), (0, ROWS - SLOT), (0, 0)))
    grad_mixed, *accs = back_call(classes, mixed, probs, shares, grad_att, attended_low)
    local_table = table_call(offset_table, accs)[:, :NOFF]
    grad_mixed = grad_mixed[:, :SLOT].astype(jnp.float32).reshape(length, -1)
    dz_qkv, qkv_gain_grad, qkv_shift_grad = norm_backward(
        grad_mixed, hat_qkv, scale_qkv, total, qkv_gains, weights
    )
    dz_qkv_low = dz_qkv.astype(jnp.bfloat16)
    qkv_grad = left_product(flat, dz_qkv_low)
    qkv_grad = restore(qkv_grad)
    qkv_gain_grad = restore(qkv_gain_grad[None])[0]
    qkv_shift_grad = restore(qkv_shift_grad[None])[0]
    input_grad = (grad_middle + right_product(dz_qkv_low, qkv_full)).reshape(inputs.shape)
    table_grad = lax.psum(local_table, ("dp", "fsdp"))
    whole = (
        lax.psum(qkv_grad.astype(jnp.bfloat16), "dp").astype(jnp.float32),
        lax.psum(out_grad.astype(jnp.bfloat16), "dp").astype(jnp.float32),
        lax.psum(up_grad.astype(jnp.bfloat16), "dp").astype(jnp.float32),
        lax.psum(down_grad.astype(jnp.bfloat16), "dp").astype(jnp.float32),
    )
    summed = (
        lax.psum_scatter(
            whole[0].astype(jnp.bfloat16), "fsdp", scatter_dimension=0, tiled=True
        ).astype(jnp.float32),
        lax.psum_scatter(
            whole[1].astype(jnp.bfloat16), "fsdp", scatter_dimension=0, tiled=True
        ).astype(jnp.float32),
        lax.psum_scatter(
            whole[2].astype(jnp.bfloat16), "fsdp", scatter_dimension=0, tiled=True
        ).astype(jnp.float32),
        lax.psum_scatter(
            whole[3].astype(jnp.bfloat16), "fsdp", scatter_dimension=0, tiled=True
        ).astype(jnp.float32),
    )
    return (
        output,
        input_grad,
        table_grad,
        summed[0],
        own_slice(qkv_gain_grad),
        own_slice(qkv_shift_grad),
        summed[1],
        own_slice(out_gain_grad),
        own_slice(out_shift_grad),
        summed[2],
        own_slice(up_gain_grad),
        own_slice(up_shift_grad),
        summed[3],
        own_slice(down_gain_grad),
        own_slice(down_shift_grad),
    )


def solution(mesh):
    placed = (
        P(("dp", "fsdp"), None, None),
        P(("dp", "fsdp")),
        P(),
        P(),
        P("fsdp", None),
        P("fsdp"),
        P("fsdp"),
        P("fsdp", None),
        P("fsdp"),
        P("fsdp"),
        P("fsdp", None),
        P("fsdp"),
        P("fsdp"),
        P("fsdp", None),
        P("fsdp"),
        P("fsdp"),
        P(("dp", "fsdp"), None, None),
    )
    return jax.shard_map(
        shards,
        mesh=mesh,
        in_specs=placed,
        out_specs=(
            P(("dp", "fsdp"), None, None),
            P(("dp", "fsdp"), None, None),
            P(),
            P("fsdp", None),
            P("fsdp"),
            P("fsdp"),
            P("fsdp", None),
            P("fsdp"),
            P("fsdp"),
            P("fsdp", None),
            P("fsdp"),
            P("fsdp"),
            P("fsdp", None),
            P("fsdp"),
            P("fsdp"),
        ),
        check_vma=False,
    )
```

```python
import functools

import jax
import jax.numpy as jnp
from jax import lax
from jax.experimental import pallas as pl
from jax.experimental.pallas import tpu as pltpu
from jax.sharding import PartitionSpec as P

HEADS = 4
KEY = 32
VALD = 128
GRID = 18
CLASSES = 3
SLOT = 324
NOFF = 324


EPS = 1e-05
LOG2E = 1.4426950408889634
LN2 = 0.6931471805599453
ROWS = 336
PARTS = ((10, 100, 112, 128), (14, 196, 208, 256), (18, 324, 336, 384))
VMEM = pl.BlockSpec(memory_space=pltpu.VMEM)


def dot_nn(left, right):
    return jnp.dot(left, right, preferred_element_type=jnp.float32)


def dot_nt(left, right):
    return lax.dot_general(left, right, (((1,), (1,)), ((), ())), preferred_element_type=jnp.float32)


def dot_tn(left, right):
    return lax.dot_general(left, right, (((0,), (0,)), ((), ())), preferred_element_type=jnp.float32)


def pad_rows(value, rows):
    if value.shape[0] == rows:
        return value
    return jnp.concatenate([value, jnp.zeros((rows - value.shape[0], value.shape[1]), value.dtype)], axis=0)


def pad_lanes(value, lanes):
    if value.shape[1] == lanes:
        return value
    return jnp.concatenate([value, jnp.zeros((value.shape[0], lanes - value.shape[1]), value.dtype)], axis=1)


def bias_tables(off_ref, table_ref, index_ref, outs):
    tables = []
    for head in range(HEADS):
        row = pad_lanes(table_ref[head : head + 1, :], 384) * LOG2E
        tables.append([jnp.broadcast_to(row[:, 128 * k : 128 * k + 128], (8, 128)) for k in range(3)])
    index_ref[...] = jnp.zeros_like(index_ref)
    for number, (_, amount, rows, lanes) in enumerate(PARTS):
        index_ref[:SLOT, :SLOT] = off_ref[number]

        def tile(step, _, amount=amount, lanes=lanes, out=outs[number]):
            at = pl.multiple_of(step * 8, 8)
            for block in range(lanes // 128):
                index = index_ref[pl.ds(at, 8), 128 * block : 128 * block + 128]
                low = index & 127
                part = index >> 7
                valid = lax.broadcasted_iota(jnp.int32, (8, 128), 1) + 128 * block < amount
                for head in range(HEADS):
                    found = [
                        jnp.take_along_axis(tables[head][k], low, axis=1, mode="promise_in_bounds")
                        for k in range(3)
                    ]
                    value = jnp.where(part == 0, found[0], jnp.where(part == 1, found[1], found[2]))
                    column = (head % 2) * lanes + 128 * block
                    out[head // 2, pl.ds(at, 8), column : column + 128] = jnp.where(valid, value, -1e30)
            return 0

        lax.fori_loop(0, rows // 8, tile, 0)


def head_keys(keys, pair, lanes):
    owner = lax.broadcasted_iota(jnp.int32, keys.shape, 1) // KEY
    zero = jnp.zeros_like(keys)
    return jnp.concatenate(
        [pad_rows(jnp.where(owner == 2 * pair + side, keys, zero), lanes) for side in range(2)], axis=0
    )


def pair_values(values, lanes):
    zero = jnp.zeros((lanes, VALD), values.dtype)
    top = jnp.concatenate([pad_rows(values[:, :VALD], lanes), zero], axis=1)
    low = jnp.concatenate([zero, pad_rows(values[:, VALD:], lanes)], axis=1)
    return jnp.concatenate([top, low], axis=0)


def attend_kernel(class_ref, mixed_ref, bias0, bias1, bias2, att_ref, p_ref, r_ref):
    kind = class_ref[pl.program_id(0)]
    for number, (_, amount, rows, lanes) in enumerate(PARTS):

        @pl.when(kind == number)
        def _(amount=amount, rows=rows, lanes=lanes, bias=(bias0, bias1, bias2)[number]):
            query = mixed_ref[0, :rows, :128]
            keys = mixed_ref[0, :rows, 128:256]
            kept = lax.broadcasted_iota(jnp.int32, (rows, VALD), 0) < amount
            lane = lax.broadcasted_iota(jnp.int32, (rows, 128), 1)
            shares = jnp.zeros((rows, 128), jnp.float32)
            for pair in range(2):
                scores = dot_nt(query, head_keys(keys, pair, lanes)) + bias[pair]
                parts, inverse = [], []
                for side in range(2):
                    own = scores[:, side * lanes : (side + 1) * lanes]
                    expo = jnp.exp2(own - jnp.max(own, axis=1, keepdims=True))
                    share = 1.0 / jnp.sum(expo, axis=1, keepdims=True)
                    shares = jnp.where(lane == 2 * pair + side, share, shares)
                    parts.append(expo.astype(jnp.bfloat16))
                    inverse.append(share)
                both = jnp.concatenate(parts, axis=1)
                p_ref[0, :rows, 2 * pair * lanes : 2 * (pair + 1) * lanes] = both
                values = mixed_ref[0, :rows, 256 + 256 * pair : 512 + 256 * pair]
                sums = dot_nn(both, pair_values(values, lanes))
                for side in range(2):
                    own = sums[:, side * VALD : (side + 1) * VALD] * inverse[side]
                    at = (2 * pair + side) * VALD
                    att_ref[0, :rows, at : at + VALD] = jnp.where(kept, own, 0.0).astype(jnp.bfloat16)
            r_ref[0, :rows, :] = shares
            if rows < ROWS:
                att_ref[0, rows:, :] = jnp.zeros((ROWS - rows, att_ref.shape[2]), jnp.bfloat16)


def back_kernel(class_ref, mixed_ref, p_ref, r_ref, g_ref, att_ref, gmix_ref, acc0, acc1, acc2):
    accs = (acc0, acc1, acc2)

    @pl.when(pl.program_id(0) == 0)
    def _():
        for acc in accs:
            acc[...] = jnp.zeros_like(acc)

    kind = class_ref[pl.program_id(0)]
    for number, (_, amount, rows, lanes) in enumerate(PARTS):

        @pl.when(kind == number)
        def _(rows=rows, lanes=lanes, acc=accs[number]):
            query = mixed_ref[0, :rows, :128]
            keys = mixed_ref[0, :rows, 128:256]
            owner = lax.broadcasted_iota(jnp.int32, (rows, 128), 1) // KEY
            d_query = jnp.zeros((rows, 128), jnp.float32)
            d_keys = jnp.zeros((rows, 128), jnp.float32)
            for pair in range(2):
                grads, deltas = [], []
                for side in range(2):
                    head = 2 * pair + side
                    at = head * VALD
                    grad = g_ref[0, :rows, at : at + VALD].astype(jnp.float32) * r_ref[0, :rows, head : head + 1]
                    own = att_ref[0, :rows, at : at + VALD].astype(jnp.float32)
                    deltas.append(jnp.sum(grad * own, axis=1, keepdims=True))
                    grads.append(grad.astype(jnp.bfloat16))
                both = jnp.concatenate(grads, axis=1)
                values = mixed_ref[0, :rows, 256 + 256 * pair : 512 + 256 * pair]
                d_probs = dot_nt(both, pair_values(values, lanes))
                probs = p_ref[0, :rows, 2 * pair * lanes : 2 * (pair + 1) * lanes]
                low = []
                for side in range(2):
                    cut = slice(side * lanes, (side + 1) * lanes)
                    d_score = probs[:, cut].astype(jnp.float32) * (d_probs[:, cut] - deltas[side])
                    acc[pair, :, cut] += d_score
                    low.append(d_score.astype(jnp.bfloat16))
                d_low = jnp.concatenate(low, axis=1)
                d_query = d_query + dot_nn(d_low, head_keys(keys, pair, lanes))
                turned = dot_tn(d_low, query)
                d_values = dot_tn(probs, both)
                for side in range(2):
                    head = 2 * pair + side
                    d_keys = jnp.where(owner == head, turned[side * lanes : side * lanes + rows], d_keys)
                    at = 256 + head * VALD
                    gmix_ref[0, :rows, at : at + VALD] = d_values[
                        side * lanes : side * lanes + rows, side * VALD : (side + 1) * VALD
                    ].astype(jnp.bfloat16)
            gmix_ref[0, :rows, :128] = (d_query * KEY ** (-0.5)).astype(jnp.bfloat16)
            gmix_ref[0, :rows, 128:256] = (d_keys * LN2).astype(jnp.bfloat16)
            if rows < ROWS:
                gmix_ref[0, rows:, :] = jnp.zeros((ROWS - rows, gmix_ref.shape[2]), jnp.bfloat16)


def table_sums(off_ref, accs):
    totals = [jnp.zeros((24, 640), jnp.float32) for _ in range(HEADS)]
    for number, (side_of, amount, rows, lanes) in enumerate(PARTS):
        offsets = off_ref[number]
        row = lax.broadcasted_iota(jnp.int32, (SLOT, 1), 0)
        most = jnp.max(offsets, axis=1, keepdims=True)
        corner = jnp.min(jnp.where(most == (side_of - 1) * (GRID + 1), row, SLOT), axis=0, keepdims=True)
        place = jnp.sum(jnp.where(row == corner, offsets, 0), axis=0, keepdims=True)
        place = jnp.where(lax.broadcasted_iota(jnp.int32, (1, SLOT), 1) < amount, place, -1)
        wide = jnp.concatenate([place, jnp.full((1, 384 - SLOT), -1, jnp.int32)], axis=1)
        cell = lax.broadcasted_iota(jnp.int32, (24 * side_of, 1), 0)
        cell_row = (cell * 2731) >> 16
        cell_col = cell - 24 * cell_row
        code = jnp.where(cell_col < side_of, cell_row * GRID + cell_col, -2)
        left = (code == wide[:, :rows]).astype(jnp.float32).astype(jnp.bfloat16)
        spot = lax.broadcasted_iota(jnp.int32, (384, 1), 0)
        right = (spot == wide[:, :lanes]).astype(jnp.float32).astype(jnp.bfloat16)
        for head in range(HEADS):
            at = (head % 2) * lanes
            score = accs[number][head // 2, :, at : at + lanes].astype(jnp.bfloat16)
            sorted_rows = dot_nn(left, score).astype(jnp.bfloat16)
            both = dot_nt(sorted_rows, right)
            for line in range(side_of):
                part = pad_lanes(both[24 * line : 24 * line + 24], 640)
                totals[head] = totals[head] + pltpu.roll(part, (GRID - 1 - line) * GRID, 1)
    lane = lax.broadcasted_iota(jnp.int32, (24, 640), 1)
    lane_row = (lane * 3641) >> 16
    away = jnp.abs(lane - GRID * lane_row - lax.broadcasted_iota(jnp.int32, (24, 640), 0))
    wide_row = lax.broadcasted_iota(jnp.int32, (640, 1), 0)
    wide_row = jnp.abs(((wide_row * 3641) >> 16) - (GRID - 1))
    out_lane = lax.broadcasted_iota(jnp.int32, (1, 384), 1)
    out_row = (out_lane * 3641) >> 16
    fold = (wide_row == out_row).astype(jnp.float32).astype(jnp.bfloat16)
    out_col = out_lane - GRID * out_row
    pick = lax.broadcasted_iota(jnp.int32, (24, 1), 0) == out_col
    rows_out = []
    for head in range(HEADS):
        lines = [
            jnp.sum(jnp.where(away == d, totals[head], 0.0), axis=0, keepdims=True) for d in range(GRID)
        ]
        lines = pad_rows(jnp.concatenate(lines, axis=0), 24)
        high = lines.astype(jnp.bfloat16)
        low = (lines - high.astype(jnp.float32)).astype(jnp.bfloat16)
        spread = dot_nn(high, fold) + dot_nn(low, fold)
        rows_out.append(jnp.sum(jnp.where(pick, spread, 0.0), axis=0, keepdims=True))
    return jnp.concatenate(rows_out, axis=0)


def image_spec(width):
    return pl.BlockSpec((1, ROWS, width), lambda i, c: (i, 0, 0))


def whole_spec(shape):
    return pl.BlockSpec(shape, lambda i, c: (0,) * len(shape))


def attend_call(classes, mixed, biases):
    images = mixed.shape[0]
    return pl.pallas_call(
        attend_kernel,
        grid_spec=pltpu.PrefetchScalarGridSpec(
            num_scalar_prefetch=1,
            grid=(images,),
            in_specs=[image_spec(768)] + [whole_spec(b.shape) for b in biases],
            out_specs=[image_spec(512), image_spec(1536), image_spec(128)],
        ),
        out_shape=[
            jax.ShapeDtypeStruct((images, ROWS, 512), jnp.bfloat16),
            jax.ShapeDtypeStruct((images, ROWS, 1536), jnp.bfloat16),
            jax.ShapeDtypeStruct((images, ROWS, 128), jnp.float32),
        ],
        compiler_params=pltpu.CompilerParams(vmem_limit_bytes=48 * 2**20),
    )(classes, mixed, *biases)


def back_call(classes, mixed, probs, shares, grad, attended):
    images = mixed.shape[0]
    shapes = [(2, r, 2 * l) for _, _, r, l in PARTS]
    return pl.pallas_call(
        back_kernel,
        grid_spec=pltpu.PrefetchScalarGridSpec(
            num_scalar_prefetch=1,
            grid=(images,),
            in_specs=[image_spec(768), image_spec(1536), image_spec(128), image_spec(512), image_spec(512)],
            out_specs=[image_spec(768)] + [whole_spec(s) for s in shapes],
        ),
        out_shape=[jax.ShapeDtypeStruct((images, ROWS, 768), jnp.bfloat16)]
        + [jax.ShapeDtypeStruct(s, jnp.float32) for s in shapes],
        compiler_params=pltpu.CompilerParams(vmem_limit_bytes=48 * 2**20),
    )(classes, mixed, probs, shares, grad, attended)


MESH = pl.DeviceIdType.MESH
ANY = pl.BlockSpec(memory_space=pl.ANY)
SMEM = pl.BlockSpec(memory_space=pltpu.SMEM)


class Place:
    def __init__(self, dp_size, fs_size):
        self.dp_size, self.fs_size = dp_size, fs_size
        self.size = dp_size * fs_size
        self.dp, self.fs = lax.axis_index("dp"), lax.axis_index("fsdp")
        self.me = self.dp * fs_size + self.fs
        self.core = lax.rem(self.dp, 2)
        self.partner = (self.dp + 1 - 2 * self.core, self.fs)

    def other(self, step):
        spot = lax.rem(self.me + step, self.size)
        return (spot // self.fs_size, lax.rem(spot, self.fs_size))

    def greet(self):
        barrier = pltpu.get_barrier_semaphore()

        def signal(step, _):
            pl.semaphore_signal(barrier, inc=1, device_id=self.other(step), device_id_type=MESH)
            return 0

        lax.fori_loop(1, self.size, signal, 0)

    def meet(self):
        pl.semaphore_wait(pltpu.get_barrier_semaphore(), self.size - 1)

    def spread(self, buf, value, send, recv):
        buf[self.me] = value

        def start(step, _):
            push(buf.at[self.me], buf.at[self.me], send, recv, self.other(step))
            return 0

        lax.fori_loop(1, self.size, start, 0)

    def collect(self, buf, recv):
        await_bytes(buf.at[pl.ds(0, self.size - 1)], recv)
        return jnp.sum(buf[...], axis=0)

    def settle(self, buf, send):
        await_bytes(buf.at[pl.ds(0, self.size - 1)], send)


def push(source, target, send, recv, device):
    pltpu.make_async_remote_copy(
        src_ref=source, dst_ref=target, send_sem=send, recv_sem=recv, device_id=device, device_id_type=MESH
    ).start()


def await_bytes(ref, sem):
    pltpu.make_async_copy(ref, ref, sem).wait()


def halves(width):
    return (width // 2,) * 2


def gather_start(place, buf, send, recv):
    half = buf.shape[2] // 2

    def start(step, _):
        target = lax.rem(place.fs + step, place.fs_size)
        for core in range(2):

            @pl.when(place.core == core)
            def _():
                part = buf.at[place.fs, :, pl.ds(core * half, half)]
                push(part, part, send, recv, (place.dp, target))

        return 0

    lax.fori_loop(1, place.fs_size, start, 0)


def gather_pass(place, buf, recv, send2, recv2):
    half = buf.shape[2] // 2
    for core in range(2):

        @pl.when(place.core == core)
        def _():
            await_bytes(buf.at[pl.ds(0, place.fs_size - 1), :, pl.ds(core * half, half)], recv)
            part = buf.at[:, :, pl.ds(core * half, half)]
            push(part, part, send2, recv2, place.partner)


def gather_end(place, buf, recv2):
    half = buf.shape[2] // 2
    await_bytes(buf.at[:, :, pl.ds(0, half)], recv2)


def gather_settle(place, buf, send, send2):
    half = buf.shape[2] // 2
    await_bytes(buf.at[pl.ds(0, place.fs_size - 1), :, pl.ds(0, half)], send)
    await_bytes(buf.at[:, :, pl.ds(0, half)], send2)


def flat_weight(buf):
    shards, rows, width = buf.shape
    if rows % 16 == 0:
        return buf[...].reshape(shards * rows, width)
    wide = jnp.concatenate([buf[k].astype(jnp.float32) for k in range(shards)], axis=0)
    return wide.astype(jnp.bfloat16)


def split_low(value):
    high = value.astype(jnp.bfloat16)
    return high, (value - high.astype(jnp.float32)).astype(jnp.bfloat16)


def precise(left, right):
    high, low = split_low(left)
    return dot_nn(high, right) + dot_nn(low, right)


def arrange(columns):
    blocks = [columns[:, (2 * KEY + VALD) * h : (2 * KEY + VALD) * (h + 1)] for h in range(HEADS)]
    parts = [b[:, :KEY] for b in blocks] + [b[:, KEY : 2 * KEY] for b in blocks] + [b[:, 2 * KEY :] for b in blocks]
    return jnp.concatenate(parts, axis=1)


def restore(columns):
    parts = []
    for h in range(HEADS):
        parts += [
            columns[:, KEY * h : KEY * (h + 1)],
            columns[:, 128 + KEY * h : 128 + KEY * (h + 1)],
            columns[:, 256 + VALD * h : 256 + VALD * (h + 1)],
        ]
    return jnp.concatenate(parts, axis=1)


def by_columns(ref, value):
    for k in range(ref.shape[0]):
        ref[k] = value[:, 128 * k : 128 * k + 128]


def take_image(ref, image, images):
    return jnp.concatenate([ref[k, pl.ds(image, SLOT, stride=images), :] for k in range(ref.shape[0])], axis=1)


def put_image(ref, image, images, value):
    for k in range(ref.shape[0]):
        ref[k, pl.ds(image, SLOT, stride=images), :] = value[:SLOT, 128 * k : 128 * k + 128]


def limits_of(kind):
    return jnp.where(kind == 0, (GRID - 8) ** 2, jnp.where(kind == 1, (GRID - 4) ** 2, SLOT))


def assemble(buf, widths, lanes):
    turned = {}
    for width in sorted(set(widths)):
        turned[width] = sum(
            pltpu.roll(pad_lanes(buf[k], lanes), k * width, 1) if k else pad_lanes(buf[k], lanes)
            for k in range(buf.shape[0])
        )
    return [turned[width][k : k + 1] for k, width in enumerate(widths)]


def first_kernel(dp_size, fs_size, *refs):
    class_ref, x_ref, off_ref, table_ref = refs[:4]
    shards, vectors = refs[4:8], refs[8:16]
    mixed_out, xs_out, bias_out, weight_out, vec_out = refs[16], refs[17], refs[18:21], refs[21:25], refs[25]
    xs, z, mixed, index, wide = refs[26:31]
    bias, weights = refs[31:34], refs[34:38]
    vbuf, stat = refs[38:40]
    send, recv, send2, recv2, local = refs[40:45]
    place = Place(dp_size, fs_size)
    images = xs.shape[0]

    for k in range(4):
        own = shards[k][...]
        if k == 0:
            own = arrange(own.astype(jnp.float32)).astype(jnp.bfloat16)
        weights[k][place.fs] = own
    vbuf[place.fs] = jnp.concatenate(
        [pad_lanes(v[...].astype(jnp.float32), 128) for v in vectors], axis=0
    )
    place.greet()

    by_columns(wide, x_ref[...].astype(jnp.float32))
    count = jnp.int32(0)
    for image in range(images):
        limit = limits_of(class_ref[image])
        row = lax.broadcasted_iota(jnp.int32, (SLOT, xs.shape[2]), 0)
        value = jnp.where(row < limit, take_image(wide, image, images), 0.0)
        xs[image] = pad_rows(value, ROWS).astype(jnp.bfloat16)
        count = count + limit

    flat = xs[...].reshape(images * ROWS, xs.shape[2])
    gram = dot_tn(flat, flat)
    total_x = dot_nn(jnp.ones((8, images * ROWS), jnp.bfloat16), flat)

    place.meet()
    gather_start(place, weights[0], send.at[0], recv.at[0])

    def start(step, _):
        target = lax.rem(place.fs + step, place.fs_size)
        push(vbuf.at[place.fs], vbuf.at[place.fs], send.at[4], recv.at[4], (place.dp, target))
        return 0

    lax.fori_loop(1, place.fs_size, start, 0)
    for k in range(1, 4):
        gather_start(place, weights[k], send.at[k], recv.at[k])
    xs_copy = pltpu.make_async_copy(xs, xs_out, local.at[0])
    xs_copy.start()
    bias_tables(off_ref, table_ref, index, bias)
    copies = [xs_copy]
    for k in range(3):
        copies.append(pltpu.make_async_copy(bias[k], bias_out[k], local.at[1 + k]))
        copies[-1].start()

    gather_pass(place, weights[0], recv.at[0], send2.at[0], recv2.at[0])
    gather_end(place, weights[0], recv2.at[0])
    weight = flat_weight(weights[0])
    high, low = split_low(gram)
    spread = dot_nn(high, weight) + dot_nn(low, weight)
    squares = jnp.sum(weight.astype(jnp.float32) * spread, axis=0, keepdims=True)
    sums = precise(total_x, weight)[:1]
    tail = jnp.full((1, 128), count.astype(jnp.float32))
    place.spread(
        stat,
        jnp.concatenate(
            [jnp.concatenate([sums, tail], axis=1), jnp.concatenate([squares, tail], axis=1)], axis=0
        ),
        send.at[5],
        recv.at[5],
    )

    def product(image, _):
        z[image] = dot_nn(xs[image], weight)
        return 0

    lax.fori_loop(0, images, product, 0)
    for k in range(1, 4):
        gather_pass(place, weights[k], recv.at[k], send2.at[k], recv2.at[k])
    await_bytes(vbuf.at[pl.ds(0, place.fs_size - 1)], recv.at[4])
    widths = [v.shape[1] for v in vectors]
    full = assemble(vbuf, widths, 768)
    full[0], full[1] = arrange(full[0]), arrange(full[1])

    got = place.collect(stat, recv.at[5])
    whole = got[0:1, 768:769]
    center = got[0:1, :768] / whole
    square = got[1:2, :768] / whole
    scale = lax.rsqrt(square - center * center + EPS)
    vec_out[...] = jnp.concatenate(
        full + [scale, center, jnp.broadcast_to(whole, (1, 768)), jnp.zeros((5, 768), jnp.float32)], axis=0
    )
    gain = scale * full[0]
    shift = full[1] - center * gain
    fold = jnp.where(lax.broadcasted_iota(jnp.int32, (1, 768), 1) < 128, KEY ** (-0.5) * LOG2E, 1.0)
    gain, shift = gain * fold, shift * fold

    def normal(image, _):
        mixed[image] = (z[image] * gain + shift).astype(jnp.bfloat16)
        pltpu.make_async_copy(mixed.at[image], mixed_out.at[image], local.at[8 + image]).start()
        return 0

    lax.fori_loop(0, images, normal, 0)
    for k in range(4):
        if k > 0:
            gather_end(place, weights[k], recv2.at[k])
        copies.append(pltpu.make_async_copy(weights[k], weight_out[k], local.at[4 + k]))
        copies[-1].start()
    for k in range(4):
        gather_settle(place, weights[k], send.at[k], send2.at[k])
    await_bytes(vbuf.at[pl.ds(0, place.fs_size - 1)], send.at[4])
    place.settle(stat, send.at[5])
    for copy in copies:
        copy.wait()

    def finish(image, _):
        pltpu.make_async_copy(mixed.at[image], mixed_out.at[image], local.at[8 + image]).wait()
        return 0

    lax.fori_loop(0, images, finish, 0)


def first_call(dp_size, fs_size, classes, inputs, offset_table, bias_table, weights, vectors):
    images, model = classes.shape[0], inputs.shape[1]
    vectors = [v.reshape(1, -1) for v in vectors]
    shapes = [(fs_size,) + w.shape for w in weights]
    biases = [(2, r, 2 * l) for _, _, r, l in PARTS]
    bf, f32 = jnp.bfloat16, jnp.float32
    return pl.pallas_call(
        functools.partial(first_kernel, dp_size, fs_size),
        out_shape=[
            jax.ShapeDtypeStruct((images, ROWS, 768), bf),
            jax.ShapeDtypeStruct((images, ROWS, model), bf),
        ]
        + [jax.ShapeDtypeStruct(s, f32) for s in biases]
        + [jax.ShapeDtypeStruct(s, bf) for s in shapes]
        + [jax.ShapeDtypeStruct((16, 768), f32)],
        in_specs=[SMEM] + [VMEM] * 15,
        out_specs=[ANY] * 9 + [VMEM],
        scratch_shapes=[
            pltpu.VMEM((images, ROWS, model), bf),
            pltpu.VMEM((images, ROWS, 768), f32),
            pltpu.VMEM((images, ROWS, 768), bf),
            pltpu.VMEM((ROWS, 384), jnp.int32),
            pltpu.VMEM((model // 128, inputs.shape[0], 128), f32),
        ]
        + [pltpu.VMEM(s, f32) for s in biases]
        + [pltpu.VMEM(s, bf) for s in shapes]
        + [
            pltpu.VMEM((fs_size, 8, 128), f32),
            pltpu.VMEM((dp_size * fs_size, 2, 896), f32),
            pltpu.SemaphoreType.DMA((6,)),
            pltpu.SemaphoreType.DMA((6,)),
            pltpu.SemaphoreType.DMA((4,)),
            pltpu.SemaphoreType.DMA((4,)),
            pltpu.SemaphoreType.DMA((8 + images,)),
        ],
        compiler_params=pltpu.CompilerParams(
            collective_id=0, has_side_effects=True, vmem_limit_bytes=56 * 2**20
        ),
    )(classes, inputs, offset_table, bias_table, *weights, *vectors)


def total_rows(value):
    return jnp.sum(value, axis=0, keepdims=True)


def sigma_of(value):
    return 0.5 * jnp.tanh(0.5 * value) + 0.5


def slope_of(value):
    sigma = sigma_of(value)
    return sigma * (1.0 + value * (1.0 - sigma))


def norm_parts(sums, squares, total, gain, shift):
    center = sums / total
    scale = lax.rsqrt(squares / total - center * center + EPS)
    return center, scale, scale * gain, shift - center * scale * gain


def back_parts(grad_sum, grad_z, total, gain, center, scale):
    gain_grad = scale * (grad_z - center * grad_sum)
    alpha = scale * gain
    slant = alpha * scale * gain_grad / total
    level = alpha * (grad_sum - center * scale * gain_grad) / total
    return gain_grad, alpha, slant, level


def outer(column, row):
    left = jnp.concatenate([column, jnp.zeros((7, column.shape[1]), jnp.float32)], axis=0)
    right = jnp.concatenate([row, jnp.zeros((7, row.shape[1]), jnp.float32)], axis=0)
    left_high, left_low = split_low(left)
    right_high, right_low = split_low(right)
    return dot_tn(left_high, right_high) + dot_tn(left_high, right_low) + dot_tn(left_low, right_high)


def middle_kernel(dp_size, fs_size, group, *refs):
    class_ref, att_in, xs_in, cot_in = refs[:4]
    weight_in, vec_ref = refs[4:7], refs[7]
    out_out, gatt_out, gm_out, grad_out, vec_out = refs[8], refs[9], refs[10], refs[11:14], refs[14]
    att, xs, cot, wo_buf, wu_buf, wd_buf = refs[15:21]
    gs, act, slope_att, zo, low, zu, hid, slope_up, zd, dzd, gu, gm, dzo, out, gatt, wide = refs[21:37]
    stat_o, stat_u, stat_d, stat_bu, stat_bo = refs[37:42]
    send, recv, local = refs[42:45]
    place = Place(dp_size, fs_size)
    images = att.shape[0]
    chunks = images // group
    size = group * ROWS
    f32, bf = jnp.float32, jnp.bfloat16

    def copy(source, target, at):
        return pltpu.make_async_copy(source, target, local.at[at])

    loads = [
        copy(weight_in[0], wo_buf, 0),
        copy(xs_in, xs, 1),
        copy(cot_in, cot, 2),
        copy(weight_in[1], wu_buf, 3),
        copy(weight_in[2], wd_buf, 4),
    ]
    loads[0].start()

    def att_copy(k):
        part = pl.ds(k * group, group)
        return copy(att_in.at[part], att.at[part], 8 + k)

    for k in range(chunks):
        att_copy(k).start()
    for load in loads[1:]:
        load.start()
    place.greet()

    def get(ref, k):
        return ref[pl.ds(k * group, group)].reshape(size, ref.shape[2])

    def put(ref, k, value):
        ref[pl.ds(k * group, group)] = value.astype(ref.dtype).reshape(group, ROWS, ref.shape[2])

    def kept(k, width):
        row = lax.broadcasted_iota(jnp.int32, (ROWS, width), 0)
        return jnp.concatenate([row < limits_of(class_ref[k * group + j]) for j in range(group)], axis=0)

    def over(body, carry):
        return lax.fori_loop(0, chunks, body, carry)

    def zero(width):
        return jnp.zeros((1, width), f32)

    model = xs.shape[2]
    hidden = zu.shape[2]
    total = vec_ref[10:11, :1]
    out_gain, out_shift = vec_ref[2:3, :model], vec_ref[3:4, :model]
    up_gain, up_shift = vec_ref[4:5, :hidden], vec_ref[5:6, :hidden]
    down_gain, down_shift = vec_ref[6:7, :model], vec_ref[7:8, :model]

    loads[0].wait()
    wo = flat_weight(wo_buf)

    def step_out(k, carry):
        att_copy(k).wait()
        value = get(att, k).astype(f32)
        active = (value * sigma_of(value)).astype(bf)
        put(act, k, active)
        z = dot_nn(active, wo)
        put(zo, k, z)
        return carry[0] + total_rows(z), carry[1] + total_rows(z * z)

    sums = over(step_out, (zero(model), zero(model)))
    place.meet()
    place.spread(stat_o, jnp.concatenate(sums, axis=0), send.at[0], recv.at[0])
    for load in loads[1:]:
        load.wait()

    def fill_out(k, _):
        put(slope_att, k, slope_of(get(att, k).astype(f32)))
        return 0

    over(fill_out, 0)
    by_columns(wide, cot[...].astype(f32))
    grad_sum = zero(model)
    for image in range(images):
        row = lax.broadcasted_iota(jnp.int32, (SLOT, model), 0)
        value = jnp.where(row < limits_of(class_ref[image]), take_image(wide, image, images), 0.0)
        gs[image] = pad_rows(value, ROWS).astype(bf)
        grad_sum = grad_sum + total_rows(value)
    wu, wd = flat_weight(wu_buf), flat_weight(wd_buf)
    got = place.collect(stat_o, recv.at[0])
    center_o, scale_o, a_o, b_o = norm_parts(got[0:1], got[1:2], total, out_gain, out_shift)

    def middle_of(k):
        return get(xs, k).astype(f32) + get(zo, k) * a_o + b_o

    def step_up(k, carry):
        lower = jnp.where(kept(k, model), middle_of(k), 0.0).astype(bf)
        put(low, k, lower)
        z = dot_nn(lower, wu)
        put(zu, k, z)
        return carry[0] + total_rows(z), carry[1] + total_rows(z * z)

    sums = over(step_up, (zero(hidden), zero(hidden)))
    place.spread(stat_u, jnp.concatenate(sums, axis=0), send.at[1], recv.at[1])
    low_flat = low[...].reshape(images * ROWS, model)
    low_gram = dot_tn(low_flat, low_flat)
    low_sum = dot_nn(jnp.ones((8, images * ROWS), bf), low_flat)[:1]
    got = place.collect(stat_u, recv.at[1])
    center_u, scale_u, a_u, b_u = norm_parts(got[0:1], got[1:2], total, up_gain, up_shift)

    def step_down(k, carry):
        value = get(zu, k) * a_u + b_u
        active = jnp.where(kept(k, hidden), value * sigma_of(value), 0.0).astype(bf)
        put(hid, k, active)
        z = dot_nn(active, wd)
        put(zd, k, z)
        return (
            carry[0] + total_rows(z),
            carry[1] + total_rows(z * z),
            carry[2] + total_rows(z * get(gs, k).astype(f32)),
        )

    sums = over(step_down, (zero(model), zero(model), zero(model)))
    place.spread(stat_d, jnp.concatenate(sums + (grad_sum,), axis=0), send.at[2], recv.at[2])

    def fill_down(k, _):
        put(slope_up, k, slope_of(get(zu, k) * a_u + b_u))
        return 0

    over(fill_down, 0)
    got = place.collect(stat_d, recv.at[2])
    center_d, scale_d, a_d, b_d = norm_parts(got[0:1], got[1:2], total, down_gain, down_shift)
    down_shift_grad = got[3:4]
    down_gain_grad, alpha, slant, level = back_parts(got[3:4], got[2:3], total, down_gain, center_d, scale_d)

    def step_back_down(k, carry):
        dz = get(gs, k).astype(f32) * alpha - get(zd, k) * slant - jnp.where(kept(k, model), level, 0.0)
        dz = dz.astype(bf)
        put(dzd, k, dz)
        grad = dot_nt(dz, wd) * get(slope_up, k).astype(f32)
        put(gu, k, grad)
        return carry[0] + total_rows(grad), carry[1] + total_rows(grad * get(zu, k))

    sums = over(step_back_down, (zero(hidden), zero(hidden)))
    place.spread(stat_bu, jnp.concatenate(sums, axis=0), send.at[3], recv.at[3])

    def fill_back_down(k, carry):
        grad = get(gu, k)
        carry = carry + dot_tn(get(low, k), grad.astype(bf))
        put(gm, k, get(gs, k).astype(f32) + dot_nt((grad * a_u).astype(bf), wu))
        return carry

    up_raw = over(fill_back_down, jnp.zeros((model, hidden), f32))
    for image in range(images):
        row = lax.broadcasted_iota(jnp.int32, (ROWS, model), 0)
        value = xs[image].astype(f32) + zo[image] * a_o + zd[image] * a_d + (b_o + b_d)
        value = jnp.where(row < limits_of(class_ref[image]), value, 0.0)
        put_image(wide, image, images, value)
    for k in range(wide.shape[0]):
        out[:, 128 * k : 128 * k + 128] = wide[k].astype(bf)
    out_copy = copy(out, out_out, 5)
    out_copy.start()
    down_grad = dot_tn(hid[...].reshape(images * ROWS, hidden), dzd[...].reshape(images * ROWS, model))
    grad_out[2][...] = down_grad.reshape(grad_out[2].shape).astype(bf)
    got = place.collect(stat_bu, recv.at[3])
    up_shift_grad = got[0:1]
    up_gain_grad, alpha_u, slant_u, level_u = back_parts(got[0:1], got[1:2], total, up_gain, center_u, scale_u)
    mix = dot_nt((wu.astype(f32) * slant_u).astype(bf), wu).astype(bf)
    high, rest = split_low(jnp.broadcast_to(level_u, (8, hidden)))
    lift = (dot_nt(high, wu) + dot_nt(rest, wu))[:1]

    def step_back_up(k, carry):
        grad = get(gm, k) - dot_nn(get(low, k), mix) - jnp.where(kept(k, model), lift, 0.0)
        put(gm, k, grad)
        part = pl.ds(k * group, group)
        copy(gm.at[part], gm_out.at[part], 8 + chunks + k).start()
        return carry[0] + total_rows(grad), carry[1] + total_rows(grad * get(zo, k))

    sums = over(step_back_up, (zero(model), zero(model)))
    place.spread(stat_bo, jnp.concatenate(sums, axis=0), send.at[4], recv.at[4])
    up_grad = up_raw * alpha_u - precise(low_gram, wu) * slant_u - outer(low_sum, level_u)
    grad_out[1][...] = up_grad.reshape(grad_out[1].shape).astype(bf)
    got = place.collect(stat_bo, recv.at[4])
    out_shift_grad = got[0:1]
    out_gain_grad, alpha_o, slant_o, level_o = back_parts(got[0:1], got[1:2], total, out_gain, center_o, scale_o)

    def step_back_out(k, _):
        dz = get(gm, k) * alpha_o - get(zo, k) * slant_o - jnp.where(kept(k, model), level_o, 0.0)
        dz = dz.astype(bf)
        put(dzo, k, dz)
        put(gatt, k, dot_nt(dz, wo) * get(slope_att, k).astype(f32))
        part = pl.ds(k * group, group)
        copy(gatt.at[part], gatt_out.at[part], 8 + 2 * chunks + k).start()
        return 0

    over(step_back_out, 0)
    out_grad = dot_tn(act[...].reshape(images * ROWS, act.shape[2]), dzo[...].reshape(images * ROWS, model))
    grad_out[0][...] = out_grad.reshape(grad_out[0].shape).astype(bf)
    vec_out[...] = jnp.concatenate(
        [
            pad_lanes(v, hidden)
            for v in (
                out_gain_grad,
                out_shift_grad,
                up_gain_grad,
                up_shift_grad,
                down_gain_grad,
                down_shift_grad,
                zero(hidden),
                zero(hidden),
            )
        ],
        axis=0,
    )
    for k, stat in enumerate((stat_o, stat_u, stat_d, stat_bu, stat_bo)):
        place.settle(stat, send.at[k])

    def finish(k, _):
        part = pl.ds(k * group, group)
        copy(gm.at[part], gm_out.at[part], 8 + chunks + k).wait()
        copy(gatt.at[part], gatt_out.at[part], 8 + 2 * chunks + k).wait()
        return 0

    over(finish, 0)
    out_copy.wait()


def middle_call(dp_size, fs_size, classes, attended, xs, cotangent, weights, vec):
    images, model, feature, hidden = xs.shape[0], xs.shape[2], attended.shape[2], weights[1].shape[2]
    group = 2 if images % 2 == 0 else 1
    chunks = images // group
    devices = dp_size * fs_size
    bf, f32 = jnp.bfloat16, jnp.float32

    def rows(width, kind):
        return pltpu.VMEM((images, ROWS, width), kind)

    return pl.pallas_call(
        functools.partial(middle_kernel, dp_size, fs_size, group),
        out_shape=[
            jax.ShapeDtypeStruct(cotangent.shape, bf),
            jax.ShapeDtypeStruct((images, ROWS, feature), bf),
            jax.ShapeDtypeStruct((images, ROWS, model), f32),
        ]
        + [jax.ShapeDtypeStruct(w.shape, bf) for w in weights]
        + [jax.ShapeDtypeStruct((8, hidden), f32)],
        in_specs=[SMEM] + [ANY] * 6 + [VMEM],
        out_specs=[ANY] * 3 + [VMEM] * 4,
        scratch_shapes=[
            rows(feature, bf),
            rows(model, bf),
            pltpu.VMEM(cotangent.shape, bf),
        ]
        + [pltpu.VMEM(w.shape, bf) for w in weights]
        + [
            rows(model, bf),
            rows(feature, bf),
            rows(feature, bf),
            rows(model, f32),
            rows(model, bf),
            rows(hidden, f32),
            rows(hidden, bf),
            rows(hidden, bf),
            rows(model, f32),
            rows(model, bf),
            rows(hidden, f32),
            rows(model, f32),
            rows(model, bf),
            pltpu.VMEM(cotangent.shape, bf),
            rows(feature, bf),
            pltpu.VMEM((model // 128, cotangent.shape[0], 128), f32),
            pltpu.VMEM((devices, 2, model), f32),
            pltpu.VMEM((devices, 2, hidden), f32),
            pltpu.VMEM((devices, 4, model), f32),
            pltpu.VMEM((devices, 2, hidden), f32),
            pltpu.VMEM((devices, 2, model), f32),
            pltpu.SemaphoreType.DMA((5,)),
            pltpu.SemaphoreType.DMA((5,)),
            pltpu.SemaphoreType.DMA((8 + 3 * chunks,)),
        ],
        compiler_params=pltpu.CompilerParams(
            collective_id=1, has_side_effects=True, vmem_limit_bytes=58 * 2**20
        ),
    )(classes, attended, xs, cotangent, *weights, vec)


class Reduce:
    def __init__(self, place, full, first, half, second, third, send, recv):
        self.place, self.full, self.first, self.half = place, full, first, half
        self.second, self.third, self.send, self.recv = second, third, send, recv
        self.width = half.shape[2]

    def by_core(self, body):
        for core in range(2):
            pl.when(self.place.core == core)(functools.partial(body, core))

    def swap(self):
        def body(core):
            part = self.full.at[:, :, pl.ds((1 - core) * self.width, self.width)]
            push(part, self.first, self.send.at[0], self.recv.at[0], self.place.partner)

        self.by_core(body)

    def scatter(self):
        place = self.place
        await_bytes(self.first, self.recv.at[0])

        def body(core):
            own = self.full[:, :, core * self.width : (core + 1) * self.width].astype(jnp.float32)
            self.half[...] = (own + self.first[...].astype(jnp.float32)).astype(jnp.bfloat16)

        self.by_core(body)
        self.second[place.fs] = self.half[place.fs]

        def start(step, _):
            target = lax.rem(place.fs + step, place.fs_size)
            push(self.half.at[target], self.second.at[place.fs], self.send.at[1], self.recv.at[1], (place.dp, target))
            return 0

        lax.fori_loop(1, place.fs_size, start, 0)

    def share(self):
        place = self.place
        await_bytes(self.second.at[pl.ds(0, place.fs_size - 1)], self.recv.at[1])
        total = jnp.sum(self.second[...].astype(jnp.float32), axis=0)
        self.third[place.dp] = total.astype(jnp.bfloat16)

        def start(step, _):
            target = lax.rem(place.dp + step, place.dp_size)
            push(self.third.at[place.dp], self.third.at[place.dp], self.send.at[2], self.recv.at[2], (target, place.fs))
            return 0

        lax.fori_loop(1, place.dp_size, start, 0)

    def result(self):
        place = self.place
        await_bytes(self.third.at[pl.ds(0, place.dp_size - 1)], self.recv.at[2])
        parts = []
        for core in range(2):
            parts.append(sum(self.third[k].astype(jnp.float32) for k in range(core, place.dp_size, 2)))
        return jnp.concatenate(parts, axis=1)

    def settle(self):
        place = self.place
        await_bytes(self.first, self.send.at[0])
        await_bytes(self.second.at[pl.ds(0, place.fs_size - 1)], self.send.at[1])
        await_bytes(self.third.at[pl.ds(0, place.dp_size - 1)], self.send.at[2])


def last_kernel(dp_size, fs_size, group, *refs):
    class_ref, xs_in, gmix_in, gm_in, wq_in, off_in = refs[:6]
    acc_in, grad_in, vec_ref = refs[6:9], refs[9:12], refs[12]
    ig_out, table_out, own_out, vec_out = refs[13], refs[14], refs[15:19], refs[19]
    xs, gmix, gm, wq_buf, off, ig, res = refs[20:27]
    acc, full = refs[27:30], refs[30:34]
    steps = [refs[34 + 4 * k : 38 + 4 * k] for k in range(4)]
    stat, stat_t = refs[50:52]
    send, recv, local, send_r, recv_r = refs[52:57]
    place = Place(dp_size, fs_size)
    images = xs.shape[0]
    chunks = images // group
    size = group * ROWS
    f32, bf = jnp.float32, jnp.bfloat16
    model, width = xs.shape[2], gmix.shape[2]

    def copy(source, target, at):
        return pltpu.make_async_copy(source, target, local.at[at])

    first_loads = [copy(xs_in, xs, 0), copy(gmix_in, gmix, 1), copy(wq_in, wq_buf, 2)]
    grad_loads = [copy(grad_in[k], full[1 + k], 3 + k) for k in range(3)]
    late_loads = [copy(off_in, off, 6)] + [copy(acc_in[k], acc[k], 7 + k) for k in range(3)] + [copy(gm_in, gm, 10)]
    for load in first_loads + grad_loads + late_loads:
        load.start()
    place.greet()
    reduces = [
        Reduce(place, full[k], *steps[k], send_r.at[k], recv_r.at[k]) for k in range(4)
    ]

    def get(ref, k):
        return ref[pl.ds(k * group, group)].reshape(size, ref.shape[2])

    def put(ref, k, value):
        ref[pl.ds(k * group, group)] = value.astype(ref.dtype).reshape(group, ROWS, ref.shape[2])

    def kept(k, lanes):
        row = lax.broadcasted_iota(jnp.int32, (ROWS, lanes), 0)
        return jnp.concatenate([row < limits_of(class_ref[k * group + j]) for j in range(group)], axis=0)

    total = vec_ref[10:11, :1]
    gain, scale, center = vec_ref[0:1, :], vec_ref[8:9, :], vec_ref[9:10, :]
    for load in first_loads:
        load.wait()
    weight = flat_weight(wq_buf)
    weight_f = weight.astype(f32)
    xs_flat = xs[...].reshape(images * ROWS, model)
    gmix_flat = gmix[...].reshape(images * ROWS, width)
    raw = dot_tn(xs_flat, gmix_flat)
    ones = jnp.ones((8, images * ROWS), bf)
    grad_sum = dot_nn(ones, gmix_flat)[:1]
    grad_z = total_rows(raw * weight_f)
    place.meet()
    place.spread(stat, jnp.concatenate([grad_sum, grad_z], axis=0), send.at[0], recv.at[0])
    for load in grad_loads:
        load.wait()
    for k in range(1, 4):
        reduces[k].swap()
    alpha = scale * gain
    gram = dot_tn(xs_flat, xs_flat)
    x_sum = dot_nn(ones, xs_flat)[:1]

    def product(k, _):
        put(ig, k, dot_nt((get(gmix, k).astype(f32) * alpha).astype(bf), weight))
        return 0

    lax.fori_loop(0, chunks, product, 0)
    for k in range(1, 4):
        reduces[k].scatter()
    for load in late_loads:
        load.wait()
    place.spread(stat_t, table_sums(off, acc), send.at[1], recv.at[1])

    got = place.collect(stat, recv.at[0])
    gain_grad, alpha, slant, level = back_parts(got[0:1], got[1:2], total, gain, center, scale)
    own = raw * alpha - precise(gram, weight) * slant - outer(x_sum, level)
    full[0][...] = restore(own).reshape(full[0].shape).astype(bf)
    reduces[0].swap()
    mix = dot_nt((weight_f * slant).astype(bf), weight).astype(bf)
    high, rest = split_low(jnp.broadcast_to(level, (8, width)))
    lift = (dot_nt(high, weight) + dot_nt(rest, weight))[:1]
    vec_out[...] = jnp.concatenate(
        [restore(gain_grad), restore(got[0:1]), jnp.zeros((6, width), f32)], axis=0
    )

    def result(k):
        value = get(gm, k) + get(ig, k) - dot_nn(get(xs, k), mix) - jnp.where(kept(k, model), lift, 0.0)
        for j in range(group):
            put_image(res, k * group + j, images, value[j * ROWS : (j + 1) * ROWS])

    reduces[0].scatter()
    for k in range(chunks):
        result(k)
    res_copies = [copy(res.at[k], ig_out.at[:, pl.ds(128 * k, 128)], 11 + k) for k in range(model // 128)]
    for res_copy in res_copies:
        res_copy.start()
    for k in range(1, 4):
        reduces[k].share()
    table_out[...] = place.collect(stat_t, recv.at[1])
    reduces[0].share()
    for k in (1, 2, 3, 0):
        own_out[k][...] = reduces[k].result()
    for k in range(4):
        reduces[k].settle()
    place.settle(stat, send.at[0])
    place.settle(stat_t, send.at[1])
    for res_copy in res_copies:
        res_copy.wait()


def last_call(dp_size, fs_size, classes, xs, gmix, gm, wq, offset_table, accs, grads, vec):
    images, model, width = xs.shape[0], xs.shape[2], gmix.shape[2]
    group = 2 if images % 2 == 0 else 1
    devices = dp_size * fs_size
    bf, f32 = jnp.bfloat16, jnp.float32
    shapes = [wq.shape] + [g.shape for g in grads]
    steps = []
    for s in shapes:
        half = s[2] // 2
        steps += [
            pltpu.VMEM((fs_size, s[1], half), bf),
            pltpu.VMEM((fs_size, s[1], half), bf),
            pltpu.VMEM((fs_size, s[1], half), bf),
            pltpu.VMEM((dp_size, s[1], half), bf),
        ]
    order = []
    for k in range(4):
        order += [steps[4 * k], steps[4 * k + 1], steps[4 * k + 2], steps[4 * k + 3]]
    return pl.pallas_call(
        functools.partial(last_kernel, dp_size, fs_size, group),
        out_shape=[jax.ShapeDtypeStruct((SLOT * images, model), f32), jax.ShapeDtypeStruct((HEADS, 384), f32)]
        + [jax.ShapeDtypeStruct(s[1:], f32) for s in shapes]
        + [jax.ShapeDtypeStruct((8, width), f32)],
        in_specs=[SMEM] + [ANY] * 11 + [VMEM],
        out_specs=[ANY] + [VMEM] * 6,
        scratch_shapes=[
            pltpu.VMEM(xs.shape, bf),
            pltpu.VMEM(gmix.shape, bf),
            pltpu.VMEM(gm.shape, f32),
            pltpu.VMEM(wq.shape, bf),
            pltpu.VMEM(offset_table.shape, jnp.int32),
            pltpu.VMEM(gm.shape, f32),
            pltpu.VMEM((model // 128, SLOT * images, 128), f32),
        ]
        + [pltpu.VMEM(a.shape, f32) for a in accs]
        + [pltpu.VMEM(s, bf) for s in shapes]
        + order
        + [
            pltpu.VMEM((devices, 2, width), f32),
            pltpu.VMEM((devices, HEADS, 384), f32),
            pltpu.SemaphoreType.DMA((2,)),
            pltpu.SemaphoreType.DMA((2,)),
            pltpu.SemaphoreType.DMA((11 + model // 128,)),
            pltpu.SemaphoreType.DMA((4, 3)),
            pltpu.SemaphoreType.DMA((4, 3)),
        ],
        compiler_params=pltpu.CompilerParams(
            collective_id=2, has_side_effects=True, vmem_limit_bytes=56 * 2**20
        ),
    )(classes, xs, gmix, gm, wq, offset_table, *accs, *grads, vec)

def own_slice(vector):
    width = vector.shape[0] // lax.axis_size("fsdp")
    return lax.dynamic_slice_in_dim(vector, lax.axis_index("fsdp") * width, width)


def shards(
    inputs,
    classes,
    offset_table,
    bias_table,
    qkv_weight,
    qkv_gain,
    qkv_shift,
    out_weight,
    out_gain,
    out_shift,
    up_weight,
    up_gain,
    up_shift,
    down_weight,
    down_gain,
    down_shift,
    cotangent,
):
    sizes = lax.axis_size("dp"), lax.axis_size("fsdp")
    images, _, model = inputs.shape

    def by_slot(array):
        return jnp.swapaxes(array, 0, 1).reshape(SLOT * images, model)

    def by_image(array):
        return jnp.swapaxes(array.reshape(SLOT, images, model), 0, 1)

    first = first_call(
        *sizes,
        classes,
        by_slot(inputs),
        offset_table,
        bias_table,
        (qkv_weight, out_weight, up_weight, down_weight),
        (qkv_gain, qkv_shift, out_gain, out_shift, up_gain, up_shift, down_gain, down_shift),
    )
    mixed, xs, biases, weights, vec = first[0], first[1], first[2:5], first[5:9], first[9]
    attended, probs, shares = attend_call(classes, mixed, biases)
    middle = middle_call(*sizes, classes, attended, xs, by_slot(cotangent), weights[1:], vec)
    output, grad_att, grad_middle = middle[:3]
    grad_mixed, *accs = back_call(classes, mixed, probs, shares, grad_att, attended)
    last = last_call(
        *sizes, classes, xs, grad_mixed, grad_middle, weights[0], offset_table, accs, middle[3:6], vec
    )
    input_grad, table_grad, owned, vec_qkv = last[0], last[1], last[2:6], last[6]
    lines = middle[6]
    return (
        by_image(output),
        by_image(input_grad),
        table_grad[:, :NOFF],
        owned[0],
        own_slice(vec_qkv[0]),
        own_slice(vec_qkv[1]),
        owned[1],
        own_slice(lines[0, :model]),
        own_slice(lines[1, :model]),
        owned[2],
        own_slice(lines[2]),
        own_slice(lines[3]),
        owned[3],
        own_slice(lines[4, :model]),
        own_slice(lines[5, :model]),
    )


def solution(mesh):
    placed = (
        P(("dp", "fsdp"), None, None),
        P(("dp", "fsdp")),
        P(),
        P(),
        P("fsdp", None),
        P("fsdp"),
        P("fsdp"),
        P("fsdp", None),
        P("fsdp"),
        P("fsdp"),
        P("fsdp", None),
        P("fsdp"),
        P("fsdp"),
        P("fsdp", None),
        P("fsdp"),
        P("fsdp"),
        P(("dp", "fsdp"), None, None),
    )
    return jax.shard_map(
        shards,
        mesh=mesh,
        in_specs=placed,
        out_specs=(
            P(("dp", "fsdp"), None, None),
            P(("dp", "fsdp"), None, None),
            P(),
            P("fsdp", None),
            P("fsdp"),
            P("fsdp"),
            P("fsdp", None),
            P("fsdp"),
            P("fsdp"),
            P("fsdp", None),
            P("fsdp"),
            P("fsdp"),
            P("fsdp", None),
            P("fsdp"),
            P("fsdp"),
        ),
        check_vma=False,
    )
```

```python
import functools

import jax
import jax.numpy as jnp
from jax import lax
from jax.experimental import pallas as pl
from jax.experimental.pallas import tpu as pltpu
from jax.sharding import PartitionSpec as P

HEADS = 4
KEY = 32
VALD = 128
GRID = 18
CLASSES = 3
SLOT = 324
NOFF = 324


EPS = 1e-05
LOG2E = 1.4426950408889634
LN2 = 0.6931471805599453
ROWS = 336
PARTS = ((10, 100, 112, 128), (14, 196, 208, 256), (18, 324, 336, 384))
VMEM = pl.BlockSpec(memory_space=pltpu.VMEM)


def dot_nn(left, right):
    return jnp.dot(left, right, preferred_element_type=jnp.float32)


def dot_nt(left, right):
    return lax.dot_general(left, right, (((1,), (1,)), ((), ())), preferred_element_type=jnp.float32)


def dot_tn(left, right):
    return lax.dot_general(left, right, (((0,), (0,)), ((), ())), preferred_element_type=jnp.float32)


def pad_rows(value, rows):
    if value.shape[0] == rows:
        return value
    return jnp.concatenate([value, jnp.zeros((rows - value.shape[0], value.shape[1]), value.dtype)], axis=0)


def pad_lanes(value, lanes):
    if value.shape[1] == lanes:
        return value
    return jnp.concatenate([value, jnp.zeros((value.shape[0], lanes - value.shape[1]), value.dtype)], axis=1)


def bias_tables(off_ref, table_ref, index_ref, outs, pair):
    tables = []
    for side in range(2):
        row = pad_lanes(table_ref[pl.ds(2 * pair + side, 1), :], 384) * LOG2E
        tables.append([jnp.broadcast_to(row[:, 128 * k : 128 * k + 128], (8, 128)) for k in range(3)])
    index_ref[...] = jnp.zeros_like(index_ref)
    for number, (_, amount, rows, lanes) in enumerate(PARTS):
        index_ref[:SLOT, :SLOT] = off_ref[number]

        tiles = rows // 8 // (number + 1)

        def strip(step, _, number=number, amount=amount, lanes=lanes, tiles=tiles, out=outs[number]):
            for line in range(tiles):
                at = pl.multiple_of((step * tiles + line) * 8, 8)
                for block in range(lanes // 128):
                    index = index_ref[pl.ds(at, 8), 128 * block : 128 * block + 128]
                    low = index & 127
                    part = index >> 7
                    valid = lax.broadcasted_iota(jnp.int32, (8, 128), 1) + 128 * block < amount
                    for side in range(2):
                        found = [
                            jnp.take_along_axis(tables[side][k], low, axis=1, mode="promise_in_bounds")
                            for k in range(3 if number == 2 else 2)
                        ]
                        value = jnp.where(part == 0, found[0], found[1])
                        if number == 2:
                            value = jnp.where(part == 2, found[2], value)
                        column = side * lanes + 128 * block
                        out[pair, pl.ds(at, 8), column : column + 128] = jnp.where(valid, value, -1e30)
            return 0

        lax.fori_loop(0, number + 1, strip, 0)


def head_keys(keys, pair, lanes):
    owner = lax.broadcasted_iota(jnp.int32, keys.shape, 1) // KEY
    zero = jnp.zeros_like(keys)
    return jnp.concatenate(
        [pad_rows(jnp.where(owner == 2 * pair + side, keys, zero), lanes) for side in range(2)], axis=0
    )


def pair_values(values, lanes):
    zero = jnp.zeros((lanes, VALD), values.dtype)
    top = jnp.concatenate([pad_rows(values[:, :VALD], lanes), zero], axis=1)
    low = jnp.concatenate([zero, pad_rows(values[:, VALD:], lanes)], axis=1)
    return jnp.concatenate([top, low], axis=0)


def by_eight(value):
    return jnp.sum(value.reshape(value.shape[0] // 8, 8, value.shape[1]), axis=0)


def attend_kernel(class_ref, mixed_ref, bias0, bias1, bias2, att_ref, p_ref, r_ref):
    kind = class_ref[pl.program_id(0)]
    for number, (_, amount, rows, lanes) in enumerate(PARTS):

        @pl.when(kind == number)
        def _(amount=amount, rows=rows, lanes=lanes, bias=(bias0, bias1, bias2)[number]):
            query = mixed_ref[0, :rows, :128]
            keys = mixed_ref[0, :rows, 128:256]
            kept = lax.broadcasted_iota(jnp.int32, (rows, VALD), 0) < amount
            lane = lax.broadcasted_iota(jnp.int32, (rows, 128), 1)
            shares = jnp.zeros((rows, 128), jnp.float32)
            for pair in range(2):
                scores = dot_nt(query, head_keys(keys, pair, lanes)) + bias[pair]
                parts, inverse = [], []
                for side in range(2):
                    own = scores[:, side * lanes : (side + 1) * lanes]
                    expo = jnp.exp2(own - jnp.max(own, axis=1, keepdims=True))
                    share = 1.0 / jnp.sum(expo, axis=1, keepdims=True)
                    shares = jnp.where(lane == 2 * pair + side, share, shares)
                    parts.append(expo.astype(jnp.bfloat16))
                    inverse.append(share)
                both = jnp.concatenate(parts, axis=1)
                p_ref[0, :rows, 2 * pair * lanes : 2 * (pair + 1) * lanes] = both
                values = mixed_ref[0, :rows, 256 + 256 * pair : 512 + 256 * pair]
                sums = dot_nn(both, pair_values(values, lanes))
                for side in range(2):
                    own = sums[:, side * VALD : (side + 1) * VALD] * inverse[side]
                    at = (2 * pair + side) * VALD
                    att_ref[0, :rows, at : at + VALD] = jnp.where(kept, own, 0.0).astype(jnp.bfloat16)
            r_ref[0, :rows, :] = shares
            if rows < ROWS:
                att_ref[0, rows:, :] = jnp.zeros((ROWS - rows, att_ref.shape[2]), jnp.bfloat16)


def back_kernel(
    fs_size,
    class_ref,
    mixed_ref,
    p_ref,
    r_ref,
    g_ref,
    att_ref,
    xs_ref,
    lines_ref,
    out_in,
    gmix_ref,
    raw_ref,
    sum_ref,
    acc0,
    acc1,
    acc2,
    *more,
):
    own_refs, out_out, held, out_sems = more[:6], more[6], more[7], more[8]
    accs = (acc0, acc1, acc2)
    out_load = pltpu.make_async_copy(out_in, held, out_sems.at[0])
    out_store = pltpu.make_async_copy(held, out_out, out_sems.at[1])

    @pl.when(pl.program_id(0) == 0)
    def _():
        out_load.start()
        for ref in (*accs, raw_ref, sum_ref):
            ref[...] = jnp.zeros_like(ref)
        spot = lax.axis_index("fsdp")
        lines = lines_ref[...]
        for k, ref in enumerate(own_refs):
            width = ref.shape[1]
            ref[...] = pltpu.roll(lines, lines.shape[1] - spot * width, 1)[k : k + 1, :width]

    kind = class_ref[pl.program_id(0)]
    for number, (_, amount, rows, lanes) in enumerate(PARTS):

        @pl.when(kind == number)
        def _(rows=rows, lanes=lanes, acc=accs[number]):
            query = mixed_ref[0, :rows, :128]
            keys = mixed_ref[0, :rows, 128:256]
            owner = lax.broadcasted_iota(jnp.int32, (rows, 128), 1) // KEY
            d_query = jnp.zeros((rows, 128), jnp.float32)
            d_keys = jnp.zeros((rows, 128), jnp.float32)
            for pair in range(2):
                grads, deltas = [], []
                for side in range(2):
                    head = 2 * pair + side
                    at = head * VALD
                    grad = g_ref[0, :rows, at : at + VALD].astype(jnp.float32) * r_ref[0, :rows, head : head + 1]
                    own = att_ref[0, :rows, at : at + VALD].astype(jnp.float32)
                    deltas.append(jnp.sum(grad * own, axis=1, keepdims=True))
                    grads.append(grad.astype(jnp.bfloat16))
                both = jnp.concatenate(grads, axis=1)
                values = mixed_ref[0, :rows, 256 + 256 * pair : 512 + 256 * pair]
                d_probs = dot_nt(both, pair_values(values, lanes))
                probs = p_ref[0, :rows, 2 * pair * lanes : 2 * (pair + 1) * lanes]
                low = []
                for side in range(2):
                    cut = slice(side * lanes, (side + 1) * lanes)
                    d_score = probs[:, cut].astype(jnp.float32) * (d_probs[:, cut] - deltas[side])
                    acc[pair, :, cut] += d_score
                    low.append(d_score.astype(jnp.bfloat16))
                d_low = jnp.concatenate(low, axis=1)
                d_query = d_query + dot_nn(d_low, head_keys(keys, pair, lanes))
                turned = dot_tn(d_low, query)
                d_values = dot_tn(probs, both)
                for side in range(2):
                    head = 2 * pair + side
                    d_keys = jnp.where(owner == head, turned[side * lanes : side * lanes + rows], d_keys)
                    at = 256 + head * VALD
                    whole = d_values[side * lanes : side * lanes + rows, side * VALD : (side + 1) * VALD]
                    sum_ref[:, at : at + VALD] += by_eight(whole)
                    gmix_ref[0, :rows, at : at + VALD] = whole.astype(jnp.bfloat16)
            d_query = d_query * KEY ** (-0.5)
            d_keys = d_keys * LN2
            sum_ref[:, :128] += by_eight(d_query)
            sum_ref[:, 128:256] += by_eight(d_keys)
            gmix_ref[0, :rows, :128] = d_query.astype(jnp.bfloat16)
            gmix_ref[0, :rows, 128:256] = d_keys.astype(jnp.bfloat16)
            raw_ref[...] += dot_tn(xs_ref[0, :rows, :], gmix_ref[0, :rows, :])
            if rows < ROWS:
                gmix_ref[0, rows:, :] = jnp.zeros((ROWS - rows, gmix_ref.shape[2]), jnp.bfloat16)

    @pl.when(pl.program_id(0) == pl.num_programs(0) // 2)
    def _():
        out_load.wait()
        out_store.start()

    @pl.when(pl.program_id(0) == pl.num_programs(0) - 1)
    def _():
        out_store.wait()


def table_sums(off_ref, accs):
    totals = [jnp.zeros((24, 640), jnp.float32) for _ in range(HEADS)]
    for number, (side_of, amount, rows, lanes) in enumerate(PARTS):
        offsets = off_ref[number]
        row = lax.broadcasted_iota(jnp.int32, (SLOT, 1), 0)
        most = jnp.max(offsets, axis=1, keepdims=True)
        corner = jnp.min(jnp.where(most == (side_of - 1) * (GRID + 1), row, SLOT), axis=0, keepdims=True)
        place = jnp.sum(jnp.where(row == corner, offsets, 0), axis=0, keepdims=True)
        place = jnp.where(lax.broadcasted_iota(jnp.int32, (1, SLOT), 1) < amount, place, -1)
        wide = jnp.concatenate([place, jnp.full((1, 384 - SLOT), -1, jnp.int32)], axis=1)
        cell = lax.broadcasted_iota(jnp.int32, (24 * side_of, 1), 0)
        cell_row = (cell * 2731) >> 16
        cell_col = cell - 24 * cell_row
        code = jnp.where(cell_col < side_of, cell_row * GRID + cell_col, -2)
        left = (code == wide[:, :rows]).astype(jnp.float32).astype(jnp.bfloat16)
        spot = lax.broadcasted_iota(jnp.int32, (384, 1), 0)
        right = (spot == wide[:, :lanes]).astype(jnp.float32).astype(jnp.bfloat16)
        for head in range(HEADS):
            at = (head % 2) * lanes
            score = accs[number][head // 2, :, at : at + lanes].astype(jnp.bfloat16)
            sorted_rows = dot_nn(left, score).astype(jnp.bfloat16)
            both = dot_nt(sorted_rows, right)
            for line in range(side_of):
                part = pad_lanes(both[24 * line : 24 * line + 24], 640)
                totals[head] = totals[head] + pltpu.roll(part, (GRID - 1 - line) * GRID, 1)
    lane = lax.broadcasted_iota(jnp.int32, (24, 640), 1)
    lane_row = (lane * 3641) >> 16
    away = jnp.abs(lane - GRID * lane_row - lax.broadcasted_iota(jnp.int32, (24, 640), 0))
    wide_row = lax.broadcasted_iota(jnp.int32, (640, 1), 0)
    wide_row = jnp.abs(((wide_row * 3641) >> 16) - (GRID - 1))
    out_lane = lax.broadcasted_iota(jnp.int32, (1, 384), 1)
    out_row = (out_lane * 3641) >> 16
    fold = (wide_row == out_row).astype(jnp.float32).astype(jnp.bfloat16)
    out_col = out_lane - GRID * out_row
    pick = lax.broadcasted_iota(jnp.int32, (24, 1), 0) == out_col
    rows_out = []
    for head in range(HEADS):
        lines = [
            jnp.sum(jnp.where(away == d, totals[head], 0.0), axis=0, keepdims=True) for d in range(GRID)
        ]
        lines = pad_rows(jnp.concatenate(lines, axis=0), 24)
        high = lines.astype(jnp.bfloat16)
        low = (lines - high.astype(jnp.float32)).astype(jnp.bfloat16)
        spread = dot_nn(high, fold) + dot_nn(low, fold)
        rows_out.append(jnp.sum(jnp.where(pick, spread, 0.0), axis=0, keepdims=True))
    return jnp.concatenate(rows_out, axis=0)


def image_spec(width):
    return pl.BlockSpec((1, ROWS, width), lambda i, c: (i, 0, 0))


def whole_spec(shape):
    return pl.BlockSpec(shape, lambda i, c: (0,) * len(shape))


def attend_call(classes, mixed, biases):
    images = mixed.shape[0]
    return pl.pallas_call(
        attend_kernel,
        grid_spec=pltpu.PrefetchScalarGridSpec(
            num_scalar_prefetch=1,
            grid=(images,),
            in_specs=[image_spec(768)] + [whole_spec(b.shape) for b in biases],
            out_specs=[image_spec(512), image_spec(1536), image_spec(128)],
        ),
        out_shape=[
            jax.ShapeDtypeStruct((images, ROWS, 512), jnp.bfloat16),
            jax.ShapeDtypeStruct((images, ROWS, 1536), jnp.bfloat16),
            jax.ShapeDtypeStruct((images, ROWS, 128), jnp.float32),
        ],
        compiler_params=pltpu.CompilerParams(vmem_limit_bytes=60 * 2**20),
    )(classes, mixed, *biases)


def back_call(fs_size, classes, mixed, probs, shares, grad, attended, xs, lines, output):
    images, model = mixed.shape[0], xs.shape[2]
    bf, f32 = jnp.bfloat16, jnp.float32
    shapes = [(2, r, 2 * l) for _, _, r, l in PARTS]
    widths = [w // fs_size for w in (model, model, lines.shape[1], lines.shape[1], model, model)]
    return pl.pallas_call(
        functools.partial(back_kernel, fs_size),
        grid_spec=pltpu.PrefetchScalarGridSpec(
            num_scalar_prefetch=1,
            grid=(images,),
            in_specs=[image_spec(w) for w in (768, 1536, 128, 512, 512, model)] + [whole_spec(lines.shape), ANY],
            out_specs=[image_spec(768), whole_spec((model, 768)), whole_spec((8, 768))]
            + [whole_spec(s) for s in shapes]
            + [whole_spec((1, w)) for w in widths]
            + [ANY],
            scratch_shapes=[pltpu.VMEM(output.shape, bf), pltpu.SemaphoreType.DMA((2,))],
        ),
        out_shape=[
            jax.ShapeDtypeStruct((images, ROWS, 768), bf),
            jax.ShapeDtypeStruct((model, 768), f32),
            jax.ShapeDtypeStruct((8, 768), f32),
        ]
        + [jax.ShapeDtypeStruct(s, f32) for s in shapes]
        + [jax.ShapeDtypeStruct((1, w), f32) for w in widths]
        + [jax.ShapeDtypeStruct(output.shape, bf)],
        compiler_params=pltpu.CompilerParams(vmem_limit_bytes=60 * 2**20),
    )(classes, mixed, probs, shares, grad, attended, xs, lines, output)


def end_kernel(ig_in, table_ref, own0, own1, own2, own3, lines_ref, *outs):
    ig_out, table_out, own_outs, line_outs = outs[0], outs[1], outs[2:6], outs[6:8]
    held, sem_in, sem_out = outs[8:11]
    pieces = sem_in.shape[0]
    step = held.shape[0] // pieces
    parts = [pl.ds(k * step, step) for k in range(pieces)]
    loads = [pltpu.make_async_copy(ig_in.at[p], held.at[p], sem_in.at[k]) for k, p in enumerate(parts)]
    stores = [pltpu.make_async_copy(held.at[p], ig_out.at[p], sem_out.at[k]) for k, p in enumerate(parts)]
    for load in loads:
        load.start()
    table_out[...] = table_ref[:, :NOFF]
    for source, target in zip((own0, own1, own2, own3), own_outs):
        target[...] = source[...]
    spot = lax.axis_index("fsdp")
    lines = lines_ref[...]
    for k, ref in enumerate(line_outs):
        width = ref.shape[1]
        ref[...] = pltpu.roll(lines, lines.shape[1] - spot * width, 1)[k : k + 1, :width]
    for load, store in zip(loads, stores):
        load.wait()
        store.start()
    for store in stores:
        store.wait()


def end_call(fs_size, input_grad, table, owned, lines):
    f32 = jnp.float32
    width = lines.shape[1] // fs_size
    shapes = [input_grad.shape, (HEADS, NOFF)] + [o.shape for o in owned] + [(1, width)] * 2
    return pl.pallas_call(
        end_kernel,
        out_shape=[jax.ShapeDtypeStruct(s, f32) for s in shapes],
        in_specs=[ANY] + [VMEM] * 6,
        out_specs=[ANY] + [VMEM] * 7,
        scratch_shapes=[
            pltpu.VMEM(input_grad.shape, f32),
            pltpu.SemaphoreType.DMA((4,)),
            pltpu.SemaphoreType.DMA((4,)),
        ],
        compiler_params=pltpu.CompilerParams(vmem_limit_bytes=60 * 2**20),
    )(input_grad, table, *owned, lines)


MESH = pl.DeviceIdType.MESH
ANY = pl.BlockSpec(memory_space=pl.ANY)
SMEM = pl.BlockSpec(memory_space=pltpu.SMEM)


class Place:
    def __init__(self, dp_size, fs_size):
        self.dp_size, self.fs_size = dp_size, fs_size
        self.size = dp_size * fs_size
        self.dp, self.fs = lax.axis_index("dp"), lax.axis_index("fsdp")
        self.me = self.dp * fs_size + self.fs
        self.core = lax.rem(self.dp, 2)
        self.partner = (self.dp + 1 - 2 * self.core, self.fs)

    def other(self, step):
        spot = lax.rem(self.me + step, self.size)
        return (spot // self.fs_size, lax.rem(spot, self.fs_size))

    def greet(self):
        barrier = pltpu.get_barrier_semaphore()

        def signal(step, _):
            pl.semaphore_signal(barrier, inc=1, device_id=self.other(step), device_id_type=MESH)
            return 0

        lax.fori_loop(1, self.size, signal, 0)

    def meet(self):
        pl.semaphore_wait(pltpu.get_barrier_semaphore(), self.size - 1)

    def spread(self, buf, value, send, recv):
        buf[self.me] = value

        def start(step, _):
            push(buf.at[self.me], buf.at[self.me], send, recv, self.other(step))
            return 0

        lax.fori_loop(1, self.size, start, 0)

    def collect(self, buf, recv):
        await_bytes(buf.at[pl.ds(0, self.size - 1)], recv)
        return jnp.sum(buf[...], axis=0)

    def spread_pair(self, buf, value, send, recv):
        buf[self.core] = value
        part = buf.at[self.core]
        push(part, part, send, recv, self.partner)

    def collect_pair(self, buf, recv):
        await_bytes(buf.at[0], recv)
        return buf[0] + buf[1]

    def spread_chips(self, buf, value, send, recv):
        chips = self.size // 2
        mine = (self.dp // 2) * self.fs_size + self.fs
        buf[mine] = value

        def start(step, _):
            spot = lax.rem(mine + step, chips)
            device = (2 * (spot // self.fs_size) + self.core, lax.rem(spot, self.fs_size))
            push(buf.at[mine], buf.at[mine], send, recv, device)
            return 0

        lax.fori_loop(1, chips, start, 0)

    def collect_chips(self, buf, recv):
        await_bytes(buf.at[pl.ds(0, self.size // 2 - 1)], recv)
        return jnp.sum(buf[...], axis=0)

    def settle_pair(self, buf, send):
        await_bytes(buf.at[0], send)

    def settle_chips(self, buf, send):
        await_bytes(buf.at[pl.ds(0, self.size // 2 - 1)], send)

    def settle(self, buf, send):
        await_bytes(buf.at[pl.ds(0, self.size - 1)], send)


def push(source, target, send, recv, device):
    pltpu.make_async_remote_copy(
        src_ref=source, dst_ref=target, send_sem=send, recv_sem=recv, device_id=device, device_id_type=MESH
    ).start()


def await_bytes(ref, sem):
    pltpu.make_async_copy(ref, ref, sem).wait()


def halves(width):
    return (width // 2,) * 2


def gather_start(place, buf, send, recv):
    half = buf.shape[2] // 2

    def start(step, _):
        target = lax.rem(place.fs + step, place.fs_size)
        for core in range(2):

            @pl.when(place.core == core)
            def _():
                part = buf.at[place.fs, :, pl.ds(core * half, half)]
                push(part, part, send, recv, (place.dp, target))

        return 0

    lax.fori_loop(1, place.fs_size, start, 0)


def gather_pass(place, buf, recv, send2, recv2):
    half = buf.shape[2] // 2
    for core in range(2):

        @pl.when(place.core == core)
        def _():
            await_bytes(buf.at[pl.ds(0, place.fs_size - 1), :, pl.ds(core * half, half)], recv)
            part = buf.at[:, :, pl.ds(core * half, half)]
            push(part, part, send2, recv2, place.partner)


def gather_end(place, buf, recv2):
    half = buf.shape[2] // 2
    await_bytes(buf.at[:, :, pl.ds(0, half)], recv2)


def gather_settle(place, buf, send, send2):
    half = buf.shape[2] // 2
    await_bytes(buf.at[pl.ds(0, place.fs_size - 1), :, pl.ds(0, half)], send)
    await_bytes(buf.at[:, :, pl.ds(0, half)], send2)


def flat_weight(buf):
    shards, rows, width = buf.shape
    if rows % 16 == 0:
        return buf[...].reshape(shards * rows, width)
    wide = jnp.concatenate([buf[k].astype(jnp.float32) for k in range(shards)], axis=0)
    return wide.astype(jnp.bfloat16)


def split_low(value):
    high = value.astype(jnp.bfloat16)
    return high, (value - high.astype(jnp.float32)).astype(jnp.bfloat16)


def precise(left, right):
    high, low = split_low(left)
    return dot_nn(high, right) + dot_nn(low, right)


def arrange(columns):
    blocks = [columns[:, (2 * KEY + VALD) * h : (2 * KEY + VALD) * (h + 1)] for h in range(HEADS)]
    parts = [b[:, :KEY] for b in blocks] + [b[:, KEY : 2 * KEY] for b in blocks] + [b[:, 2 * KEY :] for b in blocks]
    return jnp.concatenate(parts, axis=1)


def restore(columns):
    parts = []
    for h in range(HEADS):
        parts += [
            columns[:, KEY * h : KEY * (h + 1)],
            columns[:, 128 + KEY * h : 128 + KEY * (h + 1)],
            columns[:, 256 + VALD * h : 256 + VALD * (h + 1)],
        ]
    return jnp.concatenate(parts, axis=1)


def by_columns(ref, value):
    for k in range(ref.shape[0]):
        ref[k] = value[:, 128 * k : 128 * k + 128]


def take_image(ref, image, images):
    return jnp.concatenate([ref[k, pl.ds(image, SLOT, stride=images), :] for k in range(ref.shape[0])], axis=1)


def put_image(ref, image, images, value):
    for k in range(ref.shape[0]):
        ref[k, pl.ds(image, SLOT, stride=images), :] = value[:SLOT, 128 * k : 128 * k + 128]


def limits_of(kind):
    return jnp.where(kind == 0, (GRID - 8) ** 2, jnp.where(kind == 1, (GRID - 4) ** 2, SLOT))


def assemble(buf, widths, lanes):
    turned = {}
    for width in sorted(set(widths)):
        turned[width] = sum(
            pltpu.roll(pad_lanes(buf[k], lanes), k * width, 1) if k else pad_lanes(buf[k], lanes)
            for k in range(buf.shape[0])
        )
    return [turned[width][k : k + 1] for k, width in enumerate(widths)]


class Reduce:
    def __init__(self, place, full, first, half, second, third, send, recv):
        self.place, self.full, self.first, self.half = place, full, first, half
        self.second, self.third, self.send, self.recv = second, third, send, recv
        self.width = half.shape[2]

    def by_core(self, body):
        for core in range(2):
            pl.when(self.place.core == core)(functools.partial(body, core))

    def swap(self):
        def body(core):
            part = self.full.at[:, :, pl.ds((1 - core) * self.width, self.width)]
            push(part, self.first, self.send.at[0], self.recv.at[0], self.place.partner)

        self.by_core(body)

    def scatter(self):
        place = self.place
        await_bytes(self.first, self.recv.at[0])

        def body(core):
            own = self.full[:, :, core * self.width : (core + 1) * self.width].astype(jnp.float32)
            self.half[...] = (own + self.first[...].astype(jnp.float32)).astype(jnp.bfloat16)

        self.by_core(body)
        self.second[place.fs] = self.half[place.fs]

        def start(step, _):
            target = lax.rem(place.fs + step, place.fs_size)
            push(self.half.at[target], self.second.at[place.fs], self.send.at[1], self.recv.at[1], (place.dp, target))
            return 0

        lax.fori_loop(1, place.fs_size, start, 0)

    def gathered(self):
        await_bytes(self.second.at[pl.ds(0, self.place.fs_size - 1)], self.recv.at[1])
        return jnp.sum(self.second[...].astype(jnp.float32), axis=0).astype(jnp.bfloat16)

    def share(self, total=None):
        place = self.place
        self.third[place.dp] = self.gathered() if total is None else total

        def start(step, _):
            target = lax.rem(place.dp + step, place.dp_size)
            push(self.third.at[place.dp], self.third.at[place.dp], self.send.at[2], self.recv.at[2], (target, place.fs))
            return 0

        lax.fori_loop(1, place.dp_size, start, 0)

    def result(self):
        place = self.place
        await_bytes(self.third.at[pl.ds(0, place.dp_size - 1)], self.recv.at[2])
        parts = []
        for core in range(2):
            parts.append(sum(self.third[k].astype(jnp.float32) for k in range(core, place.dp_size, 2)))
        return jnp.concatenate(parts, axis=1)

    def settle(self, steps=(0, 1, 2)):
        place = self.place
        if 0 in steps:
            await_bytes(self.first, self.send.at[0])
        if 1 in steps:
            await_bytes(self.second.at[pl.ds(0, place.fs_size - 1)], self.send.at[1])
        if 2 in steps:
            await_bytes(self.third.at[pl.ds(0, place.dp_size - 1)], self.send.at[2])


def first_kernel(dp_size, fs_size, *refs):
    class_ref, x_ref, off_ref, table_ref = refs[:4]
    shards, vectors = refs[4:8], refs[8:16]
    mixed_out, xs_out, bias_out, weight_out, vec_out, gram_out = refs[16], refs[17], refs[18:21], refs[21:25], refs[25], refs[26]
    xs, z, mixed, index, wide = refs[27:32]
    bias, weights = refs[32:35], refs[35:39]
    vbuf, stat, stat2 = refs[39:42]
    send, recv, send2, recv2, local = refs[42:47]
    place = Place(dp_size, fs_size)
    images = xs.shape[0]

    for k in range(4):
        own = shards[k][...]
        if k == 0:
            own = arrange(own.astype(jnp.float32)).astype(jnp.bfloat16)
        weights[k][place.fs] = own
    vbuf[place.fs] = jnp.concatenate(
        [pad_lanes(v[...].astype(jnp.float32), 128) for v in vectors], axis=0
    )
    place.greet()

    by_columns(wide, x_ref[...].astype(jnp.float32))
    count = jnp.int32(0)
    for image in range(images):
        limit = limits_of(class_ref[image])
        row = lax.broadcasted_iota(jnp.int32, (SLOT, xs.shape[2]), 0)
        value = jnp.where(row < limit, take_image(wide, image, images), 0.0)
        xs[image] = pad_rows(value, ROWS).astype(jnp.bfloat16)
        count = count + limit

    flat = xs[...].reshape(images * ROWS, xs.shape[2])
    gram = dot_tn(flat, flat)
    total_x = dot_nn(jnp.ones((8, images * ROWS), jnp.bfloat16), flat)

    place.meet()
    gather_start(place, weights[0], send.at[0], recv.at[0])

    def start(step, _):
        target = lax.rem(place.fs + step, place.fs_size)
        push(vbuf.at[place.fs], vbuf.at[place.fs], send.at[4], recv.at[4], (place.dp, target))
        return 0

    lax.fori_loop(1, place.fs_size, start, 0)
    for k in range(1, 4):
        gather_start(place, weights[k], send.at[k], recv.at[k])
    xs_copy = pltpu.make_async_copy(xs, xs_out, local.at[0])
    xs_copy.start()
    bias_tables(off_ref, table_ref, index, bias, place.core)
    copies = [xs_copy]
    gather_pass(place, weights[0], recv.at[0], send2.at[0], recv2.at[0])
    gather_end(place, weights[0], recv2.at[0])
    weight = flat_weight(weights[0])
    high, low = split_low(gram)
    spread = dot_nn(high, weight) + dot_nn(low, weight)
    squares = jnp.sum(weight.astype(jnp.float32) * spread, axis=0, keepdims=True)
    sums = precise(total_x, weight)[:1]
    tail = jnp.full((1, 128), count.astype(jnp.float32))
    place.spread_pair(
        stat,
        jnp.concatenate(
            [jnp.concatenate([sums, tail], axis=1), jnp.concatenate([squares, tail], axis=1)], axis=0
        ),
        send.at[5],
        recv.at[5],
    )
    place.spread_chips(stat2, place.collect_pair(stat, recv.at[5]), send.at[6], recv.at[6])
    for k in range(3):
        part = bias[k].at[place.core]
        push(part, part, send.at[7 + k], recv.at[7 + k], place.partner)

    def product(image, _):
        z[image] = dot_nn(xs[image], weight)
        return 0

    lax.fori_loop(0, images, product, 0)
    for k in range(1, 4):
        gather_pass(place, weights[k], recv.at[k], send2.at[k], recv2.at[k])
    await_bytes(vbuf.at[pl.ds(0, place.fs_size - 1)], recv.at[4])
    widths = [v.shape[1] for v in vectors]
    full = assemble(vbuf, widths, 768)
    full[0], full[1] = arrange(full[0]), arrange(full[1])

    for k in range(3):
        await_bytes(bias[k].at[0], recv.at[7 + k])
        copies.append(pltpu.make_async_copy(bias[k], bias_out[k], local.at[1 + k]))
        copies[-1].start()
    gram_out[...] = gram
    got = place.collect_chips(stat2, recv.at[6])
    whole = got[0:1, 768:769]
    center = got[0:1, :768] / whole
    square = got[1:2, :768] / whole
    scale = lax.rsqrt(square - center * center + EPS)
    vec_out[...] = jnp.concatenate(
        full
        + [scale, center, jnp.broadcast_to(whole, (1, 768)), pad_lanes(total_x[:1], 768)]
        + [jnp.zeros((4, 768), jnp.float32)],
        axis=0,
    )
    gain = scale * full[0]
    shift = full[1] - center * gain
    fold = jnp.where(lax.broadcasted_iota(jnp.int32, (1, 768), 1) < 128, KEY ** (-0.5) * LOG2E, 1.0)
    gain, shift = gain * fold, shift * fold

    def normal(image, _):
        mixed[image] = (z[image] * gain + shift).astype(jnp.bfloat16)
        pltpu.make_async_copy(mixed.at[image], mixed_out.at[image], local.at[8 + image]).start()
        return 0

    lax.fori_loop(0, images, normal, 0)
    for k in range(4):
        if k > 0:
            gather_end(place, weights[k], recv2.at[k])
        copies.append(pltpu.make_async_copy(weights[k], weight_out[k], local.at[4 + k]))
        copies[-1].start()
    for k in range(4):
        gather_settle(place, weights[k], send.at[k], send2.at[k])
    await_bytes(vbuf.at[pl.ds(0, place.fs_size - 1)], send.at[4])
    place.settle_pair(stat, send.at[5])
    place.settle_chips(stat2, send.at[6])
    for k in range(3):
        await_bytes(bias[k].at[0], send.at[7 + k])
    for copy in copies:
        copy.wait()

    def finish(image, _):
        pltpu.make_async_copy(mixed.at[image], mixed_out.at[image], local.at[8 + image]).wait()
        return 0

    lax.fori_loop(0, images, finish, 0)


def first_call(dp_size, fs_size, classes, inputs, offset_table, bias_table, weights, vectors):
    images, model = classes.shape[0], inputs.shape[1]
    vectors = [v.reshape(1, -1) for v in vectors]
    shapes = [(fs_size,) + w.shape for w in weights]
    biases = [(2, r, 2 * l) for _, _, r, l in PARTS]
    bf, f32 = jnp.bfloat16, jnp.float32
    return pl.pallas_call(
        functools.partial(first_kernel, dp_size, fs_size),
        out_shape=[
            jax.ShapeDtypeStruct((images, ROWS, 768), bf),
            jax.ShapeDtypeStruct((images, ROWS, model), bf),
        ]
        + [jax.ShapeDtypeStruct(s, f32) for s in biases]
        + [jax.ShapeDtypeStruct(s, bf) for s in shapes]
        + [jax.ShapeDtypeStruct((16, 768), f32), jax.ShapeDtypeStruct((model, model), f32)],
        in_specs=[SMEM] + [VMEM] * 15,
        out_specs=[ANY] * 9 + [VMEM] * 2,
        scratch_shapes=[
            pltpu.VMEM((images, ROWS, model), bf),
            pltpu.VMEM((images, ROWS, 768), f32),
            pltpu.VMEM((images, ROWS, 768), bf),
            pltpu.VMEM((ROWS, 384), jnp.int32),
            pltpu.VMEM((model // 128, inputs.shape[0], 128), f32),
        ]
        + [pltpu.VMEM(s, f32) for s in biases]
        + [pltpu.VMEM(s, bf) for s in shapes]
        + [
            pltpu.VMEM((fs_size, 8, 128), f32),
            pltpu.VMEM((2, 2, 896), f32),
            pltpu.VMEM((dp_size * fs_size // 2, 2, 896), f32),
            pltpu.SemaphoreType.DMA((10,)),
            pltpu.SemaphoreType.DMA((10,)),
            pltpu.SemaphoreType.DMA((4,)),
            pltpu.SemaphoreType.DMA((4,)),
            pltpu.SemaphoreType.DMA((8 + images,)),
        ],
        compiler_params=pltpu.CompilerParams(
            collective_id=0, has_side_effects=True, vmem_limit_bytes=56 * 2**20
        ),
    )(classes, inputs, offset_table, bias_table, *weights, *vectors)


def total_rows(value):
    return jnp.sum(value, axis=0, keepdims=True)


def sigma_of(value):
    return 0.5 * jnp.tanh(0.5 * value) + 0.5


def slope_of(value):
    sigma = sigma_of(value)
    return sigma * (1.0 + value * (1.0 - sigma))


def norm_parts(sums, squares, total, gain, shift):
    center = sums / total
    scale = lax.rsqrt(squares / total - center * center + EPS)
    return center, scale, scale * gain, shift - center * scale * gain


def back_parts(grad_sum, grad_z, total, gain, center, scale):
    gain_grad = scale * (grad_z - center * grad_sum)
    alpha = scale * gain
    slant = alpha * scale * gain_grad / total
    level = alpha * (grad_sum - center * scale * gain_grad) / total
    return gain_grad, alpha, slant, level


def outer(column, row):
    left = jnp.concatenate([column, jnp.zeros((7, column.shape[1]), jnp.float32)], axis=0)
    right = jnp.concatenate([row, jnp.zeros((7, row.shape[1]), jnp.float32)], axis=0)
    left_high, left_low = split_low(left)
    right_high, right_low = split_low(right)
    return dot_tn(left_high, right_high) + dot_tn(left_high, right_low) + dot_tn(left_low, right_high)


def middle_kernel(dp_size, fs_size, group, *refs):
    class_ref, att_in, xs_in, cot_in = refs[:4]
    weight_in, vec_ref, gram_ref = refs[4:7], refs[7], refs[8]
    out_out, gatt_out, gm_out, grad_out, vec_out, own_gram = refs[9], refs[10], refs[11], refs[12:15], refs[15], refs[16]
    refs = refs[2:]
    att, xs, cot, wo_buf, wu_buf, wd_buf = refs[15:21]
    gs, act, slope_att, zo, low, zu, hid, slope_up, zd, dzd, gu, gm, out, gatt, wide = refs[21:36]
    stat_o, stat_u, stat_d, stat_bu, stat_bo = refs[36:41]
    send, recv, local = refs[41:44]
    gram_steps, send_r, recv_r = refs[44:49], refs[49], refs[50]
    down_steps, send_w, recv_w = refs[51:55], refs[55], refs[56]
    place = Place(dp_size, fs_size)
    images = att.shape[0]
    chunks = images // group
    size = group * ROWS
    f32, bf = jnp.float32, jnp.bfloat16
    gram_sum = Reduce(place, *gram_steps, send_r, recv_r)
    down_sum = Reduce(place, *down_steps, None, send_w, recv_w)

    def copy(source, target, at):
        return pltpu.make_async_copy(source, target, local.at[at])

    loads = [
        copy(weight_in[0], wo_buf, 0),
        copy(xs_in, xs, 1),
        copy(cot_in, cot, 2),
        copy(weight_in[1], wu_buf, 3),
        copy(weight_in[2], wd_buf, 4),
    ]
    loads[0].start()

    def att_copy(k):
        part = pl.ds(k * group, group)
        return copy(att_in.at[part], att.at[part], 8 + k)

    for k in range(chunks):
        att_copy(k).start()
    for load in loads[1:]:
        load.start()
    place.greet()

    def get(ref, k):
        return ref[pl.ds(k * group, group)].reshape(size, ref.shape[2])

    def put(ref, k, value):
        ref[pl.ds(k * group, group)] = value.astype(ref.dtype).reshape(group, ROWS, ref.shape[2])

    def kept(k, width):
        row = lax.broadcasted_iota(jnp.int32, (ROWS, width), 0)
        return jnp.concatenate([row < limits_of(class_ref[k * group + j]) for j in range(group)], axis=0)

    def over(body, carry):
        return lax.fori_loop(0, chunks, body, carry, unroll=True)

    def zero(width):
        return jnp.zeros((1, width), f32)

    model = xs.shape[2]
    hidden = zu.shape[2]
    total = vec_ref[10:11, :1]
    out_gain, out_shift = vec_ref[2:3, :model], vec_ref[3:4, :model]
    up_gain, up_shift = vec_ref[4:5, :hidden], vec_ref[5:6, :hidden]
    down_gain, down_shift = vec_ref[6:7, :model], vec_ref[7:8, :model]

    loads[0].wait()
    wo = flat_weight(wo_buf)

    def step_out(k, carry):
        att_copy(k).wait()
        value = get(att, k).astype(f32)
        active = (value * sigma_of(value)).astype(bf)
        put(act, k, active)
        z = dot_nn(active, wo)
        put(zo, k, z)
        return carry[0] + total_rows(z), carry[1] + total_rows(z * z)

    sums = over(step_out, (zero(model), zero(model)))
    place.meet()
    x_sum = vec_ref[11:12, :model]
    place.spread(stat_o, jnp.concatenate(sums + (x_sum,), axis=0), send.at[0], recv.at[0])
    for load in loads[1:]:
        load.wait()

    def fill_out(k, _):
        put(slope_att, k, slope_of(get(att, k).astype(f32)))
        return 0

    over(fill_out, 0)
    by_columns(wide, cot[...].astype(f32))
    grad_sum = zero(model)
    for image in range(images):
        row = lax.broadcasted_iota(jnp.int32, (SLOT, model), 0)
        value = jnp.where(row < limits_of(class_ref[image]), take_image(wide, image, images), 0.0)
        gs[image] = pad_rows(value, ROWS).astype(bf)
        grad_sum = grad_sum + total_rows(value)
    wu, wd = flat_weight(wu_buf), flat_weight(wd_buf)
    got = place.collect(stat_o, recv.at[0])
    center_o, scale_o, a_o, b_o = norm_parts(got[0:1], got[1:2], total, out_gain, out_shift)
    x_mean = got[2:3] / total

    def middle_of(k):
        return get(xs, k).astype(f32) + get(zo, k) * a_o + b_o

    def step_up(k, carry):
        lower = jnp.where(kept(k, model), middle_of(k), 0.0).astype(bf)
        put(low, k, lower)
        z = dot_nn(lower, wu)
        put(zu, k, z)
        return carry[0] + total_rows(z), carry[1] + total_rows(z * z)

    sums = over(step_up, (zero(hidden), zero(hidden)))
    place.spread(stat_u, jnp.concatenate(sums, axis=0), send.at[1], recv.at[1])
    low_flat = low[...].reshape(images * ROWS, model)
    low_gram = dot_tn(low_flat, low_flat)
    low_sum = dot_nn(jnp.ones((8, images * ROWS), bf), low_flat)[:1]
    count = sum(limits_of(class_ref[k]) for k in range(images)).astype(f32)
    moved = x_sum - 0.5 * count * x_mean
    gram = gram_ref[...] - outer(x_mean, moved) - outer(moved, x_mean)
    gram_steps[0][...] = gram.reshape(gram_steps[0].shape).astype(bf)
    gram_sum.swap()

    def fill_up(k, carry):
        centered = jnp.where(kept(k, model), get(zo, k) - center_o, 0.0).astype(bf)
        return carry + dot_tn(get(act, k), centered)

    act_z = over(fill_up, jnp.zeros((act.shape[2], model), f32))
    got = place.collect(stat_u, recv.at[1])
    center_u, scale_u, a_u, b_u = norm_parts(got[0:1], got[1:2], total, up_gain, up_shift)

    def step_down(k, carry):
        value = get(zu, k) * a_u + b_u
        active = jnp.where(kept(k, hidden), value * sigma_of(value), 0.0).astype(bf)
        put(hid, k, active)
        z = dot_nn(active, wd)
        put(zd, k, z)
        return (
            carry[0] + total_rows(z),
            carry[1] + total_rows(z * z),
            carry[2] + total_rows(z * get(gs, k).astype(f32)),
        )

    sums = over(step_down, (zero(model), zero(model), zero(model)))
    place.spread(stat_d, jnp.concatenate(sums + (grad_sum,), axis=0), send.at[2], recv.at[2])

    def fill_down(k, _):
        put(slope_up, k, slope_of(get(zu, k) * a_u + b_u))
        return 0

    over(fill_down, 0)
    gram_sum.scatter()
    got = place.collect(stat_d, recv.at[2])
    center_d, scale_d, a_d, b_d = norm_parts(got[0:1], got[1:2], total, down_gain, down_shift)
    down_shift_grad = got[3:4]
    down_gain_grad, alpha, slant, level = back_parts(got[3:4], got[2:3], total, down_gain, center_d, scale_d)

    def step_back_down(k, carry):
        dz = get(gs, k).astype(f32) * alpha - get(zd, k) * slant - jnp.where(kept(k, model), level, 0.0)
        dz = dz.astype(bf)
        put(dzd, k, dz)
        grad = dot_nt(dz, wd) * get(slope_up, k).astype(f32)
        put(gu, k, grad)
        return carry[0] + total_rows(grad), carry[1] + total_rows(grad * get(zu, k))

    sums = over(step_back_down, (zero(hidden), zero(hidden)))
    place.spread(stat_bu, jnp.concatenate(sums, axis=0), send.at[3], recv.at[3])

    def fill_back_down(k, carry):
        grad = get(gu, k)
        carry = carry + dot_tn(get(low, k), grad.astype(bf))
        put(gm, k, get(gs, k).astype(f32) + dot_nt((grad * a_u).astype(bf), wu))
        return carry

    up_raw = over(fill_back_down, jnp.zeros((model, hidden), f32))
    down_grad = dot_tn(hid[...].reshape(images * ROWS, hidden), dzd[...].reshape(images * ROWS, model))
    down_steps[0][...] = down_grad.reshape(down_steps[0].shape).astype(bf)
    down_sum.swap()
    gram_sum.share()
    got = place.collect(stat_bu, recv.at[3])
    up_shift_grad = got[0:1]
    up_gain_grad, alpha_u, slant_u, level_u = back_parts(got[0:1], got[1:2], total, up_gain, center_u, scale_u)
    mix = dot_nt((wu.astype(f32) * slant_u).astype(bf), wu).astype(bf)
    high, rest = split_low(jnp.broadcast_to(level_u, (8, hidden)))
    lift = (dot_nt(high, wu) + dot_nt(rest, wu))[:1]

    def step_back_up(k, carry):
        grad = get(gm, k) - dot_nn(get(low, k), mix) - jnp.where(kept(k, model), lift, 0.0)
        put(gm, k, grad)
        part = pl.ds(k * group, group)
        copy(gm.at[part], gm_out.at[part], 8 + chunks + k).start()
        return carry[0] + total_rows(grad), carry[1] + total_rows(grad * get(zo, k))

    sums = over(step_back_up, (zero(model), zero(model)))
    place.spread(stat_bo, jnp.concatenate(sums, axis=0), send.at[4], recv.at[4])
    down_sum.scatter()
    up_grad = up_raw * alpha_u - precise(low_gram, wu) * slant_u - outer(low_sum, level_u)
    grad_out[1][...] = up_grad.reshape(grad_out[1].shape).astype(bf)
    out_mean = down_shift_grad / total

    def fill_back_up(k, carry):
        centered = jnp.where(kept(k, model), get(gm, k) - out_mean, 0.0).astype(bf)
        return carry + dot_tn(get(act, k), centered)

    act_g = over(fill_back_up, jnp.zeros((act.shape[2], model), f32))
    for image in range(images):
        row = lax.broadcasted_iota(jnp.int32, (ROWS, model), 0)
        value = xs[image].astype(f32) + zo[image] * a_o + zd[image] * a_d + (b_o + b_d)
        value = jnp.where(row < limits_of(class_ref[image]), value, 0.0)
        put_image(wide, image, images, value)
    for k in range(wide.shape[0]):
        out[:, 128 * k : 128 * k + 128] = wide[k].astype(bf)
    out_copy = copy(out, out_out, 5)
    out_copy.start()
    own_gram[...] = gram_sum.result()
    got = place.collect(stat_bo, recv.at[4])
    out_shift_grad = got[0:1]
    out_gain_grad, alpha_o, slant_o, level_o = back_parts(got[0:1], got[1:2], total, out_gain, center_o, scale_o)

    def step_back_out(k, _):
        dz = get(gm, k) * alpha_o - get(zo, k) * slant_o - jnp.where(kept(k, model), level_o, 0.0)
        dz = dz.astype(bf)
        put(gatt, k, dot_nt(dz, wo) * get(slope_att, k).astype(f32))
        part = pl.ds(k * group, group)
        copy(gatt.at[part], gatt_out.at[part], 8 + 2 * chunks + k).start()
        return 0

    over(step_back_out, 0)
    out_grad = act_g * alpha_o - act_z * slant_o
    grad_out[0][...] = out_grad.reshape(grad_out[0].shape).astype(bf)
    vec_out[...] = jnp.concatenate(
        [
            pad_lanes(v, hidden)
            for v in (
                out_gain_grad,
                out_shift_grad,
                up_gain_grad,
                up_shift_grad,
                down_gain_grad,
                down_shift_grad,
                x_mean,
                zero(hidden),
            )
        ],
        axis=0,
    )
    for k, stat in enumerate((stat_o, stat_u, stat_d, stat_bu, stat_bo)):
        place.settle(stat, send.at[k])
    gram_sum.settle()
    grad_out[2][...] = down_sum.gathered()
    down_sum.settle((0, 1))

    def finish(k, _):
        part = pl.ds(k * group, group)
        copy(gm.at[part], gm_out.at[part], 8 + chunks + k).wait()
        copy(gatt.at[part], gatt_out.at[part], 8 + 2 * chunks + k).wait()
        return 0

    over(finish, 0)
    out_copy.wait()


def middle_call(dp_size, fs_size, classes, attended, xs, cotangent, weights, vec, gram):
    images, model, feature, hidden = xs.shape[0], xs.shape[2], attended.shape[2], weights[1].shape[2]
    group = 2 if images % 2 == 0 else 1
    chunks = images // group
    devices = dp_size * fs_size
    own = model // fs_size
    bf, f32 = jnp.bfloat16, jnp.float32

    def rows(width, kind):
        return pltpu.VMEM((images, ROWS, width), kind)

    return pl.pallas_call(
        functools.partial(middle_kernel, dp_size, fs_size, group),
        out_shape=[
            jax.ShapeDtypeStruct(cotangent.shape, bf),
            jax.ShapeDtypeStruct((images, ROWS, feature), bf),
            jax.ShapeDtypeStruct((images, ROWS, model), f32),
        ]
        + [jax.ShapeDtypeStruct(w.shape, bf) for w in weights[:2]]
        + [jax.ShapeDtypeStruct(weights[2].shape[1:2] + (model // 2,), bf)]
        + [jax.ShapeDtypeStruct((8, hidden), f32), jax.ShapeDtypeStruct((own, model), f32)],
        in_specs=[SMEM] + [ANY] * 6 + [VMEM] * 2,
        out_specs=[ANY] * 3 + [VMEM] * 5,
        scratch_shapes=[
            rows(feature, bf),
            rows(model, bf),
            pltpu.VMEM(cotangent.shape, bf),
        ]
        + [pltpu.VMEM(w.shape, bf) for w in weights]
        + [
            rows(model, bf),
            rows(feature, bf),
            rows(feature, bf),
            rows(model, f32),
            rows(model, bf),
            rows(hidden, f32),
            rows(hidden, bf),
            rows(hidden, bf),
            rows(model, f32),
            rows(model, bf),
            rows(hidden, f32),
            rows(model, f32),
            pltpu.VMEM(cotangent.shape, bf),
            rows(feature, bf),
            pltpu.VMEM((model // 128, cotangent.shape[0], 128), f32),
            pltpu.VMEM((devices, 3, model), f32),
            pltpu.VMEM((devices, 2, hidden), f32),
            pltpu.VMEM((devices, 4, model), f32),
            pltpu.VMEM((devices, 2, hidden), f32),
            pltpu.VMEM((devices, 2, model), f32),
            pltpu.SemaphoreType.DMA((5,)),
            pltpu.SemaphoreType.DMA((5,)),
            pltpu.SemaphoreType.DMA((8 + 3 * chunks,)),
            pltpu.VMEM((fs_size, own, model), bf),
        ]
        + [pltpu.VMEM((fs_size, own, model // 2), bf)] * 3
        + [
            pltpu.VMEM((dp_size, own, model // 2), bf),
            pltpu.SemaphoreType.DMA((3,)),
            pltpu.SemaphoreType.DMA((3,)),
            pltpu.VMEM(weights[2].shape, bf),
        ]
        + [pltpu.VMEM(weights[2].shape[:2] + (model // 2,), bf)] * 3
        + [
            pltpu.SemaphoreType.DMA((2,)),
            pltpu.SemaphoreType.DMA((2,)),
        ],
        compiler_params=pltpu.CompilerParams(
            collective_id=1, has_side_effects=True, vmem_limit_bytes=58 * 2**20
        ),
    )(classes, attended, xs, cotangent, *weights, vec, gram)


def last_kernel(dp_size, fs_size, group, *refs):
    class_ref, xs_in, gmix_in, gm_in, off_in = refs[:5]
    acc_in, grad_in, down_part = refs[5:8], refs[8:10], refs[10]
    wq_buf, raw_ref, sum_ref, gram_ref, vec_ref, lines_ref = refs[11:17]
    ig_out, table_out, own_out, vec_out = refs[17], refs[18], refs[19:23], refs[23]
    xs, gmix, gm, off, ig, res = refs[24:30]
    acc, full = refs[30:33], refs[33:36]
    steps = [refs[36 + 4 * k : 40 + 4 * k] for k in range(3)]
    down_third = refs[48]
    stat, stat_t = refs[49:51]
    send, recv, local, send_r, recv_r = refs[51:56]
    place = Place(dp_size, fs_size)
    images = xs.shape[0]
    chunks = images // group
    size = group * ROWS
    f32, bf = jnp.float32, jnp.bfloat16
    model, width = xs.shape[2], gmix.shape[2]

    def copy(source, target, at):
        return pltpu.make_async_copy(source, target, local.at[at])

    grad_loads = [copy(grad_in[k], full[1 + k], k) for k in range(2)]
    mix_load = copy(gmix_in, gmix, 3)
    table_loads = [copy(off_in, off, 4)] + [copy(acc_in[k], acc[k], 5 + k) for k in range(3)]
    late_loads = [copy(xs_in, xs, 8), copy(gm_in, gm, 9)]
    place.greet()
    for load in grad_loads + [mix_load] + table_loads + late_loads:
        load.start()
    reduces = [Reduce(place, full[k], *steps[k], send_r.at[k], recv_r.at[k]) for k in range(3)]
    down_sum = Reduce(place, None, None, down_third, None, down_third, send_r.at[3], recv_r.at[3])

    def get(ref, k):
        return ref[pl.ds(k * group, group)].reshape(size, ref.shape[2])

    def put(ref, k, value):
        ref[pl.ds(k * group, group)] = value.astype(ref.dtype).reshape(group, ROWS, ref.shape[2])

    def kept(k, lanes):
        row = lax.broadcasted_iota(jnp.int32, (ROWS, lanes), 0)
        return jnp.concatenate([row < limits_of(class_ref[k * group + j]) for j in range(group)], axis=0)

    total = vec_ref[10:11, :1]
    gain, scale, center = vec_ref[0:1, :], vec_ref[8:9, :], vec_ref[9:10, :]
    x_mean = lines_ref[6:7, :model]
    weight = flat_weight(wq_buf)
    weight_f = weight.astype(f32)
    raw = raw_ref[...]
    grad_sum = total_rows(sum_ref[...])
    grad_z = total_rows(raw * weight_f)
    full[0][...] = (raw - outer(x_mean, grad_sum)).reshape(full[0].shape).astype(bf)
    for load in grad_loads:
        load.wait()
    place.meet()
    place.spread(stat, jnp.concatenate([grad_sum, grad_z], axis=0), send.at[0], recv.at[0])
    for k in range(3):
        reduces[k].swap()
    down_sum.share(down_part[...])
    alpha = scale * gain
    mix_load.wait()

    def product(k, _):
        put(ig, k, dot_nt((get(gmix, k).astype(f32) * alpha).astype(bf), weight))
        return 0

    lax.fori_loop(0, chunks, product, 0)
    for k in range(3):
        reduces[k].scatter()
    for load in table_loads + late_loads:
        load.wait()
    place.spread(stat_t, table_sums(off, acc), send.at[1], recv.at[1])

    got = place.collect(stat, recv.at[0])
    gain_grad, alpha, slant, level = back_parts(got[0:1], got[1:2], total, gain, center, scale)
    mix = dot_nt((weight_f * slant).astype(bf), weight).astype(bf)
    high, rest = split_low(jnp.broadcast_to(level, (8, width)))
    lift = (dot_nt(high, weight) + dot_nt(rest, weight))[:1]
    vec_out[...] = jnp.concatenate(
        [restore(gain_grad), restore(got[0:1]), jnp.zeros((6, width), f32)], axis=0
    )
    for k in range(3):
        reduces[k].share()
    for k in range(chunks):
        value = get(gm, k) + get(ig, k) - dot_nn(get(xs, k), mix) - jnp.where(kept(k, model), lift, 0.0)
        for j in range(group):
            put_image(res, k * group + j, images, value[j * ROWS : (j + 1) * ROWS])
    res_copies = [copy(res.at[k], ig_out.at[:, pl.ds(128 * k, 128)], 10 + k) for k in range(model // 128)]
    for res_copy in res_copies:
        res_copy.start()
    own_out[0][...] = restore(reduces[0].result() * alpha - precise(gram_ref[...], weight) * slant)
    for k in (1, 2):
        own_out[k][...] = reduces[k].result()
    own_out[3][...] = down_sum.result()
    table_out[...] = place.collect(stat_t, recv.at[1])
    for k in range(3):
        reduces[k].settle()
    down_sum.settle((2,))
    place.settle(stat, send.at[0])
    place.settle(stat_t, send.at[1])
    for res_copy in res_copies:
        res_copy.wait()


def last_call(dp_size, fs_size, classes, xs, gmix, gm, offset_table, accs, grads, wq, raw, sums, gram, vec, lines):
    images, model, width = xs.shape[0], xs.shape[2], gmix.shape[2]
    group = 2 if images % 2 == 0 else 1
    devices = dp_size * fs_size
    bf, f32 = jnp.bfloat16, jnp.float32
    down_part = grads[2]
    shapes = [wq.shape] + [g.shape for g in grads[:2]]
    own_shapes = [s[1:] for s in shapes] + [(down_part.shape[0], 2 * down_part.shape[1])]
    steps = []
    for s in shapes:
        half = s[2] // 2
        steps += [
            pltpu.VMEM((fs_size, s[1], half), bf),
            pltpu.VMEM((fs_size, s[1], half), bf),
            pltpu.VMEM((fs_size, s[1], half), bf),
            pltpu.VMEM((dp_size, s[1], half), bf),
        ]
    order = []
    for k in range(3):
        order += [steps[4 * k], steps[4 * k + 1], steps[4 * k + 2], steps[4 * k + 3]]
    return pl.pallas_call(
        functools.partial(last_kernel, dp_size, fs_size, group),
        out_shape=[jax.ShapeDtypeStruct((SLOT * images, model), f32), jax.ShapeDtypeStruct((HEADS, 384), f32)]
        + [jax.ShapeDtypeStruct(s, f32) for s in own_shapes]
        + [jax.ShapeDtypeStruct((8, width), f32)],
        in_specs=[SMEM] + [ANY] * 9 + [VMEM] * 7,
        out_specs=[ANY] + [VMEM] * 6,
        scratch_shapes=[
            pltpu.VMEM(xs.shape, bf),
            pltpu.VMEM(gmix.shape, bf),
            pltpu.VMEM(gm.shape, f32),
            pltpu.VMEM(offset_table.shape, jnp.int32),
            pltpu.VMEM(gm.shape, f32),
            pltpu.VMEM((model // 128, SLOT * images, 128), f32),
        ]
        + [pltpu.VMEM(a.shape, f32) for a in accs]
        + [pltpu.VMEM(s, bf) for s in shapes]
        + order
        + [
            pltpu.VMEM((dp_size,) + down_part.shape, bf),
            pltpu.VMEM((devices, 2, width), f32),
            pltpu.VMEM((devices, HEADS, 384), f32),
            pltpu.SemaphoreType.DMA((2,)),
            pltpu.SemaphoreType.DMA((2,)),
            pltpu.SemaphoreType.DMA((10 + model // 128,)),
            pltpu.SemaphoreType.DMA((4, 3)),
            pltpu.SemaphoreType.DMA((4, 3)),
        ],
        compiler_params=pltpu.CompilerParams(
            collective_id=2, has_side_effects=True, vmem_limit_bytes=56 * 2**20
        ),
    )(classes, xs, gmix, gm, offset_table, *accs, *grads, wq, raw, sums, gram, vec, lines)

def shards(
    inputs,
    classes,
    offset_table,
    bias_table,
    qkv_weight,
    qkv_gain,
    qkv_shift,
    out_weight,
    out_gain,
    out_shift,
    up_weight,
    up_gain,
    up_shift,
    down_weight,
    down_gain,
    down_shift,
    cotangent,
):
    sizes = lax.axis_size("dp"), lax.axis_size("fsdp")
    images, _, model = inputs.shape

    def by_slot(array):
        return jnp.swapaxes(array, 0, 1).reshape(SLOT * images, model)

    def by_image(array):
        return jnp.swapaxes(array.reshape(SLOT, images, model), 0, 1)

    first = first_call(
        *sizes,
        classes,
        by_slot(inputs),
        offset_table,
        bias_table,
        (qkv_weight, out_weight, up_weight, down_weight),
        (qkv_gain, qkv_shift, out_gain, out_shift, up_gain, up_shift, down_gain, down_shift),
    )
    mixed, xs, biases, weights, vec, gram = first[0], first[1], first[2:5], first[5:9], first[9], first[10]
    attended, probs, shares = attend_call(classes, mixed, biases)
    middle = middle_call(*sizes, classes, attended, xs, by_slot(cotangent), weights[1:], vec, gram)
    output, grad_att, grad_middle, grads, lines, own_gram = *middle[:3], middle[3:6], middle[6], middle[7]
    back = back_call(sizes[1], classes, mixed, probs, shares, grad_att, attended, xs, lines, output)
    grad_mixed, raw, sums, accs, own_lines, output = *back[:3], back[3:6], back[6:12], back[12]
    last = last_call(
        *sizes,
        classes,
        xs,
        grad_mixed,
        grad_middle,
        offset_table,
        accs,
        grads,
        weights[0],
        raw,
        sums,
        own_gram,
        vec,
        lines,
    )
    input_grad, table_grad, *rest = end_call(sizes[1], last[0], last[1], last[2:6], last[6])
    own_lines = [line.reshape(-1) for line in (*own_lines, *rest[4:])]
    return (
        by_image(output),
        by_image(input_grad),
        table_grad,
        rest[0],
        *own_lines[6:8],
        rest[1],
        *own_lines[0:2],
        rest[2],
        *own_lines[2:4],
        rest[3],
        *own_lines[4:6],
    )


def solution(mesh):
    placed = (
        P(("dp", "fsdp"), None, None),
        P(("dp", "fsdp")),
        P(),
        P(),
        P("fsdp", None),
        P("fsdp"),
        P("fsdp"),
        P("fsdp", None),
        P("fsdp"),
        P("fsdp"),
        P("fsdp", None),
        P("fsdp"),
        P("fsdp"),
        P("fsdp", None),
        P("fsdp"),
        P("fsdp"),
        P(("dp", "fsdp"), None, None),
    )
    return jax.shard_map(
        shards,
        mesh=mesh,
        in_specs=placed,
        out_specs=(
            P(("dp", "fsdp"), None, None),
            P(("dp", "fsdp"), None, None),
            P(),
            P("fsdp", None),
            P("fsdp"),
            P("fsdp"),
            P("fsdp", None),
            P("fsdp"),
            P("fsdp"),
            P("fsdp", None),
            P("fsdp"),
            P("fsdp"),
            P("fsdp", None),
            P("fsdp"),
            P("fsdp"),
        ),
        check_vma=False,
    )
```

```python
import functools

import jax
import jax.numpy as jnp
from jax import lax
from jax.experimental import pallas as pl
from jax.experimental.pallas import tpu as pltpu
from jax.sharding import PartitionSpec as P

HEADS = 4
KEY = 32
VALD = 128
GRID = 18
CLASSES = 3
SLOT = 324
NOFF = 324


EPS = 1e-05
LOG2E = 1.4426950408889634
LN2 = 0.6931471805599453
ROWS = 336
PARTS = ((10, 100, 112, 128), (14, 196, 208, 256), (18, 324, 336, 384))
VMEM = pl.BlockSpec(memory_space=pltpu.VMEM)


def dot_nn(left, right):
    return jnp.dot(left, right, preferred_element_type=jnp.float32)


def dot_nt(left, right):
    return lax.dot_general(left, right, (((1,), (1,)), ((), ())), preferred_element_type=jnp.float32)


def dot_tn(left, right):
    return lax.dot_general(left, right, (((0,), (0,)), ((), ())), preferred_element_type=jnp.float32)


def pad_rows(value, rows):
    if value.shape[0] == rows:
        return value
    return jnp.concatenate([value, jnp.zeros((rows - value.shape[0], value.shape[1]), value.dtype)], axis=0)


def pad_lanes(value, lanes):
    if value.shape[1] == lanes:
        return value
    return jnp.concatenate([value, jnp.zeros((value.shape[0], lanes - value.shape[1]), value.dtype)], axis=1)


def bias_tables(off_ref, table_ref, index_ref, outs, pair):
    tables = []
    for side in range(2):
        row = pad_lanes(table_ref[pl.ds(2 * pair + side, 1), :], 384) * LOG2E
        tables.append([jnp.broadcast_to(row[:, 128 * k : 128 * k + 128], (8, 128)) for k in range(3)])
    index_ref[...] = jnp.zeros_like(index_ref)
    for number, (_, amount, rows, lanes) in enumerate(PARTS):
        index_ref[:SLOT, :SLOT] = off_ref[number]

        tiles = rows // 8 // (number + 1)

        def strip(step, _, number=number, amount=amount, lanes=lanes, tiles=tiles, out=outs[number]):
            for line in range(tiles):
                at = pl.multiple_of((step * tiles + line) * 8, 8)
                for block in range(lanes // 128):
                    index = index_ref[pl.ds(at, 8), 128 * block : 128 * block + 128]
                    low = index & 127
                    part = index >> 7
                    valid = lax.broadcasted_iota(jnp.int32, (8, 128), 1) + 128 * block < amount
                    for side in range(2):
                        found = [
                            jnp.take_along_axis(tables[side][k], low, axis=1, mode="promise_in_bounds")
                            for k in range(3 if number == 2 else 2)
                        ]
                        value = jnp.where(part == 0, found[0], found[1])
                        if number == 2:
                            value = jnp.where(part == 2, found[2], value)
                        column = side * lanes + 128 * block
                        out[pair, pl.ds(at, 8), column : column + 128] = jnp.where(valid, value, -1e30)
            return 0

        lax.fori_loop(0, number + 1, strip, 0)


def head_keys(keys, pair, lanes):
    owner = lax.broadcasted_iota(jnp.int32, keys.shape, 1) // KEY
    zero = jnp.zeros_like(keys)
    return jnp.concatenate(
        [pad_rows(jnp.where(owner == 2 * pair + side, keys, zero), lanes) for side in range(2)], axis=0
    )


def pair_values(values, lanes):
    zero = jnp.zeros((lanes, VALD), values.dtype)
    top = jnp.concatenate([pad_rows(values[:, :VALD], lanes), zero], axis=1)
    low = jnp.concatenate([zero, pad_rows(values[:, VALD:], lanes)], axis=1)
    return jnp.concatenate([top, low], axis=0)


def by_eight(value):
    return jnp.sum(value.reshape(value.shape[0] // 8, 8, value.shape[1]), axis=0)


def attend_kernel(class_ref, mixed_ref, bias0, bias1, bias2, att_ref, p_ref, r_ref):
    kind = class_ref[pl.program_id(0)]
    for number, (_, amount, rows, lanes) in enumerate(PARTS):

        @pl.when(kind == number)
        def _(amount=amount, rows=rows, lanes=lanes, bias=(bias0, bias1, bias2)[number]):
            query = mixed_ref[0, :rows, :128]
            keys = mixed_ref[0, :rows, 128:256]
            kept = lax.broadcasted_iota(jnp.int32, (rows, VALD), 0) < amount
            lane = lax.broadcasted_iota(jnp.int32, (rows, 128), 1)
            shares = jnp.zeros((rows, 128), jnp.float32)
            for pair in range(2):
                scores = dot_nt(query, head_keys(keys, pair, lanes)) + bias[pair]
                parts, inverse = [], []
                for side in range(2):
                    own = scores[:, side * lanes : (side + 1) * lanes]
                    expo = jnp.exp2(own - jnp.max(own, axis=1, keepdims=True))
                    share = 1.0 / jnp.sum(expo, axis=1, keepdims=True)
                    shares = jnp.where(lane == 2 * pair + side, share, shares)
                    parts.append(expo.astype(jnp.bfloat16))
                    inverse.append(share)
                both = jnp.concatenate(parts, axis=1)
                p_ref[0, :rows, 2 * pair * lanes : 2 * (pair + 1) * lanes] = both
                values = mixed_ref[0, :rows, 256 + 256 * pair : 512 + 256 * pair]
                sums = dot_nn(both, pair_values(values, lanes))
                for side in range(2):
                    own = sums[:, side * VALD : (side + 1) * VALD] * inverse[side]
                    at = (2 * pair + side) * VALD
                    att_ref[0, :rows, at : at + VALD] = jnp.where(kept, own, 0.0).astype(jnp.bfloat16)
            r_ref[0, :rows, :] = shares
            if rows < ROWS:
                att_ref[0, rows:, :] = jnp.zeros((ROWS - rows, att_ref.shape[2]), jnp.bfloat16)


def back_kernel(
    fs_size,
    class_ref,
    mixed_ref,
    p_ref,
    r_ref,
    g_ref,
    att_ref,
    xs_ref,
    lines_ref,
    out_in,
    gmix_ref,
    raw_ref,
    sum_ref,
    acc0,
    acc1,
    acc2,
    *more,
):
    own_refs, out_out, accs, held, out_sems = more[:6], more[6], more[7:10], more[10], more[11]
    out_load = pltpu.make_async_copy(out_in, held, out_sems.at[0])
    out_store = pltpu.make_async_copy(held, out_out, out_sems.at[1])

    @pl.when(pl.program_id(0) == 0)
    def _():
        out_load.start()
        for ref in (*accs, raw_ref, sum_ref):
            ref[...] = jnp.zeros_like(ref)
        spot = lax.axis_index("fsdp")
        lines = lines_ref[...]
        for k, ref in enumerate(own_refs):
            width = ref.shape[1]
            ref[...] = pltpu.roll(lines, lines.shape[1] - spot * width, 1)[k : k + 1, :width]

    kind = class_ref[pl.program_id(0)]
    for number, (_, amount, rows, lanes) in enumerate(PARTS):

        @pl.when(kind == number)
        def _(rows=rows, lanes=lanes, acc=accs[number]):
            query = mixed_ref[0, :rows, :128]
            keys = mixed_ref[0, :rows, 128:256]
            owner = lax.broadcasted_iota(jnp.int32, (rows, 128), 1) // KEY
            d_query = jnp.zeros((rows, 128), jnp.float32)
            d_keys = jnp.zeros((rows, 128), jnp.float32)
            for pair in range(2):
                grads, deltas = [], []
                for side in range(2):
                    head = 2 * pair + side
                    at = head * VALD
                    grad = g_ref[0, :rows, at : at + VALD].astype(jnp.float32) * r_ref[0, :rows, head : head + 1]
                    own = att_ref[0, :rows, at : at + VALD].astype(jnp.float32)
                    deltas.append(jnp.sum(grad * own, axis=1, keepdims=True))
                    grads.append(grad.astype(jnp.bfloat16))
                both = jnp.concatenate(grads, axis=1)
                values = mixed_ref[0, :rows, 256 + 256 * pair : 512 + 256 * pair]
                d_probs = dot_nt(both, pair_values(values, lanes))
                probs = p_ref[0, :rows, 2 * pair * lanes : 2 * (pair + 1) * lanes]
                low = []
                for side in range(2):
                    cut = slice(side * lanes, (side + 1) * lanes)
                    d_score = probs[:, cut].astype(jnp.float32) * (d_probs[:, cut] - deltas[side])
                    acc[pair, :, cut] += d_score
                    low.append(d_score.astype(jnp.bfloat16))
                d_low = jnp.concatenate(low, axis=1)
                d_query = d_query + dot_nn(d_low, head_keys(keys, pair, lanes))
                turned = dot_tn(d_low, query)
                d_values = dot_tn(probs, both)
                for side in range(2):
                    head = 2 * pair + side
                    d_keys = jnp.where(owner == head, turned[side * lanes : side * lanes + rows], d_keys)
                    at = 256 + head * VALD
                    whole = d_values[side * lanes : side * lanes + rows, side * VALD : (side + 1) * VALD]
                    sum_ref[:, at : at + VALD] += by_eight(whole)
                    gmix_ref[0, :rows, at : at + VALD] = whole.astype(jnp.bfloat16)
            d_query = d_query * KEY ** (-0.5)
            d_keys = d_keys * LN2
            sum_ref[:, :128] += by_eight(d_query)
            sum_ref[:, 128:256] += by_eight(d_keys)
            gmix_ref[0, :rows, :128] = d_query.astype(jnp.bfloat16)
            gmix_ref[0, :rows, 128:256] = d_keys.astype(jnp.bfloat16)
            raw_ref[...] += dot_tn(xs_ref[0, :rows, :], gmix_ref[0, :rows, :])
            if rows < ROWS:
                gmix_ref[0, rows:, :] = jnp.zeros((ROWS - rows, gmix_ref.shape[2]), jnp.bfloat16)

    @pl.when(pl.program_id(0) == pl.num_programs(0) // 2)
    def _():
        out_load.wait()
        out_store.start()

    @pl.when(pl.program_id(0) == pl.num_programs(0) - 1)
    def _():
        for low, acc in zip((acc0, acc1, acc2), accs):
            low[...] = acc[...].astype(jnp.bfloat16)
        out_store.wait()


def grid_places(off_ref):
    found = []
    for number, (side_of, amount, _, _) in enumerate(PARTS):
        offsets = off_ref[number]
        row = lax.broadcasted_iota(jnp.int32, (SLOT, 1), 0)
        most = jnp.max(offsets, axis=1, keepdims=True)
        corner = jnp.min(jnp.where(most == (side_of - 1) * (GRID + 1), row, SLOT), axis=0, keepdims=True)
        place = jnp.sum(jnp.where(row == corner, offsets, 0), axis=0, keepdims=True)
        place = jnp.where(lax.broadcasted_iota(jnp.int32, (1, SLOT), 1) < amount, place, -1)
        found.append(jnp.concatenate([place, jnp.full((1, 384 - SLOT), -1, jnp.int32)], axis=1))
    return jnp.concatenate(found + [jnp.full((8 - len(found), 384), -1, jnp.int32)], axis=0)


def one_hot(left, right):
    return (left == right).astype(jnp.float32).astype(jnp.bfloat16)


def table_sums(places, accs):
    zero = (jnp.zeros((8, 128), jnp.float32), jnp.zeros((16, 128), jnp.float32))
    totals = [[zero] * 6 for _ in range(HEADS)]
    for number, (side_of, _, rows, lanes) in enumerate(PARTS):
        pad = 24 if side_of > 16 else 16
        reach = 384 if side_of > 14 else 256
        place = places[number : number + 1, :]
        cell = lax.broadcasted_iota(jnp.int32, (pad * side_of, 1), 0)
        cell_row = (cell * 2731) >> 16 if pad == 24 else cell >> 4
        cell_col = pad - 1 - (cell - pad * cell_row)
        code = jnp.where(cell_col < side_of, cell_row * GRID + cell_col, -2)
        left = one_hot(code, place[:, :rows])
        right = one_hot(lax.broadcasted_iota(jnp.int32, (reach, 1), 0), place[:, :lanes])
        for pair in range(2):
            by_row = dot_nn(left, accs[number][pair]).astype(jnp.bfloat16)
            for side in range(2):
                both = dot_nt(by_row[:, side * lanes : (side + 1) * lanes], right)
                total = totals[2 * pair + side]
                for line in range(side_of):
                    far, near = divmod((GRID - 1 - line) * GRID, 128)
                    part = pad_lanes(both[pad * line : pad * line + pad], reach + 128)
                    if near:
                        part = pltpu.roll(part, near, 1)
                    for k in range(min(reach // 128 + 1, 5 - far)):
                        piece = part[:, 128 * k : 128 * k + 128]
                        top, low = total[far + k]
                        if pad == 24:
                            top = top + piece[:8]
                        total[far + k] = (top, low + piece[pad - 16 :])
    width = 768
    lane = lax.broadcasted_iota(jnp.int32, (24, width), 1)
    ahead = lane - GRID * ((lane * 3641) >> 16) + lax.broadcasted_iota(jnp.int32, (24, width), 0) >= 23
    level, below = [], []
    for head in range(HEADS):
        whole = jnp.concatenate([jnp.concatenate(t, axis=0) for t in totals[head]], axis=1)
        for keep, group in ((ahead, level), (jnp.logical_not(ahead), below)):
            turned = pltpu.roll(jnp.where(keep, whole, 0.0), 0, 1, stride=1, stride_axis=0)
            group.append(jnp.sum(turned, axis=0, keepdims=True))
    spot = lax.broadcasted_iota(jnp.int32, (width, 1), 0) - 23
    target = lax.broadcasted_iota(jnp.int32, (1, 384), 1)
    spot_row = jnp.where(spot >= 0, (spot * 3641) >> 16, -1)
    spot_col = spot - GRID * spot_row
    straight = one_hot(jnp.abs(spot_row - (GRID - 1)) * GRID + spot_col, target)
    back = one_hot(jnp.abs(spot_row + 1 - (GRID - 1)) * GRID + GRID - spot_col, target)
    out = jnp.zeros((HEADS, 384), jnp.float32)
    for group, fold in ((level, straight), (below, back)):
        high, low = split_low(jnp.concatenate(group, axis=0))
        spread = dot_nn(jnp.concatenate([high.astype(jnp.float32), low.astype(jnp.float32)], axis=0).astype(jnp.bfloat16), fold)
        out = out + spread[:HEADS] + spread[HEADS:]
    return out


def image_spec(width):
    return pl.BlockSpec((1, ROWS, width), lambda i, c: (i, 0, 0))


def whole_spec(shape):
    return pl.BlockSpec(shape, lambda i, c: (0,) * len(shape))


def attend_call(classes, mixed, biases):
    images = mixed.shape[0]
    return pl.pallas_call(
        attend_kernel,
        grid_spec=pltpu.PrefetchScalarGridSpec(
            num_scalar_prefetch=1,
            grid=(images,),
            in_specs=[image_spec(768)] + [whole_spec(b.shape) for b in biases],
            out_specs=[image_spec(512), image_spec(1536), image_spec(128)],
        ),
        out_shape=[
            jax.ShapeDtypeStruct((images, ROWS, 512), jnp.bfloat16),
            jax.ShapeDtypeStruct((images, ROWS, 1536), jnp.bfloat16),
            jax.ShapeDtypeStruct((images, ROWS, 128), jnp.float32),
        ],
        compiler_params=pltpu.CompilerParams(vmem_limit_bytes=60 * 2**20),
    )(classes, mixed, *biases)


def back_call(fs_size, classes, mixed, probs, shares, grad, attended, xs, lines, output):
    images, model = mixed.shape[0], xs.shape[2]
    bf, f32 = jnp.bfloat16, jnp.float32
    shapes = [(2, r, 2 * l) for _, _, r, l in PARTS]
    widths = [w // fs_size for w in (model, model, lines.shape[1], lines.shape[1], model, model)]
    return pl.pallas_call(
        functools.partial(back_kernel, fs_size),
        grid_spec=pltpu.PrefetchScalarGridSpec(
            num_scalar_prefetch=1,
            grid=(images,),
            in_specs=[image_spec(w) for w in (768, 1536, 128, 512, 512, model)] + [whole_spec(lines.shape), ANY],
            out_specs=[image_spec(768), whole_spec((model, 768)), whole_spec((8, 768))]
            + [whole_spec(s) for s in shapes]
            + [whole_spec((1, w)) for w in widths]
            + [ANY],
            scratch_shapes=[pltpu.VMEM(s, f32) for s in shapes]
            + [pltpu.VMEM(output.shape, bf), pltpu.SemaphoreType.DMA((2,))],
        ),
        out_shape=[
            jax.ShapeDtypeStruct((images, ROWS, 768), bf),
            jax.ShapeDtypeStruct((model, 768), f32),
            jax.ShapeDtypeStruct((8, 768), f32),
        ]
        + [jax.ShapeDtypeStruct(s, bf) for s in shapes]
        + [jax.ShapeDtypeStruct((1, w), f32) for w in widths]
        + [jax.ShapeDtypeStruct(output.shape, bf)],
        compiler_params=pltpu.CompilerParams(vmem_limit_bytes=60 * 2**20),
    )(classes, mixed, probs, shares, grad, attended, xs, lines, output)


def end_kernel(*refs):
    ins, outs = refs[:7], refs[7:15]
    held, kept, table_in, table, lines_in, own_lines = refs[15], refs[16:20], refs[20], refs[21], refs[22], refs[23:25]
    sem_in, sem_out = refs[25:27]
    step = held.shape[0] // 4
    pairs = [(ins[0].at[pl.ds(k * step, step)], held.at[pl.ds(k * step, step)], outs[0]) for k in range(4)]
    pairs = [(a, b, c.at[pl.ds(k * step, step)]) for k, (a, b, c) in enumerate(pairs)]
    pairs = [(ins[1], table_in, None), (ins[6], lines_in, None)] + pairs
    pairs += [(ins[2 + k], kept[k], outs[2 + k]) for k in range(4)]
    loads = [pltpu.make_async_copy(a, b, sem_in.at[k]) for k, (a, b, _) in enumerate(pairs)]
    stores = [pltpu.make_async_copy(b, c, sem_out.at[k]) for k, (_, b, c) in enumerate(pairs) if c is not None]
    for load in loads:
        load.start()
    loads[0].wait()
    loads[1].wait()
    table[...] = table_in[:, :NOFF]
    spot = lax.axis_index("fsdp")
    lines = lines_in[...]
    for k, ref in enumerate(own_lines):
        width = ref.shape[1]
        ref[...] = pltpu.roll(lines, lines.shape[1] - spot * width, 1)[k : k + 1, :width]
    for k, (a, b) in enumerate(((table, outs[1]), (own_lines[0], outs[6]), (own_lines[1], outs[7]))):
        stores.append(pltpu.make_async_copy(a, b, sem_out.at[len(pairs) + k]))
        stores[-1].start()
    for load, store in zip(loads[2:], stores):
        load.wait()
        store.start()
    for store in stores:
        store.wait()


def end_call(fs_size, input_grad, table, owned, lines):
    f32 = jnp.float32
    width = lines.shape[1] // fs_size
    shapes = [input_grad.shape, (HEADS, NOFF)] + [o.shape for o in owned] + [(1, width)] * 2
    held = [input_grad.shape] + [o.shape for o in owned] + [table.shape, (HEADS, NOFF), lines.shape] + [(1, width)] * 2
    return pl.pallas_call(
        end_kernel,
        out_shape=[jax.ShapeDtypeStruct(s, f32) for s in shapes],
        in_specs=[ANY] * 7,
        out_specs=[ANY] * 8,
        scratch_shapes=[pltpu.VMEM(s, f32) for s in held]
        + [pltpu.SemaphoreType.DMA((13,)), pltpu.SemaphoreType.DMA((13,))],
        compiler_params=pltpu.CompilerParams(vmem_limit_bytes=60 * 2**20),
    )(input_grad, table, *owned, lines)


MESH = pl.DeviceIdType.MESH
ANY = pl.BlockSpec(memory_space=pl.ANY)
SMEM = pl.BlockSpec(memory_space=pltpu.SMEM)


class Place:
    def __init__(self, dp_size, fs_size):
        self.dp_size, self.fs_size = dp_size, fs_size
        self.size = dp_size * fs_size
        self.dp, self.fs = lax.axis_index("dp"), lax.axis_index("fsdp")
        self.me = self.dp * fs_size + self.fs
        self.core = lax.rem(self.dp, 2)
        self.partner = (self.dp + 1 - 2 * self.core, self.fs)

    def other(self, step, cores=2):
        number = self.size // 2 * cores - step
        rows, lines = self.fs_size // 2, self.dp_size // 2
        core = lax.rem(self.core + lax.rem(number, cores), 2)
        number = number // cores
        line = lax.rem(self.dp // 2 + lax.rem(number // rows, lines), lines)
        row = lax.rem(self.fs // 2 + lax.rem(number, rows), rows)
        return (2 * line + core, 2 * row + lax.rem(self.fs + number // (rows * lines), 2))

    def all_others(self):
        rows, lines = self.fs_size // 2, self.dp_size // 2
        row_at = [2 * lax.rem(self.fs // 2 + d, rows) for d in range(rows)]
        line_at = [2 * lax.rem(self.dp // 2 + d, lines) for d in range(lines)]
        side_at = [lax.rem(self.fs, 2), 1 - lax.rem(self.fs, 2)]
        core_at = [self.core, 1 - self.core]
        steps = [(z, x, y, c) for z in range(rows) for x in range(2) for y in range(lines) for c in range(2)][1:]
        steps.sort(key=lambda s: -(20 * (s[0] > 0) + 10 * s[1] + 10 * (s[2] > 0) + s[3]))
        return [(line_at[y] + core_at[c], row_at[z] + side_at[x]) for z, x, y, c in steps]

    def greet(self):
        barrier = pltpu.get_barrier_semaphore()

        def signal(step, _):
            pl.semaphore_signal(barrier, inc=1, device_id=self.other(step), device_id_type=MESH)
            return 0

        lax.fori_loop(1, self.size, signal, 0)

    def meet(self):
        pl.semaphore_wait(pltpu.get_barrier_semaphore(), self.size - 1)

    def spread(self, buf, value, send, recv):
        buf[self.me] = value

        if self.size <= 64:
            for device in self.all_others():
                push(buf.at[self.me], buf.at[self.me], send, recv, device)
            return

        def start(step, _):
            push(buf.at[self.me], buf.at[self.me], send, recv, self.other(step))
            return 0

        lax.fori_loop(1, self.size, start, 0)

    def collect(self, buf, recv):
        await_bytes(buf.at[pl.ds(0, self.size - 1)], recv)
        return jnp.sum(buf[...], axis=0)

    def spread_pair(self, buf, value, send, recv):
        buf[self.core] = value
        part = buf.at[self.core]
        push(part, part, send, recv, self.partner)

    def collect_pair(self, buf, recv):
        await_bytes(buf.at[0], recv)
        return buf[0] + buf[1]

    def spread_chips(self, buf, value, send, recv):
        chips = self.size // 2
        mine = (self.dp // 2) * self.fs_size + self.fs
        buf[mine] = value

        def start(step, _):
            push(buf.at[mine], buf.at[mine], send, recv, self.other(step, 1))
            return 0

        lax.fori_loop(1, chips, start, 0)

    def collect_chips(self, buf, recv):
        await_bytes(buf.at[pl.ds(0, self.size // 2 - 1)], recv)
        return jnp.sum(buf[...], axis=0)

    def settle_pair(self, buf, send):
        await_bytes(buf.at[0], send)

    def settle_chips(self, buf, send):
        await_bytes(buf.at[pl.ds(0, self.size // 2 - 1)], send)

    def settle(self, buf, send):
        await_bytes(buf.at[pl.ds(0, self.size - 1)], send)


def push(source, target, send, recv, device):
    pltpu.make_async_remote_copy(
        src_ref=source, dst_ref=target, send_sem=send, recv_sem=recv, device_id=device, device_id_type=MESH
    ).start()


def await_bytes(ref, sem):
    pltpu.make_async_copy(ref, ref, sem).wait()


def gather_start(place, buf, send, recv):
    half = buf.shape[2] // 2
    part = buf.at[place.fs, :, pl.ds(pl.multiple_of(place.core * half, half), half)]

    def start(step, _):
        push(part, part, send, recv, (place.dp, lax.rem(place.fs + place.fs_size - step, place.fs_size)))
        return 0

    lax.fori_loop(1, place.fs_size, start, 0)


def gather_pass(place, buf, recv, send2, recv2):
    half = buf.shape[2] // 2
    await_bytes(buf.at[pl.ds(0, place.fs_size - 1), :, pl.ds(0, half)], recv)
    part = buf.at[:, :, pl.ds(pl.multiple_of(place.core * half, half), half)]
    push(part, part, send2, recv2, place.partner)


def gather_end(place, buf, recv2):
    half = buf.shape[2] // 2
    await_bytes(buf.at[:, :, pl.ds(0, half)], recv2)


def gather_settle(place, buf, send, send2):
    half = buf.shape[2] // 2
    await_bytes(buf.at[pl.ds(0, place.fs_size - 1), :, pl.ds(0, half)], send)
    await_bytes(buf.at[:, :, pl.ds(0, half)], send2)


def flat_weight(buf):
    shards, rows, width = buf.shape
    if rows % 16 == 0:
        return buf[...].reshape(shards * rows, width)
    wide = jnp.concatenate([buf[k].astype(jnp.float32) for k in range(shards)], axis=0)
    return wide.astype(jnp.bfloat16)


def split_low(value):
    high = value.astype(jnp.bfloat16)
    return high, (value - high.astype(jnp.float32)).astype(jnp.bfloat16)


def precise(left, right):
    high, low = split_low(left)
    return dot_nn(high, right) + dot_nn(low, right)


def arrange(columns):
    blocks = [columns[:, (2 * KEY + VALD) * h : (2 * KEY + VALD) * (h + 1)] for h in range(HEADS)]
    parts = [b[:, :KEY] for b in blocks] + [b[:, KEY : 2 * KEY] for b in blocks] + [b[:, 2 * KEY :] for b in blocks]
    return jnp.concatenate(parts, axis=1)


def restore(columns):
    parts = []
    for h in range(HEADS):
        parts += [
            columns[:, KEY * h : KEY * (h + 1)],
            columns[:, 128 + KEY * h : 128 + KEY * (h + 1)],
            columns[:, 256 + VALD * h : 256 + VALD * (h + 1)],
        ]
    return jnp.concatenate(parts, axis=1)


def by_columns(ref, value):
    for k in range(ref.shape[0]):
        ref[k] = value[:, 128 * k : 128 * k + 128]


def take_image(ref, image, images):
    return jnp.concatenate([ref[k, pl.ds(image, SLOT, stride=images), :] for k in range(ref.shape[0])], axis=1)


def put_image(ref, image, images, value):
    for k in range(ref.shape[0]):
        ref[k, pl.ds(image, SLOT, stride=images), :] = value[:SLOT, 128 * k : 128 * k + 128]


def limits_of(kind):
    return jnp.where(kind == 0, (GRID - 8) ** 2, jnp.where(kind == 1, (GRID - 4) ** 2, SLOT))


def assemble(buf, widths, lanes):
    turned = {}
    for width in sorted(set(widths)):
        turned[width] = sum(
            pltpu.roll(pad_lanes(buf[k], lanes), k * width, 1) if k else pad_lanes(buf[k], lanes)
            for k in range(buf.shape[0])
        )
    return [turned[width][k : k + 1] for k, width in enumerate(widths)]


class Reduce:
    def __init__(self, place, full, first, half, second, third, send, recv):
        self.place, self.full, self.first, self.half = place, full, first, half
        self.second, self.third, self.send, self.recv = second, third, send, recv
        self.width = half.shape[2]

    def swap(self):
        at = pl.multiple_of((1 - self.place.core) * self.width, self.width)
        push(self.full.at[:, :, pl.ds(at, self.width)], self.first, self.send.at[0], self.recv.at[0], self.place.partner)

    def scatter(self):
        place = self.place
        await_bytes(self.first, self.recv.at[0])

        at = pl.multiple_of(self.place.core * self.width, self.width)
        own = self.full[:, :, pl.ds(at, self.width)].astype(jnp.float32)
        self.half[...] = (own + self.first[...].astype(jnp.float32)).astype(jnp.bfloat16)
        self.second[place.fs] = self.half[place.fs]

        def start(step, _):
            target = lax.rem(place.fs + step, place.fs_size)
            push(self.half.at[target], self.second.at[place.fs], self.send.at[1], self.recv.at[1], (place.dp, target))
            return 0

        lax.fori_loop(1, place.fs_size, start, 0)

    def gathered(self):
        await_bytes(self.second.at[pl.ds(0, self.place.fs_size - 1)], self.recv.at[1])
        return jnp.sum(self.second[...].astype(jnp.float32), axis=0).astype(jnp.bfloat16)

    def share(self, total=None):
        place = self.place
        self.third[place.dp] = self.gathered() if total is None else total

        def start(step, _):
            target = lax.rem(place.dp + step, place.dp_size)
            push(self.third.at[place.dp], self.third.at[place.dp], self.send.at[2], self.recv.at[2], (target, place.fs))
            return 0

        lax.fori_loop(1, place.dp_size, start, 0)

    def result(self):
        place = self.place
        await_bytes(self.third.at[pl.ds(0, place.dp_size - 1)], self.recv.at[2])
        parts = []
        for core in range(2):
            parts.append(sum(self.third[k].astype(jnp.float32) for k in range(core, place.dp_size, 2)))
        return jnp.concatenate(parts, axis=1)

    def settle(self, steps=(0, 1, 2)):
        place = self.place
        if 0 in steps:
            await_bytes(self.first, self.send.at[0])
        if 1 in steps:
            await_bytes(self.second.at[pl.ds(0, place.fs_size - 1)], self.send.at[1])
        if 2 in steps:
            await_bytes(self.third.at[pl.ds(0, place.dp_size - 1)], self.send.at[2])


def staged(body, ins, outs, n_in):
    def kernel(*refs):
        refs, sem = list(refs[:-1]), refs[-1]
        count = len(ins) + len(outs)
        held, refs = refs[len(refs) - count :], refs[: len(refs) - count]
        loads, stores = {}, {}
        for k, at in enumerate(ins):
            loads[at] = pltpu.make_async_copy(refs[at], held[k], sem.at[k])
            refs[at] = held[k]
        for k, at in enumerate(outs, len(ins)):
            stores[at] = pltpu.make_async_copy(held[k], refs[n_in + at], sem.at[k])
            refs[n_in + at] = held[k]
        for load in loads.values():
            load.start()
        started = []

        def arrive(*places):
            for at in places:
                loads.pop(at).wait()

        def leave(*places):
            for at in places:
                stores[at].start()
                started.append(at)

        body(arrive, leave, *refs)
        leave(*[at for at in stores if at not in started])
        for store in stores.values():
            store.wait()

    return kernel


def stage_scratch(ins, outs, args, out_shape):
    held = [pltpu.VMEM(args[k].shape, args[k].dtype) for k in ins] + [
        pltpu.VMEM(out_shape[k].shape, out_shape[k].dtype) for k in outs
    ]
    return held + [pltpu.SemaphoreType.DMA((len(held),))]


def first_kernel(dp_size, fs_size, arrive, leave, *refs):
    class_ref, x_ref, off_ref, table_ref = refs[:4]
    shards, vectors = refs[4:8], refs[8:16]
    mixed_out, xs_out, bias_out, weight_out, vec_out, gram_out = refs[16], refs[17], refs[18:21], refs[21:25], refs[25], refs[26]
    place_out = refs[27]
    refs = refs[1:]
    xs, z, mixed, index, wide = refs[27:32]
    bias, weights = refs[32:35], refs[35:39]
    vbuf, stat, stat2 = refs[39:42]
    send, recv, send2, recv2, local = refs[42:47]
    place = Place(dp_size, fs_size)
    images = xs.shape[0]

    place.greet()
    arrive(*range(4, 16))
    for k in range(4):
        own = shards[k][...]
        if k == 0:
            own = arrange(own.astype(jnp.float32)).astype(jnp.bfloat16)
        half = own.shape[1] // 2
        own = jnp.where(place.core == 0, own[:, :half], own[:, half:])
        weights[k][place.fs, :, pl.ds(pl.multiple_of(place.core * half, half), half)] = own
    vbuf[place.fs] = jnp.concatenate(
        [pad_lanes(v[...].astype(jnp.float32), 128) for v in vectors], axis=0
    )
    arrive(1)
    by_columns(wide, x_ref[...].astype(jnp.float32))
    count = jnp.int32(0)
    for image in range(images):
        limit = limits_of(class_ref[image])
        row = lax.broadcasted_iota(jnp.int32, (SLOT, xs.shape[2]), 0)
        value = jnp.where(row < limit, take_image(wide, image, images), 0.0)
        xs[image] = pad_rows(value, ROWS).astype(jnp.bfloat16)
        count = count + limit

    flat = xs[...].reshape(images * ROWS, xs.shape[2])
    gram = dot_tn(flat, flat)
    total_x = dot_nn(jnp.ones((8, images * ROWS), jnp.bfloat16), flat)

    place.meet()
    gather_start(place, weights[0], send.at[0], recv.at[0])

    def start(step, _):
        target = lax.rem(place.fs + step, place.fs_size)
        push(vbuf.at[place.fs], vbuf.at[place.fs], send.at[4], recv.at[4], (place.dp, target))
        return 0

    lax.fori_loop(1, place.fs_size, start, 0)
    for k in range(1, 4):
        gather_start(place, weights[k], send.at[k], recv.at[k])
    xs_copy = pltpu.make_async_copy(xs, xs_out, local.at[0])
    xs_copy.start()
    arrive(2, 3)
    bias_tables(off_ref, table_ref, index, bias, place.core)
    place_out[...] = grid_places(off_ref)
    gram_out[...] = gram
    leave(10, 11)
    copies = [xs_copy]
    gather_pass(place, weights[0], recv.at[0], send2.at[0], recv2.at[0])
    gather_end(place, weights[0], recv2.at[0])
    weight = flat_weight(weights[0])
    high, low = split_low(gram)
    spread = dot_nn(high, weight) + dot_nn(low, weight)
    squares = jnp.sum(weight.astype(jnp.float32) * spread, axis=0, keepdims=True)
    sums = precise(total_x, weight)[:1]
    tail = jnp.full((1, 128), count.astype(jnp.float32))
    place.spread_pair(
        stat,
        jnp.concatenate(
            [jnp.concatenate([sums, tail], axis=1), jnp.concatenate([squares, tail], axis=1)], axis=0
        ),
        send.at[5],
        recv.at[5],
    )
    place.spread_chips(stat2, place.collect_pair(stat, recv.at[5]), send.at[6], recv.at[6])
    for k in range(3):
        part = bias[k].at[place.core]
        push(part, part, send.at[7 + k], recv.at[7 + k], place.partner)

    def product(image, _):
        z[image] = dot_nn(xs[image], weight)
        return 0

    lax.fori_loop(0, images, product, 0)
    for k in range(1, 4):
        gather_pass(place, weights[k], recv.at[k], send2.at[k], recv2.at[k])
    await_bytes(vbuf.at[pl.ds(0, place.fs_size - 1)], recv.at[4])
    widths = [v.shape[1] for v in vectors]
    full = assemble(vbuf, widths, 768)
    full[0], full[1] = arrange(full[0]), arrange(full[1])

    for k in range(3):
        await_bytes(bias[k].at[0], recv.at[7 + k])
        copies.append(pltpu.make_async_copy(bias[k], bias_out[k], local.at[1 + k]))
        copies[-1].start()
    got = place.collect_chips(stat2, recv.at[6])
    whole = got[0:1, 768:769]
    center = got[0:1, :768] / whole
    square = got[1:2, :768] / whole
    scale = lax.rsqrt(square - center * center + EPS)
    vec_out[...] = jnp.concatenate(
        full
        + [scale, center, jnp.broadcast_to(whole, (1, 768)), pad_lanes(total_x[:1], 768)]
        + [jnp.zeros((4, 768), jnp.float32)],
        axis=0,
    )
    leave(9)
    gain = scale * full[0]
    shift = full[1] - center * gain
    fold = jnp.where(lax.broadcasted_iota(jnp.int32, (1, 768), 1) < 128, KEY ** (-0.5) * LOG2E, 1.0)
    gain, shift = gain * fold, shift * fold

    def normal(image, _):
        mixed[image] = (z[image] * gain + shift).astype(jnp.bfloat16)
        pltpu.make_async_copy(mixed.at[image], mixed_out.at[image], local.at[8 + image]).start()
        return 0

    lax.fori_loop(0, images, normal, 0)
    for k in range(4):
        if k > 0:
            gather_end(place, weights[k], recv2.at[k])
        copies.append(pltpu.make_async_copy(weights[k], weight_out[k], local.at[4 + k]))
        copies[-1].start()
    for k in range(4):
        gather_settle(place, weights[k], send.at[k], send2.at[k])
    await_bytes(vbuf.at[pl.ds(0, place.fs_size - 1)], send.at[4])
    place.settle_pair(stat, send.at[5])
    place.settle_chips(stat2, send.at[6])
    for k in range(3):
        await_bytes(bias[k].at[0], send.at[7 + k])
    for copy in copies:
        copy.wait()

    def finish(image, _):
        pltpu.make_async_copy(mixed.at[image], mixed_out.at[image], local.at[8 + image]).wait()
        return 0

    lax.fori_loop(0, images, finish, 0)


def first_call(dp_size, fs_size, classes, inputs, offset_table, bias_table, weights, vectors):
    images, model = classes.shape[0], inputs.shape[1]
    vectors = [v.reshape(1, -1) for v in vectors]
    shapes = [(fs_size,) + w.shape for w in weights]
    biases = [(2, r, 2 * l) for _, _, r, l in PARTS]
    bf, f32 = jnp.bfloat16, jnp.float32
    out_shape = (
        [
            jax.ShapeDtypeStruct((images, ROWS, 768), bf),
            jax.ShapeDtypeStruct((images, ROWS, model), bf),
        ]
        + [jax.ShapeDtypeStruct(s, f32) for s in biases]
        + [jax.ShapeDtypeStruct(s, bf) for s in shapes]
        + [jax.ShapeDtypeStruct((16, 768), f32), jax.ShapeDtypeStruct((model, model), f32)]
        + [jax.ShapeDtypeStruct((8, 384), jnp.int32)]
    )
    args = (classes, inputs, offset_table, bias_table, *weights, *vectors)
    ins, outs = (*range(4, 16), 1, 2, 3), (9, 10, 11)
    return pl.pallas_call(
        staged(functools.partial(first_kernel, dp_size, fs_size), ins, outs, len(args)),
        out_shape=out_shape,
        in_specs=[SMEM] + [ANY] * 15,
        out_specs=[ANY] * 12,
        scratch_shapes=[
            pltpu.VMEM((images, ROWS, model), bf),
            pltpu.VMEM((images, ROWS, 768), f32),
            pltpu.VMEM((images, ROWS, 768), bf),
            pltpu.VMEM((ROWS, 384), jnp.int32),
            pltpu.VMEM((model // 128, inputs.shape[0], 128), f32),
        ]
        + [pltpu.VMEM(s, f32) for s in biases]
        + [pltpu.VMEM(s, bf) for s in shapes]
        + [
            pltpu.VMEM((fs_size, 8, 128), f32),
            pltpu.VMEM((2, 2, 896), f32),
            pltpu.VMEM((dp_size * fs_size // 2, 2, 896), f32),
            pltpu.SemaphoreType.DMA((10,)),
            pltpu.SemaphoreType.DMA((10,)),
            pltpu.SemaphoreType.DMA((4,)),
            pltpu.SemaphoreType.DMA((4,)),
            pltpu.SemaphoreType.DMA((8 + images,)),
        ]
        + stage_scratch(ins, outs, args, out_shape),
        compiler_params=pltpu.CompilerParams(
            collective_id=0, has_side_effects=True, vmem_limit_bytes=56 * 2**20
        ),
    )(*args)


def total_rows(value):
    return jnp.sum(value, axis=0, keepdims=True)


def sigma_of(value):
    return 0.5 * jnp.tanh(0.5 * value) + 0.5


def slope_of(value):
    sigma = sigma_of(value)
    return sigma * (1.0 + value * (1.0 - sigma))


def norm_parts(sums, squares, total, gain, shift):
    center = sums / total
    scale = lax.rsqrt(squares / total - center * center + EPS)
    return center, scale, scale * gain, shift - center * scale * gain


def back_parts(grad_sum, grad_z, total, gain, center, scale):
    gain_grad = scale * (grad_z - center * grad_sum)
    alpha = scale * gain
    slant = alpha * scale * gain_grad / total
    level = alpha * (grad_sum - center * scale * gain_grad) / total
    return gain_grad, alpha, slant, level


def outer(column, row):
    left = jnp.concatenate([column, jnp.zeros((7, column.shape[1]), jnp.float32)], axis=0)
    right = jnp.concatenate([row, jnp.zeros((7, row.shape[1]), jnp.float32)], axis=0)
    left_high, left_low = split_low(left)
    right_high, right_low = split_low(right)
    return dot_tn(left_high, right_high) + dot_tn(left_high, right_low) + dot_tn(left_low, right_high)


def middle_kernel(dp_size, fs_size, group, arrive, leave, *refs):
    class_ref, att_in, xs_in, cot_in = refs[:4]
    weight_in, vec_ref, gram_ref = refs[4:7], refs[7], refs[8]
    out_out, gatt_out, gm_out, grad_out, vec_out, own_gram = refs[9], refs[10], refs[11], refs[12:15], refs[15], refs[16]
    refs = refs[2:]
    att, xs, cot, wo_buf, wu_buf, wd_buf = refs[15:21]
    gs, act, slope_att, zo, low, zu, hid, slope_up, zd, dzd, gu, gm, out, gatt, wide = refs[21:36]
    stat_o, stat_u, stat_d, stat_bu, stat_bo = refs[36:41]
    send, recv, local = refs[41:44]
    gram_steps, send_r, recv_r = refs[44:49], refs[49], refs[50]
    down_steps, send_w, recv_w = refs[51:55], refs[55], refs[56]
    up_steps, send_v, recv_v = refs[57:61], refs[61], refs[62]
    place = Place(dp_size, fs_size)
    images = att.shape[0]
    chunks = images // group
    size = group * ROWS
    f32, bf = jnp.float32, jnp.bfloat16
    gram_sum = Reduce(place, *gram_steps, send_r, recv_r)
    down_sum = Reduce(place, *down_steps, None, send_w, recv_w)
    up_sum = Reduce(place, *up_steps, None, send_v, recv_v)

    def copy(source, target, at):
        return pltpu.make_async_copy(source, target, local.at[at])

    loads = [
        copy(weight_in[0], wo_buf, 0),
        copy(xs_in, xs, 1),
        copy(cot_in, cot, 2),
        copy(weight_in[1], wu_buf, 3),
        copy(weight_in[2], wd_buf, 4),
    ]
    loads[0].start()

    def att_copy(k):
        part = pl.ds(k * group, group)
        return copy(att_in.at[part], att.at[part], 8 + k)

    for k in range(chunks):
        att_copy(k).start()
    for load in loads[1:]:
        load.start()
    place.greet()
    arrive(7)

    def get(ref, k):
        return ref[pl.ds(k * group, group)].reshape(size, ref.shape[2])

    def put(ref, k, value):
        ref[pl.ds(k * group, group)] = value.astype(ref.dtype).reshape(group, ROWS, ref.shape[2])

    def kept(k, width):
        row = lax.broadcasted_iota(jnp.int32, (ROWS, width), 0)
        return jnp.concatenate([row < limits_of(class_ref[k * group + j]) for j in range(group)], axis=0)

    def over(body, carry):
        return lax.fori_loop(0, chunks, body, carry, unroll=True)

    def zero(width):
        return jnp.zeros((1, width), f32)

    model = xs.shape[2]
    hidden = zu.shape[2]
    total = vec_ref[10:11, :1]
    out_gain, out_shift = vec_ref[2:3, :model], vec_ref[3:4, :model]
    up_gain, up_shift = vec_ref[4:5, :hidden], vec_ref[5:6, :hidden]
    down_gain, down_shift = vec_ref[6:7, :model], vec_ref[7:8, :model]

    loads[0].wait()
    wo = flat_weight(wo_buf)

    def step_out(k, carry):
        att_copy(k).wait()
        value = get(att, k).astype(f32)
        active = (value * sigma_of(value)).astype(bf)
        put(act, k, active)
        z = dot_nn(active, wo)
        put(zo, k, z)
        return carry[0] + total_rows(z), carry[1] + total_rows(z * z)

    sums = over(step_out, (zero(model), zero(model)))
    place.meet()
    x_sum = vec_ref[11:12, :model]
    place.spread(stat_o, jnp.concatenate(sums + (x_sum,), axis=0), send.at[0], recv.at[0])
    for load in loads[1:]:
        load.wait()

    def fill_out(k, _):
        put(slope_att, k, slope_of(get(att, k).astype(f32)))
        return 0

    over(fill_out, 0)
    by_columns(wide, cot[...].astype(f32))
    grad_sum = zero(model)
    for image in range(images):
        row = lax.broadcasted_iota(jnp.int32, (SLOT, model), 0)
        value = jnp.where(row < limits_of(class_ref[image]), take_image(wide, image, images), 0.0)
        gs[image] = pad_rows(value, ROWS).astype(bf)
        grad_sum = grad_sum + total_rows(value)
    wu, wd = flat_weight(wu_buf), flat_weight(wd_buf)
    got = place.collect(stat_o, recv.at[0])
    center_o, scale_o, a_o, b_o = norm_parts(got[0:1], got[1:2], total, out_gain, out_shift)
    x_mean = got[2:3] / total

    def middle_of(k):
        return get(xs, k).astype(f32) + get(zo, k) * a_o + b_o

    def step_up(k, carry):
        lower = jnp.where(kept(k, model), middle_of(k), 0.0).astype(bf)
        put(low, k, lower)
        z = dot_nn(lower, wu)
        put(zu, k, z)
        return carry[0] + total_rows(z), carry[1] + total_rows(z * z)

    sums = over(step_up, (zero(hidden), zero(hidden)))
    place.spread(stat_u, jnp.concatenate(sums, axis=0), send.at[1], recv.at[1])
    low_flat = low[...].reshape(images * ROWS, model)
    low_gram = dot_tn(low_flat, low_flat)
    low_sum = dot_nn(jnp.ones((8, images * ROWS), bf), low_flat)[:1]
    count = sum(limits_of(class_ref[k]) for k in range(images)).astype(f32)
    moved = x_sum - 0.5 * count * x_mean
    arrive(8)
    gram = gram_ref[...] - outer(x_mean, moved) - outer(moved, x_mean)
    gram_steps[0][...] = gram.reshape(gram_steps[0].shape).astype(bf)
    gram_sum.swap()

    def fill_up(k, carry):
        centered = jnp.where(kept(k, model), get(zo, k) - center_o, 0.0).astype(bf)
        return carry + dot_tn(get(act, k), centered)

    act_z = over(fill_up, jnp.zeros((act.shape[2], model), f32))
    got = place.collect(stat_u, recv.at[1])
    center_u, scale_u, a_u, b_u = norm_parts(got[0:1], got[1:2], total, up_gain, up_shift)

    def step_down(k, carry):
        value = get(zu, k) * a_u + b_u
        active = jnp.where(kept(k, hidden), value * sigma_of(value), 0.0).astype(bf)
        put(hid, k, active)
        z = dot_nn(active, wd)
        put(zd, k, z)
        return (
            carry[0] + total_rows(z),
            carry[1] + total_rows(z * z),
            carry[2] + total_rows(z * get(gs, k).astype(f32)),
        )

    sums = over(step_down, (zero(model), zero(model), zero(model)))
    place.spread(stat_d, jnp.concatenate(sums + (grad_sum,), axis=0), send.at[2], recv.at[2])

    def fill_down(k, _):
        put(slope_up, k, slope_of(get(zu, k) * a_u + b_u))
        return 0

    over(fill_down, 0)
    gram_sum.scatter()
    got = place.collect(stat_d, recv.at[2])
    center_d, scale_d, a_d, b_d = norm_parts(got[0:1], got[1:2], total, down_gain, down_shift)
    down_shift_grad = got[3:4]
    down_gain_grad, alpha, slant, level = back_parts(got[3:4], got[2:3], total, down_gain, center_d, scale_d)

    def step_back_down(k, carry):
        dz = get(gs, k).astype(f32) * alpha - get(zd, k) * slant - jnp.where(kept(k, model), level, 0.0)
        dz = dz.astype(bf)
        put(dzd, k, dz)
        grad = dot_nt(dz, wd) * get(slope_up, k).astype(f32)
        put(gu, k, grad)
        return carry[0] + total_rows(grad), carry[1] + total_rows(grad * get(zu, k))

    sums = over(step_back_down, (zero(hidden), zero(hidden)))
    place.spread(stat_bu, jnp.concatenate(sums, axis=0), send.at[3], recv.at[3])

    down_grad = dot_tn(hid[...].reshape(images * ROWS, hidden), dzd[...].reshape(images * ROWS, model))
    down_steps[0][...] = down_grad.reshape(down_steps[0].shape).astype(bf)
    down_sum.swap()

    def fill_back_down(k, carry):
        grad = get(gu, k)
        carry = carry + dot_tn(get(low, k), grad.astype(bf))
        put(gm, k, get(gs, k).astype(f32) + dot_nt((grad * a_u).astype(bf), wu))
        return carry

    up_raw = over(fill_back_down, jnp.zeros((model, hidden), f32))
    down_sum.scatter()
    gram_sum.share()
    got = place.collect(stat_bu, recv.at[3])
    up_shift_grad = got[0:1]
    up_gain_grad, alpha_u, slant_u, level_u = back_parts(got[0:1], got[1:2], total, up_gain, center_u, scale_u)
    mix = dot_nt((wu.astype(f32) * slant_u).astype(bf), wu).astype(bf)
    high, rest = split_low(jnp.broadcast_to(level_u, (8, hidden)))
    lift = (dot_nt(high, wu) + dot_nt(rest, wu))[:1]

    def step_back_up(k, carry):
        grad = get(gm, k) - dot_nn(get(low, k), mix) - jnp.where(kept(k, model), lift, 0.0)
        put(gm, k, grad)
        part = pl.ds(k * group, group)
        copy(gm.at[part], gm_out.at[part], 8 + chunks + k).start()
        return carry[0] + total_rows(grad), carry[1] + total_rows(grad * get(zo, k))

    sums = over(step_back_up, (zero(model), zero(model)))
    place.spread(stat_bo, jnp.concatenate(sums, axis=0), send.at[4], recv.at[4])
    up_grad = up_raw * alpha_u - precise(low_gram, wu) * slant_u - outer(low_sum, level_u)
    up_steps[0][...] = up_grad.reshape(up_steps[0].shape).astype(bf)
    up_sum.swap()
    out_mean = down_shift_grad / total

    def fill_back_up(k, carry):
        centered = jnp.where(kept(k, model), get(gm, k) - out_mean, 0.0).astype(bf)
        return carry + dot_tn(get(act, k), centered)

    act_g = over(fill_back_up, jnp.zeros((act.shape[2], model), f32))
    up_sum.scatter()
    for image in range(images):
        row = lax.broadcasted_iota(jnp.int32, (ROWS, model), 0)
        value = xs[image].astype(f32) + zo[image] * a_o + zd[image] * a_d + (b_o + b_d)
        value = jnp.where(row < limits_of(class_ref[image]), value, 0.0)
        put_image(wide, image, images, value)
    for k in range(wide.shape[0]):
        out[:, 128 * k : 128 * k + 128] = wide[k].astype(bf)
    out_copy = copy(out, out_out, 5)
    out_copy.start()
    own_gram[...] = gram_sum.result()
    leave(7)
    got = place.collect(stat_bo, recv.at[4])
    out_shift_grad = got[0:1]
    out_gain_grad, alpha_o, slant_o, level_o = back_parts(got[0:1], got[1:2], total, out_gain, center_o, scale_o)

    out_grad = act_g * alpha_o - act_z * slant_o
    grad_out[0][...] = out_grad.reshape(grad_out[0].shape).astype(bf)
    leave(3)
    vec_out[...] = jnp.concatenate(
        [
            pad_lanes(v, hidden)
            for v in (
                out_gain_grad,
                out_shift_grad,
                up_gain_grad,
                up_shift_grad,
                down_gain_grad,
                down_shift_grad,
                x_mean,
                zero(hidden),
            )
        ],
        axis=0,
    )
    leave(6)

    def step_back_out(k, _):
        dz = get(gm, k) * alpha_o - get(zo, k) * slant_o - jnp.where(kept(k, model), level_o, 0.0)
        dz = dz.astype(bf)
        put(gatt, k, dot_nt(dz, wo) * get(slope_att, k).astype(f32))
        part = pl.ds(k * group, group)
        copy(gatt.at[part], gatt_out.at[part], 8 + 2 * chunks + k).start()
        return 0

    over(step_back_out, 0)
    grad_out[2][...] = down_sum.gathered()
    leave(5)
    down_sum.settle((0, 1))
    grad_out[1][...] = up_sum.gathered()
    leave(4)
    up_sum.settle((0, 1))

    for k, stat in enumerate((stat_o, stat_u, stat_d, stat_bu, stat_bo)):
        place.settle(stat, send.at[k])
    gram_sum.settle()

    def finish(k, _):
        part = pl.ds(k * group, group)
        copy(gm.at[part], gm_out.at[part], 8 + chunks + k).wait()
        copy(gatt.at[part], gatt_out.at[part], 8 + 2 * chunks + k).wait()
        return 0

    over(finish, 0)
    out_copy.wait()


def half_steps(shape):
    halved = pltpu.VMEM(shape[:2] + (shape[2] // 2,), jnp.bfloat16)
    return [pltpu.VMEM(shape, jnp.bfloat16)] + [halved] * 3 + [pltpu.SemaphoreType.DMA((2,))] * 2


def middle_call(dp_size, fs_size, classes, attended, xs, cotangent, weights, vec, gram):
    images, model, feature, hidden = xs.shape[0], xs.shape[2], attended.shape[2], weights[1].shape[2]
    group = 2 if images % 2 == 0 else 1
    chunks = images // group
    devices = dp_size * fs_size
    own = model // fs_size
    bf, f32 = jnp.bfloat16, jnp.float32

    def rows(width, kind):
        return pltpu.VMEM((images, ROWS, width), kind)

    out_shape = (
        [
            jax.ShapeDtypeStruct(cotangent.shape, bf),
            jax.ShapeDtypeStruct((images, ROWS, feature), bf),
            jax.ShapeDtypeStruct((images, ROWS, model), f32),
        ]
        + [jax.ShapeDtypeStruct(weights[0].shape, bf)]
        + [jax.ShapeDtypeStruct((w.shape[1], w.shape[2] // 2), bf) for w in weights[1:]]
        + [jax.ShapeDtypeStruct((8, hidden), f32), jax.ShapeDtypeStruct((own, model), f32)]
    )
    args = (classes, attended, xs, cotangent, *weights, vec, gram)
    ins, outs = (7, 8), (3, 4, 5, 6, 7)
    return pl.pallas_call(
        staged(functools.partial(middle_kernel, dp_size, fs_size, group), ins, outs, len(args)),
        out_shape=out_shape,
        in_specs=[SMEM] + [ANY] * 8,
        out_specs=[ANY] * 8,
        scratch_shapes=[
            rows(feature, bf),
            rows(model, bf),
            pltpu.VMEM(cotangent.shape, bf),
        ]
        + [pltpu.VMEM(w.shape, bf) for w in weights]
        + [
            rows(model, bf),
            rows(feature, bf),
            rows(feature, bf),
            rows(model, f32),
            rows(model, bf),
            rows(hidden, f32),
            rows(hidden, bf),
            rows(hidden, bf),
            rows(model, f32),
            rows(model, bf),
            rows(hidden, f32),
            rows(model, f32),
            pltpu.VMEM(cotangent.shape, bf),
            rows(feature, bf),
            pltpu.VMEM((model // 128, cotangent.shape[0], 128), f32),
            pltpu.VMEM((devices, 3, model), f32),
            pltpu.VMEM((devices, 2, hidden), f32),
            pltpu.VMEM((devices, 4, model), f32),
            pltpu.VMEM((devices, 2, hidden), f32),
            pltpu.VMEM((devices, 2, model), f32),
            pltpu.SemaphoreType.DMA((5,)),
            pltpu.SemaphoreType.DMA((5,)),
            pltpu.SemaphoreType.DMA((8 + 3 * chunks,)),
            pltpu.VMEM((fs_size, own, model), bf),
        ]
        + [pltpu.VMEM((fs_size, own, model // 2), bf)] * 3
        + [
            pltpu.VMEM((dp_size, own, model // 2), bf),
            pltpu.SemaphoreType.DMA((3,)),
            pltpu.SemaphoreType.DMA((3,)),
        ]
        + half_steps(weights[2].shape)
        + half_steps(weights[1].shape)
        + stage_scratch(ins, outs, args, out_shape),
        compiler_params=pltpu.CompilerParams(
            collective_id=1, has_side_effects=True, vmem_limit_bytes=58 * 2**20
        ),
    )(*args)


def last_kernel(dp_size, fs_size, group, arrive, leave, *refs):
    class_ref, xs_in, gmix_in, gm_in, places = refs[:5]
    acc_in, grad_in, part_in = refs[5:8], refs[8:9], refs[9:11]
    wq_buf, raw_ref, sum_ref, gram_ref, vec_ref, lines_ref = refs[11:17]
    ig_out, table_out, own_out, vec_out = refs[17], refs[18], refs[19:23], refs[23]
    refs = refs[:27] + (None,) + refs[27:]
    xs, gmix, gm, _, ig, res = refs[24:30]
    acc, full = refs[30:33], refs[33:35]
    steps = [refs[35 + 4 * k : 39 + 4 * k] for k in range(2)]
    thirds = refs[43:45]
    stat, stat_t, stat_c, stat_tc = refs[45:49]
    send, recv, local, send_r, recv_r = refs[49:54]
    place = Place(dp_size, fs_size)
    images = xs.shape[0]
    chunks = images // group
    size = group * ROWS
    f32, bf = jnp.float32, jnp.bfloat16
    model, width = xs.shape[2], gmix.shape[2]

    def copy(source, target, at):
        return pltpu.make_async_copy(source, target, local.at[at])

    grad_loads = [copy(grad_in[k], full[1 + k], k) for k in range(1)]
    mix_load = copy(gmix_in, gmix, 3)
    table_loads = [copy(acc_in[k], acc[k], 5 + k) for k in range(3)]
    late_loads = [copy(xs_in, xs, 8), copy(gm_in, gm, 9)]
    place.greet()
    for load in grad_loads + [mix_load] + table_loads + late_loads:
        load.start()
    reduces = [Reduce(place, full[k], *steps[k], send_r.at[k], recv_r.at[k]) for k in range(2)]
    shared = [
        Reduce(place, None, None, thirds[k], None, thirds[k], send_r.at[2 + k], recv_r.at[2 + k]) for k in range(2)
    ]

    def get(ref, k):
        return ref[pl.ds(k * group, group)].reshape(size, ref.shape[2])

    def put(ref, k, value):
        ref[pl.ds(k * group, group)] = value.astype(ref.dtype).reshape(group, ROWS, ref.shape[2])

    def kept(k, lanes):
        row = lax.broadcasted_iota(jnp.int32, (ROWS, lanes), 0)
        return jnp.concatenate([row < limits_of(class_ref[k * group + j]) for j in range(group)], axis=0)

    arrive(11, 12, 13, 15, 16)
    total = vec_ref[10:11, :1]
    gain, scale, center = vec_ref[0:1, :], vec_ref[8:9, :], vec_ref[9:10, :]
    x_mean = lines_ref[6:7, :model]
    weight = flat_weight(wq_buf)
    weight_f = weight.astype(f32)
    raw = raw_ref[...]
    grad_sum = total_rows(sum_ref[...])
    grad_z = total_rows(raw * weight_f)
    full[0][...] = (raw - outer(x_mean, grad_sum)).reshape(full[0].shape).astype(bf)
    for load in grad_loads:
        load.wait()
    place.meet()
    reduces[0].swap()
    place.spread_pair(stat, jnp.concatenate([grad_sum, grad_z], axis=0), send.at[0], recv.at[0])
    reduces[1].swap()
    alpha = scale * gain
    place.spread_chips(stat_c, place.collect_pair(stat, recv.at[0]), send.at[2], recv.at[2])
    for k in range(2):
        reduces[k].scatter()
    arrive(9, 10)
    for k in range(2):
        shared[k].share(part_in[k][...])
    for load in table_loads:
        load.wait()
    arrive(4, 14)
    place.spread_pair(stat_t, table_sums(places[...], acc), send.at[1], recv.at[1])
    mix_load.wait()
    for k in range(chunks):
        put(ig, k, dot_nt((get(gmix, k).astype(f32) * alpha).astype(bf), weight))
    place.spread_chips(stat_tc, place.collect_pair(stat_t, recv.at[1]), send.at[3], recv.at[3])
    for load in late_loads:
        load.wait()

    got = place.collect_chips(stat_c, recv.at[2])
    gain_grad, alpha, slant, level = back_parts(got[0:1], got[1:2], total, gain, center, scale)
    mix = dot_nt((weight_f * slant).astype(bf), weight).astype(bf)
    high, rest = split_low(jnp.broadcast_to(level, (8, width)))
    lift = (dot_nt(high, weight) + dot_nt(rest, weight))[:1]
    vec_out[...] = jnp.concatenate(
        [restore(gain_grad), restore(got[0:1]), jnp.zeros((6, width), f32)], axis=0
    )
    leave(6)
    for k in range(2):
        reduces[k].share()
    for k in range(chunks):
        value = get(gm, k) + get(ig, k) - dot_nn(get(xs, k), mix) - jnp.where(kept(k, model), lift, 0.0)
        for j in range(group):
            put_image(res, k * group + j, images, value[j * ROWS : (j + 1) * ROWS])
    res_copies = [copy(res.at[k], ig_out.at[:, pl.ds(128 * k, 128)], 10 + k) for k in range(model // 128)]
    for res_copy in res_copies:
        res_copy.start()
    own_out[0][...] = restore(reduces[0].result() * alpha - precise(gram_ref[...], weight) * slant)
    own_out[1][...] = reduces[1].result()
    for k in range(2):
        own_out[2 + k][...] = shared[k].result()
    table_out[...] = place.collect_chips(stat_tc, recv.at[3])
    for k in range(2):
        reduces[k].settle()
        shared[k].settle((2,))
    place.settle_pair(stat, send.at[0])
    place.settle_pair(stat_t, send.at[1])
    place.settle_chips(stat_c, send.at[2])
    place.settle_chips(stat_tc, send.at[3])
    for res_copy in res_copies:
        res_copy.wait()


def last_call(dp_size, fs_size, classes, xs, gmix, gm, places, accs, grads, wq, raw, sums, gram, vec, lines):
    images, model, width = xs.shape[0], xs.shape[2], gmix.shape[2]
    group = 2 if images % 2 == 0 else 1
    devices = dp_size * fs_size
    bf, f32 = jnp.bfloat16, jnp.float32
    shapes = [wq.shape, grads[0].shape]
    own_shapes = [s[1:] for s in shapes] + [(g.shape[0], 2 * g.shape[1]) for g in grads[1:]]
    steps = []
    for s in shapes:
        half = s[2] // 2
        steps += [
            pltpu.VMEM((fs_size, s[1], half), bf),
            pltpu.VMEM((fs_size, s[1], half), bf),
            pltpu.VMEM((fs_size, s[1], half), bf),
            pltpu.VMEM((dp_size, s[1], half), bf),
        ]
    order = []
    for k in range(2):
        order += [steps[4 * k], steps[4 * k + 1], steps[4 * k + 2], steps[4 * k + 3]]
    out_shape = (
        [jax.ShapeDtypeStruct((SLOT * images, model), f32), jax.ShapeDtypeStruct((HEADS, 384), f32)]
        + [jax.ShapeDtypeStruct(s, f32) for s in own_shapes]
        + [jax.ShapeDtypeStruct((8, width), f32)]
    )
    args = (classes, xs, gmix, gm, places, *accs, *grads, wq, raw, sums, gram, vec, lines)
    ins, outs = (13, 15, 16, 11, 12, 9, 10, 4, 14), (1, 2, 3, 4, 5, 6)
    return pl.pallas_call(
        staged(functools.partial(last_kernel, dp_size, fs_size, group), ins, outs, len(args)),
        out_shape=out_shape,
        in_specs=[SMEM] + [ANY] * 16,
        out_specs=[ANY] * 7,
        scratch_shapes=[
            pltpu.VMEM(xs.shape, bf),
            pltpu.VMEM(gmix.shape, bf),
            pltpu.VMEM(gm.shape, f32),
            pltpu.VMEM(gm.shape, f32),
            pltpu.VMEM((model // 128, SLOT * images, 128), f32),
        ]
        + [pltpu.VMEM(a.shape, bf) for a in accs]
        + [pltpu.VMEM(s, bf) for s in shapes]
        + order
        + [
            pltpu.VMEM((dp_size,) + grads[1].shape, bf),
            pltpu.VMEM((dp_size,) + grads[2].shape, bf),
            pltpu.VMEM((2, 2, width), f32),
            pltpu.VMEM((2, HEADS, 384), f32),
            pltpu.VMEM((devices // 2, 2, width), f32),
            pltpu.VMEM((devices // 2, HEADS, 384), f32),
            pltpu.SemaphoreType.DMA((4,)),
            pltpu.SemaphoreType.DMA((4,)),
            pltpu.SemaphoreType.DMA((10 + model // 128,)),
            pltpu.SemaphoreType.DMA((4, 3)),
            pltpu.SemaphoreType.DMA((4, 3)),
        ]
        + stage_scratch(ins, outs, args, out_shape),
        compiler_params=pltpu.CompilerParams(
            collective_id=2, has_side_effects=True, vmem_limit_bytes=56 * 2**20
        ),
    )(*args)

def shards(
    inputs,
    classes,
    offset_table,
    bias_table,
    qkv_weight,
    qkv_gain,
    qkv_shift,
    out_weight,
    out_gain,
    out_shift,
    up_weight,
    up_gain,
    up_shift,
    down_weight,
    down_gain,
    down_shift,
    cotangent,
):
    sizes = lax.axis_size("dp"), lax.axis_size("fsdp")
    images, _, model = inputs.shape

    def by_slot(array):
        return jnp.swapaxes(array, 0, 1).reshape(SLOT * images, model)

    def by_image(array):
        return jnp.swapaxes(array.reshape(SLOT, images, model), 0, 1)

    first = first_call(
        *sizes,
        classes,
        by_slot(inputs),
        offset_table,
        bias_table,
        (qkv_weight, out_weight, up_weight, down_weight),
        (qkv_gain, qkv_shift, out_gain, out_shift, up_gain, up_shift, down_gain, down_shift),
    )
    mixed, xs, biases, weights, vec, gram, places = first[0], first[1], first[2:5], first[5:9], *first[9:12]
    attended, probs, shares = attend_call(classes, mixed, biases)
    middle = middle_call(*sizes, classes, attended, xs, by_slot(cotangent), weights[1:], vec, gram)
    output, grad_att, grad_middle, grads, lines, own_gram = *middle[:3], middle[3:6], middle[6], middle[7]
    back = back_call(sizes[1], classes, mixed, probs, shares, grad_att, attended, xs, lines, output)
    grad_mixed, raw, sums, accs, own_lines, output = *back[:3], back[3:6], back[6:12], back[12]
    last = last_call(
        *sizes,
        classes,
        xs,
        grad_mixed,
        grad_middle,
        places,
        accs,
        grads,
        weights[0],
        raw,
        sums,
        own_gram,
        vec,
        lines,
    )
    input_grad, table_grad, *rest = end_call(sizes[1], last[0], last[1], last[2:6], last[6])
    own_lines = [line.reshape(-1) for line in (*own_lines, *rest[4:])]
    return (
        by_image(output),
        by_image(input_grad),
        table_grad,
        rest[0],
        *own_lines[6:8],
        rest[1],
        *own_lines[0:2],
        rest[2],
        *own_lines[2:4],
        rest[3],
        *own_lines[4:6],
    )


def solution(mesh):
    placed = (
        P(("dp", "fsdp"), None, None),
        P(("dp", "fsdp")),
        P(),
        P(),
        P("fsdp", None),
        P("fsdp"),
        P("fsdp"),
        P("fsdp", None),
        P("fsdp"),
        P("fsdp"),
        P("fsdp", None),
        P("fsdp"),
        P("fsdp"),
        P("fsdp", None),
        P("fsdp"),
        P("fsdp"),
        P(("dp", "fsdp"), None, None),
    )
    return jax.shard_map(
        shards,
        mesh=mesh,
        in_specs=placed,
        out_specs=(
            P(("dp", "fsdp"), None, None),
            P(("dp", "fsdp"), None, None),
            P(),
            P("fsdp", None),
            P("fsdp"),
            P("fsdp"),
            P("fsdp", None),
            P("fsdp"),
            P("fsdp"),
            P("fsdp", None),
            P("fsdp"),
            P("fsdp"),
            P("fsdp", None),
            P("fsdp"),
            P("fsdp"),
        ),
        check_vma=False,
    )
```

```python
import functools

import jax
import jax.numpy as jnp
from jax import lax
from jax.experimental import pallas as pl
from jax.experimental.pallas import tpu as pltpu
from jax.sharding import PartitionSpec as P

HEADS = 4
KEY = 32
VALD = 128
GRID = 18
CLASSES = 3
SLOT = 324
NOFF = 324


EPS = 1e-05
LOG2E = 1.4426950408889634
LN2 = 0.6931471805599453
ROWS = 336
PARTS = ((10, 100, 112, 128), (14, 196, 208, 256), (18, 324, 336, 384))
VMEM = pl.BlockSpec(memory_space=pltpu.VMEM)


def dot_nn(left, right):
    return jnp.dot(left, right, preferred_element_type=jnp.float32)


def dot_nt(left, right):
    return lax.dot_general(left, right, (((1,), (1,)), ((), ())), preferred_element_type=jnp.float32)


def dot_tn(left, right):
    return lax.dot_general(left, right, (((0,), (0,)), ((), ())), preferred_element_type=jnp.float32)


def pad_rows(value, rows):
    if value.shape[0] == rows:
        return value
    return jnp.concatenate([value, jnp.zeros((rows - value.shape[0], value.shape[1]), value.dtype)], axis=0)


def pad_lanes(value, lanes):
    if value.shape[1] == lanes:
        return value
    return jnp.concatenate([value, jnp.zeros((value.shape[0], lanes - value.shape[1]), value.dtype)], axis=1)


def bias_tables(off_ref, table_ref, index_ref, outs, pair):
    tables = []
    for side in range(2):
        row = pad_lanes(table_ref[pl.ds(2 * pair + side, 1), :], 384) * LOG2E
        tables.append([jnp.broadcast_to(row[:, 128 * k : 128 * k + 128], (8, 128)) for k in range(3)])
    index_ref[...] = jnp.zeros_like(index_ref)
    for number, (_, amount, rows, lanes) in enumerate(PARTS):
        index_ref[:SLOT, :SLOT] = off_ref[number]

        tiles = rows // 8 // (number + 1)

        def strip(step, _, number=number, amount=amount, lanes=lanes, tiles=tiles, out=outs[number]):
            for line in range(tiles):
                at = pl.multiple_of((step * tiles + line) * 8, 8)
                for block in range(lanes // 128):
                    index = index_ref[pl.ds(at, 8), 128 * block : 128 * block + 128]
                    low = index & 127
                    part = index >> 7
                    valid = lax.broadcasted_iota(jnp.int32, (8, 128), 1) + 128 * block < amount
                    for side in range(2):
                        found = [
                            jnp.take_along_axis(tables[side][k], low, axis=1, mode="promise_in_bounds")
                            for k in range(3 if number == 2 else 2)
                        ]
                        value = jnp.where(part == 0, found[0], found[1])
                        if number == 2:
                            value = jnp.where(part == 2, found[2], value)
                        column = side * lanes + 128 * block
                        out[pair, pl.ds(at, 8), column : column + 128] = jnp.where(valid, value, -1e30)
            return 0

        lax.fori_loop(0, number + 1, strip, 0)


def head_keys(keys, pair, lanes):
    owner = lax.broadcasted_iota(jnp.int32, keys.shape, 1) // KEY
    zero = jnp.zeros_like(keys)
    return jnp.concatenate(
        [pad_rows(jnp.where(owner == 2 * pair + side, keys, zero), lanes) for side in range(2)], axis=0
    )


def pair_values(values, lanes):
    zero = jnp.zeros((lanes, VALD), values.dtype)
    top = jnp.concatenate([pad_rows(values[:, :VALD], lanes), zero], axis=1)
    low = jnp.concatenate([zero, pad_rows(values[:, VALD:], lanes)], axis=1)
    return jnp.concatenate([top, low], axis=0)


def by_eight(value):
    return jnp.sum(value.reshape(value.shape[0] // 8, 8, value.shape[1]), axis=0)


def attend_kernel(class_ref, mixed_in, bias_in0, bias_in1, bias_in2, att_out, p_out, r_out, *held):
    mixed, biases, att, p, r = held[0], held[1:4], held[4], held[5], held[6]
    sem_in, sem_bias, sem_out, score = held[7:11]
    images = mixed.shape[0]

    def load(at):
        return pltpu.make_async_copy(mixed_in.at[at], mixed.at[at], sem_in.at[at])

    def load_bias(number):
        source = (bias_in0, bias_in1, bias_in2)[number]
        return pltpu.make_async_copy(source, biases[number], sem_bias.at[number])

    def store(at, rows, lanes):
        part = (at, pl.ds(0, rows), pl.ds(0, 4 * lanes))
        return (
            pltpu.make_async_copy(p.at[part], p_out.at[part], sem_out.at[0, at]),
            pltpu.make_async_copy(r.at[part[:2]], r_out.at[part[:2]], sem_out.at[1, at]),
        )

    def store_att(at):
        return pltpu.make_async_copy(att.at[at], att_out.at[at], sem_out.at[2, at])

    def absent(number, before):
        found = jnp.bool_(True)
        for k in range(images):
            found = jnp.logical_and(found, jnp.logical_or(class_ref[k] != number, k >= before))
        return found

    load(0).start()
    for number in (2, 1, 0):
        load_bias(number).start()
    for k in range(1, images):
        load(k).start()

    def one(at, _):
        load(at).wait()
        kind = class_ref[at]
        for number, (_, amount, rows, lanes) in enumerate(PARTS):

            @pl.when(jnp.logical_and(kind == number, absent(number, at)))
            def _(number=number):
                load_bias(number).wait()

            @pl.when(kind == number)
            def _(amount=amount, rows=rows, lanes=lanes, bias=biases[number]):
                query = mixed[at, :rows, :128]
                keys = mixed[at, :rows, 128:256]
                kept = lax.broadcasted_iota(jnp.int32, (rows, VALD), 0) < amount
                lane = lax.broadcasted_iota(jnp.int32, (rows, 128), 1)
                shares = jnp.zeros((rows, 128), jnp.float32)
                for pair in range(2):
                    score[pair, :rows, : 2 * lanes] = dot_nt(query, head_keys(keys, pair, lanes)) + bias[pair]
                for pair in range(2):
                    scores = score[pair, :rows, : 2 * lanes]
                    parts, inverse = [], []
                    for side in range(2):
                        own = scores[:, side * lanes : (side + 1) * lanes]
                        expo = jnp.exp2(own - jnp.max(own, axis=1, keepdims=True))
                        share = 1.0 / jnp.sum(expo, axis=1, keepdims=True)
                        shares = jnp.where(lane == 2 * pair + side, share, shares)
                        parts.append(expo.astype(jnp.bfloat16))
                        inverse.append(share)
                    both = jnp.concatenate(parts, axis=1)
                    p[at, :rows, 2 * pair * lanes : 2 * (pair + 1) * lanes] = both
                    values = mixed[at, :rows, 256 + 256 * pair : 512 + 256 * pair]
                    sums = dot_nn(both, pair_values(values, lanes))
                    for side in range(2):
                        own = sums[:, side * VALD : (side + 1) * VALD] * inverse[side]
                        spot = (2 * pair + side) * VALD
                        att[at, :rows, spot : spot + VALD] = jnp.where(kept, own, 0.0).astype(jnp.bfloat16)
                r[at, :rows, :] = shares
                if rows < ROWS:
                    att[at, rows:, :] = jnp.zeros((ROWS - rows, att.shape[2]), jnp.bfloat16)
                for copy in store(at, rows, lanes):
                    copy.start()

        store_att(at).start()
        return 0

    lax.fori_loop(0, images, one, 0)

    def finish(at, _):
        for number, (_, _, rows, lanes) in enumerate(PARTS):

            @pl.when(class_ref[at] == number)
            def _(rows=rows, lanes=lanes):
                for copy in store(at, rows, lanes):
                    copy.wait()

        store_att(at).wait()
        return 0

    lax.fori_loop(0, images, finish, 0)
    for number in range(3):

        @pl.when(absent(number, images))
        def _(number=number):
            load_bias(number).wait()


def back_kernel(fs_size, arrive, leave, *refs):
    class_ref, mixed_in, p_in, r_in, g_in, att_in, xs_in, lines_ref, out_in = refs[:9]
    gmix_out, raw_ref, sum_ref, low_accs, own_refs, out_out = refs[9], refs[10], refs[11], refs[12:15], refs[15:21], refs[21]
    mixed, p, r, g, att, xs, gmix = refs[22:29]
    accs, held, out_sems, sem_in, sem_out = refs[29:32], refs[32], refs[33], refs[34], refs[35]
    images = mixed.shape[0]
    out_load = pltpu.make_async_copy(out_in, held, out_sems.at[0])
    out_store = pltpu.make_async_copy(held, out_out, out_sems.at[1])

    def loads(at, rows, lanes):
        part = (at, pl.ds(0, rows), pl.ds(0, 4 * lanes))
        pairs = [(p_in.at[part], p.at[part]), (r_in.at[part[:2]], r.at[part[:2]])]
        pairs += [(a.at[at], b.at[at]) for a, b in ((mixed_in, mixed), (g_in, g), (att_in, att), (xs_in, xs))]
        return [pltpu.make_async_copy(a, b, sem_in.at[k, at]) for k, (a, b) in enumerate(pairs)]

    def store(at):
        return pltpu.make_async_copy(gmix.at[at], gmix_out.at[at], sem_out.at[at])

    def request(at, _):
        for number, (_, _, rows, lanes) in enumerate(PARTS):

            @pl.when(class_ref[at] == number)
            def _(rows=rows, lanes=lanes):
                for copy in loads(at, rows, lanes):
                    copy.start()

        return 0

    lax.fori_loop(0, images, request, 0)
    out_load.start()
    for ref in (*accs, raw_ref, sum_ref):
        ref[...] = jnp.zeros_like(ref)

    def one(at, _):
        kind = class_ref[at]
        for number, (_, amount, rows, lanes) in enumerate(PARTS):

            @pl.when(kind == number)
            def _(rows=rows, lanes=lanes, acc=accs[number]):
                for copy in loads(at, rows, lanes):
                    copy.wait()
                query = mixed[at, :rows, :128]
                keys = mixed[at, :rows, 128:256]
                owner = lax.broadcasted_iota(jnp.int32, (rows, 128), 1) // KEY
                d_query = jnp.zeros((rows, 128), jnp.float32)
                stacked = []
                for pair in range(2):
                    grads, deltas = [], []
                    for side in range(2):
                        head = 2 * pair + side
                        spot = head * VALD
                        grad = g[at, :rows, spot : spot + VALD].astype(jnp.float32) * r[at, :rows, head : head + 1]
                        own = att[at, :rows, spot : spot + VALD].astype(jnp.float32)
                        deltas.append(jnp.sum(grad * own, axis=1, keepdims=True))
                        grads.append(grad.astype(jnp.bfloat16))
                    both = jnp.concatenate(grads, axis=1)
                    values = mixed[at, :rows, 256 + 256 * pair : 512 + 256 * pair]
                    d_probs = dot_nt(both, pair_values(values, lanes))
                    probs = p[at, :rows, 2 * pair * lanes : 2 * (pair + 1) * lanes]
                    low = []
                    for side in range(2):
                        cut = slice(side * lanes, (side + 1) * lanes)
                        d_score = probs[:, cut].astype(jnp.float32) * (d_probs[:, cut] - deltas[side])
                        acc[pair, :, cut] += d_score
                        low.append(d_score.astype(jnp.bfloat16))
                    d_low = jnp.concatenate(low, axis=1)
                    d_query = d_query + dot_nn(d_low, head_keys(keys, pair, lanes))
                    stacked += low
                    tall = jnp.concatenate([probs[:, :lanes], probs[:, lanes:]], axis=0)
                    d_values = dot_tn(tall, pair_values(both, rows))
                    spot = 256 + 256 * pair
                    sum_ref[:, spot : spot + 256] += by_eight(d_values[:rows])
                    gmix[at, :rows, spot : spot + 256] = d_values[:rows].astype(jnp.bfloat16)
                d_keys = sum(
                    jnp.where(owner == head, dot_tn(stacked[head], query)[:rows], 0.0) for head in range(HEADS)
                )
                d_query = d_query * KEY ** (-0.5)
                d_keys = d_keys * LN2
                sum_ref[:, :128] += by_eight(d_query)
                sum_ref[:, 128:256] += by_eight(d_keys)
                gmix[at, :rows, :128] = d_query.astype(jnp.bfloat16)
                gmix[at, :rows, 128:256] = d_keys.astype(jnp.bfloat16)
                raw_ref[...] += dot_tn(xs[at, :rows, :], gmix[at, :rows, :])
                if rows < ROWS:
                    gmix[at, rows:, :] = jnp.zeros((ROWS - rows, gmix.shape[2]), jnp.bfloat16)

        store(at).start()
        return 0

    lax.fori_loop(0, images, one, 0)
    leave(1, 2)
    for low, acc in zip(low_accs, accs):
        low[...] = acc[...].astype(jnp.bfloat16)
    leave(3, 4, 5)
    out_load.wait()
    out_store.start()
    arrive(7)
    place = lax.axis_index("fsdp")
    lines = lines_ref[...]
    for k, ref in enumerate(own_refs):
        width = ref.shape[1]
        ref[...] = pltpu.roll(lines, lines.shape[1] - place * width, 1)[k : k + 1, :width]
    leave(6, 7, 8, 9, 10, 11)

    def finish(at, _):
        store(at).wait()
        return 0

    lax.fori_loop(0, images, finish, 0)
    out_store.wait()


def grid_places(off_ref):
    found = []
    for number, (side_of, amount, _, _) in enumerate(PARTS):
        offsets = off_ref[number]
        row = lax.broadcasted_iota(jnp.int32, (SLOT, 1), 0)
        most = jnp.max(offsets, axis=1, keepdims=True)
        corner = jnp.min(jnp.where(most == (side_of - 1) * (GRID + 1), row, SLOT), axis=0, keepdims=True)
        place = jnp.sum(jnp.where(row == corner, offsets, 0), axis=0, keepdims=True)
        place = jnp.where(lax.broadcasted_iota(jnp.int32, (1, SLOT), 1) < amount, place, -1)
        found.append(jnp.concatenate([place, jnp.full((1, 384 - SLOT), -1, jnp.int32)], axis=1))
    return jnp.concatenate(found + [jnp.full((8 - len(found), 384), -1, jnp.int32)], axis=0)


def one_hot(left, right):
    return (left == right).astype(jnp.float32).astype(jnp.bfloat16)


def table_sums(places, accs):
    zero = (jnp.zeros((8, 128), jnp.float32), jnp.zeros((16, 128), jnp.float32))
    totals = [[zero] * 6 for _ in range(HEADS)]
    for number, (side_of, _, rows, lanes) in enumerate(PARTS):
        pad = 24 if side_of > 16 else 16
        reach = 384 if side_of > 14 else 256
        place = places[number : number + 1, :]
        cell = lax.broadcasted_iota(jnp.int32, (pad * side_of, 1), 0)
        cell_row = (cell * 2731) >> 16 if pad == 24 else cell >> 4
        cell_col = pad - 1 - (cell - pad * cell_row)
        code = jnp.where(cell_col < side_of, cell_row * GRID + cell_col, -2)
        left = one_hot(code, place[:, :rows])
        right = one_hot(lax.broadcasted_iota(jnp.int32, (reach, 1), 0), place[:, :lanes])
        for pair in range(2):
            by_row = dot_nn(left, accs[number][pair]).astype(jnp.bfloat16)
            for side in range(2):
                both = dot_nt(by_row[:, side * lanes : (side + 1) * lanes], right)
                total = totals[2 * pair + side]
                for line in range(side_of):
                    far, near = divmod((GRID - 1 - line) * GRID, 128)
                    part = pad_lanes(both[pad * line : pad * line + pad], reach + 128)
                    if near:
                        part = pltpu.roll(part, near, 1)
                    for k in range(min(reach // 128 + 1, 5 - far)):
                        piece = part[:, 128 * k : 128 * k + 128]
                        top, low = total[far + k]
                        if pad == 24:
                            top = top + piece[:8]
                        total[far + k] = (top, low + piece[pad - 16 :])
    width = 768
    lane = lax.broadcasted_iota(jnp.int32, (24, width), 1)
    ahead = lane - GRID * ((lane * 3641) >> 16) + lax.broadcasted_iota(jnp.int32, (24, width), 0) >= 23
    level, below = [], []
    for head in range(HEADS):
        whole = jnp.concatenate([jnp.concatenate(t, axis=0) for t in totals[head]], axis=1)
        for keep, group in ((ahead, level), (jnp.logical_not(ahead), below)):
            turned = pltpu.roll(jnp.where(keep, whole, 0.0), 0, 1, stride=1, stride_axis=0)
            group.append(jnp.sum(turned, axis=0, keepdims=True))
    spot = lax.broadcasted_iota(jnp.int32, (width, 1), 0) - 23
    target = lax.broadcasted_iota(jnp.int32, (1, 384), 1)
    spot_row = jnp.where(spot >= 0, (spot * 3641) >> 16, -1)
    spot_col = spot - GRID * spot_row
    straight = one_hot(jnp.abs(spot_row - (GRID - 1)) * GRID + spot_col, target)
    back = one_hot(jnp.abs(spot_row + 1 - (GRID - 1)) * GRID + GRID - spot_col, target)
    out = jnp.zeros((HEADS, 384), jnp.float32)
    for group, fold in ((level, straight), (below, back)):
        high, low = split_low(jnp.concatenate(group, axis=0))
        spread = dot_nn(jnp.concatenate([high.astype(jnp.float32), low.astype(jnp.float32)], axis=0).astype(jnp.bfloat16), fold)
        out = out + spread[:HEADS] + spread[HEADS:]
    return out


def attend_call(classes, mixed, biases):
    images = mixed.shape[0]
    bf, f32 = jnp.bfloat16, jnp.float32
    shapes = [
        jax.ShapeDtypeStruct((images, ROWS, 512), bf),
        jax.ShapeDtypeStruct((images, ROWS, 1536), bf),
        jax.ShapeDtypeStruct((images, ROWS, 128), f32),
    ]
    return pl.pallas_call(
        attend_kernel,
        in_specs=[SMEM] + [ANY] * 4,
        out_specs=[ANY] * 3,
        out_shape=shapes,
        scratch_shapes=[pltpu.VMEM(a.shape, a.dtype) for a in (mixed, *biases, *shapes)]
        + [
            pltpu.SemaphoreType.DMA((images,)),
            pltpu.SemaphoreType.DMA((3,)),
            pltpu.SemaphoreType.DMA((3, images)),
            pltpu.VMEM((2, ROWS, 768), f32),
        ],
        compiler_params=pltpu.CompilerParams(vmem_limit_bytes=60 * 2**20),
    )(classes, mixed, *biases)


def back_call(fs_size, classes, mixed, probs, shares, grad, attended, xs, lines, output):
    images, model = mixed.shape[0], xs.shape[2]
    bf, f32 = jnp.bfloat16, jnp.float32
    tables = [(2, r, 2 * l) for _, _, r, l in PARTS]
    widths = [w // fs_size for w in (model, model, lines.shape[1], lines.shape[1], model, model)]
    args = (classes, mixed, probs, shares, grad, attended, xs, lines, output)
    out_shape = (
        [
            jax.ShapeDtypeStruct((images, ROWS, 768), bf),
            jax.ShapeDtypeStruct((model, 768), f32),
            jax.ShapeDtypeStruct((8, 768), f32),
        ]
        + [jax.ShapeDtypeStruct(s, bf) for s in tables]
        + [jax.ShapeDtypeStruct((1, w), f32) for w in widths]
        + [jax.ShapeDtypeStruct(output.shape, bf)]
    )
    ins, outs = (7,), tuple(range(1, 12))
    return pl.pallas_call(
        staged(functools.partial(back_kernel, fs_size), ins, outs, len(args)),
        in_specs=[SMEM] + [ANY] * 8,
        out_specs=[ANY] * 13,
        out_shape=out_shape,
        scratch_shapes=[pltpu.VMEM(a.shape, a.dtype) for a in (mixed, probs, shares, grad, attended, xs, out_shape[0])]
        + [pltpu.VMEM(s, f32) for s in tables]
        + [
            pltpu.VMEM(output.shape, bf),
            pltpu.SemaphoreType.DMA((2,)),
            pltpu.SemaphoreType.DMA((6, images)),
            pltpu.SemaphoreType.DMA((images,)),
        ]
        + stage_scratch(ins, outs, args, out_shape),
        compiler_params=pltpu.CompilerParams(vmem_limit_bytes=60 * 2**20),
    )(*args)


def end_kernel(*refs):
    ins, outs = refs[:7], refs[7:15]
    held, kept, table_in, table, lines_in, own_lines = refs[15], refs[16:20], refs[20], refs[21], refs[22], refs[23:25]
    sem_in, sem_out = refs[25:27]
    step = held.shape[0] // 4
    pairs = [(ins[0].at[pl.ds(k * step, step)], held.at[pl.ds(k * step, step)], outs[0]) for k in range(4)]
    pairs = [(a, b, c.at[pl.ds(k * step, step)]) for k, (a, b, c) in enumerate(pairs)]
    pairs = [(ins[1], table_in, None), (ins[6], lines_in, None)] + pairs
    pairs += [(ins[2 + k], kept[k], outs[2 + k]) for k in range(4)]
    loads = [pltpu.make_async_copy(a, b, sem_in.at[k]) for k, (a, b, _) in enumerate(pairs)]
    stores = [pltpu.make_async_copy(b, c, sem_out.at[k]) for k, (_, b, c) in enumerate(pairs) if c is not None]
    for load in loads:
        load.start()
    loads[0].wait()
    loads[1].wait()
    table[...] = table_in[:, :NOFF]
    spot = lax.axis_index("fsdp")
    lines = lines_in[...]
    for k, ref in enumerate(own_lines):
        width = ref.shape[1]
        ref[...] = pltpu.roll(lines, lines.shape[1] - spot * width, 1)[k : k + 1, :width]
    for k, (a, b) in enumerate(((table, outs[1]), (own_lines[0], outs[6]), (own_lines[1], outs[7]))):
        stores.append(pltpu.make_async_copy(a, b, sem_out.at[len(pairs) + k]))
        stores[-1].start()
    for load, store in zip(loads[2:], stores):
        load.wait()
        store.start()
    for store in stores:
        store.wait()


def end_call(fs_size, input_grad, table, owned, lines):
    f32 = jnp.float32
    width = lines.shape[1] // fs_size
    shapes = [input_grad.shape, (HEADS, NOFF)] + [o.shape for o in owned] + [(1, width)] * 2
    held = [input_grad.shape] + [o.shape for o in owned] + [table.shape, (HEADS, NOFF), lines.shape] + [(1, width)] * 2
    return pl.pallas_call(
        end_kernel,
        out_shape=[jax.ShapeDtypeStruct(s, f32) for s in shapes],
        in_specs=[ANY] * 7,
        out_specs=[ANY] * 8,
        scratch_shapes=[pltpu.VMEM(s, f32) for s in held]
        + [pltpu.SemaphoreType.DMA((13,)), pltpu.SemaphoreType.DMA((13,))],
        compiler_params=pltpu.CompilerParams(vmem_limit_bytes=60 * 2**20),
    )(input_grad, table, *owned, lines)


MESH = pl.DeviceIdType.MESH
ANY = pl.BlockSpec(memory_space=pl.ANY)
SMEM = pl.BlockSpec(memory_space=pltpu.SMEM)


class Place:
    def __init__(self, dp_size, fs_size):
        self.dp_size, self.fs_size = dp_size, fs_size
        self.size = dp_size * fs_size
        self.dp, self.fs = lax.axis_index("dp"), lax.axis_index("fsdp")
        self.me = self.dp * fs_size + self.fs
        self.core = lax.rem(self.dp, 2)
        self.partner = (self.dp + 1 - 2 * self.core, self.fs)

    def other(self, step, cores=2):
        number = self.size // 2 * cores - step
        rows, lines = self.fs_size // 2, self.dp_size // 2
        core = lax.rem(self.core + lax.rem(number, cores), 2)
        number = number // cores
        line = lax.rem(self.dp // 2 + lax.rem(number // rows, lines), lines)
        row = lax.rem(self.fs // 2 + lax.rem(number, rows), rows)
        return (2 * line + core, 2 * row + lax.rem(self.fs + number // (rows * lines), 2))

    def all_others(self):
        rows, lines = self.fs_size // 2, self.dp_size // 2
        row_at = [2 * lax.rem(self.fs // 2 + d, rows) for d in range(rows)]
        line_at = [2 * lax.rem(self.dp // 2 + d, lines) for d in range(lines)]
        side_at = [lax.rem(self.fs, 2), 1 - lax.rem(self.fs, 2)]
        core_at = [self.core, 1 - self.core]
        steps = [(z, x, y, c) for z in range(rows) for x in range(2) for y in range(lines) for c in range(2)][1:]
        steps.sort(key=lambda s: -(20 * (s[0] > 0) + 10 * s[1] + 10 * (s[2] > 0) + s[3]))
        return [(line_at[y] + core_at[c], row_at[z] + side_at[x]) for z, x, y, c in steps]

    def greet(self):
        barrier = pltpu.get_barrier_semaphore()

        def signal(step, _):
            pl.semaphore_signal(barrier, inc=1, device_id=self.other(step), device_id_type=MESH)
            return 0

        lax.fori_loop(1, self.size, signal, 0)

    def meet(self):
        pl.semaphore_wait(pltpu.get_barrier_semaphore(), self.size - 1)

    def spread(self, buf, value, send, recv):
        buf[self.me] = value

        if self.size <= 64:
            for device in self.all_others():
                push(buf.at[self.me], buf.at[self.me], send, recv, device)
            return

        def start(step, _):
            push(buf.at[self.me], buf.at[self.me], send, recv, self.other(step))
            return 0

        lax.fori_loop(1, self.size, start, 0)

    def collect(self, buf, recv):
        await_bytes(buf.at[pl.ds(0, self.size - 1)], recv)
        return jnp.sum(buf[...], axis=0)

    def spread_pair(self, buf, value, send, recv):
        buf[self.core] = value
        part = buf.at[self.core]
        push(part, part, send, recv, self.partner)

    def collect_pair(self, buf, recv):
        await_bytes(buf.at[0], recv)
        return buf[0] + buf[1]

    def spread_chips(self, buf, value, send, recv):
        chips = self.size // 2
        mine = (self.dp // 2) * self.fs_size + self.fs
        buf[mine] = value

        def start(step, _):
            push(buf.at[mine], buf.at[mine], send, recv, self.other(step, 1))
            return 0

        lax.fori_loop(1, chips, start, 0)

    def collect_chips(self, buf, recv):
        await_bytes(buf.at[pl.ds(0, self.size // 2 - 1)], recv)
        return jnp.sum(buf[...], axis=0)

    def settle_pair(self, buf, send):
        await_bytes(buf.at[0], send)

    def settle_chips(self, buf, send):
        await_bytes(buf.at[pl.ds(0, self.size // 2 - 1)], send)

    def settle(self, buf, send):
        await_bytes(buf.at[pl.ds(0, self.size - 1)], send)


def push(source, target, send, recv, device):
    pltpu.make_async_remote_copy(
        src_ref=source, dst_ref=target, send_sem=send, recv_sem=recv, device_id=device, device_id_type=MESH
    ).start()


def await_bytes(ref, sem):
    pltpu.make_async_copy(ref, ref, sem).wait()


def gather_start(place, buf, send, recv):
    half = buf.shape[2] // 2
    part = buf.at[place.fs, :, pl.ds(pl.multiple_of(place.core * half, half), half)]

    def start(step, _):
        push(part, part, send, recv, (place.dp, lax.rem(place.fs + place.fs_size - step, place.fs_size)))
        return 0

    lax.fori_loop(1, place.fs_size, start, 0)


def gather_pass(place, buf, recv, send2, recv2):
    half = buf.shape[2] // 2
    await_bytes(buf.at[pl.ds(0, place.fs_size - 1), :, pl.ds(0, half)], recv)
    part = buf.at[:, :, pl.ds(pl.multiple_of(place.core * half, half), half)]
    push(part, part, send2, recv2, place.partner)


def gather_end(place, buf, recv2):
    half = buf.shape[2] // 2
    await_bytes(buf.at[:, :, pl.ds(0, half)], recv2)


def gather_settle(place, buf, send, send2):
    half = buf.shape[2] // 2
    await_bytes(buf.at[pl.ds(0, place.fs_size - 1), :, pl.ds(0, half)], send)
    await_bytes(buf.at[:, :, pl.ds(0, half)], send2)


def flat_weight(buf):
    shards, rows, width = buf.shape
    if rows % 16 == 0:
        return buf[...].reshape(shards * rows, width)
    wide = jnp.concatenate([buf[k].astype(jnp.float32) for k in range(shards)], axis=0)
    return wide.astype(jnp.bfloat16)


def split_low(value):
    high = value.astype(jnp.bfloat16)
    return high, (value - high.astype(jnp.float32)).astype(jnp.bfloat16)


def precise(left, right):
    high, low = split_low(left)
    return dot_nn(high, right) + dot_nn(low, right)


def arrange(columns):
    blocks = [columns[:, (2 * KEY + VALD) * h : (2 * KEY + VALD) * (h + 1)] for h in range(HEADS)]
    parts = [b[:, :KEY] for b in blocks] + [b[:, KEY : 2 * KEY] for b in blocks] + [b[:, 2 * KEY :] for b in blocks]
    return jnp.concatenate(parts, axis=1)


def restore(columns):
    parts = []
    for h in range(HEADS):
        parts += [
            columns[:, KEY * h : KEY * (h + 1)],
            columns[:, 128 + KEY * h : 128 + KEY * (h + 1)],
            columns[:, 256 + VALD * h : 256 + VALD * (h + 1)],
        ]
    return jnp.concatenate(parts, axis=1)


def by_columns(ref, value):
    for k in range(ref.shape[0]):
        ref[k] = value[:, 128 * k : 128 * k + 128]


def take_image(ref, image, images):
    return jnp.concatenate([ref[k, pl.ds(image, SLOT, stride=images), :] for k in range(ref.shape[0])], axis=1)


def put_image(ref, image, images, value):
    for k in range(ref.shape[0]):
        ref[k, pl.ds(image, SLOT, stride=images), :] = value[:SLOT, 128 * k : 128 * k + 128]


def limits_of(kind):
    return jnp.where(kind == 0, (GRID - 8) ** 2, jnp.where(kind == 1, (GRID - 4) ** 2, SLOT))


def assemble(buf, widths, lanes):
    turned = {}
    for width in sorted(set(widths)):
        turned[width] = sum(
            pltpu.roll(pad_lanes(buf[k], lanes), k * width, 1) if k else pad_lanes(buf[k], lanes)
            for k in range(buf.shape[0])
        )
    return [turned[width][k : k + 1] for k, width in enumerate(widths)]


class Reduce:
    def __init__(self, place, full, first, half, second, third, send, recv):
        self.place, self.full, self.first, self.half = place, full, first, half
        self.second, self.third, self.send, self.recv = second, third, send, recv
        self.width = half.shape[2]

    def swap(self):
        at = pl.multiple_of((1 - self.place.core) * self.width, self.width)
        push(self.full.at[:, :, pl.ds(at, self.width)], self.first, self.send.at[0], self.recv.at[0], self.place.partner)

    def scatter(self):
        place = self.place
        await_bytes(self.first, self.recv.at[0])

        at = pl.multiple_of(self.place.core * self.width, self.width)
        own = self.full[:, :, pl.ds(at, self.width)].astype(jnp.float32)
        self.half[...] = (own + self.first[...].astype(jnp.float32)).astype(jnp.bfloat16)
        self.second[place.fs] = self.half[place.fs]

        def start(step, _):
            target = lax.rem(place.fs + step, place.fs_size)
            push(self.half.at[target], self.second.at[place.fs], self.send.at[1], self.recv.at[1], (place.dp, target))
            return 0

        lax.fori_loop(1, place.fs_size, start, 0)

    def gathered(self):
        await_bytes(self.second.at[pl.ds(0, self.place.fs_size - 1)], self.recv.at[1])
        return jnp.sum(self.second[...].astype(jnp.float32), axis=0).astype(jnp.bfloat16)

    def share(self, total=None):
        place = self.place
        self.third[place.dp] = self.gathered() if total is None else total

        def start(step, _):
            target = lax.rem(place.dp + step, place.dp_size)
            push(self.third.at[place.dp], self.third.at[place.dp], self.send.at[2], self.recv.at[2], (target, place.fs))
            return 0

        lax.fori_loop(1, place.dp_size, start, 0)

    def result(self):
        place = self.place
        await_bytes(self.third.at[pl.ds(0, place.dp_size - 1)], self.recv.at[2])
        parts = []
        for core in range(2):
            parts.append(sum(self.third[k].astype(jnp.float32) for k in range(core, place.dp_size, 2)))
        return jnp.concatenate(parts, axis=1)

    def settle(self, steps=(0, 1, 2)):
        place = self.place
        if 0 in steps:
            await_bytes(self.first, self.send.at[0])
        if 1 in steps:
            await_bytes(self.second.at[pl.ds(0, place.fs_size - 1)], self.send.at[1])
        if 2 in steps:
            await_bytes(self.third.at[pl.ds(0, place.dp_size - 1)], self.send.at[2])


def staged(body, ins, outs, n_in):
    def kernel(*refs):
        refs, sem = list(refs[:-1]), refs[-1]
        count = len(ins) + len(outs)
        held, refs = refs[len(refs) - count :], refs[: len(refs) - count]
        loads, stores = {}, {}
        for k, at in enumerate(ins):
            loads[at] = pltpu.make_async_copy(refs[at], held[k], sem.at[k])
            refs[at] = held[k]
        for k, at in enumerate(outs, len(ins)):
            stores[at] = pltpu.make_async_copy(held[k], refs[n_in + at], sem.at[k])
            refs[n_in + at] = held[k]
        for load in loads.values():
            load.start()
        started = []

        def arrive(*places):
            for at in places:
                loads.pop(at).wait()

        def leave(*places):
            for at in places:
                stores[at].start()
                started.append(at)

        body(arrive, leave, *refs)
        leave(*[at for at in stores if at not in started])
        for store in stores.values():
            store.wait()

    return kernel


def stage_scratch(ins, outs, args, out_shape):
    held = [pltpu.VMEM(args[k].shape, args[k].dtype) for k in ins] + [
        pltpu.VMEM(out_shape[k].shape, out_shape[k].dtype) for k in outs
    ]
    return held + [pltpu.SemaphoreType.DMA((len(held),))]


def first_kernel(dp_size, fs_size, arrive, leave, *refs):
    class_ref, x_ref, off_ref, table_ref = refs[:4]
    shards, vectors = refs[4:8], refs[8:16]
    mixed_out, xs_out, bias_out, weight_out, vec_out, gram_out = refs[16], refs[17], refs[18:21], refs[21:25], refs[25], refs[26]
    place_out = refs[27]
    refs = refs[1:]
    xs, z, mixed, index, wide = refs[27:32]
    bias, weights = refs[32:35], refs[35:39]
    vbuf, stat, stat2 = refs[39:42]
    send, recv, send2, recv2, local = refs[42:47]
    place = Place(dp_size, fs_size)
    images = xs.shape[0]

    place.greet()
    arrive(*range(4, 16))
    for k in range(4):
        own = shards[k][...]
        if k == 0:
            own = arrange(own.astype(jnp.float32)).astype(jnp.bfloat16)
        half = own.shape[1] // 2
        own = jnp.where(place.core == 0, own[:, :half], own[:, half:])
        weights[k][place.fs, :, pl.ds(pl.multiple_of(place.core * half, half), half)] = own
    vbuf[place.fs] = jnp.concatenate(
        [pad_lanes(v[...].astype(jnp.float32), 128) for v in vectors], axis=0
    )
    arrive(1)
    by_columns(wide, x_ref[...].astype(jnp.float32))
    count = jnp.int32(0)
    for image in range(images):
        limit = limits_of(class_ref[image])
        row = lax.broadcasted_iota(jnp.int32, (SLOT, xs.shape[2]), 0)
        value = jnp.where(row < limit, take_image(wide, image, images), 0.0)
        xs[image] = pad_rows(value, ROWS).astype(jnp.bfloat16)
        count = count + limit

    flat = xs[...].reshape(images * ROWS, xs.shape[2])
    gram = dot_tn(flat, flat)
    total_x = dot_nn(jnp.ones((8, images * ROWS), jnp.bfloat16), flat)

    place.meet()
    gather_start(place, weights[0], send.at[0], recv.at[0])

    def start(step, _):
        target = lax.rem(place.fs + step, place.fs_size)
        push(vbuf.at[place.fs], vbuf.at[place.fs], send.at[4], recv.at[4], (place.dp, target))
        return 0

    lax.fori_loop(1, place.fs_size, start, 0)
    for k in range(1, 4):
        gather_start(place, weights[k], send.at[k], recv.at[k])
    xs_copy = pltpu.make_async_copy(xs, xs_out, local.at[0])
    xs_copy.start()
    arrive(2, 3)
    bias_tables(off_ref, table_ref, index, bias, place.core)
    place_out[...] = grid_places(off_ref)
    gram_out[...] = gram
    leave(10, 11)
    copies = [xs_copy]
    gather_pass(place, weights[0], recv.at[0], send2.at[0], recv2.at[0])
    gather_end(place, weights[0], recv2.at[0])
    weight = flat_weight(weights[0])
    high, low = split_low(gram)
    spread = dot_nn(high, weight) + dot_nn(low, weight)
    squares = jnp.sum(weight.astype(jnp.float32) * spread, axis=0, keepdims=True)
    sums = precise(total_x, weight)[:1]
    tail = jnp.full((1, 128), count.astype(jnp.float32))
    place.spread_pair(
        stat,
        jnp.concatenate(
            [jnp.concatenate([sums, tail], axis=1), jnp.concatenate([squares, tail], axis=1)], axis=0
        ),
        send.at[5],
        recv.at[5],
    )
    place.spread_chips(stat2, place.collect_pair(stat, recv.at[5]), send.at[6], recv.at[6])
    for k in range(3):
        part = bias[k].at[place.core]
        push(part, part, send.at[7 + k], recv.at[7 + k], place.partner)

    def product(image, _):
        z[image] = dot_nn(xs[image], weight)
        return 0

    lax.fori_loop(0, images, product, 0)
    for k in range(1, 4):
        gather_pass(place, weights[k], recv.at[k], send2.at[k], recv2.at[k])
    await_bytes(vbuf.at[pl.ds(0, place.fs_size - 1)], recv.at[4])
    widths = [v.shape[1] for v in vectors]
    full = assemble(vbuf, widths, 768)
    full[0], full[1] = arrange(full[0]), arrange(full[1])

    for k in range(3):
        await_bytes(bias[k].at[0], recv.at[7 + k])
        copies.append(pltpu.make_async_copy(bias[k], bias_out[k], local.at[1 + k]))
        copies[-1].start()
    got = place.collect_chips(stat2, recv.at[6])
    whole = got[0:1, 768:769]
    center = got[0:1, :768] / whole
    square = got[1:2, :768] / whole
    scale = lax.rsqrt(square - center * center + EPS)
    vec_out[...] = jnp.concatenate(
        full
        + [scale, center, jnp.broadcast_to(whole, (1, 768)), pad_lanes(total_x[:1], 768)]
        + [jnp.zeros((4, 768), jnp.float32)],
        axis=0,
    )
    leave(9)
    gain = scale * full[0]
    shift = full[1] - center * gain
    fold = jnp.where(lax.broadcasted_iota(jnp.int32, (1, 768), 1) < 128, KEY ** (-0.5) * LOG2E, 1.0)
    gain, shift = gain * fold, shift * fold

    def normal(image, _):
        mixed[image] = (z[image] * gain + shift).astype(jnp.bfloat16)
        pltpu.make_async_copy(mixed.at[image], mixed_out.at[image], local.at[8 + image]).start()
        return 0

    lax.fori_loop(0, images, normal, 0)
    for k in range(4):
        if k > 0:
            gather_end(place, weights[k], recv2.at[k])
        copies.append(pltpu.make_async_copy(weights[k], weight_out[k], local.at[4 + k]))
        copies[-1].start()
    for k in range(4):
        gather_settle(place, weights[k], send.at[k], send2.at[k])
    await_bytes(vbuf.at[pl.ds(0, place.fs_size - 1)], send.at[4])
    place.settle_pair(stat, send.at[5])
    place.settle_chips(stat2, send.at[6])
    for k in range(3):
        await_bytes(bias[k].at[0], send.at[7 + k])
    for copy in copies:
        copy.wait()

    def finish(image, _):
        pltpu.make_async_copy(mixed.at[image], mixed_out.at[image], local.at[8 + image]).wait()
        return 0

    lax.fori_loop(0, images, finish, 0)


def first_call(dp_size, fs_size, classes, inputs, offset_table, bias_table, weights, vectors):
    images, model = classes.shape[0], inputs.shape[1]
    vectors = [v.reshape(1, -1) for v in vectors]
    shapes = [(fs_size,) + w.shape for w in weights]
    biases = [(2, r, 2 * l) for _, _, r, l in PARTS]
    bf, f32 = jnp.bfloat16, jnp.float32
    out_shape = (
        [
            jax.ShapeDtypeStruct((images, ROWS, 768), bf),
            jax.ShapeDtypeStruct((images, ROWS, model), bf),
        ]
        + [jax.ShapeDtypeStruct(s, f32) for s in biases]
        + [jax.ShapeDtypeStruct(s, bf) for s in shapes]
        + [jax.ShapeDtypeStruct((16, 768), f32), jax.ShapeDtypeStruct((model, model), f32)]
        + [jax.ShapeDtypeStruct((8, 384), jnp.int32)]
    )
    args = (classes, inputs, offset_table, bias_table, *weights, *vectors)
    ins, outs = (*range(4, 16), 1, 2, 3), (9, 10, 11)
    return pl.pallas_call(
        staged(functools.partial(first_kernel, dp_size, fs_size), ins, outs, len(args)),
        out_shape=out_shape,
        in_specs=[SMEM] + [ANY] * 15,
        out_specs=[ANY] * 12,
        scratch_shapes=[
            pltpu.VMEM((images, ROWS, model), bf),
            pltpu.VMEM((images, ROWS, 768), f32),
            pltpu.VMEM((images, ROWS, 768), bf),
            pltpu.VMEM((ROWS, 384), jnp.int32),
            pltpu.VMEM((model // 128, inputs.shape[0], 128), f32),
        ]
        + [pltpu.VMEM(s, f32) for s in biases]
        + [pltpu.VMEM(s, bf) for s in shapes]
        + [
            pltpu.VMEM((fs_size, 8, 128), f32),
            pltpu.VMEM((2, 2, 896), f32),
            pltpu.VMEM((dp_size * fs_size // 2, 2, 896), f32),
            pltpu.SemaphoreType.DMA((10,)),
            pltpu.SemaphoreType.DMA((10,)),
            pltpu.SemaphoreType.DMA((4,)),
            pltpu.SemaphoreType.DMA((4,)),
            pltpu.SemaphoreType.DMA((8 + images,)),
        ]
        + stage_scratch(ins, outs, args, out_shape),
        compiler_params=pltpu.CompilerParams(
            collective_id=0, has_side_effects=True, vmem_limit_bytes=56 * 2**20
        ),
    )(*args)


def total_rows(value):
    return jnp.sum(value, axis=0, keepdims=True)


def sigma_of(value):
    return 0.5 * jnp.tanh(0.5 * value) + 0.5


def slope_of(value):
    sigma = sigma_of(value)
    return sigma * (1.0 + value * (1.0 - sigma))


def norm_parts(sums, squares, total, gain, shift):
    center = sums / total
    scale = lax.rsqrt(squares / total - center * center + EPS)
    return center, scale, scale * gain, shift - center * scale * gain


def back_parts(grad_sum, grad_z, total, gain, center, scale):
    gain_grad = scale * (grad_z - center * grad_sum)
    alpha = scale * gain
    slant = alpha * scale * gain_grad / total
    level = alpha * (grad_sum - center * scale * gain_grad) / total
    return gain_grad, alpha, slant, level


def outer(column, row):
    left = jnp.concatenate([column, jnp.zeros((7, column.shape[1]), jnp.float32)], axis=0)
    right = jnp.concatenate([row, jnp.zeros((7, row.shape[1]), jnp.float32)], axis=0)
    left_high, left_low = split_low(left)
    right_high, right_low = split_low(right)
    return dot_tn(left_high, right_high) + dot_tn(left_high, right_low) + dot_tn(left_low, right_high)


def middle_kernel(dp_size, fs_size, group, arrive, leave, *refs):
    class_ref, att_in, xs_in, cot_in = refs[:4]
    weight_in, vec_ref, gram_ref = refs[4:7], refs[7], refs[8]
    out_out, gatt_out, gm_out, grad_out, vec_out, own_gram = refs[9], refs[10], refs[11], refs[12:15], refs[15], refs[16]
    refs = refs[2:]
    att, xs, cot, wo_buf, wu_buf, wd_buf = refs[15:21]
    gs, act, slope_att, zo, low, zu, hid, slope_up, zd, dzd, gu, gm, out, gatt, wide = refs[21:36]
    stat_o, stat_u, stat_d, stat_bu, stat_bo = refs[36:41]
    send, recv, local = refs[41:44]
    gram_steps, send_r, recv_r = refs[44:49], refs[49], refs[50]
    down_steps, send_w, recv_w = refs[51:55], refs[55], refs[56]
    up_steps, send_v, recv_v = refs[57:61], refs[61], refs[62]
    place = Place(dp_size, fs_size)
    images = att.shape[0]
    chunks = images // group
    size = group * ROWS
    f32, bf = jnp.float32, jnp.bfloat16
    gram_sum = Reduce(place, *gram_steps, send_r, recv_r)
    down_sum = Reduce(place, *down_steps, None, send_w, recv_w)
    up_sum = Reduce(place, *up_steps, None, send_v, recv_v)

    def copy(source, target, at):
        return pltpu.make_async_copy(source, target, local.at[at])

    loads = [
        copy(weight_in[0], wo_buf, 0),
        copy(xs_in, xs, 1),
        copy(cot_in, cot, 2),
        copy(weight_in[1], wu_buf, 3),
        copy(weight_in[2], wd_buf, 4),
    ]
    loads[0].start()

    def att_copy(k):
        part = pl.ds(k * group, group)
        return copy(att_in.at[part], att.at[part], 8 + k)

    for k in range(chunks):
        att_copy(k).start()
    for load in loads[1:]:
        load.start()
    place.greet()
    arrive(7)

    def get(ref, k):
        return ref[pl.ds(k * group, group)].reshape(size, ref.shape[2])

    def put(ref, k, value):
        ref[pl.ds(k * group, group)] = value.astype(ref.dtype).reshape(group, ROWS, ref.shape[2])

    def kept(k, width):
        row = lax.broadcasted_iota(jnp.int32, (ROWS, width), 0)
        return jnp.concatenate([row < limits_of(class_ref[k * group + j]) for j in range(group)], axis=0)

    def over(body, carry):
        return lax.fori_loop(0, chunks, body, carry, unroll=True)

    def zero(width):
        return jnp.zeros((1, width), f32)

    model = xs.shape[2]
    hidden = zu.shape[2]
    total = vec_ref[10:11, :1]
    out_gain, out_shift = vec_ref[2:3, :model], vec_ref[3:4, :model]
    up_gain, up_shift = vec_ref[4:5, :hidden], vec_ref[5:6, :hidden]
    down_gain, down_shift = vec_ref[6:7, :model], vec_ref[7:8, :model]

    loads[0].wait()
    wo = flat_weight(wo_buf)

    def step_out(k, carry):
        att_copy(k).wait()
        value = get(att, k).astype(f32)
        active = (value * sigma_of(value)).astype(bf)
        put(act, k, active)
        z = dot_nn(active, wo)
        put(zo, k, z)
        return carry[0] + total_rows(z), carry[1] + total_rows(z * z)

    sums = over(step_out, (zero(model), zero(model)))
    place.meet()
    x_sum = vec_ref[11:12, :model]
    place.spread(stat_o, jnp.concatenate(sums + (x_sum,), axis=0), send.at[0], recv.at[0])
    for load in loads[1:]:
        load.wait()

    def fill_out(k, _):
        put(slope_att, k, slope_of(get(att, k).astype(f32)))
        return 0

    over(fill_out, 0)
    by_columns(wide, cot[...].astype(f32))
    grad_sum = zero(model)
    for image in range(images):
        row = lax.broadcasted_iota(jnp.int32, (SLOT, model), 0)
        value = jnp.where(row < limits_of(class_ref[image]), take_image(wide, image, images), 0.0)
        gs[image] = pad_rows(value, ROWS).astype(bf)
        grad_sum = grad_sum + total_rows(value)
    wu, wd = flat_weight(wu_buf), flat_weight(wd_buf)
    got = place.collect(stat_o, recv.at[0])
    center_o, scale_o, a_o, b_o = norm_parts(got[0:1], got[1:2], total, out_gain, out_shift)
    x_mean = got[2:3] / total

    def middle_of(k):
        return get(xs, k).astype(f32) + get(zo, k) * a_o + b_o

    def step_up(k, carry):
        lower = jnp.where(kept(k, model), middle_of(k), 0.0).astype(bf)
        put(low, k, lower)
        z = dot_nn(lower, wu)
        put(zu, k, z)
        return carry[0] + total_rows(z), carry[1] + total_rows(z * z)

    sums = over(step_up, (zero(hidden), zero(hidden)))
    place.spread(stat_u, jnp.concatenate(sums, axis=0), send.at[1], recv.at[1])
    low_flat = low[...].reshape(images * ROWS, model)
    low_gram = dot_tn(low_flat, low_flat)
    low_sum = dot_nn(jnp.ones((8, images * ROWS), bf), low_flat)[:1]
    count = sum(limits_of(class_ref[k]) for k in range(images)).astype(f32)
    moved = x_sum - 0.5 * count * x_mean
    arrive(8)
    gram = gram_ref[...] - outer(x_mean, moved) - outer(moved, x_mean)
    gram_steps[0][...] = gram.reshape(gram_steps[0].shape).astype(bf)
    gram_sum.swap()

    def fill_up(k, carry):
        centered = jnp.where(kept(k, model), get(zo, k) - center_o, 0.0).astype(bf)
        return carry + dot_tn(get(act, k), centered)

    act_z = over(fill_up, jnp.zeros((act.shape[2], model), f32))
    got = place.collect(stat_u, recv.at[1])
    center_u, scale_u, a_u, b_u = norm_parts(got[0:1], got[1:2], total, up_gain, up_shift)

    def step_down(k, carry):
        value = get(zu, k) * a_u + b_u
        active = jnp.where(kept(k, hidden), value * sigma_of(value), 0.0).astype(bf)
        put(hid, k, active)
        z = dot_nn(active, wd)
        put(zd, k, z)
        return (
            carry[0] + total_rows(z),
            carry[1] + total_rows(z * z),
            carry[2] + total_rows(z * get(gs, k).astype(f32)),
        )

    sums = over(step_down, (zero(model), zero(model), zero(model)))
    place.spread(stat_d, jnp.concatenate(sums + (grad_sum,), axis=0), send.at[2], recv.at[2])

    def fill_down(k, _):
        put(slope_up, k, slope_of(get(zu, k) * a_u + b_u))
        return 0

    over(fill_down, 0)
    gram_sum.scatter()
    got = place.collect(stat_d, recv.at[2])
    center_d, scale_d, a_d, b_d = norm_parts(got[0:1], got[1:2], total, down_gain, down_shift)
    down_shift_grad = got[3:4]
    down_gain_grad, alpha, slant, level = back_parts(got[3:4], got[2:3], total, down_gain, center_d, scale_d)

    def step_back_down(k, carry):
        dz = get(gs, k).astype(f32) * alpha - get(zd, k) * slant - jnp.where(kept(k, model), level, 0.0)
        dz = dz.astype(bf)
        put(dzd, k, dz)
        grad = dot_nt(dz, wd) * get(slope_up, k).astype(f32)
        put(gu, k, grad)
        return carry[0] + total_rows(grad), carry[1] + total_rows(grad * get(zu, k))

    sums = over(step_back_down, (zero(hidden), zero(hidden)))
    place.spread(stat_bu, jnp.concatenate(sums, axis=0), send.at[3], recv.at[3])

    down_grad = dot_tn(hid[...].reshape(images * ROWS, hidden), dzd[...].reshape(images * ROWS, model))
    down_steps[0][...] = down_grad.reshape(down_steps[0].shape).astype(bf)
    down_sum.swap()

    def fill_back_down(k, carry):
        grad = get(gu, k)
        carry = carry + dot_tn(get(low, k), grad.astype(bf))
        put(gm, k, get(gs, k).astype(f32) + dot_nt((grad * a_u).astype(bf), wu))
        return carry

    up_raw = over(fill_back_down, jnp.zeros((model, hidden), f32))
    down_sum.scatter()
    gram_sum.share()
    got = place.collect(stat_bu, recv.at[3])
    up_shift_grad = got[0:1]
    up_gain_grad, alpha_u, slant_u, level_u = back_parts(got[0:1], got[1:2], total, up_gain, center_u, scale_u)
    mix = dot_nt((wu.astype(f32) * slant_u).astype(bf), wu).astype(bf)
    high, rest = split_low(jnp.broadcast_to(level_u, (8, hidden)))
    lift = (dot_nt(high, wu) + dot_nt(rest, wu))[:1]

    def step_back_up(k, carry):
        grad = get(gm, k) - dot_nn(get(low, k), mix) - jnp.where(kept(k, model), lift, 0.0)
        put(gm, k, grad)
        part = pl.ds(k * group, group)
        copy(gm.at[part], gm_out.at[part], 8 + chunks + k).start()
        return carry[0] + total_rows(grad), carry[1] + total_rows(grad * get(zo, k))

    sums = over(step_back_up, (zero(model), zero(model)))
    place.spread(stat_bo, jnp.concatenate(sums, axis=0), send.at[4], recv.at[4])
    up_grad = up_raw * alpha_u - precise(low_gram, wu) * slant_u - outer(low_sum, level_u)
    up_steps[0][...] = up_grad.reshape(up_steps[0].shape).astype(bf)
    up_sum.swap()
    out_mean = down_shift_grad / total

    def fill_back_up(k, carry):
        centered = jnp.where(kept(k, model), get(gm, k) - out_mean, 0.0).astype(bf)
        return carry + dot_tn(get(act, k), centered)

    act_g = over(fill_back_up, jnp.zeros((act.shape[2], model), f32))
    up_sum.scatter()
    for image in range(images):
        row = lax.broadcasted_iota(jnp.int32, (ROWS, model), 0)
        value = xs[image].astype(f32) + zo[image] * a_o + zd[image] * a_d + (b_o + b_d)
        value = jnp.where(row < limits_of(class_ref[image]), value, 0.0)
        put_image(wide, image, images, value)
    for k in range(wide.shape[0]):
        out[:, 128 * k : 128 * k + 128] = wide[k].astype(bf)
    out_copy = copy(out, out_out, 5)
    out_copy.start()
    own_gram[...] = gram_sum.result()
    leave(7)
    got = place.collect(stat_bo, recv.at[4])
    out_shift_grad = got[0:1]
    out_gain_grad, alpha_o, slant_o, level_o = back_parts(got[0:1], got[1:2], total, out_gain, center_o, scale_o)

    out_grad = act_g * alpha_o - act_z * slant_o
    grad_out[0][...] = out_grad.reshape(grad_out[0].shape).astype(bf)
    leave(3)
    vec_out[...] = jnp.concatenate(
        [
            pad_lanes(v, hidden)
            for v in (
                out_gain_grad,
                out_shift_grad,
                up_gain_grad,
                up_shift_grad,
                down_gain_grad,
                down_shift_grad,
                x_mean,
                zero(hidden),
            )
        ],
        axis=0,
    )
    leave(6)

    def step_back_out(k, _):
        dz = get(gm, k) * alpha_o - get(zo, k) * slant_o - jnp.where(kept(k, model), level_o, 0.0)
        dz = dz.astype(bf)
        put(gatt, k, dot_nt(dz, wo) * get(slope_att, k).astype(f32))
        part = pl.ds(k * group, group)
        copy(gatt.at[part], gatt_out.at[part], 8 + 2 * chunks + k).start()
        return 0

    over(step_back_out, 0)
    grad_out[2][...] = down_sum.gathered()
    leave(5)
    down_sum.settle((0, 1))
    grad_out[1][...] = up_sum.gathered()
    leave(4)
    up_sum.settle((0, 1))

    for k, stat in enumerate((stat_o, stat_u, stat_d, stat_bu, stat_bo)):
        place.settle(stat, send.at[k])
    gram_sum.settle()

    def finish(k, _):
        part = pl.ds(k * group, group)
        copy(gm.at[part], gm_out.at[part], 8 + chunks + k).wait()
        copy(gatt.at[part], gatt_out.at[part], 8 + 2 * chunks + k).wait()
        return 0

    over(finish, 0)
    out_copy.wait()


def half_steps(shape):
    halved = pltpu.VMEM(shape[:2] + (shape[2] // 2,), jnp.bfloat16)
    return [pltpu.VMEM(shape, jnp.bfloat16)] + [halved] * 3 + [pltpu.SemaphoreType.DMA((2,))] * 2


def middle_call(dp_size, fs_size, classes, attended, xs, cotangent, weights, vec, gram):
    images, model, feature, hidden = xs.shape[0], xs.shape[2], attended.shape[2], weights[1].shape[2]
    group = 2 if images % 2 == 0 else 1
    chunks = images // group
    devices = dp_size * fs_size
    own = model // fs_size
    bf, f32 = jnp.bfloat16, jnp.float32

    def rows(width, kind):
        return pltpu.VMEM((images, ROWS, width), kind)

    out_shape = (
        [
            jax.ShapeDtypeStruct(cotangent.shape, bf),
            jax.ShapeDtypeStruct((images, ROWS, feature), bf),
            jax.ShapeDtypeStruct((images, ROWS, model), f32),
        ]
        + [jax.ShapeDtypeStruct(weights[0].shape, bf)]
        + [jax.ShapeDtypeStruct((w.shape[1], w.shape[2] // 2), bf) for w in weights[1:]]
        + [jax.ShapeDtypeStruct((8, hidden), f32), jax.ShapeDtypeStruct((own, model), f32)]
    )
    args = (classes, attended, xs, cotangent, *weights, vec, gram)
    ins, outs = (7, 8), (3, 4, 5, 6, 7)
    return pl.pallas_call(
        staged(functools.partial(middle_kernel, dp_size, fs_size, group), ins, outs, len(args)),
        out_shape=out_shape,
        in_specs=[SMEM] + [ANY] * 8,
        out_specs=[ANY] * 8,
        scratch_shapes=[
            rows(feature, bf),
            rows(model, bf),
            pltpu.VMEM(cotangent.shape, bf),
        ]
        + [pltpu.VMEM(w.shape, bf) for w in weights]
        + [
            rows(model, bf),
            rows(feature, bf),
            rows(feature, bf),
            rows(model, f32),
            rows(model, bf),
            rows(hidden, f32),
            rows(hidden, bf),
            rows(hidden, bf),
            rows(model, f32),
            rows(model, bf),
            rows(hidden, f32),
            rows(model, f32),
            pltpu.VMEM(cotangent.shape, bf),
            rows(feature, bf),
            pltpu.VMEM((model // 128, cotangent.shape[0], 128), f32),
            pltpu.VMEM((devices, 3, model), f32),
            pltpu.VMEM((devices, 2, hidden), f32),
            pltpu.VMEM((devices, 4, model), f32),
            pltpu.VMEM((devices, 2, hidden), f32),
            pltpu.VMEM((devices, 2, model), f32),
            pltpu.SemaphoreType.DMA((5,)),
            pltpu.SemaphoreType.DMA((5,)),
            pltpu.SemaphoreType.DMA((8 + 3 * chunks,)),
            pltpu.VMEM((fs_size, own, model), bf),
        ]
        + [pltpu.VMEM((fs_size, own, model // 2), bf)] * 3
        + [
            pltpu.VMEM((dp_size, own, model // 2), bf),
            pltpu.SemaphoreType.DMA((3,)),
            pltpu.SemaphoreType.DMA((3,)),
        ]
        + half_steps(weights[2].shape)
        + half_steps(weights[1].shape)
        + stage_scratch(ins, outs, args, out_shape),
        compiler_params=pltpu.CompilerParams(
            collective_id=1, has_side_effects=True, vmem_limit_bytes=58 * 2**20
        ),
    )(*args)


def last_kernel(dp_size, fs_size, group, arrive, leave, *refs):
    class_ref, xs_in, gmix_in, gm_in, places = refs[:5]
    acc_in, grad_in, part_in = refs[5:8], refs[8:9], refs[9:11]
    wq_buf, raw_ref, sum_ref, gram_ref, vec_ref, lines_ref = refs[11:17]
    ig_out, table_out, own_out, vec_out = refs[17], refs[18], refs[19:23], refs[23]
    refs = refs[:27] + (None,) + refs[27:]
    xs, gmix, gm, _, ig, res = refs[24:30]
    acc, full = refs[30:33], refs[33:35]
    steps = [refs[35 + 4 * k : 39 + 4 * k] for k in range(2)]
    thirds = refs[43:45]
    stat, stat_t, stat_c, stat_tc = refs[45:49]
    send, recv, local, send_r, recv_r = refs[49:54]
    place = Place(dp_size, fs_size)
    images = xs.shape[0]
    chunks = images // group
    size = group * ROWS
    f32, bf = jnp.float32, jnp.bfloat16
    model, width = xs.shape[2], gmix.shape[2]

    def copy(source, target, at):
        return pltpu.make_async_copy(source, target, local.at[at])

    grad_loads = [copy(grad_in[k], full[1 + k], k) for k in range(1)]
    mix_load = copy(gmix_in, gmix, 3)
    table_loads = [copy(acc_in[k], acc[k], 5 + k) for k in range(3)]
    late_loads = [copy(xs_in, xs, 8), copy(gm_in, gm, 9)]
    place.greet()
    for load in grad_loads + [mix_load] + table_loads + late_loads:
        load.start()
    reduces = [Reduce(place, full[k], *steps[k], send_r.at[k], recv_r.at[k]) for k in range(2)]
    shared = [
        Reduce(place, None, None, thirds[k], None, thirds[k], send_r.at[2 + k], recv_r.at[2 + k]) for k in range(2)
    ]

    def get(ref, k):
        return ref[pl.ds(k * group, group)].reshape(size, ref.shape[2])

    def put(ref, k, value):
        ref[pl.ds(k * group, group)] = value.astype(ref.dtype).reshape(group, ROWS, ref.shape[2])

    def kept(k, lanes):
        row = lax.broadcasted_iota(jnp.int32, (ROWS, lanes), 0)
        return jnp.concatenate([row < limits_of(class_ref[k * group + j]) for j in range(group)], axis=0)

    arrive(11, 12, 13, 15, 16)
    total = vec_ref[10:11, :1]
    gain, scale, center = vec_ref[0:1, :], vec_ref[8:9, :], vec_ref[9:10, :]
    x_mean = lines_ref[6:7, :model]
    weight = flat_weight(wq_buf)
    weight_f = weight.astype(f32)
    raw = raw_ref[...]
    grad_sum = total_rows(sum_ref[...])
    grad_z = total_rows(raw * weight_f)
    full[0][...] = (raw - outer(x_mean, grad_sum)).reshape(full[0].shape).astype(bf)
    for load in grad_loads:
        load.wait()
    place.meet()
    reduces[0].swap()
    place.spread_pair(stat, jnp.concatenate([grad_sum, grad_z], axis=0), send.at[0], recv.at[0])
    reduces[1].swap()
    alpha = scale * gain
    place.spread_chips(stat_c, place.collect_pair(stat, recv.at[0]), send.at[2], recv.at[2])
    for k in range(2):
        reduces[k].scatter()
    arrive(9, 10)
    for k in range(2):
        shared[k].share(part_in[k][...])
    for load in table_loads:
        load.wait()
    arrive(4, 14)
    place.spread_pair(stat_t, table_sums(places[...], acc), send.at[1], recv.at[1])
    mix_load.wait()
    for k in range(chunks):
        put(ig, k, dot_nt((get(gmix, k).astype(f32) * alpha).astype(bf), weight))
    place.spread_chips(stat_tc, place.collect_pair(stat_t, recv.at[1]), send.at[3], recv.at[3])
    for load in late_loads:
        load.wait()

    got = place.collect_chips(stat_c, recv.at[2])
    gain_grad, alpha, slant, level = back_parts(got[0:1], got[1:2], total, gain, center, scale)
    mix = dot_nt((weight_f * slant).astype(bf), weight).astype(bf)
    high, rest = split_low(jnp.broadcast_to(level, (8, width)))
    lift = (dot_nt(high, weight) + dot_nt(rest, weight))[:1]
    vec_out[...] = jnp.concatenate(
        [restore(gain_grad), restore(got[0:1]), jnp.zeros((6, width), f32)], axis=0
    )
    leave(6)
    for k in range(2):
        reduces[k].share()
    for k in range(chunks):
        value = get(gm, k) + get(ig, k) - dot_nn(get(xs, k), mix) - jnp.where(kept(k, model), lift, 0.0)
        for j in range(group):
            put_image(res, k * group + j, images, value[j * ROWS : (j + 1) * ROWS])
    res_copies = [copy(res.at[k], ig_out.at[:, pl.ds(128 * k, 128)], 10 + k) for k in range(model // 128)]
    for res_copy in res_copies:
        res_copy.start()
    own_out[0][...] = restore(reduces[0].result() * alpha - precise(gram_ref[...], weight) * slant)
    own_out[1][...] = reduces[1].result()
    for k in range(2):
        own_out[2 + k][...] = shared[k].result()
    table_out[...] = place.collect_chips(stat_tc, recv.at[3])
    for k in range(2):
        reduces[k].settle()
        shared[k].settle((2,))
    place.settle_pair(stat, send.at[0])
    place.settle_pair(stat_t, send.at[1])
    place.settle_chips(stat_c, send.at[2])
    place.settle_chips(stat_tc, send.at[3])
    for res_copy in res_copies:
        res_copy.wait()


def last_call(dp_size, fs_size, classes, xs, gmix, gm, places, accs, grads, wq, raw, sums, gram, vec, lines):
    images, model, width = xs.shape[0], xs.shape[2], gmix.shape[2]
    group = 2 if images % 2 == 0 else 1
    devices = dp_size * fs_size
    bf, f32 = jnp.bfloat16, jnp.float32
    shapes = [wq.shape, grads[0].shape]
    own_shapes = [s[1:] for s in shapes] + [(g.shape[0], 2 * g.shape[1]) for g in grads[1:]]
    steps = []
    for s in shapes:
        half = s[2] // 2
        steps += [
            pltpu.VMEM((fs_size, s[1], half), bf),
            pltpu.VMEM((fs_size, s[1], half), bf),
            pltpu.VMEM((fs_size, s[1], half), bf),
            pltpu.VMEM((dp_size, s[1], half), bf),
        ]
    order = []
    for k in range(2):
        order += [steps[4 * k], steps[4 * k + 1], steps[4 * k + 2], steps[4 * k + 3]]
    out_shape = (
        [jax.ShapeDtypeStruct((SLOT * images, model), f32), jax.ShapeDtypeStruct((HEADS, 384), f32)]
        + [jax.ShapeDtypeStruct(s, f32) for s in own_shapes]
        + [jax.ShapeDtypeStruct((8, width), f32)]
    )
    args = (classes, xs, gmix, gm, places, *accs, *grads, wq, raw, sums, gram, vec, lines)
    ins, outs = (13, 15, 16, 11, 12, 9, 10, 4, 14), (1, 2, 3, 4, 5, 6)
    return pl.pallas_call(
        staged(functools.partial(last_kernel, dp_size, fs_size, group), ins, outs, len(args)),
        out_shape=out_shape,
        in_specs=[SMEM] + [ANY] * 16,
        out_specs=[ANY] * 7,
        scratch_shapes=[
            pltpu.VMEM(xs.shape, bf),
            pltpu.VMEM(gmix.shape, bf),
            pltpu.VMEM(gm.shape, f32),
            pltpu.VMEM(gm.shape, f32),
            pltpu.VMEM((model // 128, SLOT * images, 128), f32),
        ]
        + [pltpu.VMEM(a.shape, bf) for a in accs]
        + [pltpu.VMEM(s, bf) for s in shapes]
        + order
        + [
            pltpu.VMEM((dp_size,) + grads[1].shape, bf),
            pltpu.VMEM((dp_size,) + grads[2].shape, bf),
            pltpu.VMEM((2, 2, width), f32),
            pltpu.VMEM((2, HEADS, 384), f32),
            pltpu.VMEM((devices // 2, 2, width), f32),
            pltpu.VMEM((devices // 2, HEADS, 384), f32),
            pltpu.SemaphoreType.DMA((4,)),
            pltpu.SemaphoreType.DMA((4,)),
            pltpu.SemaphoreType.DMA((10 + model // 128,)),
            pltpu.SemaphoreType.DMA((4, 3)),
            pltpu.SemaphoreType.DMA((4, 3)),
        ]
        + stage_scratch(ins, outs, args, out_shape),
        compiler_params=pltpu.CompilerParams(
            collective_id=2, has_side_effects=True, vmem_limit_bytes=56 * 2**20
        ),
    )(*args)

def shards(
    inputs,
    classes,
    offset_table,
    bias_table,
    qkv_weight,
    qkv_gain,
    qkv_shift,
    out_weight,
    out_gain,
    out_shift,
    up_weight,
    up_gain,
    up_shift,
    down_weight,
    down_gain,
    down_shift,
    cotangent,
):
    sizes = lax.axis_size("dp"), lax.axis_size("fsdp")
    images, _, model = inputs.shape

    def by_slot(array):
        return jnp.swapaxes(array, 0, 1).reshape(SLOT * images, model)

    def by_image(array):
        return jnp.swapaxes(array.reshape(SLOT, images, model), 0, 1)

    first = first_call(
        *sizes,
        classes,
        by_slot(inputs),
        offset_table,
        bias_table,
        (qkv_weight, out_weight, up_weight, down_weight),
        (qkv_gain, qkv_shift, out_gain, out_shift, up_gain, up_shift, down_gain, down_shift),
    )
    mixed, xs, biases, weights, vec, gram, places = first[0], first[1], first[2:5], first[5:9], *first[9:12]
    attended, probs, shares = attend_call(classes, mixed, biases)
    middle = middle_call(*sizes, classes, attended, xs, by_slot(cotangent), weights[1:], vec, gram)
    output, grad_att, grad_middle, grads, lines, own_gram = *middle[:3], middle[3:6], middle[6], middle[7]
    back = back_call(sizes[1], classes, mixed, probs, shares, grad_att, attended, xs, lines, output)
    grad_mixed, raw, sums, accs, own_lines, output = *back[:3], back[3:6], back[6:12], back[12]
    last = last_call(
        *sizes,
        classes,
        xs,
        grad_mixed,
        grad_middle,
        places,
        accs,
        grads,
        weights[0],
        raw,
        sums,
        own_gram,
        vec,
        lines,
    )
    input_grad, table_grad, *rest = end_call(sizes[1], last[0], last[1], last[2:6], last[6])
    own_lines = [line.reshape(-1) for line in (*own_lines, *rest[4:])]
    return (
        by_image(output),
        by_image(input_grad),
        table_grad,
        rest[0],
        *own_lines[6:8],
        rest[1],
        *own_lines[0:2],
        rest[2],
        *own_lines[2:4],
        rest[3],
        *own_lines[4:6],
    )


def solution(mesh):
    placed = (
        P(("dp", "fsdp"), None, None),
        P(("dp", "fsdp")),
        P(),
        P(),
        P("fsdp", None),
        P("fsdp"),
        P("fsdp"),
        P("fsdp", None),
        P("fsdp"),
        P("fsdp"),
        P("fsdp", None),
        P("fsdp"),
        P("fsdp"),
        P("fsdp", None),
        P("fsdp"),
        P("fsdp"),
        P(("dp", "fsdp"), None, None),
    )
    return jax.shard_map(
        shards,
        mesh=mesh,
        in_specs=placed,
        out_specs=(
            P(("dp", "fsdp"), None, None),
            P(("dp", "fsdp"), None, None),
            P(),
            P("fsdp", None),
            P("fsdp"),
            P("fsdp"),
            P("fsdp", None),
            P("fsdp"),
            P("fsdp"),
            P("fsdp", None),
            P("fsdp"),
            P("fsdp"),
            P("fsdp", None),
            P("fsdp"),
            P("fsdp"),
        ),
        check_vma=False,
    )
```

```python
import functools

import jax
import jax.numpy as jnp
from jax import lax
from jax.experimental import pallas as pl
from jax.experimental.pallas import tpu as pltpu
from jax.sharding import PartitionSpec as P

HEADS = 4
KEY = 32
VALD = 128
GRID = 18
CLASSES = 3
SLOT = 324
NOFF = 324


EPS = 1e-05
LOG2E = 1.4426950408889634
LN2 = 0.6931471805599453
ROWS = 336
PARTS = ((10, 100, 112, 128), (14, 196, 208, 256), (18, 324, 336, 384))
VMEM = pl.BlockSpec(memory_space=pltpu.VMEM)


def dot_nn(left, right):
    return jnp.dot(left, right, preferred_element_type=jnp.float32)


def dot_nt(left, right):
    return lax.dot_general(left, right, (((1,), (1,)), ((), ())), preferred_element_type=jnp.float32)


def dot_tn(left, right):
    return lax.dot_general(left, right, (((0,), (0,)), ((), ())), preferred_element_type=jnp.float32)


def pad_rows(value, rows):
    if value.shape[0] == rows:
        return value
    return jnp.concatenate([value, jnp.zeros((rows - value.shape[0], value.shape[1]), value.dtype)], axis=0)


def pad_lanes(value, lanes):
    if value.shape[1] == lanes:
        return value
    return jnp.concatenate([value, jnp.zeros((value.shape[0], lanes - value.shape[1]), value.dtype)], axis=1)


def bias_tables(off_ref, table_ref, index_ref, outs, pair):
    tables = []
    for side in range(2):
        row = pad_lanes(table_ref[pl.ds(2 * pair + side, 1), :], 384) * LOG2E
        tables.append([jnp.broadcast_to(row[:, 128 * k : 128 * k + 128], (8, 128)) for k in range(3)])
    index_ref[...] = jnp.zeros_like(index_ref)
    for number, (_, amount, rows, lanes) in enumerate(PARTS):
        index_ref[:SLOT, :SLOT] = off_ref[number]

        tiles = rows // 8 // (number + 1)

        def strip(step, _, number=number, amount=amount, lanes=lanes, tiles=tiles, out=outs[number]):
            for line in range(tiles):
                at = pl.multiple_of((step * tiles + line) * 8, 8)
                for block in range(lanes // 128):
                    index = index_ref[pl.ds(at, 8), 128 * block : 128 * block + 128]
                    low = index & 127
                    part = index >> 7
                    valid = lax.broadcasted_iota(jnp.int32, (8, 128), 1) + 128 * block < amount
                    for side in range(2):
                        found = [
                            jnp.take_along_axis(tables[side][k], low, axis=1, mode="promise_in_bounds")
                            for k in range(3 if number == 2 else 2)
                        ]
                        value = jnp.where(part == 0, found[0], found[1])
                        if number == 2:
                            value = jnp.where(part == 2, found[2], value)
                        column = side * lanes + 128 * block
                        out[pair, pl.ds(at, 8), column : column + 128] = jnp.where(valid, value, -1e30)
            return 0

        lax.fori_loop(0, number + 1, strip, 0)


def head_keys(keys, pair, lanes):
    owner = lax.broadcasted_iota(jnp.int32, keys.shape, 1) // KEY
    zero = jnp.zeros_like(keys)
    return jnp.concatenate(
        [pad_rows(jnp.where(owner == 2 * pair + side, keys, zero), lanes) for side in range(2)], axis=0
    )


def pair_values(values, lanes):
    zero = jnp.zeros((lanes, VALD), values.dtype)
    top = jnp.concatenate([pad_rows(values[:, :VALD], lanes), zero], axis=1)
    low = jnp.concatenate([zero, pad_rows(values[:, VALD:], lanes)], axis=1)
    return jnp.concatenate([top, low], axis=0)


def by_eight(value):
    return jnp.sum(value.reshape(value.shape[0] // 8, 8, value.shape[1]), axis=0)


def attend_kernel(class_ref, mixed_in, bias_in0, bias_in1, bias_in2, att_out, p_out, r_out, *held):
    mixed, biases, att, p, r = held[0], held[1:4], held[4], held[5], held[6]
    sem_in, sem_bias, sem_out, score = held[7:11]
    images = mixed.shape[0]

    def load(at):
        return pltpu.make_async_copy(mixed_in.at[at], mixed.at[at], sem_in.at[at])

    def load_bias(number):
        source = (bias_in0, bias_in1, bias_in2)[number]
        return pltpu.make_async_copy(source, biases[number], sem_bias.at[number])

    def store(at, rows, lanes):
        part = (at, pl.ds(0, rows), pl.ds(0, 4 * lanes))
        return (
            pltpu.make_async_copy(p.at[part], p_out.at[part], sem_out.at[0, at]),
            pltpu.make_async_copy(r.at[part[:2]], r_out.at[part[:2]], sem_out.at[1, at]),
        )

    def store_att(at):
        return pltpu.make_async_copy(att.at[at], att_out.at[at], sem_out.at[2, at])

    def absent(number, before):
        found = jnp.bool_(True)
        for k in range(images):
            found = jnp.logical_and(found, jnp.logical_or(class_ref[k] != number, k >= before))
        return found

    load(0).start()
    for number in (2, 1, 0):
        load_bias(number).start()
    for k in range(1, images):
        load(k).start()

    def one(at, _):
        load(at).wait()
        kind = class_ref[at]
        for number, (_, amount, rows, lanes) in enumerate(PARTS):

            @pl.when(jnp.logical_and(kind == number, absent(number, at)))
            def _(number=number):
                load_bias(number).wait()

            @pl.when(kind == number)
            def _(amount=amount, rows=rows, lanes=lanes, bias=biases[number]):
                query = mixed[at, :rows, :128]
                keys = mixed[at, :rows, 128:256]
                kept = lax.broadcasted_iota(jnp.int32, (rows, VALD), 0) < amount
                lane = lax.broadcasted_iota(jnp.int32, (rows, 128), 1)
                shares = jnp.zeros((rows, 128), jnp.float32)
                for pair in range(2):
                    score[pair, :rows, : 2 * lanes] = dot_nt(query, head_keys(keys, pair, lanes)) + bias[pair]
                for pair in range(2):
                    scores = score[pair, :rows, : 2 * lanes]
                    parts, inverse = [], []
                    for side in range(2):
                        own = scores[:, side * lanes : (side + 1) * lanes]
                        expo = jnp.exp2(own - jnp.max(own, axis=1, keepdims=True))
                        share = 1.0 / jnp.sum(expo, axis=1, keepdims=True)
                        shares = jnp.where(lane == 2 * pair + side, share, shares)
                        parts.append(expo.astype(jnp.bfloat16))
                        inverse.append(share)
                    both = jnp.concatenate(parts, axis=1)
                    p[at, :rows, 2 * pair * lanes : 2 * (pair + 1) * lanes] = both
                    values = mixed[at, :rows, 256 + 256 * pair : 512 + 256 * pair]
                    sums = dot_nn(both, pair_values(values, lanes))
                    for side in range(2):
                        own = sums[:, side * VALD : (side + 1) * VALD] * inverse[side]
                        spot = (2 * pair + side) * VALD
                        att[at, :rows, spot : spot + VALD] = jnp.where(kept, own, 0.0).astype(jnp.bfloat16)
                r[at, :rows, :] = shares
                if rows < ROWS:
                    att[at, rows:, :] = jnp.zeros((ROWS - rows, att.shape[2]), jnp.bfloat16)
                for copy in store(at, rows, lanes):
                    copy.start()

        store_att(at).start()
        return 0

    lax.fori_loop(0, images, one, 0)

    def finish(at, _):
        for number, (_, _, rows, lanes) in enumerate(PARTS):

            @pl.when(class_ref[at] == number)
            def _(rows=rows, lanes=lanes):
                for copy in store(at, rows, lanes):
                    copy.wait()

        store_att(at).wait()
        return 0

    lax.fori_loop(0, images, finish, 0)
    for number in range(3):

        @pl.when(absent(number, images))
        def _(number=number):
            load_bias(number).wait()


def back_kernel(fs_size, arrive, leave, *refs):
    class_ref, mixed_in, p_in, r_in, g_in, att_in, xs_in, lines_ref, out_in = refs[:9]
    gmix_out, raw_ref, sum_ref, low_accs, own_refs, out_out = refs[9], refs[10], refs[11], refs[12:15], refs[15:21], refs[21]
    mixed, p, r, g, att, xs, gmix = refs[22:29]
    accs, held, out_sems, sem_in, sem_out = refs[29:32], refs[32], refs[33], refs[34], refs[35]
    images = mixed.shape[0]
    out_load = pltpu.make_async_copy(out_in, held, out_sems.at[0])
    out_store = pltpu.make_async_copy(held, out_out, out_sems.at[1])

    def loads(at, rows, lanes):
        part = (at, pl.ds(0, rows), pl.ds(0, 4 * lanes))
        pairs = [(p_in.at[part], p.at[part]), (r_in.at[part[:2]], r.at[part[:2]])]
        pairs += [(a.at[at], b.at[at]) for a, b in ((mixed_in, mixed), (g_in, g), (att_in, att), (xs_in, xs))]
        return [pltpu.make_async_copy(a, b, sem_in.at[k, at]) for k, (a, b) in enumerate(pairs)]

    def store(at):
        return pltpu.make_async_copy(gmix.at[at], gmix_out.at[at], sem_out.at[at])

    def request(at, _):
        for number, (_, _, rows, lanes) in enumerate(PARTS):

            @pl.when(class_ref[at] == number)
            def _(rows=rows, lanes=lanes):
                for copy in loads(at, rows, lanes):
                    copy.start()

        return 0

    lax.fori_loop(0, images, request, 0)
    out_load.start()
    for ref in (*accs, raw_ref, sum_ref):
        ref[...] = jnp.zeros_like(ref)

    def one(at, _):
        kind = class_ref[at]
        for number, (_, amount, rows, lanes) in enumerate(PARTS):

            @pl.when(kind == number)
            def _(rows=rows, lanes=lanes, acc=accs[number]):
                for copy in loads(at, rows, lanes):
                    copy.wait()
                query = mixed[at, :rows, :128]
                keys = mixed[at, :rows, 128:256]
                owner = lax.broadcasted_iota(jnp.int32, (rows, 128), 1) // KEY
                d_query = jnp.zeros((rows, 128), jnp.float32)
                stacked = []
                for pair in range(2):
                    grads, deltas = [], []
                    for side in range(2):
                        head = 2 * pair + side
                        spot = head * VALD
                        grad = g[at, :rows, spot : spot + VALD].astype(jnp.float32) * r[at, :rows, head : head + 1]
                        own = att[at, :rows, spot : spot + VALD].astype(jnp.float32)
                        deltas.append(jnp.sum(grad * own, axis=1, keepdims=True))
                        grads.append(grad.astype(jnp.bfloat16))
                    both = jnp.concatenate(grads, axis=1)
                    values = mixed[at, :rows, 256 + 256 * pair : 512 + 256 * pair]
                    d_probs = dot_nt(both, pair_values(values, lanes))
                    probs = p[at, :rows, 2 * pair * lanes : 2 * (pair + 1) * lanes]
                    low = []
                    for side in range(2):
                        cut = slice(side * lanes, (side + 1) * lanes)
                        d_score = probs[:, cut].astype(jnp.float32) * (d_probs[:, cut] - deltas[side])
                        acc[pair, :, cut] += d_score
                        low.append(d_score.astype(jnp.bfloat16))
                    d_low = jnp.concatenate(low, axis=1)
                    d_query = d_query + dot_nn(d_low, head_keys(keys, pair, lanes))
                    stacked += low
                    tall = jnp.concatenate([probs[:, :lanes], probs[:, lanes:]], axis=0)
                    d_values = dot_tn(tall, pair_values(both, rows))
                    spot = 256 + 256 * pair
                    sum_ref[:, spot : spot + 256] += by_eight(d_values[:rows])
                    gmix[at, :rows, spot : spot + 256] = d_values[:rows].astype(jnp.bfloat16)
                d_keys = sum(
                    jnp.where(owner == head, dot_tn(stacked[head], query)[:rows], 0.0) for head in range(HEADS)
                )
                d_query = d_query * KEY ** (-0.5)
                d_keys = d_keys * LN2
                sum_ref[:, :128] += by_eight(d_query)
                sum_ref[:, 128:256] += by_eight(d_keys)
                gmix[at, :rows, :128] = d_query.astype(jnp.bfloat16)
                gmix[at, :rows, 128:256] = d_keys.astype(jnp.bfloat16)
                raw_ref[...] += dot_tn(xs[at, :rows, :], gmix[at, :rows, :])
                if rows < ROWS:
                    gmix[at, rows:, :] = jnp.zeros((ROWS - rows, gmix.shape[2]), jnp.bfloat16)

        store(at).start()
        return 0

    lax.fori_loop(0, images, one, 0)
    leave(1, 2)
    for low, acc in zip(low_accs, accs):
        low[...] = acc[...].astype(jnp.bfloat16)
    leave(3, 4, 5)
    out_load.wait()
    out_store.start()
    arrive(7)
    place = lax.axis_index("fsdp")
    lines = lines_ref[...]
    for k, ref in enumerate(own_refs):
        width = ref.shape[1]
        ref[...] = pltpu.roll(lines, lines.shape[1] - place * width, 1)[k : k + 1, :width]
    leave(6, 7, 8, 9, 10, 11)

    def finish(at, _):
        store(at).wait()
        return 0

    lax.fori_loop(0, images, finish, 0)
    out_store.wait()


def grid_places(off_ref):
    found = []
    for number, (side_of, amount, _, _) in enumerate(PARTS):
        offsets = off_ref[number]
        row = lax.broadcasted_iota(jnp.int32, (SLOT, 1), 0)
        most = jnp.max(offsets, axis=1, keepdims=True)
        corner = jnp.min(jnp.where(most == (side_of - 1) * (GRID + 1), row, SLOT), axis=0, keepdims=True)
        place = jnp.sum(jnp.where(row == corner, offsets, 0), axis=0, keepdims=True)
        place = jnp.where(lax.broadcasted_iota(jnp.int32, (1, SLOT), 1) < amount, place, -1)
        found.append(jnp.concatenate([place, jnp.full((1, 384 - SLOT), -1, jnp.int32)], axis=1))
    return jnp.concatenate(found + [jnp.full((8 - len(found), 384), -1, jnp.int32)], axis=0)


def one_hot(left, right):
    return (left == right).astype(jnp.float32).astype(jnp.bfloat16)


def table_sums(places, accs):
    zero = (jnp.zeros((8, 128), jnp.float32), jnp.zeros((16, 128), jnp.float32))
    totals = [[zero] * 6 for _ in range(HEADS)]
    for number, (side_of, _, rows, lanes) in enumerate(PARTS):
        pad = 24 if side_of > 16 else 16
        reach = 384 if side_of > 14 else 256
        place = places[number : number + 1, :]
        cell = lax.broadcasted_iota(jnp.int32, (pad * side_of, 1), 0)
        cell_row = (cell * 2731) >> 16 if pad == 24 else cell >> 4
        cell_col = pad - 1 - (cell - pad * cell_row)
        code = jnp.where(cell_col < side_of, cell_row * GRID + cell_col, -2)
        left = one_hot(code, place[:, :rows])
        right = one_hot(lax.broadcasted_iota(jnp.int32, (reach, 1), 0), place[:, :lanes])
        for pair in range(2):
            by_row = dot_nn(left, accs[number][pair]).astype(jnp.bfloat16)
            for side in range(2):
                both = dot_nt(by_row[:, side * lanes : (side + 1) * lanes], right)
                total = totals[2 * pair + side]
                for line in range(side_of):
                    far, near = divmod((GRID - 1 - line) * GRID, 128)
                    part = pad_lanes(both[pad * line : pad * line + pad], reach + 128)
                    if near:
                        part = pltpu.roll(part, near, 1)
                    for k in range(min(reach // 128 + 1, 5 - far)):
                        piece = part[:, 128 * k : 128 * k + 128]
                        top, low = total[far + k]
                        if pad == 24:
                            top = top + piece[:8]
                        total[far + k] = (top, low + piece[pad - 16 :])
    width = 768
    lane = lax.broadcasted_iota(jnp.int32, (24, width), 1)
    ahead = lane - GRID * ((lane * 3641) >> 16) + lax.broadcasted_iota(jnp.int32, (24, width), 0) >= 23
    level, below = [], []
    for head in range(HEADS):
        whole = jnp.concatenate([jnp.concatenate(t, axis=0) for t in totals[head]], axis=1)
        for keep, group in ((ahead, level), (jnp.logical_not(ahead), below)):
            turned = pltpu.roll(jnp.where(keep, whole, 0.0), 0, 1, stride=1, stride_axis=0)
            group.append(jnp.sum(turned, axis=0, keepdims=True))
    spot = lax.broadcasted_iota(jnp.int32, (width, 1), 0) - 23
    target = lax.broadcasted_iota(jnp.int32, (1, 384), 1)
    spot_row = jnp.where(spot >= 0, (spot * 3641) >> 16, -1)
    spot_col = spot - GRID * spot_row
    straight = one_hot(jnp.abs(spot_row - (GRID - 1)) * GRID + spot_col, target)
    back = one_hot(jnp.abs(spot_row + 1 - (GRID - 1)) * GRID + GRID - spot_col, target)
    out = jnp.zeros((HEADS, 384), jnp.float32)
    for group, fold in ((level, straight), (below, back)):
        high, low = split_low(jnp.concatenate(group, axis=0))
        spread = dot_nn(jnp.concatenate([high.astype(jnp.float32), low.astype(jnp.float32)], axis=0).astype(jnp.bfloat16), fold)
        out = out + spread[:HEADS] + spread[HEADS:]
    return out


def attend_call(classes, mixed, biases):
    images = mixed.shape[0]
    bf, f32 = jnp.bfloat16, jnp.float32
    shapes = [
        jax.ShapeDtypeStruct((images, ROWS, 512), bf),
        jax.ShapeDtypeStruct((images, ROWS, 1536), bf),
        jax.ShapeDtypeStruct((images, ROWS, 128), f32),
    ]
    return pl.pallas_call(
        attend_kernel,
        in_specs=[SMEM] + [ANY] * 4,
        out_specs=[ANY] * 3,
        out_shape=shapes,
        scratch_shapes=[pltpu.VMEM(a.shape, a.dtype) for a in (mixed, *biases, *shapes)]
        + [
            pltpu.SemaphoreType.DMA((images,)),
            pltpu.SemaphoreType.DMA((3,)),
            pltpu.SemaphoreType.DMA((3, images)),
            pltpu.VMEM((2, ROWS, 768), f32),
        ],
        compiler_params=pltpu.CompilerParams(vmem_limit_bytes=60 * 2**20),
    )(classes, mixed, *biases)


def back_call(fs_size, classes, mixed, probs, shares, grad, attended, xs, lines, output):
    images, model = mixed.shape[0], xs.shape[2]
    bf, f32 = jnp.bfloat16, jnp.float32
    tables = [(2, r, 2 * l) for _, _, r, l in PARTS]
    widths = [w // fs_size for w in (model, model, lines.shape[1], lines.shape[1], model, model)]
    args = (classes, mixed, probs, shares, grad, attended, xs, lines, output)
    out_shape = (
        [
            jax.ShapeDtypeStruct((images, ROWS, 768), bf),
            jax.ShapeDtypeStruct((model, 768), f32),
            jax.ShapeDtypeStruct((8, 768), f32),
        ]
        + [jax.ShapeDtypeStruct(s, bf) for s in tables]
        + [jax.ShapeDtypeStruct((1, w), f32) for w in widths]
        + [jax.ShapeDtypeStruct(output.shape, bf)]
    )
    ins, outs = (7,), tuple(range(1, 12))
    return pl.pallas_call(
        staged(functools.partial(back_kernel, fs_size), ins, outs, len(args)),
        in_specs=[SMEM] + [ANY] * 8,
        out_specs=[ANY] * 13,
        out_shape=out_shape,
        scratch_shapes=[pltpu.VMEM(a.shape, a.dtype) for a in (mixed, probs, shares, grad, attended, xs, out_shape[0])]
        + [pltpu.VMEM(s, f32) for s in tables]
        + [
            pltpu.VMEM(output.shape, bf),
            pltpu.SemaphoreType.DMA((2,)),
            pltpu.SemaphoreType.DMA((6, images)),
            pltpu.SemaphoreType.DMA((images,)),
        ]
        + stage_scratch(ins, outs, args, out_shape),
        compiler_params=pltpu.CompilerParams(vmem_limit_bytes=60 * 2**20),
    )(*args)


def end_kernel(*refs):
    ins, outs = refs[:7], refs[7:15]
    held, kept, table_in, table, lines_in, own_lines = refs[15], refs[16:20], refs[20], refs[21], refs[22], refs[23:25]
    sem_in, sem_out = refs[25:27]
    step = held.shape[0] // 4
    pairs = [(ins[0].at[pl.ds(k * step, step)], held.at[pl.ds(k * step, step)], outs[0]) for k in range(4)]
    pairs = [(a, b, c.at[pl.ds(k * step, step)]) for k, (a, b, c) in enumerate(pairs)]
    pairs = [(ins[1], table_in, None), (ins[6], lines_in, None)] + pairs
    pairs += [(ins[2 + k], kept[k], outs[2 + k]) for k in range(4)]
    loads = [pltpu.make_async_copy(a, b, sem_in.at[k]) for k, (a, b, _) in enumerate(pairs)]
    stores = [pltpu.make_async_copy(b, c, sem_out.at[k]) for k, (_, b, c) in enumerate(pairs) if c is not None]
    for load in loads:
        load.start()
    loads[0].wait()
    loads[1].wait()
    table[...] = table_in[:, :NOFF]
    spot = lax.axis_index("fsdp")
    lines = lines_in[...]
    for k, ref in enumerate(own_lines):
        width = ref.shape[1]
        ref[...] = pltpu.roll(lines, lines.shape[1] - spot * width, 1)[k : k + 1, :width]
    for k, (a, b) in enumerate(((table, outs[1]), (own_lines[0], outs[6]), (own_lines[1], outs[7]))):
        stores.append(pltpu.make_async_copy(a, b, sem_out.at[len(pairs) + k]))
        stores[-1].start()
    for load, store in zip(loads[2:], stores):
        load.wait()
        store.start()
    for store in stores:
        store.wait()


def end_call(fs_size, input_grad, table, owned, lines):
    f32 = jnp.float32
    width = lines.shape[1] // fs_size
    shapes = [input_grad.shape, (HEADS, NOFF)] + [o.shape for o in owned] + [(1, width)] * 2
    held = [input_grad.shape] + [o.shape for o in owned] + [table.shape, (HEADS, NOFF), lines.shape] + [(1, width)] * 2
    return pl.pallas_call(
        end_kernel,
        out_shape=[jax.ShapeDtypeStruct(s, f32) for s in shapes],
        in_specs=[ANY] * 7,
        out_specs=[ANY] * 8,
        scratch_shapes=[pltpu.VMEM(s, f32) for s in held]
        + [pltpu.SemaphoreType.DMA((13,)), pltpu.SemaphoreType.DMA((13,))],
        compiler_params=pltpu.CompilerParams(vmem_limit_bytes=60 * 2**20),
    )(input_grad, table, *owned, lines)


MESH = pl.DeviceIdType.MESH
ANY = pl.BlockSpec(memory_space=pl.ANY)
SMEM = pl.BlockSpec(memory_space=pltpu.SMEM)


class Place:
    def __init__(self, dp_size, fs_size):
        self.dp_size, self.fs_size = dp_size, fs_size
        self.size = dp_size * fs_size
        self.dp, self.fs = lax.axis_index("dp"), lax.axis_index("fsdp")
        self.me = self.dp * fs_size + self.fs
        self.core = lax.rem(self.dp, 2)
        self.partner = (self.dp + 1 - 2 * self.core, self.fs)

    def other(self, step, cores=2):
        number = self.size // 2 * cores - step
        rows, lines = self.fs_size // 2, self.dp_size // 2
        core = lax.rem(self.core + lax.rem(number, cores), 2)
        number = number // cores
        line = lax.rem(self.dp // 2 + lax.rem(number // rows, lines), lines)
        row = lax.rem(self.fs // 2 + lax.rem(number, rows), rows)
        return (2 * line + core, 2 * row + lax.rem(self.fs + number // (rows * lines), 2))

    def all_others(self, cores=2):
        rows, lines = self.fs_size // 2, self.dp_size // 2
        row_at = [2 * lax.rem(self.fs // 2 + d, rows) for d in range(rows)]
        line_at = [2 * lax.rem(self.dp // 2 + d, lines) for d in range(lines)]
        side_at = [lax.rem(self.fs, 2), 1 - lax.rem(self.fs, 2)]
        core_at = [self.core, 1 - self.core]
        steps = [(z, x, y, c) for z in range(rows) for x in range(2) for y in range(lines) for c in range(cores)][1:]
        steps.sort(key=lambda s: -(20 * (s[0] > 0) + 10 * s[1] + 10 * (s[2] > 0) + s[3]))
        return [(line_at[y] + core_at[c], row_at[z] + side_at[x]) for z, x, y, c in steps]

    def greet(self):
        barrier = pltpu.get_barrier_semaphore()

        def signal(step, _):
            pl.semaphore_signal(barrier, inc=1, device_id=self.other(step), device_id_type=MESH)
            return 0

        lax.fori_loop(1, self.size, signal, 0)

    def meet(self):
        pl.semaphore_wait(pltpu.get_barrier_semaphore(), self.size - 1)

    def spread(self, buf, value, send, recv):
        buf[self.me] = value

        if self.size <= 64:
            for device in self.all_others():
                push(buf.at[self.me], buf.at[self.me], send, recv, device)
            return

        def start(step, _):
            push(buf.at[self.me], buf.at[self.me], send, recv, self.other(step))
            return 0

        lax.fori_loop(1, self.size, start, 0)

    def collect(self, buf, recv):
        await_bytes(buf.at[pl.ds(0, self.size - 1)], recv)
        return jnp.sum(buf[...], axis=0)

    def spread_pair(self, buf, value, send, recv):
        buf[self.core] = value
        part = buf.at[self.core]
        push(part, part, send, recv, self.partner)

    def collect_pair(self, buf, recv):
        await_bytes(buf.at[0], recv)
        return buf[0] + buf[1]

    def spread_chips(self, buf, value, send, recv):
        chips = self.size // 2
        mine = (self.dp // 2) * self.fs_size + self.fs
        buf[mine] = value
        if self.size <= 64:
            for device in self.all_others(1):
                push(buf.at[mine], buf.at[mine], send, recv, device)
            return

        def start(step, _):
            push(buf.at[mine], buf.at[mine], send, recv, self.other(step, 1))
            return 0

        lax.fori_loop(1, chips, start, 0)

    def collect_chips(self, buf, recv):
        await_bytes(buf.at[pl.ds(0, self.size // 2 - 1)], recv)
        return jnp.sum(buf[...], axis=0)

    def settle_pair(self, buf, send):
        await_bytes(buf.at[0], send)

    def settle_chips(self, buf, send):
        await_bytes(buf.at[pl.ds(0, self.size // 2 - 1)], send)

    def settle(self, buf, send):
        await_bytes(buf.at[pl.ds(0, self.size - 1)], send)


def push(source, target, send, recv, device):
    pltpu.make_async_remote_copy(
        src_ref=source, dst_ref=target, send_sem=send, recv_sem=recv, device_id=device, device_id_type=MESH
    ).start()


def await_bytes(ref, sem):
    pltpu.make_async_copy(ref, ref, sem).wait()


def own_half(place, buf, own):
    half = own.shape[1] // 2
    own = jnp.where(place.core == 0, own[:, :half], own[:, half:])
    buf[place.fs, :, pl.ds(pl.multiple_of(place.core * half, half), half)] = own


def gather_start(place, buf, send, recv):
    half = buf.shape[2] // 2
    part = buf.at[place.fs, :, pl.ds(pl.multiple_of(place.core * half, half), half)]

    def start(step, _):
        push(part, part, send, recv, (place.dp, lax.rem(place.fs + place.fs_size - step, place.fs_size)))
        return 0

    lax.fori_loop(1, place.fs_size, start, 0)


def gather_pass(place, buf, recv, send2, recv2):
    half = buf.shape[2] // 2
    await_bytes(buf.at[pl.ds(0, place.fs_size - 1), :, pl.ds(0, half)], recv)
    part = buf.at[:, :, pl.ds(pl.multiple_of(place.core * half, half), half)]
    push(part, part, send2, recv2, place.partner)


def gather_end(place, buf, recv2):
    half = buf.shape[2] // 2
    await_bytes(buf.at[:, :, pl.ds(0, half)], recv2)


def gather_settle(place, buf, send, send2):
    half = buf.shape[2] // 2
    await_bytes(buf.at[pl.ds(0, place.fs_size - 1), :, pl.ds(0, half)], send)
    await_bytes(buf.at[:, :, pl.ds(0, half)], send2)


def flat_weight(buf):
    shards, rows, width = buf.shape
    if rows % 16 == 0:
        return buf[...].reshape(shards * rows, width)
    wide = jnp.concatenate([buf[k].astype(jnp.float32) for k in range(shards)], axis=0)
    return wide.astype(jnp.bfloat16)


def split_low(value):
    high = value.astype(jnp.bfloat16)
    return high, (value - high.astype(jnp.float32)).astype(jnp.bfloat16)


def precise(left, right):
    high, low = split_low(left)
    return dot_nn(high, right) + dot_nn(low, right)


def arrange(columns):
    blocks = [columns[:, (2 * KEY + VALD) * h : (2 * KEY + VALD) * (h + 1)] for h in range(HEADS)]
    parts = [b[:, :KEY] for b in blocks] + [b[:, KEY : 2 * KEY] for b in blocks] + [b[:, 2 * KEY :] for b in blocks]
    return jnp.concatenate(parts, axis=1)


def restore(columns):
    parts = []
    for h in range(HEADS):
        parts += [
            columns[:, KEY * h : KEY * (h + 1)],
            columns[:, 128 + KEY * h : 128 + KEY * (h + 1)],
            columns[:, 256 + VALD * h : 256 + VALD * (h + 1)],
        ]
    return jnp.concatenate(parts, axis=1)


def by_columns(ref, value):
    for k in range(ref.shape[0]):
        ref[k] = value[:, 128 * k : 128 * k + 128]


def take_image(ref, image, images):
    return jnp.concatenate([ref[k, pl.ds(image, SLOT, stride=images), :] for k in range(ref.shape[0])], axis=1)


def put_image(ref, image, images, value):
    for k in range(ref.shape[0]):
        ref[k, pl.ds(image, SLOT, stride=images), :] = value[:SLOT, 128 * k : 128 * k + 128]


def limits_of(kind):
    return jnp.where(kind == 0, (GRID - 8) ** 2, jnp.where(kind == 1, (GRID - 4) ** 2, SLOT))


def assemble(buf, widths, lanes):
    turned = {}
    for width in sorted(set(widths)):
        turned[width] = sum(
            pltpu.roll(pad_lanes(buf[k], lanes), k * width, 1) if k else pad_lanes(buf[k], lanes)
            for k in range(buf.shape[0])
        )
    return [turned[width][k : k + 1] for k, width in enumerate(widths)]


class Reduce:
    def __init__(self, place, full, first, half, second, third, send, recv):
        self.place, self.full, self.first, self.half = place, full, first, half
        self.second, self.third, self.send, self.recv = second, third, send, recv
        self.width = half.shape[2]

    def swap(self):
        at = pl.multiple_of((1 - self.place.core) * self.width, self.width)
        push(self.full.at[:, :, pl.ds(at, self.width)], self.first, self.send.at[0], self.recv.at[0], self.place.partner)

    def scatter(self):
        place = self.place
        await_bytes(self.first, self.recv.at[0])

        at = pl.multiple_of(self.place.core * self.width, self.width)
        own = self.full[:, :, pl.ds(at, self.width)].astype(jnp.float32)
        self.half[...] = (own + self.first[...].astype(jnp.float32)).astype(jnp.bfloat16)
        self.second[place.fs] = self.half[place.fs]

        def start(step, _):
            target = lax.rem(place.fs + step, place.fs_size)
            push(self.half.at[target], self.second.at[place.fs], self.send.at[1], self.recv.at[1], (place.dp, target))
            return 0

        lax.fori_loop(1, place.fs_size, start, 0)

    def gathered(self):
        await_bytes(self.second.at[pl.ds(0, self.place.fs_size - 1)], self.recv.at[1])
        return jnp.sum(self.second[...].astype(jnp.float32), axis=0).astype(jnp.bfloat16)

    def share(self, total=None):
        place = self.place
        self.third[place.dp] = self.gathered() if total is None else total

        def start(step, _):
            target = lax.rem(place.dp + step, place.dp_size)
            push(self.third.at[place.dp], self.third.at[place.dp], self.send.at[2], self.recv.at[2], (target, place.fs))
            return 0

        lax.fori_loop(1, place.dp_size, start, 0)

    def result(self):
        place = self.place
        await_bytes(self.third.at[pl.ds(0, place.dp_size - 1)], self.recv.at[2])
        parts = []
        for core in range(2):
            parts.append(sum(self.third[k].astype(jnp.float32) for k in range(core, place.dp_size, 2)))
        return jnp.concatenate(parts, axis=1)

    def settle(self, steps=(0, 1, 2)):
        place = self.place
        if 0 in steps:
            await_bytes(self.first, self.send.at[0])
        if 1 in steps:
            await_bytes(self.second.at[pl.ds(0, place.fs_size - 1)], self.send.at[1])
        if 2 in steps:
            await_bytes(self.third.at[pl.ds(0, place.dp_size - 1)], self.send.at[2])


def staged(body, ins, outs, n_in):
    def kernel(*refs):
        refs, sem = list(refs[:-1]), refs[-1]
        count = len(ins) + len(outs)
        held, refs = refs[len(refs) - count :], refs[: len(refs) - count]
        loads, stores = {}, {}
        for k, at in enumerate(ins):
            loads[at] = pltpu.make_async_copy(refs[at], held[k], sem.at[k])
            refs[at] = held[k]
        for k, at in enumerate(outs, len(ins)):
            stores[at] = pltpu.make_async_copy(held[k], refs[n_in + at], sem.at[k])
            refs[n_in + at] = held[k]
        for load in loads.values():
            load.start()
        started = []

        def arrive(*places):
            for at in places:
                loads.pop(at).wait()

        def leave(*places):
            for at in places:
                stores[at].start()
                started.append(at)

        body(arrive, leave, *refs)
        leave(*[at for at in stores if at not in started])
        for store in stores.values():
            store.wait()

    return kernel


def stage_scratch(ins, outs, args, out_shape):
    held = [pltpu.VMEM(args[k].shape, args[k].dtype) for k in ins] + [
        pltpu.VMEM(out_shape[k].shape, out_shape[k].dtype) for k in outs
    ]
    return held + [pltpu.SemaphoreType.DMA((len(held),))]


def first_kernel(dp_size, fs_size, arrive, leave, *refs):
    class_ref, x_ref, off_ref, table_ref = refs[:4]
    shards, vectors = refs[4:7], refs[7:15]
    mixed_out, xs_out, bias_out, weight_out = refs[15], refs[16], refs[17:20], refs[20:23]
    vec_out, gram_out, place_out = refs[23:26]
    refs = (None,) + refs
    xs, z, mixed, index, wide = refs[27:32]
    bias, weights = refs[32:35], refs[35:38]
    vbuf, stat, stat2 = refs[38:41]
    send, recv, send2, recv2, local = refs[41:46]
    place = Place(dp_size, fs_size)
    images = xs.shape[0]

    place.greet()
    arrive(*range(4, 15))
    for k in range(3):
        own = shards[k][...]
        if k == 0:
            own = arrange(own.astype(jnp.float32)).astype(jnp.bfloat16)
        own_half(place, weights[k], own)
    vbuf[place.fs] = jnp.concatenate(
        [pad_lanes(v[...].astype(jnp.float32), 128) for v in vectors], axis=0
    )
    arrive(1)
    by_columns(wide, x_ref[...].astype(jnp.float32))
    count = jnp.int32(0)
    for image in range(images):
        limit = limits_of(class_ref[image])
        row = lax.broadcasted_iota(jnp.int32, (SLOT, xs.shape[2]), 0)
        value = jnp.where(row < limit, take_image(wide, image, images), 0.0)
        xs[image] = pad_rows(value, ROWS).astype(jnp.bfloat16)
        count = count + limit

    flat = xs[...].reshape(images * ROWS, xs.shape[2])
    gram = dot_tn(flat, flat)
    total_x = dot_nn(jnp.ones((8, images * ROWS), jnp.bfloat16), flat)

    place.meet()
    gather_start(place, weights[0], send.at[0], recv.at[0])

    def start(step, _):
        target = lax.rem(place.fs + step, place.fs_size)
        push(vbuf.at[place.fs], vbuf.at[place.fs], send.at[4], recv.at[4], (place.dp, target))
        return 0

    lax.fori_loop(1, place.fs_size, start, 0)
    for k in range(1, 3):
        gather_start(place, weights[k], send.at[k], recv.at[k])
    xs_copy = pltpu.make_async_copy(xs, xs_out, local.at[0])
    xs_copy.start()
    arrive(2, 3)
    bias_tables(off_ref, table_ref, index, bias, place.core)
    place_out[...] = grid_places(off_ref)
    gram_out[...] = gram
    leave(9, 10)
    copies = [xs_copy]
    gather_pass(place, weights[0], recv.at[0], send2.at[0], recv2.at[0])
    gather_end(place, weights[0], recv2.at[0])
    weight = flat_weight(weights[0])
    high, low = split_low(gram)
    spread = dot_nn(high, weight) + dot_nn(low, weight)
    squares = jnp.sum(weight.astype(jnp.float32) * spread, axis=0, keepdims=True)
    sums = precise(total_x, weight)[:1]
    tail = jnp.full((1, 128), count.astype(jnp.float32))
    place.spread_pair(
        stat,
        jnp.concatenate(
            [jnp.concatenate([sums, tail], axis=1), jnp.concatenate([squares, tail], axis=1)], axis=0
        ),
        send.at[5],
        recv.at[5],
    )
    place.spread_chips(stat2, place.collect_pair(stat, recv.at[5]), send.at[6], recv.at[6])
    for k in range(3):
        part = bias[k].at[place.core]
        push(part, part, send.at[7 + k], recv.at[7 + k], place.partner)

    def product(image, _):
        z[image] = dot_nn(xs[image], weight)
        return 0

    lax.fori_loop(0, images, product, 0)
    for k in range(1, 3):
        gather_pass(place, weights[k], recv.at[k], send2.at[k], recv2.at[k])
    await_bytes(vbuf.at[pl.ds(0, place.fs_size - 1)], recv.at[4])
    widths = [v.shape[1] for v in vectors]
    full = assemble(vbuf, widths, 768)
    full[0], full[1] = arrange(full[0]), arrange(full[1])

    for k in range(3):
        await_bytes(bias[k].at[0], recv.at[7 + k])
        copies.append(pltpu.make_async_copy(bias[k], bias_out[k], local.at[1 + k]))
        copies[-1].start()
    got = place.collect_chips(stat2, recv.at[6])
    whole = got[0:1, 768:769]
    center = got[0:1, :768] / whole
    square = got[1:2, :768] / whole
    scale = lax.rsqrt(square - center * center + EPS)
    vec_out[...] = jnp.concatenate(
        full
        + [scale, center, jnp.broadcast_to(whole, (1, 768)), pad_lanes(total_x[:1], 768)]
        + [jnp.zeros((4, 768), jnp.float32)],
        axis=0,
    )
    leave(8)
    gain = scale * full[0]
    shift = full[1] - center * gain
    fold = jnp.where(lax.broadcasted_iota(jnp.int32, (1, 768), 1) < 128, KEY ** (-0.5) * LOG2E, 1.0)
    gain, shift = gain * fold, shift * fold

    def normal(image, _):
        mixed[image] = (z[image] * gain + shift).astype(jnp.bfloat16)
        pltpu.make_async_copy(mixed.at[image], mixed_out.at[image], local.at[8 + image]).start()
        return 0

    lax.fori_loop(0, images, normal, 0)
    for k in range(3):
        if k > 0:
            gather_end(place, weights[k], recv2.at[k])
        copies.append(pltpu.make_async_copy(weights[k], weight_out[k], local.at[4 + k]))
        copies[-1].start()
    for k in range(3):
        gather_settle(place, weights[k], send.at[k], send2.at[k])
    await_bytes(vbuf.at[pl.ds(0, place.fs_size - 1)], send.at[4])
    place.settle_pair(stat, send.at[5])
    place.settle_chips(stat2, send.at[6])
    for k in range(3):
        await_bytes(bias[k].at[0], send.at[7 + k])
    for copy in copies:
        copy.wait()

    def finish(image, _):
        pltpu.make_async_copy(mixed.at[image], mixed_out.at[image], local.at[8 + image]).wait()
        return 0

    lax.fori_loop(0, images, finish, 0)


def first_call(dp_size, fs_size, classes, inputs, offset_table, bias_table, weights, vectors):
    images, model = classes.shape[0], inputs.shape[1]
    vectors = [v.reshape(1, -1) for v in vectors]
    shapes = [(fs_size,) + w.shape for w in weights]
    biases = [(2, r, 2 * l) for _, _, r, l in PARTS]
    bf, f32 = jnp.bfloat16, jnp.float32
    out_shape = (
        [
            jax.ShapeDtypeStruct((images, ROWS, 768), bf),
            jax.ShapeDtypeStruct((images, ROWS, model), bf),
        ]
        + [jax.ShapeDtypeStruct(s, f32) for s in biases]
        + [jax.ShapeDtypeStruct(s, bf) for s in shapes]
        + [jax.ShapeDtypeStruct((16, 768), f32), jax.ShapeDtypeStruct((model, model), f32)]
        + [jax.ShapeDtypeStruct((8, 384), jnp.int32)]
    )
    args = (classes, inputs, offset_table, bias_table, *weights, *vectors)
    ins, outs = (*range(4, 15), 1, 2, 3), (8, 9, 10)
    return pl.pallas_call(
        staged(functools.partial(first_kernel, dp_size, fs_size), ins, outs, len(args)),
        out_shape=out_shape,
        in_specs=[SMEM] + [ANY] * 14,
        out_specs=[ANY] * 11,
        scratch_shapes=[
            pltpu.VMEM((images, ROWS, model), bf),
            pltpu.VMEM((images, ROWS, 768), f32),
            pltpu.VMEM((images, ROWS, 768), bf),
            pltpu.VMEM((ROWS, 384), jnp.int32),
            pltpu.VMEM((model // 128, inputs.shape[0], 128), f32),
        ]
        + [pltpu.VMEM(s, f32) for s in biases]
        + [pltpu.VMEM(s, bf) for s in shapes]
        + [
            pltpu.VMEM((fs_size, 8, 128), f32),
            pltpu.VMEM((2, 2, 896), f32),
            pltpu.VMEM((dp_size * fs_size // 2, 2, 896), f32),
            pltpu.SemaphoreType.DMA((10,)),
            pltpu.SemaphoreType.DMA((10,)),
            pltpu.SemaphoreType.DMA((4,)),
            pltpu.SemaphoreType.DMA((4,)),
            pltpu.SemaphoreType.DMA((8 + images,)),
        ]
        + stage_scratch(ins, outs, args, out_shape),
        compiler_params=pltpu.CompilerParams(
            collective_id=0, has_side_effects=True, vmem_limit_bytes=56 * 2**20
        ),
    )(*args)


def total_rows(value):
    return jnp.sum(value, axis=0, keepdims=True)


def sigma_of(value):
    return 0.5 * jnp.tanh(0.5 * value) + 0.5


def slope_of(value):
    sigma = sigma_of(value)
    return sigma * (1.0 + value * (1.0 - sigma))


def norm_parts(sums, squares, total, gain, shift):
    center = sums / total
    scale = lax.rsqrt(squares / total - center * center + EPS)
    return center, scale, scale * gain, shift - center * scale * gain


def back_parts(grad_sum, grad_z, total, gain, center, scale):
    gain_grad = scale * (grad_z - center * grad_sum)
    alpha = scale * gain
    slant = alpha * scale * gain_grad / total
    level = alpha * (grad_sum - center * scale * gain_grad) / total
    return gain_grad, alpha, slant, level


def outer(column, row):
    left = jnp.concatenate([column, jnp.zeros((7, column.shape[1]), jnp.float32)], axis=0)
    right = jnp.concatenate([row, jnp.zeros((7, row.shape[1]), jnp.float32)], axis=0)
    left_high, left_low = split_low(left)
    right_high, right_low = split_low(right)
    return dot_tn(left_high, right_high) + dot_tn(left_high, right_low) + dot_tn(left_low, right_high)


def middle_kernel(dp_size, fs_size, group, arrive, leave, *refs):
    class_ref, att_in, xs_in, cot_in = refs[:4]
    weight_in, vec_ref, gram_ref = refs[4:7], refs[7], refs[8]
    out_out, gatt_out, gm_out, grad_out, vec_out, own_gram = refs[9], refs[10], refs[11], refs[12:15], refs[15], refs[16]
    refs = refs[2:]
    att, xs, cot, wo_buf, wu_buf, wd_buf = refs[15:21]
    gs, act, slope_att, zo, low, zu, hid, slope_up, zd, dzd, gu, gm, out, gatt, wide = refs[21:36]
    stat_o, stat_u, stat_d, stat_bu, stat_bo = refs[36:41]
    send, recv, local = refs[41:44]
    gram_steps, send_r, recv_r = refs[44:49], refs[49], refs[50]
    down_steps, send_w, recv_w = refs[51:55], refs[55], refs[56]
    up_steps, send_v, recv_v = refs[57:61], refs[61], refs[62]
    send_g, recv_g = refs[63:65]
    place = Place(dp_size, fs_size)
    images = att.shape[0]
    chunks = images // group
    size = group * ROWS
    f32, bf = jnp.float32, jnp.bfloat16
    gram_sum = Reduce(place, *gram_steps, send_r, recv_r)
    down_sum = Reduce(place, *down_steps, None, send_w, recv_w)
    up_sum = Reduce(place, *up_steps, None, send_v, recv_v)

    def copy(source, target, at):
        return pltpu.make_async_copy(source, target, local.at[at])

    loads = [
        copy(weight_in[0], wo_buf, 0),
        copy(xs_in, xs, 1),
        copy(cot_in, cot, 2),
        copy(weight_in[1], wu_buf, 3),
    ]
    loads[0].start()

    def att_copy(k):
        part = pl.ds(k * group, group)
        return copy(att_in.at[part], att.at[part], 8 + k)

    for k in range(chunks):
        att_copy(k).start()
    for load in loads[1:]:
        load.start()
    place.greet()
    arrive(7, 6)
    own_half(place, wd_buf, weight_in[2][...])

    def get(ref, k):
        return ref[pl.ds(k * group, group)].reshape(size, ref.shape[2])

    def put(ref, k, value):
        ref[pl.ds(k * group, group)] = value.astype(ref.dtype).reshape(group, ROWS, ref.shape[2])

    def kept(k, width):
        row = lax.broadcasted_iota(jnp.int32, (ROWS, width), 0)
        return jnp.concatenate([row < limits_of(class_ref[k * group + j]) for j in range(group)], axis=0)

    def over(body, carry):
        return lax.fori_loop(0, chunks, body, carry, unroll=True)

    def zero(width):
        return jnp.zeros((1, width), f32)

    model = xs.shape[2]
    hidden = zu.shape[2]
    total = vec_ref[10:11, :1]
    out_gain, out_shift = vec_ref[2:3, :model], vec_ref[3:4, :model]
    up_gain, up_shift = vec_ref[4:5, :hidden], vec_ref[5:6, :hidden]
    down_gain, down_shift = vec_ref[6:7, :model], vec_ref[7:8, :model]

    loads[0].wait()
    wo = flat_weight(wo_buf)

    def step_out(k, carry):
        att_copy(k).wait()
        value = get(att, k).astype(f32)
        active = (value * sigma_of(value)).astype(bf)
        put(act, k, active)
        z = dot_nn(active, wo)
        put(zo, k, z)
        return carry[0] + total_rows(z), carry[1] + total_rows(z * z)

    sums = over(step_out, (zero(model), zero(model)))
    place.meet()
    x_sum = vec_ref[11:12, :model]
    place.spread(stat_o, jnp.concatenate(sums + (x_sum,), axis=0), send.at[0], recv.at[0])
    gather_start(place, wd_buf, send_g.at[0], recv_g.at[0])
    for load in loads[1:]:
        load.wait()

    def fill_out(k, _):
        put(slope_att, k, slope_of(get(att, k).astype(f32)))
        return 0

    over(fill_out, 0)
    by_columns(wide, cot[...].astype(f32))
    grad_sum = zero(model)
    for image in range(images):
        row = lax.broadcasted_iota(jnp.int32, (SLOT, model), 0)
        value = jnp.where(row < limits_of(class_ref[image]), take_image(wide, image, images), 0.0)
        gs[image] = pad_rows(value, ROWS).astype(bf)
        grad_sum = grad_sum + total_rows(value)
    wu = flat_weight(wu_buf)
    got = place.collect(stat_o, recv.at[0])
    center_o, scale_o, a_o, b_o = norm_parts(got[0:1], got[1:2], total, out_gain, out_shift)
    x_mean = got[2:3] / total

    def middle_of(k):
        return get(xs, k).astype(f32) + get(zo, k) * a_o + b_o

    def step_up(k, carry):
        lower = jnp.where(kept(k, model), middle_of(k), 0.0).astype(bf)
        put(low, k, lower)
        z = dot_nn(lower, wu)
        put(zu, k, z)
        return carry[0] + total_rows(z), carry[1] + total_rows(z * z)

    sums = over(step_up, (zero(hidden), zero(hidden)))
    place.spread(stat_u, jnp.concatenate(sums, axis=0), send.at[1], recv.at[1])
    low_flat = low[...].reshape(images * ROWS, model)
    low_gram = dot_tn(low_flat, low_flat)
    low_sum = dot_nn(jnp.ones((8, images * ROWS), bf), low_flat)[:1]
    count = sum(limits_of(class_ref[k]) for k in range(images)).astype(f32)
    moved = x_sum - 0.5 * count * x_mean
    arrive(8)
    gram = gram_ref[...] - outer(x_mean, moved) - outer(moved, x_mean)
    gram_steps[0][...] = gram.reshape(gram_steps[0].shape).astype(bf)
    gram_sum.swap()

    def fill_up(k, carry):
        centered = jnp.where(kept(k, model), get(zo, k) - center_o, 0.0).astype(bf)
        return carry + dot_tn(get(act, k), centered)

    gather_pass(place, wd_buf, recv_g.at[0], send_g.at[1], recv_g.at[1])
    act_z = over(fill_up, jnp.zeros((act.shape[2], model), f32))
    gather_end(place, wd_buf, recv_g.at[1])
    wd = flat_weight(wd_buf)
    got = place.collect(stat_u, recv.at[1])
    center_u, scale_u, a_u, b_u = norm_parts(got[0:1], got[1:2], total, up_gain, up_shift)

    def step_down(k, carry):
        value = get(zu, k) * a_u + b_u
        active = jnp.where(kept(k, hidden), value * sigma_of(value), 0.0).astype(bf)
        put(hid, k, active)
        z = dot_nn(active, wd)
        put(zd, k, z)
        return (
            carry[0] + total_rows(z),
            carry[1] + total_rows(z * z),
            carry[2] + total_rows(z * get(gs, k).astype(f32)),
        )

    sums = over(step_down, (zero(model), zero(model), zero(model)))
    place.spread(stat_d, jnp.concatenate(sums + (grad_sum,), axis=0), send.at[2], recv.at[2])

    def fill_down(k, _):
        put(slope_up, k, slope_of(get(zu, k) * a_u + b_u))
        return 0

    over(fill_down, 0)
    gram_sum.scatter()
    got = place.collect(stat_d, recv.at[2])
    center_d, scale_d, a_d, b_d = norm_parts(got[0:1], got[1:2], total, down_gain, down_shift)
    down_shift_grad = got[3:4]
    down_gain_grad, alpha, slant, level = back_parts(got[3:4], got[2:3], total, down_gain, center_d, scale_d)

    def step_back_down(k, carry):
        dz = get(gs, k).astype(f32) * alpha - get(zd, k) * slant - jnp.where(kept(k, model), level, 0.0)
        dz = dz.astype(bf)
        put(dzd, k, dz)
        grad = dot_nt(dz, wd) * get(slope_up, k).astype(f32)
        put(gu, k, grad)
        return carry[0] + total_rows(grad), carry[1] + total_rows(grad * get(zu, k))

    sums = over(step_back_down, (zero(hidden), zero(hidden)))
    place.spread(stat_bu, jnp.concatenate(sums, axis=0), send.at[3], recv.at[3])

    down_grad = dot_tn(hid[...].reshape(images * ROWS, hidden), dzd[...].reshape(images * ROWS, model))
    down_steps[0][...] = down_grad.reshape(down_steps[0].shape).astype(bf)
    down_sum.swap()

    def fill_back_down(k, carry):
        grad = get(gu, k)
        carry = carry + dot_tn(get(low, k), grad.astype(bf))
        put(gm, k, get(gs, k).astype(f32) + dot_nt((grad * a_u).astype(bf), wu))
        return carry

    up_raw = over(fill_back_down, jnp.zeros((model, hidden), f32))
    down_sum.scatter()
    gram_sum.share()
    got = place.collect(stat_bu, recv.at[3])
    up_shift_grad = got[0:1]
    up_gain_grad, alpha_u, slant_u, level_u = back_parts(got[0:1], got[1:2], total, up_gain, center_u, scale_u)
    mix = dot_nt((wu.astype(f32) * slant_u).astype(bf), wu).astype(bf)
    high, rest = split_low(jnp.broadcast_to(level_u, (8, hidden)))
    lift = (dot_nt(high, wu) + dot_nt(rest, wu))[:1]

    def step_back_up(k, carry):
        grad = get(gm, k) - dot_nn(get(low, k), mix) - jnp.where(kept(k, model), lift, 0.0)
        put(gm, k, grad)
        part = pl.ds(k * group, group)
        copy(gm.at[part], gm_out.at[part], 8 + chunks + k).start()
        return carry[0] + total_rows(grad), carry[1] + total_rows(grad * get(zo, k))

    sums = over(step_back_up, (zero(model), zero(model)))
    place.spread(stat_bo, jnp.concatenate(sums, axis=0), send.at[4], recv.at[4])
    up_grad = up_raw * alpha_u - precise(low_gram, wu) * slant_u - outer(low_sum, level_u)
    up_steps[0][...] = up_grad.reshape(up_steps[0].shape).astype(bf)
    up_sum.swap()
    out_mean = down_shift_grad / total

    def fill_back_up(k, carry):
        centered = jnp.where(kept(k, model), get(gm, k) - out_mean, 0.0).astype(bf)
        return carry + dot_tn(get(act, k), centered)

    act_g = over(fill_back_up, jnp.zeros((act.shape[2], model), f32))
    up_sum.scatter()
    for image in range(images):
        row = lax.broadcasted_iota(jnp.int32, (ROWS, model), 0)
        value = xs[image].astype(f32) + zo[image] * a_o + zd[image] * a_d + (b_o + b_d)
        value = jnp.where(row < limits_of(class_ref[image]), value, 0.0)
        put_image(wide, image, images, value)
    for k in range(wide.shape[0]):
        out[:, 128 * k : 128 * k + 128] = wide[k].astype(bf)
    out_copy = copy(out, out_out, 5)
    out_copy.start()
    own_gram[...] = gram_sum.result()
    leave(7)
    got = place.collect(stat_bo, recv.at[4])
    out_shift_grad = got[0:1]
    out_gain_grad, alpha_o, slant_o, level_o = back_parts(got[0:1], got[1:2], total, out_gain, center_o, scale_o)

    out_grad = act_g * alpha_o - act_z * slant_o
    grad_out[0][...] = out_grad.reshape(grad_out[0].shape).astype(bf)
    leave(3)
    vec_out[...] = jnp.concatenate(
        [
            pad_lanes(v, hidden)
            for v in (
                out_gain_grad,
                out_shift_grad,
                up_gain_grad,
                up_shift_grad,
                down_gain_grad,
                down_shift_grad,
                x_mean,
                zero(hidden),
            )
        ],
        axis=0,
    )
    leave(6)

    def step_back_out(k, _):
        dz = get(gm, k) * alpha_o - get(zo, k) * slant_o - jnp.where(kept(k, model), level_o, 0.0)
        dz = dz.astype(bf)
        put(gatt, k, dot_nt(dz, wo) * get(slope_att, k).astype(f32))
        part = pl.ds(k * group, group)
        copy(gatt.at[part], gatt_out.at[part], 8 + 2 * chunks + k).start()
        return 0

    over(step_back_out, 0)
    grad_out[2][...] = down_sum.gathered()
    leave(5)
    down_sum.settle((0, 1))
    grad_out[1][...] = up_sum.gathered()
    leave(4)
    up_sum.settle((0, 1))

    for k, stat in enumerate((stat_o, stat_u, stat_d, stat_bu, stat_bo)):
        place.settle(stat, send.at[k])
    gram_sum.settle()
    gather_settle(place, wd_buf, send_g.at[0], send_g.at[1])

    def finish(k, _):
        part = pl.ds(k * group, group)
        copy(gm.at[part], gm_out.at[part], 8 + chunks + k).wait()
        copy(gatt.at[part], gatt_out.at[part], 8 + 2 * chunks + k).wait()
        return 0

    over(finish, 0)
    out_copy.wait()


def half_steps(shape):
    halved = pltpu.VMEM(shape[:2] + (shape[2] // 2,), jnp.bfloat16)
    return [pltpu.VMEM(shape, jnp.bfloat16)] + [halved] * 3 + [pltpu.SemaphoreType.DMA((2,))] * 2


def middle_call(dp_size, fs_size, classes, attended, xs, cotangent, weights, vec, gram):
    full = (fs_size,) + weights[2].shape
    images, model, feature, hidden = xs.shape[0], xs.shape[2], attended.shape[2], weights[1].shape[2]
    group = 2 if images % 2 == 0 else 1
    chunks = images // group
    devices = dp_size * fs_size
    own = model // fs_size
    bf, f32 = jnp.bfloat16, jnp.float32

    def rows(width, kind):
        return pltpu.VMEM((images, ROWS, width), kind)

    out_shape = (
        [
            jax.ShapeDtypeStruct(cotangent.shape, bf),
            jax.ShapeDtypeStruct((images, ROWS, feature), bf),
            jax.ShapeDtypeStruct((images, ROWS, model), f32),
        ]
        + [jax.ShapeDtypeStruct(weights[0].shape, bf)]
        + [jax.ShapeDtypeStruct((s[1], s[2] // 2), bf) for s in (weights[1].shape, full)]
        + [jax.ShapeDtypeStruct((8, hidden), f32), jax.ShapeDtypeStruct((own, model), f32)]
    )
    args = (classes, attended, xs, cotangent, *weights, vec, gram)
    ins, outs = (6, 7, 8), (3, 4, 5, 6, 7)
    return pl.pallas_call(
        staged(functools.partial(middle_kernel, dp_size, fs_size, group), ins, outs, len(args)),
        out_shape=out_shape,
        in_specs=[SMEM] + [ANY] * 8,
        out_specs=[ANY] * 8,
        scratch_shapes=[
            rows(feature, bf),
            rows(model, bf),
            pltpu.VMEM(cotangent.shape, bf),
        ]
        + [pltpu.VMEM(w.shape, bf) for w in weights[:2]]
        + [pltpu.VMEM(full, bf)]
        + [
            rows(model, bf),
            rows(feature, bf),
            rows(feature, bf),
            rows(model, f32),
            rows(model, bf),
            rows(hidden, f32),
            rows(hidden, bf),
            rows(hidden, bf),
            rows(model, f32),
            rows(model, bf),
            rows(hidden, f32),
            rows(model, f32),
            pltpu.VMEM(cotangent.shape, bf),
            rows(feature, bf),
            pltpu.VMEM((model // 128, cotangent.shape[0], 128), f32),
            pltpu.VMEM((devices, 3, model), f32),
            pltpu.VMEM((devices, 2, hidden), f32),
            pltpu.VMEM((devices, 4, model), f32),
            pltpu.VMEM((devices, 2, hidden), f32),
            pltpu.VMEM((devices, 2, model), f32),
            pltpu.SemaphoreType.DMA((5,)),
            pltpu.SemaphoreType.DMA((5,)),
            pltpu.SemaphoreType.DMA((8 + 3 * chunks,)),
            pltpu.VMEM((fs_size, own, model), bf),
        ]
        + [pltpu.VMEM((fs_size, own, model // 2), bf)] * 3
        + [
            pltpu.VMEM((dp_size, own, model // 2), bf),
            pltpu.SemaphoreType.DMA((3,)),
            pltpu.SemaphoreType.DMA((3,)),
        ]
        + half_steps(full)
        + half_steps(weights[1].shape)
        + [pltpu.SemaphoreType.DMA((2,))] * 2
        + stage_scratch(ins, outs, args, out_shape),
        compiler_params=pltpu.CompilerParams(
            collective_id=1, has_side_effects=True, vmem_limit_bytes=58 * 2**20
        ),
    )(*args)


def last_kernel(dp_size, fs_size, group, arrive, leave, *refs):
    class_ref, xs_in, gmix_in, gm_in, places = refs[:5]
    acc_in, grad_in, part_in = refs[5:8], refs[8:9], refs[9:11]
    wq_buf, raw_ref, sum_ref, gram_ref, vec_ref, lines_ref = refs[11:17]
    ig_out, table_out, own_out, vec_out = refs[17], refs[18], refs[19:23], refs[23]
    refs = refs[:27] + (None,) + refs[27:]
    xs, gmix, gm, _, ig, res = refs[24:30]
    acc, full = refs[30:33], refs[33:35]
    steps = [refs[35 + 4 * k : 39 + 4 * k] for k in range(2)]
    thirds = refs[43:45]
    stat, stat_t, stat_c, stat_tc = refs[45:49]
    send, recv, local, send_r, recv_r = refs[49:54]
    place = Place(dp_size, fs_size)
    images = xs.shape[0]
    chunks = images // group
    size = group * ROWS
    f32, bf = jnp.float32, jnp.bfloat16
    model, width = xs.shape[2], gmix.shape[2]

    def copy(source, target, at):
        return pltpu.make_async_copy(source, target, local.at[at])

    grad_loads = [copy(grad_in[k], full[1 + k], k) for k in range(1)]
    mix_load = copy(gmix_in, gmix, 3)
    table_loads = [copy(acc_in[k], acc[k], 5 + k) for k in range(3)]
    late_loads = [copy(xs_in, xs, 8), copy(gm_in, gm, 9)]
    place.greet()
    for load in grad_loads + [mix_load] + table_loads + late_loads:
        load.start()
    reduces = [Reduce(place, full[k], *steps[k], send_r.at[k], recv_r.at[k]) for k in range(2)]
    shared = [
        Reduce(place, None, None, thirds[k], None, thirds[k], send_r.at[2 + k], recv_r.at[2 + k]) for k in range(2)
    ]

    def get(ref, k):
        return ref[pl.ds(k * group, group)].reshape(size, ref.shape[2])

    def put(ref, k, value):
        ref[pl.ds(k * group, group)] = value.astype(ref.dtype).reshape(group, ROWS, ref.shape[2])

    def kept(k, lanes):
        row = lax.broadcasted_iota(jnp.int32, (ROWS, lanes), 0)
        return jnp.concatenate([row < limits_of(class_ref[k * group + j]) for j in range(group)], axis=0)

    arrive(11, 12, 13, 15, 16)
    total = vec_ref[10:11, :1]
    gain, scale, center = vec_ref[0:1, :], vec_ref[8:9, :], vec_ref[9:10, :]
    x_mean = lines_ref[6:7, :model]
    weight = flat_weight(wq_buf)
    weight_f = weight.astype(f32)
    raw = raw_ref[...]
    grad_sum = total_rows(sum_ref[...])
    grad_z = total_rows(raw * weight_f)
    full[0][...] = (raw - outer(x_mean, grad_sum)).reshape(full[0].shape).astype(bf)
    for load in grad_loads:
        load.wait()
    place.meet()
    reduces[0].swap()
    place.spread_pair(stat, jnp.concatenate([grad_sum, grad_z], axis=0), send.at[0], recv.at[0])
    reduces[1].swap()
    alpha = scale * gain
    place.spread_chips(stat_c, place.collect_pair(stat, recv.at[0]), send.at[2], recv.at[2])
    for k in range(2):
        reduces[k].scatter()
    arrive(9, 10)
    for k in range(2):
        shared[k].share(part_in[k][...])
    for load in table_loads:
        load.wait()
    arrive(4, 14)
    place.spread_pair(stat_t, table_sums(places[...], acc), send.at[1], recv.at[1])
    mix_load.wait()
    for k in range(chunks):
        put(ig, k, dot_nt((get(gmix, k).astype(f32) * alpha).astype(bf), weight))
    place.spread_chips(stat_tc, place.collect_pair(stat_t, recv.at[1]), send.at[3], recv.at[3])
    for load in late_loads:
        load.wait()

    got = place.collect_chips(stat_c, recv.at[2])
    gain_grad, alpha, slant, level = back_parts(got[0:1], got[1:2], total, gain, center, scale)
    mix = dot_nt((weight_f * slant).astype(bf), weight).astype(bf)
    high, rest = split_low(jnp.broadcast_to(level, (8, width)))
    lift = (dot_nt(high, weight) + dot_nt(rest, weight))[:1]
    vec_out[...] = jnp.concatenate(
        [restore(gain_grad), restore(got[0:1]), jnp.zeros((6, width), f32)], axis=0
    )
    leave(6)
    for k in range(2):
        reduces[k].share()
    for k in range(chunks):
        value = get(gm, k) + get(ig, k) - dot_nn(get(xs, k), mix) - jnp.where(kept(k, model), lift, 0.0)
        for j in range(group):
            put_image(res, k * group + j, images, value[j * ROWS : (j + 1) * ROWS])
    res_copies = [copy(res.at[k], ig_out.at[:, pl.ds(128 * k, 128)], 10 + k) for k in range(model // 128)]
    for res_copy in res_copies:
        res_copy.start()
    own_out[0][...] = restore(reduces[0].result() * alpha - precise(gram_ref[...], weight) * slant)
    own_out[1][...] = reduces[1].result()
    for k in range(2):
        own_out[2 + k][...] = shared[k].result()
    table_out[...] = place.collect_chips(stat_tc, recv.at[3])
    for k in range(2):
        reduces[k].settle()
        shared[k].settle((2,))
    place.settle_pair(stat, send.at[0])
    place.settle_pair(stat_t, send.at[1])
    place.settle_chips(stat_c, send.at[2])
    place.settle_chips(stat_tc, send.at[3])
    for res_copy in res_copies:
        res_copy.wait()


def last_call(dp_size, fs_size, classes, xs, gmix, gm, places, accs, grads, wq, raw, sums, gram, vec, lines):
    images, model, width = xs.shape[0], xs.shape[2], gmix.shape[2]
    group = 2 if images % 2 == 0 else 1
    devices = dp_size * fs_size
    bf, f32 = jnp.bfloat16, jnp.float32
    shapes = [wq.shape, grads[0].shape]
    own_shapes = [s[1:] for s in shapes] + [(g.shape[0], 2 * g.shape[1]) for g in grads[1:]]
    steps = []
    for s in shapes:
        half = s[2] // 2
        steps += [
            pltpu.VMEM((fs_size, s[1], half), bf),
            pltpu.VMEM((fs_size, s[1], half), bf),
            pltpu.VMEM((fs_size, s[1], half), bf),
            pltpu.VMEM((dp_size, s[1], half), bf),
        ]
    order = []
    for k in range(2):
        order += [steps[4 * k], steps[4 * k + 1], steps[4 * k + 2], steps[4 * k + 3]]
    out_shape = (
        [jax.ShapeDtypeStruct((SLOT * images, model), f32), jax.ShapeDtypeStruct((HEADS, 384), f32)]
        + [jax.ShapeDtypeStruct(s, f32) for s in own_shapes]
        + [jax.ShapeDtypeStruct((8, width), f32)]
    )
    args = (classes, xs, gmix, gm, places, *accs, *grads, wq, raw, sums, gram, vec, lines)
    ins, outs = (13, 15, 16, 11, 12, 9, 10, 4, 14), (1, 2, 3, 4, 5, 6)
    return pl.pallas_call(
        staged(functools.partial(last_kernel, dp_size, fs_size, group), ins, outs, len(args)),
        out_shape=out_shape,
        in_specs=[SMEM] + [ANY] * 16,
        out_specs=[ANY] * 7,
        scratch_shapes=[
            pltpu.VMEM(xs.shape, bf),
            pltpu.VMEM(gmix.shape, bf),
            pltpu.VMEM(gm.shape, f32),
            pltpu.VMEM(gm.shape, f32),
            pltpu.VMEM((model // 128, SLOT * images, 128), f32),
        ]
        + [pltpu.VMEM(a.shape, bf) for a in accs]
        + [pltpu.VMEM(s, bf) for s in shapes]
        + order
        + [
            pltpu.VMEM((dp_size,) + grads[1].shape, bf),
            pltpu.VMEM((dp_size,) + grads[2].shape, bf),
            pltpu.VMEM((2, 2, width), f32),
            pltpu.VMEM((2, HEADS, 384), f32),
            pltpu.VMEM((devices // 2, 2, width), f32),
            pltpu.VMEM((devices // 2, HEADS, 384), f32),
            pltpu.SemaphoreType.DMA((4,)),
            pltpu.SemaphoreType.DMA((4,)),
            pltpu.SemaphoreType.DMA((10 + model // 128,)),
            pltpu.SemaphoreType.DMA((4, 3)),
            pltpu.SemaphoreType.DMA((4, 3)),
        ]
        + stage_scratch(ins, outs, args, out_shape),
        compiler_params=pltpu.CompilerParams(
            collective_id=2, has_side_effects=True, vmem_limit_bytes=56 * 2**20
        ),
    )(*args)

def shards(
    inputs,
    classes,
    offset_table,
    bias_table,
    qkv_weight,
    qkv_gain,
    qkv_shift,
    out_weight,
    out_gain,
    out_shift,
    up_weight,
    up_gain,
    up_shift,
    down_weight,
    down_gain,
    down_shift,
    cotangent,
):
    sizes = lax.axis_size("dp"), lax.axis_size("fsdp")
    images, _, model = inputs.shape

    def by_slot(array):
        return jnp.swapaxes(array, 0, 1).reshape(SLOT * images, model)

    def by_image(array):
        return jnp.swapaxes(array.reshape(SLOT, images, model), 0, 1)

    first = first_call(
        *sizes,
        classes,
        by_slot(inputs),
        offset_table,
        bias_table,
        (qkv_weight, out_weight, up_weight),
        (qkv_gain, qkv_shift, out_gain, out_shift, up_gain, up_shift, down_gain, down_shift),
    )
    mixed, xs, biases, weights, vec, gram, places = first[0], first[1], first[2:5], first[5:8], *first[8:11]
    attended, probs, shares = attend_call(classes, mixed, biases)
    middle = middle_call(*sizes, classes, attended, xs, by_slot(cotangent), (*weights[1:], down_weight), vec, gram)
    output, grad_att, grad_middle, grads, lines, own_gram = *middle[:3], middle[3:6], middle[6], middle[7]
    back = back_call(sizes[1], classes, mixed, probs, shares, grad_att, attended, xs, lines, output)
    grad_mixed, raw, sums, accs, own_lines, output = *back[:3], back[3:6], back[6:12], back[12]
    last = last_call(
        *sizes,
        classes,
        xs,
        grad_mixed,
        grad_middle,
        places,
        accs,
        grads,
        weights[0],
        raw,
        sums,
        own_gram,
        vec,
        lines,
    )
    input_grad, table_grad, *rest = end_call(sizes[1], last[0], last[1], last[2:6], last[6])
    own_lines = [line.reshape(-1) for line in (*own_lines, *rest[4:])]
    return (
        by_image(output),
        by_image(input_grad),
        table_grad,
        rest[0],
        *own_lines[6:8],
        rest[1],
        *own_lines[0:2],
        rest[2],
        *own_lines[2:4],
        rest[3],
        *own_lines[4:6],
    )


def solution(mesh):
    placed = (
        P(("dp", "fsdp"), None, None),
        P(("dp", "fsdp")),
        P(),
        P(),
        P("fsdp", None),
        P("fsdp"),
        P("fsdp"),
        P("fsdp", None),
        P("fsdp"),
        P("fsdp"),
        P("fsdp", None),
        P("fsdp"),
        P("fsdp"),
        P("fsdp", None),
        P("fsdp"),
        P("fsdp"),
        P(("dp", "fsdp"), None, None),
    )
    return jax.shard_map(
        shards,
        mesh=mesh,
        in_specs=placed,
        out_specs=(
            P(("dp", "fsdp"), None, None),
            P(("dp", "fsdp"), None, None),
            P(),
            P("fsdp", None),
            P("fsdp"),
            P("fsdp"),
            P("fsdp", None),
            P("fsdp"),
            P("fsdp"),
            P("fsdp", None),
            P("fsdp"),
            P("fsdp"),
            P("fsdp", None),
            P("fsdp"),
            P("fsdp"),
        ),
        check_vma=False,
    )
```

```python
import functools

import jax
import jax.numpy as jnp
from jax import lax
from jax.experimental import pallas as pl
from jax.experimental.pallas import tpu as pltpu
from jax.sharding import PartitionSpec as P

HEADS = 4
KEY = 32
VALD = 128
GRID = 18
CLASSES = 3
SLOT = 324
NOFF = 324


EPS = 1e-05
LOG2E = 1.4426950408889634
LN2 = 0.6931471805599453
ROWS = 336
PARTS = ((10, 100, 112, 128), (14, 196, 208, 256), (18, 324, 336, 384))
VMEM = pl.BlockSpec(memory_space=pltpu.VMEM)


def dot_nn(left, right):
    return jnp.dot(left, right, preferred_element_type=jnp.float32)


def dot_nt(left, right):
    return lax.dot_general(left, right, (((1,), (1,)), ((), ())), preferred_element_type=jnp.float32)


def dot_tn(left, right):
    return lax.dot_general(left, right, (((0,), (0,)), ((), ())), preferred_element_type=jnp.float32)


def pad_rows(value, rows):
    if value.shape[0] == rows:
        return value
    return jnp.concatenate([value, jnp.zeros((rows - value.shape[0], value.shape[1]), value.dtype)], axis=0)


def pad_lanes(value, lanes):
    if value.shape[1] == lanes:
        return value
    return jnp.concatenate([value, jnp.zeros((value.shape[0], lanes - value.shape[1]), value.dtype)], axis=1)


def bias_tables(off_ref, table_ref, index_ref, outs, pair):
    tables = []
    for side in range(2):
        row = pad_lanes(table_ref[pl.ds(2 * pair + side, 1), :], 384) * LOG2E
        tables.append([jnp.broadcast_to(row[:, 128 * k : 128 * k + 128], (8, 128)) for k in range(3)])
    index_ref[...] = jnp.zeros_like(index_ref)
    for number, (_, amount, rows, lanes) in enumerate(PARTS):
        index_ref[:SLOT, :SLOT] = off_ref[number]

        tiles = rows // 8 // (number + 1)

        def strip(step, _, number=number, amount=amount, lanes=lanes, tiles=tiles, out=outs[number]):
            for line in range(tiles):
                at = pl.multiple_of((step * tiles + line) * 8, 8)
                for block in range(lanes // 128):
                    index = index_ref[pl.ds(at, 8), 128 * block : 128 * block + 128]
                    low = index & 127
                    part = index >> 7
                    valid = lax.broadcasted_iota(jnp.int32, (8, 128), 1) + 128 * block < amount
                    for side in range(2):
                        found = [
                            jnp.take_along_axis(tables[side][k], low, axis=1, mode="promise_in_bounds")
                            for k in range(3 if number == 2 else 2)
                        ]
                        value = jnp.where(part == 0, found[0], found[1])
                        if number == 2:
                            value = jnp.where(part == 2, found[2], value)
                        column = side * lanes + 128 * block
                        out[pair, pl.ds(at, 8), column : column + 128] = jnp.where(valid, value, -1e30)
            return 0

        lax.fori_loop(0, number + 1, strip, 0)


def head_keys(keys, pair, lanes):
    owner = lax.broadcasted_iota(jnp.int32, keys.shape, 1) // KEY
    zero = jnp.zeros_like(keys)
    return jnp.concatenate(
        [pad_rows(jnp.where(owner == 2 * pair + side, keys, zero), lanes) for side in range(2)], axis=0
    )


def pair_values(values, lanes):
    zero = jnp.zeros((lanes, VALD), values.dtype)
    top = jnp.concatenate([pad_rows(values[:, :VALD], lanes), zero], axis=1)
    low = jnp.concatenate([zero, pad_rows(values[:, VALD:], lanes)], axis=1)
    return jnp.concatenate([top, low], axis=0)


def by_eight(value):
    return jnp.sum(value.reshape(value.shape[0] // 8, 8, value.shape[1]), axis=0)


def attend_kernel(class_ref, mixed_in, bias_in0, bias_in1, bias_in2, att_out, p_out, r_out, *held):
    mixed, biases, att, p, r = held[0], held[1:4], held[4], held[5], held[6]
    sem_in, sem_bias, sem_out, score = held[7:11]
    images = mixed.shape[0]

    def load(at):
        return pltpu.make_async_copy(mixed_in.at[at], mixed.at[at], sem_in.at[at])

    def load_bias(number):
        source = (bias_in0, bias_in1, bias_in2)[number]
        return pltpu.make_async_copy(source, biases[number], sem_bias.at[number])

    def store(at, rows, lanes):
        part = (at, pl.ds(0, rows), pl.ds(0, 4 * lanes))
        return (
            pltpu.make_async_copy(p.at[part], p_out.at[part], sem_out.at[0, at]),
            pltpu.make_async_copy(r.at[part[:2]], r_out.at[part[:2]], sem_out.at[1, at]),
        )

    def store_att(at):
        return pltpu.make_async_copy(att.at[at], att_out.at[at], sem_out.at[2, at])

    def absent(number, before):
        found = jnp.bool_(True)
        for k in range(images):
            found = jnp.logical_and(found, jnp.logical_or(class_ref[k] != number, k >= before))
        return found

    load(0).start()
    for number in (2, 1, 0):
        load_bias(number).start()
    for k in range(1, images):
        load(k).start()

    def one(at, _):
        load(at).wait()
        kind = class_ref[at]
        for number, (_, amount, rows, lanes) in enumerate(PARTS):

            @pl.when(jnp.logical_and(kind == number, absent(number, at)))
            def _(number=number):
                load_bias(number).wait()

            @pl.when(kind == number)
            def _(amount=amount, rows=rows, lanes=lanes, bias=biases[number]):
                query = mixed[at, :rows, :128]
                keys = mixed[at, :rows, 128:256]
                kept = lax.broadcasted_iota(jnp.int32, (rows, VALD), 0) < amount
                lane = lax.broadcasted_iota(jnp.int32, (rows, 128), 1)
                shares = jnp.zeros((rows, 128), jnp.float32)
                for pair in range(2):
                    score[pair, :rows, : 2 * lanes] = dot_nt(query, head_keys(keys, pair, lanes)) + bias[pair]
                for pair in range(2):
                    scores = score[pair, :rows, : 2 * lanes]
                    parts, inverse = [], []
                    for side in range(2):
                        own = scores[:, side * lanes : (side + 1) * lanes]
                        expo = jnp.exp2(own - jnp.max(own, axis=1, keepdims=True))
                        share = 1.0 / jnp.sum(expo, axis=1, keepdims=True)
                        shares = jnp.where(lane == 2 * pair + side, share, shares)
                        parts.append(expo.astype(jnp.bfloat16))
                        inverse.append(share)
                    both = jnp.concatenate(parts, axis=1)
                    p[at, :rows, 2 * pair * lanes : 2 * (pair + 1) * lanes] = both
                    values = mixed[at, :rows, 256 + 256 * pair : 512 + 256 * pair]
                    sums = dot_nn(both, pair_values(values, lanes))
                    for side in range(2):
                        own = sums[:, side * VALD : (side + 1) * VALD] * inverse[side]
                        spot = (2 * pair + side) * VALD
                        att[at, :rows, spot : spot + VALD] = jnp.where(kept, own, 0.0).astype(jnp.bfloat16)
                r[at, :rows, :] = shares
                if rows < ROWS:
                    att[at, rows:, :] = jnp.zeros((ROWS - rows, att.shape[2]), jnp.bfloat16)
                for copy in store(at, rows, lanes):
                    copy.start()

        store_att(at).start()
        return 0

    lax.fori_loop(0, images, one, 0)

    def finish(at, _):
        for number, (_, _, rows, lanes) in enumerate(PARTS):

            @pl.when(class_ref[at] == number)
            def _(rows=rows, lanes=lanes):
                for copy in store(at, rows, lanes):
                    copy.wait()

        store_att(at).wait()
        return 0

    lax.fori_loop(0, images, finish, 0)
    for number in range(3):

        @pl.when(absent(number, images))
        def _(number=number):
            load_bias(number).wait()


def back_kernel(fs_size, arrive, leave, *refs):
    class_ref, mixed_in, p_in, r_in, g_in, att_in, xs_in, lines_ref, out_in = refs[:9]
    gmix_out, raw_ref, sum_ref, low_accs, own_refs, out_out = refs[9], refs[10], refs[11], refs[12:15], refs[15:21], refs[21]
    mixed, p, r, g, att, xs, gmix = refs[22:29]
    accs, held, out_sems, sem_in, sem_out = refs[29:32], refs[32], refs[33], refs[34], refs[35]
    images = mixed.shape[0]
    out_load = pltpu.make_async_copy(out_in, held, out_sems.at[0])
    out_store = pltpu.make_async_copy(held, out_out, out_sems.at[1])

    def loads(at, rows, lanes):
        part = (at, pl.ds(0, rows), pl.ds(0, 4 * lanes))
        pairs = [(p_in.at[part], p.at[part]), (r_in.at[part[:2]], r.at[part[:2]])]
        pairs += [(a.at[at], b.at[at]) for a, b in ((mixed_in, mixed), (g_in, g), (att_in, att), (xs_in, xs))]
        return [pltpu.make_async_copy(a, b, sem_in.at[k, at]) for k, (a, b) in enumerate(pairs)]

    def store(at):
        return pltpu.make_async_copy(gmix.at[at], gmix_out.at[at], sem_out.at[at])

    def request(at, _):
        for number, (_, _, rows, lanes) in enumerate(PARTS):

            @pl.when(class_ref[at] == number)
            def _(rows=rows, lanes=lanes):
                for copy in loads(at, rows, lanes):
                    copy.start()

        return 0

    lax.fori_loop(0, images, request, 0)
    out_load.start()
    for ref in (*accs, raw_ref, sum_ref):
        ref[...] = jnp.zeros_like(ref)

    def one(at, _):
        kind = class_ref[at]
        for number, (_, amount, rows, lanes) in enumerate(PARTS):

            @pl.when(kind == number)
            def _(rows=rows, lanes=lanes, acc=accs[number]):
                for copy in loads(at, rows, lanes):
                    copy.wait()
                query = mixed[at, :rows, :128]
                keys = mixed[at, :rows, 128:256]
                owner = lax.broadcasted_iota(jnp.int32, (rows, 128), 1) // KEY
                d_query = jnp.zeros((rows, 128), jnp.float32)
                stacked = []
                for pair in range(2):
                    grads, deltas = [], []
                    for side in range(2):
                        head = 2 * pair + side
                        spot = head * VALD
                        grad = g[at, :rows, spot : spot + VALD].astype(jnp.float32) * r[at, :rows, head : head + 1]
                        own = att[at, :rows, spot : spot + VALD].astype(jnp.float32)
                        deltas.append(jnp.sum(grad * own, axis=1, keepdims=True))
                        grads.append(grad.astype(jnp.bfloat16))
                    both = jnp.concatenate(grads, axis=1)
                    values = mixed[at, :rows, 256 + 256 * pair : 512 + 256 * pair]
                    d_probs = dot_nt(both, pair_values(values, lanes))
                    probs = p[at, :rows, 2 * pair * lanes : 2 * (pair + 1) * lanes]
                    low = []
                    for side in range(2):
                        cut = slice(side * lanes, (side + 1) * lanes)
                        d_score = probs[:, cut].astype(jnp.float32) * (d_probs[:, cut] - deltas[side])
                        acc[pair, :, cut] += d_score
                        low.append(d_score.astype(jnp.bfloat16))
                    d_low = jnp.concatenate(low, axis=1)
                    d_query = d_query + dot_nn(d_low, head_keys(keys, pair, lanes))
                    stacked += low
                    tall = jnp.concatenate([probs[:, :lanes], probs[:, lanes:]], axis=0)
                    d_values = dot_tn(tall, pair_values(both, rows))
                    spot = 256 + 256 * pair
                    sum_ref[:, spot : spot + 256] += by_eight(d_values[:rows])
                    gmix[at, :rows, spot : spot + 256] = d_values[:rows].astype(jnp.bfloat16)
                d_keys = sum(
                    jnp.where(owner == head, dot_tn(stacked[head], query)[:rows], 0.0) for head in range(HEADS)
                )
                d_query = d_query * KEY ** (-0.5)
                d_keys = d_keys * LN2
                sum_ref[:, :128] += by_eight(d_query)
                sum_ref[:, 128:256] += by_eight(d_keys)
                gmix[at, :rows, :128] = d_query.astype(jnp.bfloat16)
                gmix[at, :rows, 128:256] = d_keys.astype(jnp.bfloat16)
                raw_ref[...] += dot_tn(xs[at, :rows, :], gmix[at, :rows, :])
                if rows < ROWS:
                    gmix[at, rows:, :] = jnp.zeros((ROWS - rows, gmix.shape[2]), jnp.bfloat16)

        store(at).start()
        return 0

    lax.fori_loop(0, images, one, 0)
    leave(1, 2)
    for low, acc in zip(low_accs, accs):
        low[...] = acc[...].astype(jnp.bfloat16)
    leave(3, 4, 5)
    out_load.wait()
    out_store.start()
    arrive(7)
    place = lax.axis_index("fsdp")
    lines = lines_ref[...]
    for k, ref in enumerate(own_refs):
        width = ref.shape[1]
        ref[...] = pltpu.roll(lines, lines.shape[1] - place * width, 1)[k : k + 1, :width]
    leave(6, 7, 8, 9, 10, 11)

    def finish(at, _):
        store(at).wait()
        return 0

    lax.fori_loop(0, images, finish, 0)
    out_store.wait()


def grid_places(off_ref):
    found = []
    for number, (side_of, amount, _, _) in enumerate(PARTS):
        offsets = off_ref[number]
        row = lax.broadcasted_iota(jnp.int32, (SLOT, 1), 0)
        most = jnp.max(offsets, axis=1, keepdims=True)
        corner = jnp.min(jnp.where(most == (side_of - 1) * (GRID + 1), row, SLOT), axis=0, keepdims=True)
        place = jnp.sum(jnp.where(row == corner, offsets, 0), axis=0, keepdims=True)
        place = jnp.where(lax.broadcasted_iota(jnp.int32, (1, SLOT), 1) < amount, place, -1)
        found.append(jnp.concatenate([place, jnp.full((1, 384 - SLOT), -1, jnp.int32)], axis=1))
    return jnp.concatenate(found + [jnp.full((8 - len(found), 384), -1, jnp.int32)], axis=0)


def one_hot(left, right):
    return (left == right).astype(jnp.float32).astype(jnp.bfloat16)


def table_sums(places, accs):
    zero = (jnp.zeros((8, 128), jnp.float32), jnp.zeros((16, 128), jnp.float32))
    totals = [[zero] * 6 for _ in range(HEADS)]
    for number, (side_of, _, rows, lanes) in enumerate(PARTS):
        pad = 24 if side_of > 16 else 16
        reach = 384 if side_of > 14 else 256
        place = places[number : number + 1, :]
        cell = lax.broadcasted_iota(jnp.int32, (pad * side_of, 1), 0)
        cell_row = (cell * 2731) >> 16 if pad == 24 else cell >> 4
        cell_col = pad - 1 - (cell - pad * cell_row)
        code = jnp.where(cell_col < side_of, cell_row * GRID + cell_col, -2)
        left = one_hot(code, place[:, :rows])
        right = one_hot(lax.broadcasted_iota(jnp.int32, (reach, 1), 0), place[:, :lanes])
        for pair in range(2):
            by_row = dot_nn(left, accs[number][pair]).astype(jnp.bfloat16)
            for side in range(2):
                both = dot_nt(by_row[:, side * lanes : (side + 1) * lanes], right)
                total = totals[2 * pair + side]
                for line in range(side_of):
                    far, near = divmod((GRID - 1 - line) * GRID, 128)
                    part = pad_lanes(both[pad * line : pad * line + pad], reach + 128)
                    if near:
                        part = pltpu.roll(part, near, 1)
                    for k in range(min(reach // 128 + 1, 5 - far)):
                        piece = part[:, 128 * k : 128 * k + 128]
                        top, low = total[far + k]
                        if pad == 24:
                            top = top + piece[:8]
                        total[far + k] = (top, low + piece[pad - 16 :])
    width = 768
    lane = lax.broadcasted_iota(jnp.int32, (24, width), 1)
    ahead = lane - GRID * ((lane * 3641) >> 16) + lax.broadcasted_iota(jnp.int32, (24, width), 0) >= 23
    level, below = [], []
    for head in range(HEADS):
        whole = jnp.concatenate([jnp.concatenate(t, axis=0) for t in totals[head]], axis=1)
        for keep, group in ((ahead, level), (jnp.logical_not(ahead), below)):
            turned = pltpu.roll(jnp.where(keep, whole, 0.0), 0, 1, stride=1, stride_axis=0)
            group.append(jnp.sum(turned, axis=0, keepdims=True))
    spot = lax.broadcasted_iota(jnp.int32, (width, 1), 0) - 23
    target = lax.broadcasted_iota(jnp.int32, (1, 384), 1)
    spot_row = jnp.where(spot >= 0, (spot * 3641) >> 16, -1)
    spot_col = spot - GRID * spot_row
    straight = one_hot(jnp.abs(spot_row - (GRID - 1)) * GRID + spot_col, target)
    back = one_hot(jnp.abs(spot_row + 1 - (GRID - 1)) * GRID + GRID - spot_col, target)
    out = jnp.zeros((HEADS, 384), jnp.float32)
    for group, fold in ((level, straight), (below, back)):
        high, low = split_low(jnp.concatenate(group, axis=0))
        spread = dot_nn(jnp.concatenate([high.astype(jnp.float32), low.astype(jnp.float32)], axis=0).astype(jnp.bfloat16), fold)
        out = out + spread[:HEADS] + spread[HEADS:]
    return out


def attend_call(classes, mixed, biases):
    images = mixed.shape[0]
    bf, f32 = jnp.bfloat16, jnp.float32
    shapes = [
        jax.ShapeDtypeStruct((images, ROWS, 512), bf),
        jax.ShapeDtypeStruct((images, ROWS, 1536), bf),
        jax.ShapeDtypeStruct((images, ROWS, 128), f32),
    ]
    return pl.pallas_call(
        attend_kernel,
        in_specs=[SMEM] + [ANY] * 4,
        out_specs=[ANY] * 3,
        out_shape=shapes,
        scratch_shapes=[pltpu.VMEM(a.shape, a.dtype) for a in (mixed, *biases, *shapes)]
        + [
            pltpu.SemaphoreType.DMA((images,)),
            pltpu.SemaphoreType.DMA((3,)),
            pltpu.SemaphoreType.DMA((3, images)),
            pltpu.VMEM((2, ROWS, 768), f32),
        ],
        compiler_params=pltpu.CompilerParams(vmem_limit_bytes=60 * 2**20),
    )(classes, mixed, *biases)


def back_call(fs_size, classes, mixed, probs, shares, grad, attended, xs, lines, output):
    images, model = mixed.shape[0], xs.shape[2]
    bf, f32 = jnp.bfloat16, jnp.float32
    tables = [(2, r, 2 * l) for _, _, r, l in PARTS]
    widths = [w // fs_size for w in (model, model, lines.shape[1], lines.shape[1], model, model)]
    args = (classes, mixed, probs, shares, grad, attended, xs, lines, output)
    out_shape = (
        [
            jax.ShapeDtypeStruct((images, ROWS, 768), bf),
            jax.ShapeDtypeStruct((model, 768), f32),
            jax.ShapeDtypeStruct((8, 768), f32),
        ]
        + [jax.ShapeDtypeStruct(s, bf) for s in tables]
        + [jax.ShapeDtypeStruct((1, w), f32) for w in widths]
        + [jax.ShapeDtypeStruct(output.shape, bf)]
    )
    ins, outs = (7,), tuple(range(1, 12))
    return pl.pallas_call(
        staged(functools.partial(back_kernel, fs_size), ins, outs, len(args)),
        in_specs=[SMEM] + [ANY] * 8,
        out_specs=[ANY] * 13,
        out_shape=out_shape,
        scratch_shapes=[pltpu.VMEM(a.shape, a.dtype) for a in (mixed, probs, shares, grad, attended, xs, out_shape[0])]
        + [pltpu.VMEM(s, f32) for s in tables]
        + [
            pltpu.VMEM(output.shape, bf),
            pltpu.SemaphoreType.DMA((2,)),
            pltpu.SemaphoreType.DMA((6, images)),
            pltpu.SemaphoreType.DMA((images,)),
        ]
        + stage_scratch(ins, outs, args, out_shape),
        compiler_params=pltpu.CompilerParams(vmem_limit_bytes=60 * 2**20),
    )(*args)


def end_kernel(*refs):
    ins, outs = refs[:7], refs[7:15]
    held, kept, table_in, table, lines_in, own_lines = refs[15], refs[16:20], refs[20], refs[21], refs[22], refs[23:25]
    sem_in, sem_out = refs[25:27]
    step = held.shape[0] // 4
    pairs = [(ins[0].at[pl.ds(k * step, step)], held.at[pl.ds(k * step, step)], outs[0]) for k in range(4)]
    pairs = [(a, b, c.at[pl.ds(k * step, step)]) for k, (a, b, c) in enumerate(pairs)]
    pairs = [(ins[1], table_in, None), (ins[6], lines_in, None)] + pairs
    pairs += [(ins[2 + k], kept[k], outs[2 + k]) for k in range(4)]
    loads = [pltpu.make_async_copy(a, b, sem_in.at[k]) for k, (a, b, _) in enumerate(pairs)]
    stores = [pltpu.make_async_copy(b, c, sem_out.at[k]) for k, (_, b, c) in enumerate(pairs) if c is not None]
    for load in loads:
        load.start()
    loads[0].wait()
    loads[1].wait()
    table[...] = table_in[:, :NOFF]
    spot = lax.axis_index("fsdp")
    lines = lines_in[...]
    for k, ref in enumerate(own_lines):
        width = ref.shape[1]
        ref[...] = pltpu.roll(lines, lines.shape[1] - spot * width, 1)[k : k + 1, :width]
    for k, (a, b) in enumerate(((table, outs[1]), (own_lines[0], outs[6]), (own_lines[1], outs[7]))):
        stores.append(pltpu.make_async_copy(a, b, sem_out.at[len(pairs) + k]))
        stores[-1].start()
    for load, store in zip(loads[2:], stores):
        load.wait()
        store.start()
    for store in stores:
        store.wait()


def end_call(fs_size, input_grad, table, owned, lines):
    f32 = jnp.float32
    width = lines.shape[1] // fs_size
    shapes = [input_grad.shape, (HEADS, NOFF)] + [o.shape for o in owned] + [(1, width)] * 2
    held = [input_grad.shape] + [o.shape for o in owned] + [table.shape, (HEADS, NOFF), lines.shape] + [(1, width)] * 2
    return pl.pallas_call(
        end_kernel,
        out_shape=[jax.ShapeDtypeStruct(s, f32) for s in shapes],
        in_specs=[ANY] * 7,
        out_specs=[ANY] * 8,
        scratch_shapes=[pltpu.VMEM(s, f32) for s in held]
        + [pltpu.SemaphoreType.DMA((13,)), pltpu.SemaphoreType.DMA((13,))],
        compiler_params=pltpu.CompilerParams(vmem_limit_bytes=60 * 2**20),
    )(input_grad, table, *owned, lines)


MESH = pl.DeviceIdType.MESH
ANY = pl.BlockSpec(memory_space=pl.ANY)
SMEM = pl.BlockSpec(memory_space=pltpu.SMEM)


class Place:
    def __init__(self, dp_size, fs_size):
        self.dp_size, self.fs_size = dp_size, fs_size
        self.size = dp_size * fs_size
        self.dp, self.fs = lax.axis_index("dp"), lax.axis_index("fsdp")
        self.me = self.dp * fs_size + self.fs
        self.core = lax.rem(self.dp, 2)
        self.partner = (self.dp + 1 - 2 * self.core, self.fs)

    def other(self, step, cores=2):
        number = self.size // 2 * cores - step
        rows, lines = self.fs_size // 2, self.dp_size // 2
        core = lax.rem(self.core + lax.rem(number, cores), 2)
        number = number // cores
        line = lax.rem(self.dp // 2 + lax.rem(number // rows, lines), lines)
        row = lax.rem(self.fs // 2 + lax.rem(number, rows), rows)
        return (2 * line + core, 2 * row + lax.rem(self.fs + number // (rows * lines), 2))

    def all_others(self, cores=2):
        rows, lines = self.fs_size // 2, self.dp_size // 2
        row_at = [2 * lax.rem(self.fs // 2 + d, rows) for d in range(rows)]
        line_at = [2 * lax.rem(self.dp // 2 + d, lines) for d in range(lines)]
        side_at = [lax.rem(self.fs, 2), 1 - lax.rem(self.fs, 2)]
        core_at = [self.core, 1 - self.core]
        steps = [(z, x, y, c) for z in range(rows) for x in range(2) for y in range(lines) for c in range(cores)][1:]
        steps.sort(key=lambda s: -(20 * (s[0] > 0) + 10 * s[1] + 10 * (s[2] > 0) + s[3]))
        return [(line_at[y] + core_at[c], row_at[z] + side_at[x]) for z, x, y, c in steps]

    def greet(self):
        barrier = pltpu.get_barrier_semaphore()

        def signal(step, _):
            pl.semaphore_signal(barrier, inc=1, device_id=self.other(step), device_id_type=MESH)
            return 0

        lax.fori_loop(1, self.size, signal, 0)

    def meet(self):
        pl.semaphore_wait(pltpu.get_barrier_semaphore(), self.size - 1)

    def spread(self, buf, value, send, recv):
        buf[self.me] = value

        if self.size <= 64:
            for device in self.all_others():
                push(buf.at[self.me], buf.at[self.me], send, recv, device)
            return

        def start(step, _):
            push(buf.at[self.me], buf.at[self.me], send, recv, self.other(step))
            return 0

        lax.fori_loop(1, self.size, start, 0)

    def collect(self, buf, recv):
        await_bytes(buf.at[pl.ds(0, self.size - 1)], recv)
        return jnp.sum(buf[...], axis=0)

    def spread_pair(self, buf, value, send, recv):
        buf[self.core] = value
        part = buf.at[self.core]
        push(part, part, send, recv, self.partner)

    def collect_pair(self, buf, recv):
        await_bytes(buf.at[0], recv)
        return buf[0] + buf[1]

    def spread_chips(self, buf, value, send, recv):
        chips = self.size // 2
        mine = (self.dp // 2) * self.fs_size + self.fs
        buf[mine] = value
        if self.size <= 64:
            for device in self.all_others(1):
                push(buf.at[mine], buf.at[mine], send, recv, device)
            return

        def start(step, _):
            push(buf.at[mine], buf.at[mine], send, recv, self.other(step, 1))
            return 0

        lax.fori_loop(1, chips, start, 0)

    def collect_chips(self, buf, recv):
        await_bytes(buf.at[pl.ds(0, self.size // 2 - 1)], recv)
        return jnp.sum(buf[...], axis=0)

    def settle_pair(self, buf, send):
        await_bytes(buf.at[0], send)

    def settle_chips(self, buf, send):
        await_bytes(buf.at[pl.ds(0, self.size // 2 - 1)], send)

    def settle(self, buf, send):
        await_bytes(buf.at[pl.ds(0, self.size - 1)], send)


def push(source, target, send, recv, device):
    pltpu.make_async_remote_copy(
        src_ref=source, dst_ref=target, send_sem=send, recv_sem=recv, device_id=device, device_id_type=MESH
    ).start()


def await_bytes(ref, sem):
    pltpu.make_async_copy(ref, ref, sem).wait()


def own_half(place, buf, own):
    half = own.shape[1] // 2
    own = jnp.where(place.core == 0, own[:, :half], own[:, half:])
    buf[place.fs, :, pl.ds(pl.multiple_of(place.core * half, half), half)] = own


def gather_start(place, buf, send, recv):
    half = buf.shape[2] // 2
    part = buf.at[place.fs, :, pl.ds(pl.multiple_of(place.core * half, half), half)]

    def start(step, _):
        push(part, part, send, recv, (place.dp, lax.rem(place.fs + place.fs_size - step, place.fs_size)))
        return 0

    lax.fori_loop(1, place.fs_size, start, 0)


def gather_pass(place, buf, recv, send2, recv2):
    half = buf.shape[2] // 2
    await_bytes(buf.at[pl.ds(0, place.fs_size - 1), :, pl.ds(0, half)], recv)
    part = buf.at[:, :, pl.ds(pl.multiple_of(place.core * half, half), half)]
    push(part, part, send2, recv2, place.partner)


def gather_end(place, buf, recv2):
    half = buf.shape[2] // 2
    await_bytes(buf.at[:, :, pl.ds(0, half)], recv2)


def gather_settle(place, buf, send, send2):
    half = buf.shape[2] // 2
    await_bytes(buf.at[pl.ds(0, place.fs_size - 1), :, pl.ds(0, half)], send)
    await_bytes(buf.at[:, :, pl.ds(0, half)], send2)


def flat_weight(buf):
    shards, rows, width = buf.shape
    if rows % 16 == 0:
        return buf[...].reshape(shards * rows, width)
    wide = jnp.concatenate([buf[k].astype(jnp.float32) for k in range(shards)], axis=0)
    return wide.astype(jnp.bfloat16)


def split_low(value):
    high = value.astype(jnp.bfloat16)
    return high, (value - high.astype(jnp.float32)).astype(jnp.bfloat16)


def precise(left, right):
    high, low = split_low(left)
    return dot_nn(high, right) + dot_nn(low, right)


def arrange(columns):
    blocks = [columns[:, (2 * KEY + VALD) * h : (2 * KEY + VALD) * (h + 1)] for h in range(HEADS)]
    parts = [b[:, :KEY] for b in blocks] + [b[:, KEY : 2 * KEY] for b in blocks] + [b[:, 2 * KEY :] for b in blocks]
    return jnp.concatenate(parts, axis=1)


def restore(columns):
    parts = []
    for h in range(HEADS):
        parts += [
            columns[:, KEY * h : KEY * (h + 1)],
            columns[:, 128 + KEY * h : 128 + KEY * (h + 1)],
            columns[:, 256 + VALD * h : 256 + VALD * (h + 1)],
        ]
    return jnp.concatenate(parts, axis=1)


def by_columns(ref, value):
    for k in range(ref.shape[0]):
        ref[k, : value.shape[0]] = value[:, 128 * k : 128 * k + 128]


def take_image(ref, image, images):
    return jnp.concatenate([ref[k, pl.ds(image, SLOT, stride=images), :] for k in range(ref.shape[0])], axis=1)


def put_image(ref, image, images, value):
    for k in range(ref.shape[0]):
        ref[k, pl.ds(image, SLOT, stride=images), :] = value[:SLOT, 128 * k : 128 * k + 128]


def limits_of(kind):
    return jnp.where(kind == 0, (GRID - 8) ** 2, jnp.where(kind == 1, (GRID - 4) ** 2, SLOT))


def assemble(buf, widths, lanes):
    turned = {}
    for width in sorted(set(widths)):
        turned[width] = sum(
            pltpu.roll(pad_lanes(buf[k], lanes), k * width, 1) if k else pad_lanes(buf[k], lanes)
            for k in range(buf.shape[0])
        )
    return [turned[width][k : k + 1] for k, width in enumerate(widths)]


class Reduce:
    def __init__(self, place, full, first, half, second, third, send, recv):
        self.place, self.full, self.first, self.half = place, full, first, half
        self.second, self.third, self.send, self.recv = second, third, send, recv
        self.width = half.shape[2]

    def swap(self):
        at = pl.multiple_of((1 - self.place.core) * self.width, self.width)
        push(self.full.at[:, :, pl.ds(at, self.width)], self.first, self.send.at[0], self.recv.at[0], self.place.partner)

    def scatter(self):
        place = self.place
        await_bytes(self.first, self.recv.at[0])

        at = pl.multiple_of(self.place.core * self.width, self.width)
        own = self.full[:, :, pl.ds(at, self.width)].astype(jnp.float32)
        self.half[...] = (own + self.first[...].astype(jnp.float32)).astype(jnp.bfloat16)
        self.second[place.fs] = self.half[place.fs]

        def start(step, _):
            target = lax.rem(place.fs + step, place.fs_size)
            push(self.half.at[target], self.second.at[place.fs], self.send.at[1], self.recv.at[1], (place.dp, target))
            return 0

        lax.fori_loop(1, place.fs_size, start, 0)

    def gathered(self):
        await_bytes(self.second.at[pl.ds(0, self.place.fs_size - 1)], self.recv.at[1])
        return jnp.sum(self.second[...].astype(jnp.float32), axis=0).astype(jnp.bfloat16)

    def share(self, total=None):
        place = self.place
        self.third[place.dp] = self.gathered() if total is None else total

        def start(step, _):
            target = lax.rem(place.dp + step, place.dp_size)
            push(self.third.at[place.dp], self.third.at[place.dp], self.send.at[2], self.recv.at[2], (target, place.fs))
            return 0

        lax.fori_loop(1, place.dp_size, start, 0)

    def result(self):
        place = self.place
        await_bytes(self.third.at[pl.ds(0, place.dp_size - 1)], self.recv.at[2])
        parts = []
        for core in range(2):
            parts.append(sum(self.third[k].astype(jnp.float32) for k in range(core, place.dp_size, 2)))
        return jnp.concatenate(parts, axis=1)

    def settle(self, steps=(0, 1, 2)):
        place = self.place
        if 0 in steps:
            await_bytes(self.first, self.send.at[0])
        if 1 in steps:
            await_bytes(self.second.at[pl.ds(0, place.fs_size - 1)], self.send.at[1])
        if 2 in steps:
            await_bytes(self.third.at[pl.ds(0, place.dp_size - 1)], self.send.at[2])


def staged(body, ins, outs, n_in):
    def kernel(*refs):
        refs, sem = list(refs[:-1]), refs[-1]
        count = len(ins) + len(outs)
        held, refs = refs[len(refs) - count :], refs[: len(refs) - count]
        loads, stores = {}, {}
        for k, at in enumerate(ins):
            loads[at] = pltpu.make_async_copy(refs[at], held[k], sem.at[k])
            refs[at] = held[k]
        for k, at in enumerate(outs, len(ins)):
            stores[at] = pltpu.make_async_copy(held[k], refs[n_in + at], sem.at[k])
            refs[n_in + at] = held[k]
        for load in loads.values():
            load.start()
        started = []

        def arrive(*places):
            for at in places:
                loads.pop(at).wait()

        def leave(*places):
            for at in places:
                stores[at].start()
                started.append(at)

        body(arrive, leave, *refs)
        leave(*[at for at in stores if at not in started])
        for store in stores.values():
            store.wait()

    return kernel


def stage_scratch(ins, outs, args, out_shape):
    held = [pltpu.VMEM(args[k].shape, args[k].dtype) for k in ins] + [
        pltpu.VMEM(out_shape[k].shape, out_shape[k].dtype) for k in outs
    ]
    return held + [pltpu.SemaphoreType.DMA((len(held),))]


def first_kernel(dp_size, fs_size, arrive, leave, *refs):
    class_ref, x_ref, off_ref, table_ref = refs[:4]
    shards, vectors = refs[4:7], refs[7:15]
    mixed_out, xs_out, bias_out, weight_out = refs[15], refs[16], refs[17:20], refs[20:23]
    vec_out, gram_out, place_out = refs[23:26]
    refs = (None,) + refs
    xs, z, mixed, index, wide = refs[27:32]
    bias, weights = refs[32:35], refs[35:38]
    vbuf, stat, stat2 = refs[38:41]
    send, recv, send2, recv2, local = refs[41:46]
    place = Place(dp_size, fs_size)
    images = xs.shape[0]

    place.greet()
    arrive(*range(4, 15))
    for k in range(3):
        own = shards[k][...]
        if k == 0:
            own = arrange(own.astype(jnp.float32)).astype(jnp.bfloat16)
        own_half(place, weights[k], own)
    vbuf[place.fs] = jnp.concatenate(
        [pad_lanes(v[...].astype(jnp.float32), 128) for v in vectors], axis=0
    )
    arrive(1)
    by_columns(wide, x_ref[...].astype(jnp.float32))
    count = jnp.int32(0)
    for image in range(images):
        limit = limits_of(class_ref[image])
        row = lax.broadcasted_iota(jnp.int32, (SLOT, xs.shape[2]), 0)
        value = jnp.where(row < limit, take_image(wide, image, images), 0.0)
        xs[image] = pad_rows(value, ROWS).astype(jnp.bfloat16)
        count = count + limit

    flat = xs[...].reshape(images * ROWS, xs.shape[2])
    gram = dot_tn(flat, flat)
    total_x = dot_nn(jnp.ones((8, images * ROWS), jnp.bfloat16), flat)

    place.meet()
    gather_start(place, weights[0], send.at[0], recv.at[0])

    def start(step, _):
        target = lax.rem(place.fs + step, place.fs_size)
        push(vbuf.at[place.fs], vbuf.at[place.fs], send.at[4], recv.at[4], (place.dp, target))
        return 0

    lax.fori_loop(1, place.fs_size, start, 0)
    for k in range(1, 3):
        gather_start(place, weights[k], send.at[k], recv.at[k])
    xs_copy = pltpu.make_async_copy(xs, xs_out, local.at[0])
    xs_copy.start()
    arrive(2, 3)
    bias_tables(off_ref, table_ref, index, bias, place.core)
    place_out[...] = grid_places(off_ref)
    gram_out[...] = gram
    leave(9, 10)
    copies = [xs_copy]
    gather_pass(place, weights[0], recv.at[0], send2.at[0], recv2.at[0])
    gather_end(place, weights[0], recv2.at[0])
    weight = flat_weight(weights[0])
    high, low = split_low(gram)
    spread = dot_nn(high, weight) + dot_nn(low, weight)
    squares = jnp.sum(weight.astype(jnp.float32) * spread, axis=0, keepdims=True)
    sums = precise(total_x, weight)[:1]
    tail = jnp.full((1, 128), count.astype(jnp.float32))
    place.spread_pair(
        stat,
        jnp.concatenate(
            [jnp.concatenate([sums, tail], axis=1), jnp.concatenate([squares, tail], axis=1)], axis=0
        ),
        send.at[5],
        recv.at[5],
    )
    place.spread_chips(stat2, place.collect_pair(stat, recv.at[5]), send.at[6], recv.at[6])
    for k in range(3):
        part = bias[k].at[place.core]
        push(part, part, send.at[7 + k], recv.at[7 + k], place.partner)

    def product(image, _):
        z[image] = dot_nn(xs[image], weight)
        return 0

    lax.fori_loop(0, images, product, 0)
    for k in range(1, 3):
        gather_pass(place, weights[k], recv.at[k], send2.at[k], recv2.at[k])
    await_bytes(vbuf.at[pl.ds(0, place.fs_size - 1)], recv.at[4])
    widths = [v.shape[1] for v in vectors]
    full = assemble(vbuf, widths, 768)
    full[0], full[1] = arrange(full[0]), arrange(full[1])

    for k in range(3):
        await_bytes(bias[k].at[0], recv.at[7 + k])
        copies.append(pltpu.make_async_copy(bias[k], bias_out[k], local.at[1 + k]))
        copies[-1].start()
    got = place.collect_chips(stat2, recv.at[6])
    whole = got[0:1, 768:769]
    center = got[0:1, :768] / whole
    square = got[1:2, :768] / whole
    scale = lax.rsqrt(square - center * center + EPS)
    vec_out[...] = jnp.concatenate(
        full
        + [scale, center, jnp.broadcast_to(whole, (1, 768)), pad_lanes(total_x[:1], 768)]
        + [jnp.zeros((4, 768), jnp.float32)],
        axis=0,
    )
    leave(8)
    gain = scale * full[0]
    shift = full[1] - center * gain
    fold = jnp.where(lax.broadcasted_iota(jnp.int32, (1, 768), 1) < 128, KEY ** (-0.5) * LOG2E, 1.0)
    gain, shift = gain * fold, shift * fold

    def normal(image, _):
        mixed[image] = (z[image] * gain + shift).astype(jnp.bfloat16)
        pltpu.make_async_copy(mixed.at[image], mixed_out.at[image], local.at[8 + image]).start()
        return 0

    lax.fori_loop(0, images, normal, 0)
    for k in range(3):
        if k > 0:
            gather_end(place, weights[k], recv2.at[k])
        copies.append(pltpu.make_async_copy(weights[k], weight_out[k], local.at[4 + k]))
        copies[-1].start()
    for k in range(3):
        gather_settle(place, weights[k], send.at[k], send2.at[k])
    await_bytes(vbuf.at[pl.ds(0, place.fs_size - 1)], send.at[4])
    place.settle_pair(stat, send.at[5])
    place.settle_chips(stat2, send.at[6])
    for k in range(3):
        await_bytes(bias[k].at[0], send.at[7 + k])
    for copy in copies:
        copy.wait()

    def finish(image, _):
        pltpu.make_async_copy(mixed.at[image], mixed_out.at[image], local.at[8 + image]).wait()
        return 0

    lax.fori_loop(0, images, finish, 0)


def first_call(dp_size, fs_size, classes, inputs, offset_table, bias_table, weights, vectors):
    images, model = classes.shape[0], inputs.shape[1]
    vectors = [v.reshape(1, -1) for v in vectors]
    shapes = [(fs_size,) + w.shape for w in weights]
    biases = [(2, r, 2 * l) for _, _, r, l in PARTS]
    bf, f32 = jnp.bfloat16, jnp.float32
    out_shape = (
        [
            jax.ShapeDtypeStruct((images, ROWS, 768), bf),
            jax.ShapeDtypeStruct((images, ROWS, model), bf),
        ]
        + [jax.ShapeDtypeStruct(s, f32) for s in biases]
        + [jax.ShapeDtypeStruct(s, bf) for s in shapes]
        + [jax.ShapeDtypeStruct((16, 768), f32), jax.ShapeDtypeStruct((model, model), f32)]
        + [jax.ShapeDtypeStruct((8, 384), jnp.int32)]
    )
    args = (classes, inputs, offset_table, bias_table, *weights, *vectors)
    ins, outs = (*range(4, 15), 1, 2, 3), (8, 9, 10)
    return pl.pallas_call(
        staged(functools.partial(first_kernel, dp_size, fs_size), ins, outs, len(args)),
        out_shape=out_shape,
        in_specs=[SMEM] + [ANY] * 14,
        out_specs=[ANY] * 11,
        scratch_shapes=[
            pltpu.VMEM((images, ROWS, model), bf),
            pltpu.VMEM((images, ROWS, 768), f32),
            pltpu.VMEM((images, ROWS, 768), bf),
            pltpu.VMEM((ROWS, 384), jnp.int32),
            pltpu.VMEM((model // 128, images * ROWS, 128), f32),
        ]
        + [pltpu.VMEM(s, f32) for s in biases]
        + [pltpu.VMEM(s, bf) for s in shapes]
        + [
            pltpu.VMEM((fs_size, 8, 128), f32),
            pltpu.VMEM((2, 2, 896), f32),
            pltpu.VMEM((dp_size * fs_size // 2, 2, 896), f32),
            pltpu.SemaphoreType.DMA((10,)),
            pltpu.SemaphoreType.DMA((10,)),
            pltpu.SemaphoreType.DMA((4,)),
            pltpu.SemaphoreType.DMA((4,)),
            pltpu.SemaphoreType.DMA((8 + images,)),
        ]
        + stage_scratch(ins, outs, args, out_shape),
        compiler_params=pltpu.CompilerParams(
            collective_id=0, has_side_effects=True, vmem_limit_bytes=56 * 2**20
        ),
    )(*args)


def total_rows(value):
    return jnp.sum(value, axis=0, keepdims=True)


def sigma_of(value):
    return 0.5 * jnp.tanh(0.5 * value) + 0.5


def slope_of(value):
    sigma = sigma_of(value)
    return sigma * (1.0 + value * (1.0 - sigma))


def norm_parts(sums, squares, total, gain, shift):
    center = sums / total
    scale = lax.rsqrt(squares / total - center * center + EPS)
    return center, scale, scale * gain, shift - center * scale * gain


def back_parts(grad_sum, grad_z, total, gain, center, scale):
    gain_grad = scale * (grad_z - center * grad_sum)
    alpha = scale * gain
    slant = alpha * scale * gain_grad / total
    level = alpha * (grad_sum - center * scale * gain_grad) / total
    return gain_grad, alpha, slant, level


def outer(column, row):
    left = jnp.concatenate([column, jnp.zeros((7, column.shape[1]), jnp.float32)], axis=0)
    right = jnp.concatenate([row, jnp.zeros((7, row.shape[1]), jnp.float32)], axis=0)
    left_high, left_low = split_low(left)
    right_high, right_low = split_low(right)
    return dot_tn(left_high, right_high) + dot_tn(left_high, right_low) + dot_tn(left_low, right_high)


def middle_kernel(dp_size, fs_size, group, arrive, leave, *refs):
    class_ref, att_in, xs_in, cot_in = refs[:4]
    weight_in, vec_ref, gram_ref = refs[4:7], refs[7], refs[8]
    out_out, gatt_out, gm_out, grad_out, vec_out, own_gram = refs[9], refs[10], refs[11], refs[12:15], refs[15], refs[16]
    refs = refs[2:]
    att, xs, cot, wo_buf, wu_buf, wd_buf = refs[15:21]
    gs, act, slope_att, zo, low, zu, hid, slope_up, zd, dzd, gu, gm, out, gatt, wide = refs[21:36]
    stat_o, stat_u, stat_d, stat_bu, stat_bo = refs[36:41]
    send, recv, local = refs[41:44]
    gram_steps, send_r, recv_r = refs[44:49], refs[49], refs[50]
    down_steps, send_w, recv_w = refs[51:55], refs[55], refs[56]
    up_steps, send_v, recv_v = refs[57:61], refs[61], refs[62]
    send_g, recv_g = refs[63:65]
    place = Place(dp_size, fs_size)
    images = att.shape[0]
    chunks = images // group
    size = group * ROWS
    f32, bf = jnp.float32, jnp.bfloat16
    gram_sum = Reduce(place, *gram_steps, send_r, recv_r)
    down_sum = Reduce(place, *down_steps, None, send_w, recv_w)
    up_sum = Reduce(place, *up_steps, None, send_v, recv_v)

    def copy(source, target, at):
        return pltpu.make_async_copy(source, target, local.at[at])

    loads = [
        copy(weight_in[0], wo_buf, 0),
        copy(xs_in, xs, 1),
        copy(cot_in, cot, 2),
        copy(weight_in[1], wu_buf, 3),
    ]
    loads[0].start()

    def att_copy(k):
        part = pl.ds(k * group, group)
        return copy(att_in.at[part], att.at[part], 8 + k)

    for k in range(chunks):
        att_copy(k).start()
    for load in loads[1:]:
        load.start()
    place.greet()
    arrive(7, 6)
    own_half(place, wd_buf, weight_in[2][...])

    def get(ref, k):
        return ref[pl.ds(k * group, group)].reshape(size, ref.shape[2])

    def put(ref, k, value):
        ref[pl.ds(k * group, group)] = value.astype(ref.dtype).reshape(group, ROWS, ref.shape[2])

    def kept(k, width):
        row = lax.broadcasted_iota(jnp.int32, (ROWS, width), 0)
        return jnp.concatenate([row < limits_of(class_ref[k * group + j]) for j in range(group)], axis=0)

    def over(body, carry):
        return lax.fori_loop(0, chunks, body, carry, unroll=True)

    def zero(width):
        return jnp.zeros((1, width), f32)

    model = xs.shape[2]
    hidden = zu.shape[2]
    total = vec_ref[10:11, :1]
    out_gain, out_shift = vec_ref[2:3, :model], vec_ref[3:4, :model]
    up_gain, up_shift = vec_ref[4:5, :hidden], vec_ref[5:6, :hidden]
    down_gain, down_shift = vec_ref[6:7, :model], vec_ref[7:8, :model]

    loads[0].wait()
    wo = flat_weight(wo_buf)

    def step_out(k, carry):
        att_copy(k).wait()
        value = get(att, k).astype(f32)
        active = (value * sigma_of(value)).astype(bf)
        put(act, k, active)
        z = dot_nn(active, wo)
        put(zo, k, z)
        return carry[0] + total_rows(z), carry[1] + total_rows(z * z)

    sums = over(step_out, (zero(model), zero(model)))
    place.meet()
    x_sum = vec_ref[11:12, :model]
    place.spread(stat_o, jnp.concatenate(sums + (x_sum,), axis=0), send.at[0], recv.at[0])
    gather_start(place, wd_buf, send_g.at[0], recv_g.at[0])
    for load in loads[1:]:
        load.wait()

    def fill_out(k, _):
        put(slope_att, k, slope_of(get(att, k).astype(f32)))
        return 0

    over(fill_out, 0)
    by_columns(wide, cot[...].astype(f32))
    grad_sum = zero(model)
    for image in range(images):
        row = lax.broadcasted_iota(jnp.int32, (SLOT, model), 0)
        value = jnp.where(row < limits_of(class_ref[image]), take_image(wide, image, images), 0.0)
        gs[image] = pad_rows(value, ROWS).astype(bf)
        grad_sum = grad_sum + total_rows(value)
    wu = flat_weight(wu_buf)
    got = place.collect(stat_o, recv.at[0])
    center_o, scale_o, a_o, b_o = norm_parts(got[0:1], got[1:2], total, out_gain, out_shift)
    x_mean = got[2:3] / total

    def middle_of(k):
        return get(xs, k).astype(f32) + get(zo, k) * a_o + b_o

    def step_up(k, carry):
        lower = jnp.where(kept(k, model), middle_of(k), 0.0).astype(bf)
        put(low, k, lower)
        z = dot_nn(lower, wu)
        put(zu, k, z)
        return carry[0] + total_rows(z), carry[1] + total_rows(z * z)

    sums = over(step_up, (zero(hidden), zero(hidden)))
    place.spread(stat_u, jnp.concatenate(sums, axis=0), send.at[1], recv.at[1])
    low_flat = low[...].reshape(images * ROWS, model)
    low_gram = dot_tn(low_flat, low_flat)
    low_sum = dot_nn(jnp.ones((8, images * ROWS), bf), low_flat)[:1]
    count = sum(limits_of(class_ref[k]) for k in range(images)).astype(f32)
    moved = x_sum - 0.5 * count * x_mean
    arrive(8)
    gram = gram_ref[...] - outer(x_mean, moved) - outer(moved, x_mean)
    gram_steps[0][...] = gram.reshape(gram_steps[0].shape).astype(bf)
    gram_sum.swap()

    def fill_up(k, carry):
        centered = jnp.where(kept(k, model), get(zo, k) - center_o, 0.0).astype(bf)
        return carry + dot_tn(get(act, k), centered)

    gather_pass(place, wd_buf, recv_g.at[0], send_g.at[1], recv_g.at[1])
    act_z = over(fill_up, jnp.zeros((act.shape[2], model), f32))
    gather_end(place, wd_buf, recv_g.at[1])
    wd = flat_weight(wd_buf)
    got = place.collect(stat_u, recv.at[1])
    center_u, scale_u, a_u, b_u = norm_parts(got[0:1], got[1:2], total, up_gain, up_shift)

    def step_down(k, carry):
        value = get(zu, k) * a_u + b_u
        active = jnp.where(kept(k, hidden), value * sigma_of(value), 0.0).astype(bf)
        put(hid, k, active)
        z = dot_nn(active, wd)
        put(zd, k, z)
        return (
            carry[0] + total_rows(z),
            carry[1] + total_rows(z * z),
            carry[2] + total_rows(z * get(gs, k).astype(f32)),
        )

    sums = over(step_down, (zero(model), zero(model), zero(model)))
    place.spread(stat_d, jnp.concatenate(sums + (grad_sum,), axis=0), send.at[2], recv.at[2])

    def fill_down(k, _):
        put(slope_up, k, slope_of(get(zu, k) * a_u + b_u))
        return 0

    over(fill_down, 0)
    gram_sum.scatter()
    got = place.collect(stat_d, recv.at[2])
    center_d, scale_d, a_d, b_d = norm_parts(got[0:1], got[1:2], total, down_gain, down_shift)
    down_shift_grad = got[3:4]
    down_gain_grad, alpha, slant, level = back_parts(got[3:4], got[2:3], total, down_gain, center_d, scale_d)

    def step_back_down(k, carry):
        dz = get(gs, k).astype(f32) * alpha - get(zd, k) * slant - jnp.where(kept(k, model), level, 0.0)
        dz = dz.astype(bf)
        put(dzd, k, dz)
        grad = dot_nt(dz, wd) * get(slope_up, k).astype(f32)
        put(gu, k, grad)
        return carry[0] + total_rows(grad), carry[1] + total_rows(grad * get(zu, k))

    sums = over(step_back_down, (zero(hidden), zero(hidden)))
    place.spread(stat_bu, jnp.concatenate(sums, axis=0), send.at[3], recv.at[3])

    down_grad = dot_tn(hid[...].reshape(images * ROWS, hidden), dzd[...].reshape(images * ROWS, model))
    down_steps[0][...] = down_grad.reshape(down_steps[0].shape).astype(bf)
    down_sum.swap()

    def fill_back_down(k, carry):
        grad = get(gu, k)
        carry = carry + dot_tn(get(low, k), grad.astype(bf))
        put(gm, k, get(gs, k).astype(f32) + dot_nt((grad * a_u).astype(bf), wu))
        return carry

    up_raw = over(fill_back_down, jnp.zeros((model, hidden), f32))
    down_sum.scatter()
    gram_sum.share()
    got = place.collect(stat_bu, recv.at[3])
    up_shift_grad = got[0:1]
    up_gain_grad, alpha_u, slant_u, level_u = back_parts(got[0:1], got[1:2], total, up_gain, center_u, scale_u)
    mix = dot_nt((wu.astype(f32) * slant_u).astype(bf), wu).astype(bf)
    high, rest = split_low(jnp.broadcast_to(level_u, (8, hidden)))
    lift = (dot_nt(high, wu) + dot_nt(rest, wu))[:1]

    def step_back_up(k, carry):
        grad = get(gm, k) - dot_nn(get(low, k), mix) - jnp.where(kept(k, model), lift, 0.0)
        put(gm, k, grad)
        part = pl.ds(k * group, group)
        copy(gm.at[part], gm_out.at[part], 8 + chunks + k).start()
        return carry[0] + total_rows(grad), carry[1] + total_rows(grad * get(zo, k))

    sums = over(step_back_up, (zero(model), zero(model)))
    place.spread(stat_bo, jnp.concatenate(sums, axis=0), send.at[4], recv.at[4])
    up_grad = up_raw * alpha_u - precise(low_gram, wu) * slant_u - outer(low_sum, level_u)
    up_steps[0][...] = up_grad.reshape(up_steps[0].shape).astype(bf)
    up_sum.swap()
    out_mean = down_shift_grad / total

    def fill_back_up(k, carry):
        centered = jnp.where(kept(k, model), get(gm, k) - out_mean, 0.0).astype(bf)
        return carry + dot_tn(get(act, k), centered)

    act_g = over(fill_back_up, jnp.zeros((act.shape[2], model), f32))
    up_sum.scatter()
    for image in range(images):
        row = lax.broadcasted_iota(jnp.int32, (ROWS, model), 0)
        value = xs[image].astype(f32) + zo[image] * a_o + zd[image] * a_d + (b_o + b_d)
        value = jnp.where(row < limits_of(class_ref[image]), value, 0.0)
        put_image(wide, image, images, value)
    for k in range(wide.shape[0]):
        out[:, 128 * k : 128 * k + 128] = wide[k, : out.shape[0]].astype(bf)
    out_copy = copy(out, out_out, 5)
    out_copy.start()
    own_gram[...] = gram_sum.result()
    leave(7)
    got = place.collect(stat_bo, recv.at[4])
    out_shift_grad = got[0:1]
    out_gain_grad, alpha_o, slant_o, level_o = back_parts(got[0:1], got[1:2], total, out_gain, center_o, scale_o)

    out_grad = act_g * alpha_o - act_z * slant_o
    grad_out[0][...] = out_grad.reshape(grad_out[0].shape).astype(bf)
    leave(3)
    vec_out[...] = jnp.concatenate(
        [
            pad_lanes(v, hidden)
            for v in (
                out_gain_grad,
                out_shift_grad,
                up_gain_grad,
                up_shift_grad,
                down_gain_grad,
                down_shift_grad,
                x_mean,
                zero(hidden),
            )
        ],
        axis=0,
    )
    leave(6)

    def step_back_out(k, _):
        dz = get(gm, k) * alpha_o - get(zo, k) * slant_o - jnp.where(kept(k, model), level_o, 0.0)
        dz = dz.astype(bf)
        put(gatt, k, dot_nt(dz, wo) * get(slope_att, k).astype(f32))
        part = pl.ds(k * group, group)
        copy(gatt.at[part], gatt_out.at[part], 8 + 2 * chunks + k).start()
        return 0

    over(step_back_out, 0)
    grad_out[2][...] = down_sum.gathered()
    leave(5)
    down_sum.settle((0, 1))
    grad_out[1][...] = up_sum.gathered()
    leave(4)
    up_sum.settle((0, 1))

    for k, stat in enumerate((stat_o, stat_u, stat_d, stat_bu, stat_bo)):
        place.settle(stat, send.at[k])
    gram_sum.settle()
    gather_settle(place, wd_buf, send_g.at[0], send_g.at[1])

    def finish(k, _):
        part = pl.ds(k * group, group)
        copy(gm.at[part], gm_out.at[part], 8 + chunks + k).wait()
        copy(gatt.at[part], gatt_out.at[part], 8 + 2 * chunks + k).wait()
        return 0

    over(finish, 0)
    out_copy.wait()


def half_steps(shape):
    halved = pltpu.VMEM(shape[:2] + (shape[2] // 2,), jnp.bfloat16)
    return [pltpu.VMEM(shape, jnp.bfloat16)] + [halved] * 3 + [pltpu.SemaphoreType.DMA((2,))] * 2


def middle_call(dp_size, fs_size, classes, attended, xs, cotangent, weights, vec, gram):
    full = (fs_size,) + weights[2].shape
    images, model, feature, hidden = xs.shape[0], xs.shape[2], attended.shape[2], weights[1].shape[2]
    group = 2 if images % 2 == 0 else 1
    chunks = images // group
    devices = dp_size * fs_size
    own = model // fs_size
    bf, f32 = jnp.bfloat16, jnp.float32

    def rows(width, kind):
        return pltpu.VMEM((images, ROWS, width), kind)

    out_shape = (
        [
            jax.ShapeDtypeStruct(cotangent.shape, bf),
            jax.ShapeDtypeStruct((images, ROWS, feature), bf),
            jax.ShapeDtypeStruct((images, ROWS, model), f32),
        ]
        + [jax.ShapeDtypeStruct(weights[0].shape, bf)]
        + [jax.ShapeDtypeStruct((s[1], s[2] // 2), bf) for s in (weights[1].shape, full)]
        + [jax.ShapeDtypeStruct((8, hidden), f32), jax.ShapeDtypeStruct((own, model), f32)]
    )
    args = (classes, attended, xs, cotangent, *weights, vec, gram)
    ins, outs = (6, 7, 8), (3, 4, 5, 6, 7)
    return pl.pallas_call(
        staged(functools.partial(middle_kernel, dp_size, fs_size, group), ins, outs, len(args)),
        out_shape=out_shape,
        in_specs=[SMEM] + [ANY] * 8,
        out_specs=[ANY] * 8,
        scratch_shapes=[
            rows(feature, bf),
            rows(model, bf),
            pltpu.VMEM(cotangent.shape, bf),
        ]
        + [pltpu.VMEM(w.shape, bf) for w in weights[:2]]
        + [pltpu.VMEM(full, bf)]
        + [
            rows(model, bf),
            rows(feature, bf),
            rows(feature, bf),
            rows(model, f32),
            rows(model, bf),
            rows(hidden, f32),
            rows(hidden, bf),
            rows(hidden, bf),
            rows(model, f32),
            rows(model, bf),
            rows(hidden, f32),
            rows(model, f32),
            pltpu.VMEM(cotangent.shape, bf),
            rows(feature, bf),
            pltpu.VMEM((model // 128, images * ROWS, 128), f32),
            pltpu.VMEM((devices, 3, model), f32),
            pltpu.VMEM((devices, 2, hidden), f32),
            pltpu.VMEM((devices, 4, model), f32),
            pltpu.VMEM((devices, 2, hidden), f32),
            pltpu.VMEM((devices, 2, model), f32),
            pltpu.SemaphoreType.DMA((5,)),
            pltpu.SemaphoreType.DMA((5,)),
            pltpu.SemaphoreType.DMA((8 + 3 * chunks,)),
            pltpu.VMEM((fs_size, own, model), bf),
        ]
        + [pltpu.VMEM((fs_size, own, model // 2), bf)] * 3
        + [
            pltpu.VMEM((dp_size, own, model // 2), bf),
            pltpu.SemaphoreType.DMA((3,)),
            pltpu.SemaphoreType.DMA((3,)),
        ]
        + half_steps(full)
        + half_steps(weights[1].shape)
        + [pltpu.SemaphoreType.DMA((2,))] * 2
        + stage_scratch(ins, outs, args, out_shape),
        compiler_params=pltpu.CompilerParams(
            collective_id=1, has_side_effects=True, vmem_limit_bytes=58 * 2**20
        ),
    )(*args)


def last_kernel(dp_size, fs_size, group, arrive, leave, *refs):
    class_ref, xs_in, gmix_in, gm_in, places = refs[:5]
    acc_in, grad_in, part_in = refs[5:8], refs[8:9], refs[9:11]
    wq_buf, raw_ref, sum_ref, gram_ref, vec_ref, lines_ref = refs[11:17]
    ig_out, table_out, own_out, vec_out = refs[17], refs[18], refs[19:23], refs[23]
    refs = refs[:27] + (None,) + refs[27:]
    xs, gmix, gm, _, ig, res = refs[24:30]
    acc, full = refs[30:33], refs[33:35]
    steps = [refs[35 + 4 * k : 39 + 4 * k] for k in range(2)]
    thirds = refs[43:45]
    stat, stat_t, stat_c, stat_tc = refs[45:49]
    send, recv, local, send_r, recv_r = refs[49:54]
    place = Place(dp_size, fs_size)
    images = xs.shape[0]
    chunks = images // group
    size = group * ROWS
    f32, bf = jnp.float32, jnp.bfloat16
    model, width = xs.shape[2], gmix.shape[2]

    def copy(source, target, at):
        return pltpu.make_async_copy(source, target, local.at[at])

    grad_loads = [copy(grad_in[k], full[1 + k], k) for k in range(1)]
    mix_load = copy(gmix_in, gmix, 3)
    table_loads = [copy(acc_in[k], acc[k], 5 + k) for k in range(3)]
    late_loads = [copy(xs_in, xs, 8), copy(gm_in, gm, 9)]
    place.greet()
    for load in grad_loads + [mix_load] + table_loads + late_loads:
        load.start()
    reduces = [Reduce(place, full[k], *steps[k], send_r.at[k], recv_r.at[k]) for k in range(2)]
    shared = [
        Reduce(place, None, None, thirds[k], None, thirds[k], send_r.at[2 + k], recv_r.at[2 + k]) for k in range(2)
    ]

    def get(ref, k):
        return ref[pl.ds(k * group, group)].reshape(size, ref.shape[2])

    def put(ref, k, value):
        ref[pl.ds(k * group, group)] = value.astype(ref.dtype).reshape(group, ROWS, ref.shape[2])

    def kept(k, lanes):
        row = lax.broadcasted_iota(jnp.int32, (ROWS, lanes), 0)
        return jnp.concatenate([row < limits_of(class_ref[k * group + j]) for j in range(group)], axis=0)

    arrive(11, 12, 13, 15, 16)
    total = vec_ref[10:11, :1]
    gain, scale, center = vec_ref[0:1, :], vec_ref[8:9, :], vec_ref[9:10, :]
    x_mean = lines_ref[6:7, :model]
    weight = flat_weight(wq_buf)
    weight_f = weight.astype(f32)
    raw = raw_ref[...]
    grad_sum = total_rows(sum_ref[...])
    grad_z = total_rows(raw * weight_f)
    full[0][...] = (raw - outer(x_mean, grad_sum)).reshape(full[0].shape).astype(bf)
    for load in grad_loads:
        load.wait()
    place.meet()
    reduces[0].swap()
    place.spread_pair(stat, jnp.concatenate([grad_sum, grad_z], axis=0), send.at[0], recv.at[0])
    reduces[1].swap()
    alpha = scale * gain
    place.spread_chips(stat_c, place.collect_pair(stat, recv.at[0]), send.at[2], recv.at[2])
    for k in range(2):
        reduces[k].scatter()
    arrive(9, 10)
    for k in range(2):
        shared[k].share(part_in[k][...])
    for load in table_loads:
        load.wait()
    arrive(4, 14)
    place.spread_pair(stat_t, table_sums(places[...], acc), send.at[1], recv.at[1])
    mix_load.wait()
    for k in range(chunks):
        put(ig, k, dot_nt((get(gmix, k).astype(f32) * alpha).astype(bf), weight))
    place.spread_chips(stat_tc, place.collect_pair(stat_t, recv.at[1]), send.at[3], recv.at[3])
    for load in late_loads:
        load.wait()

    got = place.collect_chips(stat_c, recv.at[2])
    gain_grad, alpha, slant, level = back_parts(got[0:1], got[1:2], total, gain, center, scale)
    mix = dot_nt((weight_f * slant).astype(bf), weight).astype(bf)
    high, rest = split_low(jnp.broadcast_to(level, (8, width)))
    lift = (dot_nt(high, weight) + dot_nt(rest, weight))[:1]
    vec_out[...] = jnp.concatenate(
        [restore(gain_grad), restore(got[0:1]), jnp.zeros((6, width), f32)], axis=0
    )
    leave(6)
    for k in range(2):
        reduces[k].share()
    for k in range(chunks):
        value = get(gm, k) + get(ig, k) - dot_nn(get(xs, k), mix) - jnp.where(kept(k, model), lift, 0.0)
        for j in range(group):
            put_image(res, k * group + j, images, value[j * ROWS : (j + 1) * ROWS])
    res_copies = [copy(res.at[k, pl.ds(0, SLOT * images)], ig_out.at[:, pl.ds(128 * k, 128)], 10 + k) for k in range(model // 128)]
    for res_copy in res_copies:
        res_copy.start()
    own_out[0][...] = restore(reduces[0].result() * alpha - precise(gram_ref[...], weight) * slant)
    own_out[1][...] = reduces[1].result()
    for k in range(2):
        own_out[2 + k][...] = shared[k].result()
    table_out[...] = place.collect_chips(stat_tc, recv.at[3])
    for k in range(2):
        reduces[k].settle()
        shared[k].settle((2,))
    place.settle_pair(stat, send.at[0])
    place.settle_pair(stat_t, send.at[1])
    place.settle_chips(stat_c, send.at[2])
    place.settle_chips(stat_tc, send.at[3])
    for res_copy in res_copies:
        res_copy.wait()


def last_call(dp_size, fs_size, classes, xs, gmix, gm, places, accs, grads, wq, raw, sums, gram, vec, lines):
    images, model, width = xs.shape[0], xs.shape[2], gmix.shape[2]
    group = 2 if images % 2 == 0 else 1
    devices = dp_size * fs_size
    bf, f32 = jnp.bfloat16, jnp.float32
    shapes = [wq.shape, grads[0].shape]
    own_shapes = [s[1:] for s in shapes] + [(g.shape[0], 2 * g.shape[1]) for g in grads[1:]]
    steps = []
    for s in shapes:
        half = s[2] // 2
        steps += [
            pltpu.VMEM((fs_size, s[1], half), bf),
            pltpu.VMEM((fs_size, s[1], half), bf),
            pltpu.VMEM((fs_size, s[1], half), bf),
            pltpu.VMEM((dp_size, s[1], half), bf),
        ]
    order = []
    for k in range(2):
        order += [steps[4 * k], steps[4 * k + 1], steps[4 * k + 2], steps[4 * k + 3]]
    out_shape = (
        [jax.ShapeDtypeStruct((SLOT * images, model), f32), jax.ShapeDtypeStruct((HEADS, 384), f32)]
        + [jax.ShapeDtypeStruct(s, f32) for s in own_shapes]
        + [jax.ShapeDtypeStruct((8, width), f32)]
    )
    args = (classes, xs, gmix, gm, places, *accs, *grads, wq, raw, sums, gram, vec, lines)
    ins, outs = (13, 15, 16, 11, 12, 9, 10, 4, 14), (1, 2, 3, 4, 5, 6)
    return pl.pallas_call(
        staged(functools.partial(last_kernel, dp_size, fs_size, group), ins, outs, len(args)),
        out_shape=out_shape,
        in_specs=[SMEM] + [ANY] * 16,
        out_specs=[ANY] * 7,
        scratch_shapes=[
            pltpu.VMEM(xs.shape, bf),
            pltpu.VMEM(gmix.shape, bf),
            pltpu.VMEM(gm.shape, f32),
            pltpu.VMEM(gm.shape, f32),
            pltpu.VMEM((model // 128, images * ROWS, 128), f32),
        ]
        + [pltpu.VMEM(a.shape, bf) for a in accs]
        + [pltpu.VMEM(s, bf) for s in shapes]
        + order
        + [
            pltpu.VMEM((dp_size,) + grads[1].shape, bf),
            pltpu.VMEM((dp_size,) + grads[2].shape, bf),
            pltpu.VMEM((2, 2, width), f32),
            pltpu.VMEM((2, HEADS, 384), f32),
            pltpu.VMEM((devices // 2, 2, width), f32),
            pltpu.VMEM((devices // 2, HEADS, 384), f32),
            pltpu.SemaphoreType.DMA((4,)),
            pltpu.SemaphoreType.DMA((4,)),
            pltpu.SemaphoreType.DMA((10 + model // 128,)),
            pltpu.SemaphoreType.DMA((4, 3)),
            pltpu.SemaphoreType.DMA((4, 3)),
        ]
        + stage_scratch(ins, outs, args, out_shape),
        compiler_params=pltpu.CompilerParams(
            collective_id=2, has_side_effects=True, vmem_limit_bytes=56 * 2**20
        ),
    )(*args)

def shards(
    inputs,
    classes,
    offset_table,
    bias_table,
    qkv_weight,
    qkv_gain,
    qkv_shift,
    out_weight,
    out_gain,
    out_shift,
    up_weight,
    up_gain,
    up_shift,
    down_weight,
    down_gain,
    down_shift,
    cotangent,
):
    sizes = lax.axis_size("dp"), lax.axis_size("fsdp")
    images, _, model = inputs.shape

    def by_slot(array):
        return jnp.swapaxes(array, 0, 1).reshape(SLOT * images, model)

    def by_image(array):
        return jnp.swapaxes(array.reshape(SLOT, images, model), 0, 1)

    first = first_call(
        *sizes,
        classes,
        by_slot(inputs),
        offset_table,
        bias_table,
        (qkv_weight, out_weight, up_weight),
        (qkv_gain, qkv_shift, out_gain, out_shift, up_gain, up_shift, down_gain, down_shift),
    )
    mixed, xs, biases, weights, vec, gram, places = first[0], first[1], first[2:5], first[5:8], *first[8:11]
    attended, probs, shares = attend_call(classes, mixed, biases)
    middle = middle_call(*sizes, classes, attended, xs, by_slot(cotangent), (*weights[1:], down_weight), vec, gram)
    output, grad_att, grad_middle, grads, lines, own_gram = *middle[:3], middle[3:6], middle[6], middle[7]
    back = back_call(sizes[1], classes, mixed, probs, shares, grad_att, attended, xs, lines, output)
    grad_mixed, raw, sums, accs, own_lines, output = *back[:3], back[3:6], back[6:12], back[12]
    last = last_call(
        *sizes,
        classes,
        xs,
        grad_mixed,
        grad_middle,
        places,
        accs,
        grads,
        weights[0],
        raw,
        sums,
        own_gram,
        vec,
        lines,
    )
    input_grad, table_grad, *rest = end_call(sizes[1], last[0], last[1], last[2:6], last[6])
    own_lines = [line.reshape(-1) for line in (*own_lines, *rest[4:])]
    return (
        by_image(output),
        by_image(input_grad),
        table_grad,
        rest[0],
        *own_lines[6:8],
        rest[1],
        *own_lines[0:2],
        rest[2],
        *own_lines[2:4],
        rest[3],
        *own_lines[4:6],
    )


def solution(mesh):
    placed = (
        P(("dp", "fsdp"), None, None),
        P(("dp", "fsdp")),
        P(),
        P(),
        P("fsdp", None),
        P("fsdp"),
        P("fsdp"),
        P("fsdp", None),
        P("fsdp"),
        P("fsdp"),
        P("fsdp", None),
        P("fsdp"),
        P("fsdp"),
        P("fsdp", None),
        P("fsdp"),
        P("fsdp"),
        P(("dp", "fsdp"), None, None),
    )
    return jax.shard_map(
        shards,
        mesh=mesh,
        in_specs=placed,
        out_specs=(
            P(("dp", "fsdp"), None, None),
            P(("dp", "fsdp"), None, None),
            P(),
            P("fsdp", None),
            P("fsdp"),
            P("fsdp"),
            P("fsdp", None),
            P("fsdp"),
            P("fsdp"),
            P("fsdp", None),
            P("fsdp"),
            P("fsdp"),
            P("fsdp", None),
            P("fsdp"),
            P("fsdp"),
        ),
        check_vma=False,
    )
```
